32 devices in a mesh: fsdp: 8 (over z, y), rep: 4 (over x, core).
Axes of the slice: x: 2, y: 2, z: 4, core: 2. Of those that a mesh axis runs over, the one named last changes fastest.
Arguments:
- tokens: bfloat16 [2, 4096, 2048], P(None, ('fsdp', 'rep')), may hold values from -6 to 6
- segment_ids: int32 [2, 32, 128], P(None, ('fsdp', 'rep')), may hold values from 0 to 2, never falling along the last dimension, each value on 1 to 64 neighbouring positions
- out_grad: bfloat16 [2, 4096, 2048], P(None, ('fsdp', 'rep')), may hold values from -6 to 6
- norm_gain: bfloat16 [2048], P('fsdp'), may hold values from 0.25 to 1.75
- in_proj: bfloat16 [2048, 8192], P('fsdp'), may hold values from -0.125 to 0.125
- conv_weight: bfloat16 [4096, 4], P('fsdp'), may hold values from -3 to 3
- conv_bias: bfloat16 [4096], P('fsdp'), may hold values from -3 to 3
- x_proj: bfloat16 [4096, 160], P('fsdp'), may hold values from -0.09375 to 0.09375
- step_proj: bfloat16 [4096, 128], P('fsdp'), may hold values from -0.5 to 0.5
- step_bias: bfloat16 [4096], P('fsdp'), may hold values from -4 to -1
- decay_log: bfloat16 [4096, 16], P('fsdp'), may hold values from -1 to 2.5
- skip_gain: bfloat16 [4096], P('fsdp'), may hold values from 0.5 to 1.5
- out_proj: bfloat16 [4096, 2048], P('fsdp'), may hold values from -0.375 to 0.375
Outputs:
- block_out: bfloat16 [2, 4096, 2048], P(None, ('fsdp', 'rep'))
- input_grad: bfloat16 [2, 4096, 2048], P(None, ('fsdp', 'rep'))
- gain_grad: float32 [2048], P('fsdp')
- in_proj_grad: float32 [2048, 8192], P('fsdp')
- conv_weight_grad: float32 [4096, 4], P('fsdp')
- conv_bias_grad: float32 [4096], P('fsdp')
- x_proj_grad: float32 [4096, 160], P('fsdp')
- step_proj_grad: float32 [4096, 128], P('fsdp')
- step_bias_grad: float32 [4096], P('fsdp')
- decay_log_grad: float32 [4096, 16], P('fsdp')
- skip_gain_grad: float32 [4096], P('fsdp')
- out_proj_grad: float32 [4096, 2048], P('fsdp')
The draws below stay inside these ranges and needn't reach their ends.
Inputs may be any that keep to these rules, and one draw needn't show every extreme that they name: `segment_ids`: segment numbers never fall along a sequence; each change starts a new document.
All inputs are finite; a program needn't handle non-finite values.
Results may differ from the reference program's by a relative error of at most 0.012.
Values may be sent and summed in bfloat16 or wider, within the bound.
A program may use at most 240 MiB of HBM per device.

```python
import math
import jax
import jax.numpy as jnp
import numpy as np
from jax import lax

D = 2048
DI = 4096
NSTATE = 16
RANK = 128
KCONV = 4
SEQ = 128
MB = 2
BLOCK = 16
NSEQ = 32
TOKENS = 4096


def raised(drawn, stream_key, source, target, parts, factor):
    def block_of(position):
        return (jnp.arange(drawn.shape[position]) // (drawn.shape[position] // parts)).reshape((-1,) + (1,) * (drawn.ndim - 1 - position))

    near = jax.random.permutation(stream_key, parts)[block_of(target)]
    other_side = (block_of(target) + parts // 2) % parts
    return jnp.where((block_of(source) == near) | (block_of(source) == other_side), factor * drawn, drawn)


def levels(stream_key, extent, split, least, high):
    def one(axis_at, blocks):
        heights = jax.random.uniform(jax.random.fold_in(jax.random.fold_in(stream_key, 6), axis_at), (blocks,), jnp.float32, least / len(split), high / len(split))
        return jnp.repeat(jnp.exp(heights), extent[axis_at] // blocks).reshape((-1,) + (1,) * (len(extent) - axis_at - 1))

    factor_of = one(*split[0])
    for cut in split[1:]:
        factor_of = factor_of * one(*cut)
    return factor_of


def split_up(amount, total, limit, slope):
    weights = [(1 << 20) // math.isqrt(grade ** slope) + 1 for grade in range(2, amount + 1)]
    surplus, given = total - limit - (amount - 1), [1] * (amount - 1)
    while surplus > 0:
        candidates = [i for i in range(amount - 1) if given[i] < limit]
        mass, budget = sum([weights[i] for i in candidates]), surplus
        for i in candidates:
            addition = min(limit - given[i], max(1, budget * weights[i] // mass), surplus)
            given[i] = given[i] + addition
            surplus = surplus - addition
    return np.array([limit] + given)


def uneven(stream_key, number_of, total, most, slope):
    if number_of == 2:
        one = jax.random.randint(stream_key, (), max(1, total - most), min(most, total - 1) + 1)
        return jnp.stack([one, total - one])
    lengths = jnp.asarray(split_up(number_of, total, most, slope), jnp.int32)
    twos = (number_of - 1) // 2
    giver, taker = lengths[1:1 + 2 * twos:2], lengths[2:2 + 2 * twos:2]
    margin = jnp.minimum(giver - 1, most - taker)
    shifted = jax.random.randint(jax.random.fold_in(stream_key, 1), (twos,), 0, 1 << 20) % (margin + 1)
    lengths = lengths.at[1:1 + 2 * twos:2].set(giver - shifted).at[2:2 + 2 * twos:2].set(taker + shifted)
    return lengths[jax.random.permutation(jax.random.fold_in(stream_key, 2), number_of)]


def noise(key, shape, scale, limit, cuts=(), kind=jnp.bfloat16):
    values = scale * jax.random.normal(key, shape, jnp.float32)
    if cuts:
        values = values * levels(key, shape, cuts, -0.22, 0.18)
    return jnp.clip(values, -limit, limit).astype(kind)


def gaussian_with(stream_key, extent, scale, limit, cuts, heavy, dtype=jnp.bfloat16):
    values = scale * jax.random.normal(stream_key, extent, jnp.float32)
    if cuts:
        values = values * levels(stream_key, extent, cuts, -0.22, 0.18)
    return jnp.clip(raised(values, jax.random.fold_in(stream_key, 3), *heavy), -limit, limit).astype(dtype)


def setup_inputs(seed: int = 0) -> dict:
    splits = jax.random.split(jax.random.key(seed), 14)
    return {
        "tokens": gaussian_with(splits[0], (MB, TOKENS, D), 1.0, 6.0, ((1, 32),), (1, 2, 32, 2.75)),
        "segment_ids": jax.vmap(lambda own: jnp.searchsorted(jnp.cumsum(uneven(own, 3, SEQ, SEQ // 2, 0)), jnp.arange(SEQ), side="right"))(jax.random.split(splits[1], MB * NSEQ)).reshape((MB, NSEQ, SEQ)).astype(jnp.int32),
        "out_grad": noise(splits[2], (MB, TOKENS, D), 1.0, 6.0, ((1, 32),)),
        "norm_gain": jnp.clip(1.0 + 0.15 * jax.random.normal(splits[3], (D,), jnp.float32), 0.25, 1.75).astype(jnp.bfloat16),
        "in_proj": noise(splits[4], (D, 2 * DI), D ** -0.5, 0.125, ((0, 8),)),
        "conv_weight": noise(splits[5], (DI, KCONV), KCONV ** -0.5, 3.0, ((0, 8),)),
        "conv_bias": noise(splits[6], (DI,), 0.5, 3.0, ((0, 8),)),
        "x_proj": noise(splits[7], (DI, RANK + 2 * NSTATE), DI ** -0.5, 0.09375, ((0, 8),)),
        "step_proj": noise(splits[8], (DI, RANK), RANK ** -0.5, 0.5, ((0, 8),)),
        "step_bias": jnp.clip(-4.0 + 3.0 * jax.random.uniform(splits[9], (DI,), jnp.float32) ** levels(splits[9], (DI,), ((0, 8),), -0.2, 0.2), -4.0, -1.0).astype(jnp.bfloat16),
        "decay_log": jnp.clip(-1.0 + 3.5 * jax.random.uniform(splits[10], (DI, NSTATE), jnp.float32) ** levels(splits[10], (DI, NSTATE), ((0, 8),), -0.2, 0.2), -1.0, 2.5).astype(jnp.bfloat16),
        "skip_gain": jnp.clip(0.5 + 1.0 * jax.random.uniform(splits[11], (DI,), jnp.float32) ** levels(splits[11], (DI,), ((0, 8),), -0.2, 0.2), 0.5, 1.5).astype(jnp.bfloat16),
        "out_proj": noise(splits[12], (DI, D), (DI // 16) ** -0.5, 0.375, ((0, 8),)),
    }


EPS = 1e-05
HIGH = lax.Precision.HIGHEST

@jax.custom_vjp
def low(v):
    return lax.optimization_barrier(v.astype(jnp.bfloat16)).astype(jnp.float32)

@jax.custom_vjp
def low_back(v):
    return v

def low_keep(v):
    return (low(v), None)

def low_pass(kept, grad):
    return (grad,)

def back_keep(v):
    return (v, None)

def back_low(kept, grad):
    return (low(grad),)
low.defvjp(low_keep, low_pass)
low_back.defvjp(back_keep, back_low)

def normalize(values, gain):
    scale = lax.rsqrt(lax.optimization_barrier(jnp.mean(values * values, axis=-1, keepdims=True)) + EPS)
    return values * scale * gain

def convolve(inner, segments, weight, bias):
    width = weight.shape[1]
    length = inner.shape[1]
    total = bias + weight[:, width - 1] * inner
    for shift in range(1, width):
        moved = jnp.pad(inner, ((0, 0), (shift, 0), (0, 0)))[:, :length]
        earlier = jnp.pad(segments, ((0, 0), (shift, 0)), constant_values=-1)[:, :length]
        same = (earlier == segments).astype(jnp.float32)
        total = total + weight[:, width - 1 - shift] * moved * same[:, :, None]
    return total

def keep_mask(segments):
    length = segments.shape[1]
    earlier = jnp.pad(segments, ((0, 0), (1, 0)), constant_values=-1)[:, :length]
    return (earlier == segments).astype(jnp.float32)

def selective(step_size, activated, write_coef, read_coef, keep_flag, decay_rate):
    groups, length, inner_width = step_size.shape
    nstate = decay_rate.shape[1]
    blocks = length // BLOCK
    rate_rows = jnp.transpose(decay_rate)

    def advance(states, pieces):
        size_part, act_part, write_part, read_part, keep_part = pieces
        outputs = []
        for offset in range(BLOCK):
            step_now = size_part[:, offset]
            decay = jnp.exp(step_now[:, None, :] * rate_rows[None])
            inflow = write_part[:, offset][:, :, None] * (step_now * act_part[:, offset])[:, None, :]
            states = decay * (keep_part[:, offset][:, None, None] * states) + inflow
            outputs.append(lax.optimization_barrier(jnp.sum(read_part[:, offset][:, :, None] * states, axis=1)))
        return (states, jnp.stack(outputs, axis=1))

    def blocked(values):
        return jnp.moveaxis(values.reshape(groups, blocks, BLOCK, *values.shape[2:]), 1, 0)
    start = jnp.zeros((groups, nstate, inner_width), jnp.float32)
    _, readout = lax.scan(jax.checkpoint(advance), start, (blocked(step_size), blocked(activated), blocked(write_coef), blocked(read_coef), blocked(keep_flag)))
    return jnp.moveaxis(readout, 0, 1).reshape(groups, length, inner_width)

def mix_branch(step_pre, coefs, activated, gate, step_bias, decay_log, skip_gain, keep_flag):
    nstate = decay_log.shape[1]
    step_size = jax.nn.softplus(step_pre + step_bias)
    readout = selective(step_size, activated, coefs[..., :nstate], coefs[..., nstate:], keep_flag, -jnp.exp(decay_log))
    return (readout + skip_gain * activated) * jax.nn.silu(gate)

def forward(values, segments, gain, in_proj, conv_weight, conv_bias, x_proj, step_proj, step_bias, decay_log, skip_gain, out_proj):
    inner_width = in_proj.shape[1] // 2
    rank = step_proj.shape[1]
    normed = low(normalize(values, gain))
    mixed = low_back(jnp.einsum('gld,de->gle', normed, in_proj, precision=HIGH))
    activated = jax.nn.silu(convolve(mixed[..., :inner_width], segments, conv_weight, conv_bias))
    projected = low_back(jnp.einsum('gli,ie->gle', low(activated), x_proj, precision=HIGH))
    step_low = low(projected[..., :rank])
    step_pre = low_back(jnp.einsum('glr,ir->gli', step_low, step_proj, precision=HIGH))
    gated = low(mix_branch(step_pre, projected[..., rank:], activated, mixed[..., inner_width:], step_bias, decay_log, skip_gain, keep_mask(segments)))
    return values + jnp.einsum('gli,id->gld', gated, out_proj, precision=HIGH)

def reference(tokens, segment_ids, out_grad, norm_gain, in_proj, conv_weight, conv_bias, x_proj, step_proj, step_bias, decay_log, skip_gain, out_proj):
    total_seqs = MB * NSEQ
    per_group = math.gcd(total_seqs, max(1, 2048 // SEQ))
    count = total_seqs // per_group
    inputs = tokens.reshape(count, per_group, SEQ, D)
    segments = segment_ids.reshape(count, per_group, SEQ)
    cotangents = out_grad.reshape(count, per_group, SEQ, D)
    params = tuple((p.astype(jnp.float32) for p in (norm_gain, in_proj, conv_weight, conv_bias, x_proj, step_proj, step_bias, decay_log, skip_gain, out_proj)))

    def group_step(totals, item):
        values, seg_rows, cotangent = item

        def apply(vals, weights):
            return forward(vals, seg_rows, *weights)
        result, pull = jax.vjp(apply, values.astype(jnp.float32), params)
        value_grad, weight_grads = pull(cotangent.astype(jnp.float32))
        totals = tuple((a + b for a, b in zip(totals, weight_grads)))
        return (totals, (result.astype(jnp.bfloat16), value_grad.astype(jnp.bfloat16)))
    zeros = tuple((jnp.zeros_like(p) for p in params))
    grads, (results, value_grads) = lax.scan(group_step, zeros, (inputs, segments, cotangents))
    return (results.reshape(MB, TOKENS, D), value_grads.reshape(MB, TOKENS, D), grads[0], grads[1], grads[2], grads[3], grads[4], grads[5], grads[6], grads[7], grads[8], grads[9])
```

```python
import functools

import jax
import jax.numpy as jnp
from jax import lax
from jax.experimental import pallas as pl
from jax.experimental.pallas import tpu as pltpu
from jax.sharding import PartitionSpec as P

EPS = 1e-05
BLOCK = 16
LANES = 128
GROUP = 8
COPIES = 4
LOG2E = 1.4426950408889634
LN2 = 0.6931471805599453
FAR = 1e30
F32 = jnp.float32
BF16 = jnp.bfloat16
VMEM_LIMIT = 56 * 1024 * 1024


def dot(left, right, left_dim, right_dim):
    return lax.dot_general(
        left, right, (((left_dim,), (right_dim,)), ((), ())), preferred_element_type=F32
    )


def params():
    return pltpu.CompilerParams(vmem_limit_bytes=VMEM_LIMIT)


def cost(flops, moved):
    return pl.CostEstimate(flops=int(flops), bytes_accessed=int(moved), transcendentals=0)


def ring_order(size):
    half = size // 2
    return [2 * p if p < half else 2 * (size - 1 - p) + 1 for p in range(size)]


class Ring:
    def __init__(self, size):
        order = ring_order(size)
        place = [0] * size
        for spot, member in enumerate(order):
            place[member] = spot
        self.size, self.half = size, size // 2
        self.order = jnp.array(order, jnp.int32)
        self.spot = jnp.array(place, jnp.int32)[lax.axis_index("fsdp")]
        self.above = [(order[p], order[(p + 1) % size]) for p in range(size)]
        self.below = [(order[p], order[(p - 1) % size]) for p in range(size)]

    def member(self, offset):
        return self.order[(self.spot + offset + self.size) % self.size]

    def up(self, value):
        return lax.ppermute(value, "fsdp", self.above)

    def down(self, value):
        return lax.ppermute(value, "fsdp", self.below)


class Gather:
    def __init__(self, ring, shard):
        self.ring, self.cut = ring, shard.shape[0] // 2
        self.whole = jnp.zeros((ring.size,) + shard.shape, shard.dtype)
        self.held = (shard, shard)
        self.put(shard, 0)

    def put(self, piece, offset, start=0):
        at = (self.ring.member(offset), jnp.int32(start), jnp.int32(0))
        self.whole = lax.dynamic_update_slice(self.whole, piece[None], at)

    def step(self, number):
        low, high = self.held
        if number == self.ring.half:
            low, high = low[: self.cut], high[self.cut :]
        return self.ring.up(low), self.ring.down(high)

    def take(self, number, got):
        self.held = got
        last = number == self.ring.half
        self.put(got[0], -number)
        self.put(got[1], number, self.cut if last else 0)

    def rest(self):
        def body(number, state):
            whole, low, high = state
            low, high = self.ring.up(low), self.ring.down(high)
            self.whole = whole
            self.put(low, -number)
            self.put(high, number)
            return self.whole, low, high

        self.whole, low, high = lax.fori_loop(1, self.ring.half, body, (self.whole,) + self.held)
        self.held = (low, high)
        self.take(self.ring.half, self.step(self.ring.half))


class Scatter:
    def __init__(self, ring, parts):
        self.ring, self.parts, self.cut = ring, parts, parts.shape[1] // 2
        far = self.own(ring.half)
        self.sent = (far[: self.cut], far[self.cut :])
        self.total = None

    def own(self, offset):
        return lax.dynamic_index_in_dim(self.parts, self.ring.member(offset), 0, keepdims=False)

    def step(self, number):
        return self.ring.up(self.sent[0]), self.ring.down(self.sent[1])

    def take(self, number, got):
        left = self.ring.half - number
        low, high = got
        near_low, near_high = self.own(left), self.own(-left)
        if number == 1:
            low = jnp.concatenate([low, jnp.zeros_like(near_low[self.cut :])])
            high = jnp.concatenate([jnp.zeros_like(near_high[: self.cut]), high])
        if left == 0:
            self.total = near_low.astype(F32) + low.astype(F32) + high.astype(F32)
        else:
            self.sent = (self.add(near_low, low), self.add(near_high, high))

    def add(self, near, got):
        return (near.astype(F32) + got.astype(F32)).astype(near.dtype)

    def rest(self):
        self.take(1, self.step(1))

        def body(number, sent):
            left = self.ring.half - number
            low, high = self.ring.up(sent[0]), self.ring.down(sent[1])
            return self.add(self.own(left), low), self.add(self.own(-left), high)

        self.sent = lax.fori_loop(2, self.ring.half, body, self.sent)
        self.take(self.ring.half, self.step(self.ring.half))


def slot(number, movers, *work):
    moved = tuple(m.step(number) for m in movers)
    done = tuple(w() for w in work)
    moved, done = lax.optimization_barrier((moved, done))
    for mover, got in zip(movers, moved):
        mover.take(number, got)
    return done


def swap(value, bit):
    return lax.ppermute(value, "rep", [(r, r ^ bit) for r in range(COPIES)])


def rep_gather(value):
    across = swap(value, 2)
    return [value, swap(value, 1), across, swap(across, 1)]


def rep_scatter_near(parts):
    pair = swap(jnp.stack([parts[1], parts[3]]), 1)
    near = parts[0].astype(F32) + pair[0].astype(F32)
    far = parts[2].astype(F32) + pair[1].astype(F32)
    return near, far.astype(parts.dtype)


def rep_scatter_far(near, far):
    return near + swap(far, 2).astype(F32)


def sum_near(parts):
    pair = swap(jnp.stack([parts[1], parts[3]]), 1)
    mine = jnp.stack([parts[0], parts[2]]) + pair
    return mine + swap(jnp.stack([mine[1], mine[0]]), 2)


def sum_far(mine):
    next_to = swap(mine, 1)
    return jnp.stack([mine[0], next_to[0], mine[1], next_to[1]])


def by_copy(value, batches):
    split = value.reshape(-1, COPIES, batches, value.shape[-1])
    return jnp.moveaxis(split, 1, 0)


def by_row(value):
    return jnp.moveaxis(value, 0, 1).reshape(-1, value.shape[-1])


def sigmoid(value):
    return 1.0 / (1.0 + jnp.exp(-value))


def later(value, shift):
    rows = shift * GROUP
    return jnp.concatenate([jnp.zeros_like(value[:rows]), value[:-rows]], axis=0)


def sooner(value, shift):
    rows = shift * GROUP
    return jnp.concatenate([value[rows:], jnp.zeros_like(value[:rows])], axis=0)


def conv_of(inner, masks, taps):
    total = taps[4:5] + taps[3:4] * inner
    for shift in range(1, 4):
        total = total + taps[3 - shift : 4 - shift] * (later(inner, shift) * masks[shift - 1])
    return total


def conv_kernel(inner_ref, masks_ref, taps_ref, act_ref, low_ref):
    value = conv_of(inner_ref[...], masks_ref, taps_ref[...])
    act = value * sigmoid(value)
    act_ref[...] = act
    low_ref[...] = act.astype(BF16)


def conv_forward(inner, masks, taps):
    rows, width = inner.shape
    tile = pl.BlockSpec((rows, LANES), lambda c: (0, c))
    return pl.pallas_call(
        conv_kernel,
        grid=(width // LANES,),
        in_specs=[
            tile,
            pl.BlockSpec((3, rows, LANES), lambda c: (0, 0, 0)),
            pl.BlockSpec((8, LANES), lambda c: (0, c)),
        ],
        out_specs=[tile, tile],
        out_shape=[
            jax.ShapeDtypeStruct((rows, width), F32),
            jax.ShapeDtypeStruct((rows, width), BF16),
        ],
        compiler_params=params(),
        cost_estimate=cost(30 * rows * width, 10 * rows * width),
        name="conv_forward",
    )(inner, masks, taps)


def conv_back_kernel(inner_ref, grad_ref, masks_ref, taps_ref, out_ref, sums_ref):
    inner, taps = inner_ref[...], taps_ref[...]
    value = conv_of(inner, masks_ref, taps)
    gate = sigmoid(value)
    grad = grad_ref[...] * (gate * (1.0 + value * (1.0 - gate)))
    total = taps[3:4] * grad
    sums = [None] * 4 + [jnp.sum(grad, axis=0, keepdims=True)]
    sums[3] = jnp.sum(grad * inner, axis=0, keepdims=True)
    for shift in range(1, 4):
        masked = grad * masks_ref[shift - 1]
        total = total + taps[3 - shift : 4 - shift] * sooner(masked, shift)
        sums[3 - shift] = jnp.sum(masked * later(inner, shift), axis=0, keepdims=True)
    out_ref[...] = total.astype(BF16)
    sums_ref[...] = jnp.concatenate(sums + [jnp.zeros((3, inner.shape[1]), F32)], axis=0)


def conv_backward(inner, grad, masks, taps):
    rows, width = inner.shape
    tile = pl.BlockSpec((rows, LANES), lambda c: (0, c))
    few = pl.BlockSpec((8, LANES), lambda c: (0, c))
    return pl.pallas_call(
        conv_back_kernel,
        grid=(width // LANES,),
        in_specs=[tile, tile, pl.BlockSpec((3, rows, LANES), lambda c: (0, 0, 0)), few],
        out_specs=[tile, few],
        out_shape=[
            jax.ShapeDtypeStruct((rows, width), BF16),
            jax.ShapeDtypeStruct((8, width), F32),
        ],
        compiler_params=params(),
        cost_estimate=cost(60 * rows * width, 10 * rows * width),
        name="conv_backward",
    )(inner, grad, masks, taps)


def spread(coefs, nstate):
    terms = []
    for _ in range(3):
        term = coefs.astype(BF16)
        terms.append(term)
        coefs = coefs - term.astype(F32)
    joined = jnp.concatenate(terms, axis=1)
    return jnp.pad(joined, ((0, 0), (0, LANES - joined.shape[1])))


def spreader(nstate):
    row = lax.broadcasted_iota(jnp.int32, (LANES, 2 * nstate * LANES), 0)
    tile = lax.broadcasted_iota(jnp.int32, (LANES, 2 * nstate * LANES), 1) // LANES
    return ((row % (2 * nstate) == tile) & (row < 6 * nstate)).astype(BF16)


def folder(nstate):
    tile = lax.broadcasted_iota(jnp.int32, (2 * nstate * LANES, LANES), 0) // LANES
    column = lax.broadcasted_iota(jnp.int32, (2 * nstate * LANES, LANES), 1)
    return (tile == column).astype(BF16)


def tiled(value, width):
    return jnp.concatenate([value] * (width // LANES), axis=1)


def at_time(t):
    return pl.ds(pl.multiple_of(t * GROUP, GROUP), GROUP)


def scan_kernel(
    nstate, chunk, pre_ref, act_ref, coef_ref, spread_ref, keep_ref, rate_ref, row_ref, held_ref, *refs
):
    out_ref, step_ref, start_ref, carry_ref, wide = refs[-5:]
    width = pre_ref.shape[1]

    @pl.when(pl.program_id(0) == 0)
    def _():
        carry_ref[...] = held_ref[...]

    start_ref[0] = carry_ref[...]
    wide[...] = jnp.dot(coef_ref[...], spread_ref[...], preferred_element_type=F32)
    pre = pre_ref[...] + row_ref[0:1]
    step_ref[...] = jnp.maximum(pre, 0.0) + jnp.log1p(jnp.exp(-jnp.abs(pre)))
    for c in range(width // chunk):
        cols = slice(c * chunk, (c + 1) * chunk)

        def advance(t, states):
            at = at_time(t)
            step, act = step_ref[at, cols], act_ref[at, cols]
            drive = jnp.where(tiled(keep_ref[at, :], chunk) > 0.5, step, FAR)
            inflow = step * act
            total = row_ref[1:2, cols] * act
            now = []
            for n in range(nstate):
                write = tiled(wide[at, n * LANES : (n + 1) * LANES], chunk)
                read = tiled(wide[at, (nstate + n) * LANES : (nstate + n + 1) * LANES], chunk)
                state = jnp.exp2(drive * rate_ref[n, :, cols]) * states[n] + write * inflow
                total = total + read * state
                now.append(state)
            out_ref[at, cols] = total
            return tuple(now)

        start = tuple(carry_ref[n, :, cols] for n in range(nstate))
        states = lax.fori_loop(0, BLOCK, advance, start, unroll=4)
        for n in range(nstate):
            carry_ref[n, :, cols] = states[n]


def scan_forward(pre, act, coef, spread_by, keep, rate, rows, held, before, first, count):
    total, width = pre.shape
    nstate = rate.shape[0]
    size = BLOCK * GROUP
    tile = pl.BlockSpec((size, width), lambda t: (first + t, 0))
    thin = pl.BlockSpec((size, LANES), lambda t: (first + t, 0))
    state = pl.BlockSpec((nstate, GROUP, width), lambda t: (0, 0, 0))
    work = count * size * width * nstate
    return pl.pallas_call(
        functools.partial(scan_kernel, nstate, 256),
        grid=(count,),
        in_specs=[
            tile,
            tile,
            thin,
            pl.BlockSpec(spread_by.shape, lambda t: (0, 0)),
            thin,
            state,
            pl.BlockSpec((8, width), lambda t: (0, 0)),
            state,
        ]
        + [pl.BlockSpec(memory_space=pl.ANY)] * len(before),
        out_specs=[
            tile,
            tile,
            pl.BlockSpec((1, nstate, GROUP, width), lambda t: (first + t, 0, 0, 0)),
            state,
        ],
        out_shape=[
            jax.ShapeDtypeStruct((total, width), F32),
            jax.ShapeDtypeStruct((total, width), F32),
            jax.ShapeDtypeStruct((total // size, nstate, GROUP, width), F32),
            jax.ShapeDtypeStruct((nstate, GROUP, width), F32),
        ],
        scratch_shapes=[pltpu.VMEM((size, 2 * nstate * LANES), F32)],
        input_output_aliases={8 + i: i for i in range(len(before))},
        compiler_params=params(),
        cost_estimate=cost(16 * work, 16 * count * size * width),
        name="scan_forward",
    )(pre, act, coef, spread_by, keep, rate, rows, held, *before)


def scan_back_kernel(
    nstate, chunk, pre_ref, step_ref, act_ref, grad_ref, coef_ref, spread_ref, fold_ref, keep_ref, rate_ref,
    row_ref, start_ref, held_ref, sums_in_ref, *refs,
):
    pre_grad_ref, direct_ref, coef_grad_ref, carry_ref, sums_ref, wide, states_all, decays, parts, sizes = refs[-10:]
    width = pre_ref.shape[1]

    @pl.when(pl.program_id(0) == 0)
    def _():
        carry_ref[...] = held_ref[...]
        sums_ref[...] = sums_in_ref[...]

    wide[...] = jnp.dot(coef_ref[...], spread_ref[...], preferred_element_type=F32)

    def fold(value):
        total = value[:, :LANES]
        for k in range(1, chunk // LANES):
            total = total + value[:, k * LANES : (k + 1) * LANES]
        return total

    for c in range(width // chunk):
        cols = slice(c * chunk, (c + 1) * chunk)

        def advance(t, states):
            at = at_time(t)
            step = step_ref[at, cols]
            drive = jnp.where(tiled(keep_ref[at, :], chunk) > 0.5, step, FAR)
            inflow = step * act_ref[at, cols]
            now = []
            for n in range(nstate):
                write = tiled(wide[at, n * LANES : (n + 1) * LANES], chunk)
                decay = jnp.exp2(drive * rate_ref[n, :, cols])
                decays[t, n] = decay
                states_all[t, n] = states[n]
                now.append(decay * states[n] + write * inflow)
            return tuple(now)

        start = tuple(start_ref[0, n, :, cols] for n in range(nstate))
        states = lax.fori_loop(0, BLOCK, advance, start, unroll=2)
        for n in range(nstate):
            states_all[BLOCK, n] = states[n]

        def retreat(i, carry):
            t = BLOCK - 1 - i
            at = at_time(t)
            step, act, grad = step_ref[at, cols], act_ref[at, cols], grad_ref[at, cols]
            inflow = step * act
            size = jnp.zeros_like(step)
            direct = jnp.zeros_like(step)
            now = []
            for n in range(nstate):
                tile_w = slice(n * LANES, (n + 1) * LANES)
                tile_r = slice((nstate + n) * LANES, (nstate + n + 1) * LANES)
                state_grad = tiled(wide[at, tile_r], chunk) * grad + carry[n]
                passed = decays[t, n] * state_grad
                through = passed * states_all[t, n]
                size = size + rate_ref[n, :, cols] * through
                direct = direct + state_grad * tiled(wide[at, tile_w], chunk)
                sums_ref[n, :, cols] += step * through
                write_part = fold(state_grad * inflow)
                read_part = fold(grad * states_all[t + 1, n])
                if c == 0:
                    parts[at, tile_w] = write_part
                    parts[at, tile_r] = read_part
                else:
                    parts[at, tile_w] += write_part
                    parts[at, tile_r] += read_part
                now.append(passed)
            sizes[at, cols] = LN2 * size + act * direct
            direct_ref[at, cols] = step * direct + row_ref[1:2, cols] * grad
            sums_ref[nstate, :, cols] += grad * act
            return tuple(now)

        start = tuple(carry_ref[n, :, cols] for n in range(nstate))
        carry = lax.fori_loop(0, BLOCK, retreat, start, unroll=2)
        for n in range(nstate):
            carry_ref[n, :, cols] = carry[n]

    pre_grad = sizes[...] * sigmoid(pre_ref[...] + row_ref[0:1])
    pre_grad_ref[...] = pre_grad.astype(BF16)
    total = pre_grad[:GROUP]
    for t in range(1, BLOCK):
        total = total + pre_grad[t * GROUP : (t + 1) * GROUP]
    sums_ref[nstate + 1] += total
    high = parts[...].astype(BF16)
    low = (parts[...] - high.astype(F32)).astype(BF16)
    coef_grad_ref[...] = jnp.dot(high, fold_ref[...], preferred_element_type=F32) + jnp.dot(
        low, fold_ref[...], preferred_element_type=F32
    )


def scan_backward(
    pre, step, act, grad, coef, spread_by, fold_by, keep, rate, rows, starts, held, sums, before, first, count
):
    total, width = pre.shape
    nstate = rate.shape[0]
    size = BLOCK * GROUP
    chunk = 256
    tile = pl.BlockSpec((size, width), lambda t: (first - t, 0))
    thin = pl.BlockSpec((size, LANES), lambda t: (first - t, 0))
    state = pl.BlockSpec((nstate, GROUP, width), lambda t: (0, 0, 0))
    tally = pl.BlockSpec((nstate + 2, GROUP, width), lambda t: (0, 0, 0))
    work = count * size * width * nstate
    return pl.pallas_call(
        functools.partial(scan_back_kernel, nstate, chunk),
        grid=(count,),
        in_specs=[
            tile,
            tile,
            tile,
            tile,
            thin,
            pl.BlockSpec(spread_by.shape, lambda t: (0, 0)),
            pl.BlockSpec(fold_by.shape, lambda t: (0, 0)),
            thin,
            state,
            pl.BlockSpec((8, width), lambda t: (0, 0)),
            pl.BlockSpec((1, nstate, GROUP, width), lambda t: (first - t, 0, 0, 0)),
            state,
            tally,
        ]
        + [pl.BlockSpec(memory_space=pl.ANY)] * len(before),
        out_specs=[tile, tile, thin, state, tally],
        out_shape=[
            jax.ShapeDtypeStruct((total, width), BF16),
            jax.ShapeDtypeStruct((total, width), F32),
            jax.ShapeDtypeStruct((total, LANES), F32),
            jax.ShapeDtypeStruct((nstate, GROUP, width), F32),
            jax.ShapeDtypeStruct((nstate + 2, GROUP, width), F32),
        ],
        scratch_shapes=[
            pltpu.VMEM((size, 2 * nstate * LANES), F32),
            pltpu.VMEM((BLOCK + 1, nstate, GROUP, chunk), F32),
            pltpu.VMEM((BLOCK, nstate, GROUP, chunk), F32),
            pltpu.VMEM((size, 2 * nstate * LANES), F32),
            pltpu.VMEM((size, width), F32),
        ],
        input_output_aliases={13 + i: i for i in range(len(before))},
        compiler_params=params(),
        cost_estimate=cost(40 * work, 24 * count * size * width),
        name="scan_backward",
    )(pre, step, act, grad, coef, spread_by, fold_by, keep, rate, rows, starts, held, sums, *before)


def spread_columns_kernel(copy_ref, *refs):
    pieces, weight_ref, out_ref, gain_ref = refs[:4], refs[4], refs[-2], refs[-1]
    part = pieces[0].shape[1]

    @pl.when(pl.program_id(0) == 0)
    def _():
        gain_ref[...] = jnp.zeros_like(gain_ref)

    total = gain_ref[...]
    for k, piece in enumerate(pieces):
        at = pl.ds(pl.multiple_of((copy_ref[0] ^ k) * part, part), part)
        value = piece[...].astype(F32)
        out_ref[:, at] = value
        total = total + value * weight_ref[:, at].astype(F32)
    gain_ref[...] = total


def spread_columns(copy, pieces, weight, side, before=None):
    rows, width = pieces[0].shape
    part = LANES
    shares = width // part
    block = pl.BlockSpec((rows, COPIES * part), lambda f, copy: (0, side * shares + f))
    piece = pl.BlockSpec((rows, part), lambda f, copy: (0, f))
    extra = [] if before is None else [before]
    return pl.pallas_call(
        spread_columns_kernel,
        grid_spec=pltpu.PrefetchScalarGridSpec(
            num_scalar_prefetch=1,
            grid=(shares,),
            in_specs=[piece] * 4 + [block] + [pl.BlockSpec(memory_space=pl.ANY)] * len(extra),
            out_specs=[block, pl.BlockSpec((rows, part), lambda f, copy: (0, 0))],
        ),
        out_shape=[
            jax.ShapeDtypeStruct(weight.shape, F32),
            jax.ShapeDtypeStruct((rows, part), F32),
        ],
        input_output_aliases={6: 0} if extra else {},
        compiler_params=params(),
        cost_estimate=cost(4 * rows * width, 20 * rows * width),
        name="spread_columns",
    )(copy, *pieces, weight, *extra)


def spread_rows_kernel(copy_ref, *refs):
    pieces, out_ref = refs[:4], refs[4]
    part = pieces[0].shape[0]
    for k, piece in enumerate(pieces):
        at = pl.ds(pl.multiple_of((copy_ref[0] ^ k) * part, part), part)
        out_ref[at, :] = piece[...].astype(F32)


def spread_rows(copy, pieces):
    part, columns = pieces[0].shape
    tile = 512
    return pl.pallas_call(
        spread_rows_kernel,
        grid_spec=pltpu.PrefetchScalarGridSpec(
            num_scalar_prefetch=1,
            grid=(columns // tile,),
            in_specs=[pl.BlockSpec((part, tile), lambda c, copy: (0, c))] * 4,
            out_specs=pl.BlockSpec((COPIES * part, tile), lambda c, copy: (0, c)),
        ),
        out_shape=jax.ShapeDtypeStruct((COPIES * part, columns), F32),
        compiler_params=params(),
        cost_estimate=cost(4 * part * columns, 24 * part * columns),
        name="spread_rows",
    )(copy, *pieces)


def on_device(
    tokens, segment_ids, out_grad, norm_gain, in_proj, conv_weight, conv_bias, x_proj,
    step_proj, step_bias, decay_log, skip_gain, out_proj, *, fsdp,
):
    ring = Ring(fsdp)
    copy = lax.axis_index("rep")
    batches, length, model = tokens.shape
    total = COPIES * batches * length
    slab = in_proj.shape[0]
    share = out_proj.shape[0]
    part = share // COPIES
    width = fsdp * part
    rank, nstate = step_proj.shape[1], decay_log.shape[1]
    taps_n = conv_weight.shape[1]
    gains_n = slab // part

    def mine(value):
        return lax.dynamic_slice_in_dim(value, copy * part, part, 0)

    entry = lax.dynamic_index_in_dim(
        in_proj.reshape(slab, 2, fsdp, COPIES, part), copy, 3, keepdims=False
    )
    few = jnp.concatenate(
        [
            mine(x_proj).T,
            mine(step_proj).T,
            mine(conv_weight).T,
            mine(conv_bias)[None],
            mine(step_bias)[None],
            mine(decay_log).T,
            mine(skip_gain)[None],
            norm_gain.reshape(gains_n, part),
        ],
        axis=0,
    )
    few = jnp.pad(few, ((0, -few.shape[0] % 16), (0, 0)))
    inner_gather = Gather(ring, entry[:, 0].reshape(slab, width))
    gate_gather = Gather(ring, entry[:, 1].reshape(slab, width))
    out_gather = Gather(ring, mine(out_proj))
    few_gather = Gather(ring, few)

    env = {}

    def first():
        env["segments"] = rep_gather(segment_ids[:, 0, :])
        return swap(tokens[:1], 2), swap(tokens, 1), env["segments"]

    def second(across):
        return lambda: (swap(tokens[1:], 2), swap(across, 1))

    if ring.half == 4:
        half_steps = [(1, 2), (3, 4)]

        def few_steps(numbers):
            def run():
                for number in numbers:
                    few_gather.take(number, few_gather.step(number))
                return few_gather.held, few_gather.whole

            return run

        (few_gather.held, few_gather.whole), (across0, next_to, segments) = slot(
            1, [inner_gather], few_steps(half_steps[0]), first
        )
        (few_gather.held, few_gather.whole), (across1, next0) = slot(
            2, [inner_gather], few_steps(half_steps[1]), second(across0)
        )
    else:
        few_gather.rest()
        across0, next_to, segments = first()
        across1, next0 = second(across0)()

    few = jnp.moveaxis(few_gather.whole, 0, 1).reshape(-1, width)
    sizes = [rank + 2 * nstate, rank, taps_n, 1, 1, nstate, 1, gains_n]
    pieces, start = [], 0
    for size in sizes:
        pieces.append(few[start : start + size])
        start += size
    select, stride, taps, shift_bias, size_bias, decay, skip, _ = pieces
    gain = few_gather.whole[:, start - gains_n : start].reshape(model).astype(F32)

    def masks_of(segments):
        segments = jnp.concatenate(segments, axis=0)
        masks = []
        for shift in range(1, taps_n):
            earlier = jnp.pad(segments, ((0, 0), (shift, 0)), constant_values=-1)[:, :length]
            masks.append((earlier == segments).astype(F32).T.reshape(total, 1))
        return jnp.broadcast_to(jnp.stack(masks), (taps_n - 1, total, LANES))

    def small_terms():
        tap_rows = jnp.concatenate(
            [taps.astype(F32), shift_bias.astype(F32), jnp.zeros((7 - taps_n, width), F32)]
        )
        side_rows = jnp.concatenate(
            [size_bias.astype(F32), skip.astype(F32), jnp.zeros((6, width), F32)]
        )
        decay_rate = -jnp.exp(decay.astype(F32))
        rate = jnp.broadcast_to((decay_rate * LOG2E)[:, None, :], (nstate, GROUP, width))
        return tap_rows, side_rows, decay_rate, rate, masks_of(segments), spreader(nstate), folder(nstate)

    def third():
        return swap(across1, 1), swap(out_grad[:1], 2), swap(out_grad, 1)

    def rows_of(own, near, across, far):
        joined = jnp.concatenate([own, near, across, far], axis=0)
        return jnp.swapaxes(joined, 0, 1).reshape(total, model)

    def normalize(near, across, far):
        values = rows_of(tokens, near, across, far).astype(F32)
        scale = lax.rsqrt(jnp.mean(values * values, axis=-1, keepdims=True) + EPS)
        return (values * scale * gain).astype(BF16)

    if ring.half == 4:
        (next1, grad_across0, grad_near), (tap_rows, side_rows, decay_rate, rate, masks, spread_by, fold_by) = slot(
            3, [inner_gather], third, small_terms
        )
    else:
        next1, grad_across0, grad_near = third()
        tap_rows, side_rows, decay_rate, rate, masks, spread_by, fold_by = small_terms()
    across = jnp.concatenate([across0, across1], axis=0)
    far = jnp.concatenate([next0, next1], axis=0)

    def fourth():
        return swap(out_grad[1:], 2), swap(grad_across0, 1)

    if ring.half == 4:
        (grad_across1, grad_next0), normed = slot(
            4, [inner_gather], fourth, lambda: normalize(next_to, across, far)
        )
    else:
        grad_across1, grad_next0 = fourth()
        normed = normalize(next_to, across, far)
        inner_gather.rest()
    keep = masks[0]
    inner_in = inner_gather.whole.reshape(model, width)

    def project():
        env["inner"] = dot(normed, inner_in, 1, 0)
        return (env["inner"],) + tuple(conv_forward(env["inner"], masks, tap_rows))

    def cotangents():
        env["far"] = swap(grad_across1, 1)
        return rows_of(
            out_grad,
            grad_near,
            jnp.concatenate([grad_across0, grad_across1], axis=0),
            jnp.concatenate([grad_next0, env["far"]], axis=0),
        )

    state0 = jnp.zeros((nstate, GROUP, width), F32)
    blocks = length // BLOCK
    store = {}

    def g1():
        store["inner"], store["act"], store["act_low"] = project()
        return store["inner"], store["act"], store["act_low"]

    def g2():
        part_sums = dot(store["act_low"], select, 1, 1)
        return sum_near(by_copy(part_sums, batches))

    def g3():
        projected = by_row(sum_far(store["half_sums"]))
        store["step_low"] = projected[:, :rank].astype(BF16)
        store["coef"] = spread(projected[:, rank:], nstate)
        store["pre"] = dot(store["step_low"], stride, 1, 0)
        return store["step_low"], store["coef"], store["pre"], forward_part(0, (), state0)

    def forward_part(first, before, held):
        return tuple(
            scan_forward(
                store["pre"], store["act"], store["coef"], spread_by, keep, rate, side_rows,
                held, before, first, blocks // 2,
            )
        )

    def g4():
        out = store["scan"]
        return forward_part(blocks // 2, out[:3], out[3])

    small_ring = ring.half == 4
    movers = [gate_gather] if small_ring else []
    ((store["inner"], store["act"], store["act_low"]), cotangent) = slot(1, movers, g1, cotangents)
    (store["half_sums"],) = slot(2, movers, g2)
    ((store["step_low"], store["coef"], store["pre"], store["scan"]),) = slot(3, movers, g3)
    (store["scan"],) = slot(4, movers, g4)
    if not small_ring:
        gate_gather.rest()
    readout, step, starts, _ = store["scan"]
    gate_in = gate_gather.whole.reshape(model, width)

    def o1():
        return dot(normed, gate_in, 1, 0)

    def o2():
        soft = store["gate"] * sigmoid(store["gate"])
        return (readout * soft).astype(BF16)

    def o3():
        return dot(store["gated"], cotangent, 0, 0).astype(BF16).reshape(fsdp, part, model)

    movers = [out_gather] if small_ring else []
    (store["gate"],) = slot(1, movers, o1)
    (store["gated"],) = slot(2, movers, o2)
    (out_wgrad,) = slot(3, movers, o3)
    slot(4, movers)
    if not small_ring:
        out_gather.rest()
    out_w = out_gather.whole.reshape(width, model)
    gate, gated, inner, act, act_low = (store[k] for k in ("gate", "gated", "inner", "act", "act_low"))
    pre, coef, step_low = store["pre"], store["coef"], store["step_low"]

    out_scatter = Scatter(ring, out_wgrad)
    movers = [out_scatter] if small_ring else []

    def r1():
        gated_grad = dot(cotangent, out_w, 1, 1)
        sig = sigmoid(gate)
        gate_grad = (gated_grad * readout * (sig * (1.0 + gate * (1.0 - sig)))).astype(BF16)
        return gate_grad, gated_grad * (gate * sig)

    ((gate_grad, read_grad),) = slot(1, movers, r1)

    def back_part(first, count, state):
        before, held, sums = state[:3], state[3], state[4]
        return tuple(
            scan_backward(
                pre, step, act, read_grad, coef, spread_by, fold_by, keep, rate, side_rows,
                starts, held, sums, before, first, count,
            )
        )

    tally0 = jnp.zeros((nstate + 2, GROUP, width), F32)

    def start_back():
        return tuple(
            scan_backward(
                pre, step, act, read_grad, coef, spread_by, fold_by, keep, rate, side_rows,
                starts, state0, tally0, (), blocks - 1, 1,
            )
        )

    def gate_weights():
        return dot(normed, gate_grad, 0, 0).astype(BF16).reshape(fsdp, slab, width)

    state, gate_wgrad = slot(2, movers, start_back, gate_weights)
    rest = blocks - 1

    (state,) = slot(3, movers, lambda: back_part(rest - 1, 2, state))
    (state,) = slot(4, movers, lambda: back_part(rest - 3, 2, state))
    if not small_ring:
        out_scatter.rest()
    gate_scatter = Scatter(ring, gate_wgrad)
    movers = [gate_scatter] if small_ring else []
    (state,) = slot(1, movers, lambda: back_part(rest - 5, 2, state))

    def last_back():
        out = back_part(0, 1, state)
        coef_part = out[2][:, : 2 * nstate]
        low_part = dot(out[0], stride, 1, 1)
        return out, jnp.concatenate([low_part, coef_part], axis=1)

    def out_part():
        parts = dot(gated, out_w, 1, 0).astype(BF16)
        return by_copy(parts, batches)

    ((state, proj_part),) = slot(2, movers, last_back)
    pre_low, direct, _, _, sums = state

    def proj_sums():
        return sum_near(by_copy(proj_part, batches))

    half_sums, out_parts, out_pieces = slot(
        3, movers, proj_sums, out_part, lambda: rep_gather(out_scatter.total.astype(BF16))
    )

    def conv_part():
        proj_low = by_row(sum_far(half_sums)).astype(BF16)
        act_grad = direct + dot(proj_low, select, 1, 0)
        inner_grad, conv_sums = conv_backward(inner, act_grad, masks, tap_rows)
        inner_wgrad = dot(normed, inner_grad, 0, 0).astype(BF16).reshape(fsdp, slab, width)
        small = jnp.concatenate(
            [
                dot(proj_low, act_low, 0, 0),
                dot(step_low, pre_low, 0, 0),
                conv_sums[: taps_n + 1],
                jnp.sum(sums[nstate + 1 :], axis=1),
                decay_rate * jnp.sum(sums[:nstate], axis=1),
                jnp.sum(sums[nstate : nstate + 1], axis=1),
            ],
            axis=0,
        )
        small = jnp.pad(small, ((0, -small.shape[0] % 16), (0, 0))).astype(BF16)
        small = jnp.moveaxis(small.reshape(-1, fsdp, part), 1, 0)
        return inner_grad, inner_wgrad, small

    (inner_grad, inner_wgrad, small), (out_near, out_far) = slot(
        4, movers, conv_part, lambda: rep_scatter_near(out_parts)
    )
    if not small_ring:
        gate_scatter.rest()

    inner_scatter = Scatter(ring, inner_wgrad)
    small_scatter = Scatter(ring, small)
    movers = [inner_scatter, small_scatter] if small_ring else []
    copy_index = copy.astype(jnp.int32).reshape(1)

    def norm_parts():
        grads = dot(inner_grad, inner_in, 1, 1) + dot(gate_grad, gate_in, 1, 1)
        return rep_scatter_near(by_copy(grads.astype(BF16), batches))

    def as_tokens(value):
        return jnp.swapaxes(value, 0, 1)

    def finish_out():
        summed = rep_scatter_far(out_near, out_far)
        return (tokens.astype(F32) + as_tokens(summed)).astype(BF16)

    gate_sum = gate_scatter.total.astype(BF16)
    (norm_near, norm_far), gate_across = slot(1, movers, norm_parts, lambda: swap(gate_sum, 2))

    aligned = part % LANES == 0

    def place_gate():
        pieces = [gate_sum, swap(gate_sum, 1), gate_across, swap(gate_across, 1)]
        if not aligned:
            return pieces
        return spread_columns(copy_index, pieces, in_proj, 1)

    def place_out():
        if aligned:
            return spread_rows(copy_index, out_pieces)
        return jnp.stack(out_pieces)[jnp.arange(COPIES) ^ copy].reshape(share, model).astype(F32)

    normed_far, gate_placed, out_all = slot(
        2, movers, lambda: swap(norm_far, 2), place_gate, place_out
    )

    def finish_tokens():
        normed_grad = as_tokens(norm_near + normed_far.astype(F32))
        own = tokens.astype(F32)
        own_scale = lax.rsqrt(jnp.mean(own * own, axis=-1, keepdims=True) + EPS)
        scaled = normed_grad * gain
        lean = jnp.mean(scaled * own, axis=-1, keepdims=True)
        return (
            out_grad.astype(F32) + own_scale * scaled - own * (own_scale**3) * lean
        ).astype(BF16)

    (block_out,) = slot(3, movers, finish_out)
    (input_grad,) = slot(4, movers, finish_tokens)
    if not small_ring:
        inner_scatter.rest()
        small_scatter.rest()

    small_pieces = rep_gather(small_scatter.total.astype(BF16))
    inner_pieces = rep_gather(inner_scatter.total.astype(BF16))
    order = jnp.arange(COPIES) ^ copy
    if aligned:
        entry_all, gain_inner = spread_columns(
            copy_index, inner_pieces, in_proj, 0, gate_placed[0]
        )
        gain_sum = jnp.sum(gain_inner + gate_placed[1], axis=1)
    else:
        halves = jnp.stack([jnp.stack(inner_pieces), jnp.stack(gate_placed)])[:, order]
        halves = halves.reshape(2, COPIES, slab, fsdp, part).astype(F32)
        entry_all = jnp.transpose(halves, (2, 0, 3, 1, 4)).reshape(slab, -1)
        gain_sum = jnp.sum(entry_all * in_proj.astype(F32), axis=1)
    gain_grad = gain_sum / norm_gain.astype(F32)
    small_all = jnp.stack(small_pieces)[order].astype(F32)
    small_all = jnp.moveaxis(small_all, 0, 1).reshape(-1, share)
    out, start = [], 0
    for size in sizes[:-1]:
        out.append(small_all[start : start + size])
        start += size
    select_g, stride_g, taps_g, shift_g, size_g, decay_g, skip_g = out
    return (
        block_out,
        input_grad,
        gain_grad,
        entry_all,
        taps_g.T,
        shift_g[0],
        select_g.T,
        stride_g.T,
        size_g[0],
        decay_g.T,
        skip_g[0],
        out_all,
    )


def solution(mesh):
    tokens = P(None, ("fsdp", "rep"), None)
    rows, row = P("fsdp", None), P("fsdp")
    return jax.shard_map(
        functools.partial(on_device, fsdp=mesh.shape["fsdp"]),
        mesh=mesh,
        in_specs=(tokens, tokens, tokens, row, rows, rows, row, rows, rows, row, rows, row, rows),
        out_specs=(tokens, tokens, row, rows, rows, row, rows, rows, row, rows, row, rows),
        check_vma=False,
    )
```

```python
import functools

import jax
import jax.numpy as jnp
from jax import lax
from jax.experimental import pallas as pl
from jax.experimental.pallas import tpu as pltpu
from jax.sharding import PartitionSpec as P

EPS = 1e-05
BLOCK = 16
LANES = 128
GROUP = 8
COPIES = 4
LOG2E = 1.4426950408889634
LN2 = 0.6931471805599453
FAR = 1e30
F32 = jnp.float32
BF16 = jnp.bfloat16
VMEM_LIMIT = 56 * 1024 * 1024


def dot(left, right, left_dim, right_dim):
    return lax.dot_general(
        left, right, (((left_dim,), (right_dim,)), ((), ())), preferred_element_type=F32
    )


def params():
    return pltpu.CompilerParams(vmem_limit_bytes=VMEM_LIMIT)


def cost(flops, moved):
    return pl.CostEstimate(flops=int(flops), bytes_accessed=int(moved), transcendentals=0)


def blank(shape, dtype):
    return pl.pallas_call(
        lambda ref: None,
        out_shape=jax.ShapeDtypeStruct(shape, dtype),
        out_specs=pl.BlockSpec(memory_space=pl.ANY),
        name="blank",
    )()


def ring_order(size):
    half = size // 2
    return [2 * p if p < half else 2 * (size - 1 - p) + 1 for p in range(size)]


class Ring:
    def __init__(self, size):
        order = ring_order(size)
        place = [0] * size
        for spot, member in enumerate(order):
            place[member] = spot
        self.size, self.half = size, size // 2
        self.order = jnp.array(order, jnp.int32)
        self.spot = jnp.array(place, jnp.int32)[lax.axis_index("fsdp")]
        self.above = [(order[p], order[(p + 1) % size]) for p in range(size)]
        self.below = [(order[p], order[(p - 1) % size]) for p in range(size)]

    def member(self, offset):
        return self.order[(self.spot + offset + self.size) % self.size]

    def up(self, value):
        return lax.ppermute(value, "fsdp", self.above)

    def down(self, value):
        return lax.ppermute(value, "fsdp", self.below)


class Gather:
    def __init__(self, ring, shard):
        self.ring, self.cut = ring, shard.shape[0] // 2
        self.whole = blank((ring.size,) + shard.shape, shard.dtype)
        self.held = (shard, shard)
        self.put(shard, 0)

    def put(self, piece, offset, start=0):
        at = (self.ring.member(offset), jnp.int32(start), jnp.int32(0))
        self.whole = lax.dynamic_update_slice(self.whole, piece[None], at)

    def step(self, number):
        low, high = self.held
        if number == self.ring.half:
            low, high = low[: self.cut], high[self.cut :]
        return self.ring.up(low), self.ring.down(high)

    def take(self, number, got):
        self.held = got
        last = number == self.ring.half
        self.put(got[0], -number)
        self.put(got[1], number, self.cut if last else 0)

    def rest(self):
        def body(number, state):
            whole, low, high = state
            low, high = self.ring.up(low), self.ring.down(high)
            self.whole = whole
            self.put(low, -number)
            self.put(high, number)
            return self.whole, low, high

        self.whole, low, high = lax.fori_loop(1, self.ring.half, body, (self.whole,) + self.held)
        self.held = (low, high)
        self.take(self.ring.half, self.step(self.ring.half))


class Scatter:
    def __init__(self, ring, parts):
        self.ring, self.parts, self.cut = ring, parts, parts.shape[1] // 2
        far = self.own(ring.half)
        self.sent = (far[: self.cut], far[self.cut :])
        self.total = None

    def own(self, offset):
        return lax.dynamic_index_in_dim(self.parts, self.ring.member(offset), 0, keepdims=False)

    def step(self, number):
        return self.ring.up(self.sent[0]), self.ring.down(self.sent[1])

    def take(self, number, got):
        left = self.ring.half - number
        low, high = got
        near_low, near_high = self.own(left), self.own(-left)
        if number == 1:
            low = jnp.concatenate([low, jnp.zeros_like(near_low[self.cut :])])
            high = jnp.concatenate([jnp.zeros_like(near_high[: self.cut]), high])
        if left == 0:
            self.total = near_low.astype(F32) + low.astype(F32) + high.astype(F32)
        else:
            self.sent = (self.add(near_low, low), self.add(near_high, high))

    def add(self, near, got):
        return (near.astype(F32) + got.astype(F32)).astype(near.dtype)

    def rest(self):
        self.take(1, self.step(1))

        def body(number, sent):
            left = self.ring.half - number
            low, high = self.ring.up(sent[0]), self.ring.down(sent[1])
            return self.add(self.own(left), low), self.add(self.own(-left), high)

        self.sent = lax.fori_loop(2, self.ring.half, body, self.sent)
        self.take(self.ring.half, self.step(self.ring.half))


def after(value, *held):
    return lax.optimization_barrier((value, held))[1]


def slot(number, movers, *work):
    moved = tuple(m.step(number) for m in movers)
    done = tuple(w() for w in work)
    moved, done = lax.optimization_barrier((moved, done))
    for mover, got in zip(movers, moved):
        mover.take(number, got)
    return done


def swap(value, bit):
    return lax.ppermute(value, "rep", [(r, r ^ bit) for r in range(COPIES)])


def rep_gather(value):
    across = swap(value, 2)
    return [value, swap(value, 1), across, swap(across, 1)]


def rep_scatter_near(parts):
    pair = swap(jnp.stack([parts[1], parts[3]]), 1)
    near = parts[0].astype(F32) + pair[0].astype(F32)
    far = parts[2].astype(F32) + pair[1].astype(F32)
    return near, far.astype(parts.dtype)


def rep_scatter_far(near, far):
    return near + swap(far, 2).astype(F32)


def sum_near(parts):
    pair = swap(jnp.stack([parts[1], parts[3]]), 1)
    mine = jnp.stack([parts[0], parts[2]]) + pair
    return mine + swap(jnp.stack([mine[1], mine[0]]), 2)


def sum_far(mine):
    next_to = swap(mine, 1)
    return jnp.stack([mine[0], next_to[0], mine[1], next_to[1]])


def to_time(value):
    return jnp.swapaxes(value.reshape(GROUP, -1, value.shape[-1]), 0, 1).reshape(value.shape)


def to_sequence(value):
    return jnp.swapaxes(value.reshape(-1, GROUP, value.shape[-1]), 0, 1).reshape(value.shape)


def by_copy(value):
    return value.reshape(COPIES, -1, value.shape[-1])


def sigmoid(value):
    return 1.0 / (1.0 + jnp.exp(-value))


def later(value, shift):
    rows = shift * GROUP
    return jnp.concatenate([jnp.zeros_like(value[:rows]), value[:-rows]], axis=0)


def sooner(value, shift):
    rows = shift * GROUP
    return jnp.concatenate([value[rows:], jnp.zeros_like(value[:rows])], axis=0)


def conv_of(inner, masks, taps):
    total = taps[4:5] + taps[3:4] * inner
    for shift in range(1, 4):
        total = total + taps[3 - shift : 4 - shift] * (later(inner, shift) * masks[shift - 1])
    return total


def by_sequence(held, out_ref, value):
    length = value.shape[0] // GROUP
    held[...] = value
    for s in range(GROUP):
        out_ref[s * length : (s + 1) * length, :] = held[
            pl.ds(s, length, stride=GROUP), :
        ].astype(out_ref.dtype)


def conv_kernel(inner_ref, masks_ref, taps_ref, act_ref, low_ref, held):
    value = conv_of(inner_ref[...], masks_ref, taps_ref[...])
    act = value * sigmoid(value)
    act_ref[...] = act
    by_sequence(held, low_ref, act)


def conv_forward(inner, masks, taps):
    rows, width = inner.shape
    tile = pl.BlockSpec((rows, LANES), lambda c: (0, c))
    return pl.pallas_call(
        conv_kernel,
        grid=(width // LANES,),
        in_specs=[
            tile,
            pl.BlockSpec((3, rows, LANES), lambda c: (0, 0, 0)),
            pl.BlockSpec((8, LANES), lambda c: (0, c)),
        ],
        out_specs=[tile, tile],
        out_shape=[
            jax.ShapeDtypeStruct((rows, width), F32),
            jax.ShapeDtypeStruct((rows, width), BF16),
        ],
        scratch_shapes=[pltpu.VMEM((rows, LANES), F32)],
        compiler_params=params(),
        cost_estimate=cost(30 * rows * width, 10 * rows * width),
        name="conv_forward",
    )(inner, masks, taps)


def conv_back_kernel(inner_ref, grad_ref, masks_ref, taps_ref, out_ref, natural_ref, sums_ref, held):
    inner, taps = inner_ref[...], taps_ref[...]
    value = conv_of(inner, masks_ref, taps)
    gate = sigmoid(value)
    grad = grad_ref[...] * (gate * (1.0 + value * (1.0 - gate)))
    total = taps[3:4] * grad
    sums = [None] * 4 + [jnp.sum(grad, axis=0, keepdims=True)]
    sums[3] = jnp.sum(grad * inner, axis=0, keepdims=True)
    for shift in range(1, 4):
        masked = grad * masks_ref[shift - 1]
        total = total + taps[3 - shift : 4 - shift] * sooner(masked, shift)
        sums[3 - shift] = jnp.sum(masked * later(inner, shift), axis=0, keepdims=True)
    out_ref[...] = total.astype(BF16)
    by_sequence(held, natural_ref, total)
    sums_ref[...] = jnp.concatenate(sums + [jnp.zeros((3, inner.shape[1]), F32)], axis=0)


def conv_backward(inner, grad, masks, taps):
    rows, width = inner.shape
    tile = pl.BlockSpec((rows, LANES), lambda c: (0, c))
    few = pl.BlockSpec((8, LANES), lambda c: (0, c))
    return pl.pallas_call(
        conv_back_kernel,
        grid=(width // LANES,),
        in_specs=[tile, tile, pl.BlockSpec((3, rows, LANES), lambda c: (0, 0, 0)), few],
        out_specs=[tile, tile, few],
        out_shape=[
            jax.ShapeDtypeStruct((rows, width), BF16),
            jax.ShapeDtypeStruct((rows, width), BF16),
            jax.ShapeDtypeStruct((8, width), F32),
        ],
        scratch_shapes=[pltpu.VMEM((rows, LANES), F32)],
        compiler_params=params(),
        cost_estimate=cost(60 * rows * width, 10 * rows * width),
        name="conv_backward",
    )(inner, grad, masks, taps)


def gate_kernel(readout_ref, gate_ref, out_ref, natural_ref, held):
    gate = gate_ref[...]
    gated = readout_ref[...] * (gate * sigmoid(gate))
    out_ref[...] = gated.astype(BF16)
    by_sequence(held, natural_ref, gated)


def gate_forward(readout, gate):
    rows, width = gate.shape
    tile = pl.BlockSpec((rows, LANES), lambda c: (0, c))
    return pl.pallas_call(
        gate_kernel,
        grid=(width // LANES,),
        in_specs=[tile] * 2,
        out_specs=[tile] * 2,
        out_shape=[jax.ShapeDtypeStruct((rows, width), BF16)] * 2,
        scratch_shapes=[pltpu.VMEM((rows, LANES), F32)],
        compiler_params=params(),
        cost_estimate=cost(20 * rows * width, 12 * rows * width),
        name="gate_forward",
    )(readout, gate)


def gate_back_kernel(grad_ref, readout_ref, gate_ref, read_ref, out_ref, natural_ref, held):
    gate, grad = gate_ref[...], grad_ref[...]
    sig = sigmoid(gate)
    read_ref[...] = grad * (gate * sig)
    gate_grad = grad * readout_ref[...] * (sig * (1.0 + gate * (1.0 - sig)))
    out_ref[...] = gate_grad.astype(BF16)
    by_sequence(held, natural_ref, gate_grad)


def gate_backward(grad, readout, gate):
    rows, width = gate.shape
    tile = pl.BlockSpec((rows, LANES), lambda c: (0, c))
    return pl.pallas_call(
        gate_back_kernel,
        grid=(width // LANES,),
        in_specs=[tile] * 3,
        out_specs=[tile] * 3,
        out_shape=[jax.ShapeDtypeStruct((rows, width), F32)]
        + [jax.ShapeDtypeStruct((rows, width), BF16)] * 2,
        scratch_shapes=[pltpu.VMEM((rows, LANES), F32)],
        compiler_params=params(),
        cost_estimate=cost(20 * rows * width, 20 * rows * width),
        name="gate_backward",
    )(grad, readout, gate)


def rows_kernel(scaled, *refs):
    values_ref, out_ref, held = refs[0], refs[-2], refs[-1]
    for s in range(GROUP):
        value = values_ref[s].astype(F32)
        if scaled:
            square = jnp.mean(value * value, axis=-1, keepdims=True)
            value = value * lax.rsqrt(square + EPS) * refs[1][...]
        for k in range(held.shape[0]):
            held[k, pl.ds(s, value.shape[0], stride=GROUP), :] = value[
                :, k * LANES : (k + 1) * LANES
            ]
    for k in range(held.shape[0]):
        out_ref[:, k * LANES : (k + 1) * LANES] = held[k].astype(BF16)


def interleave(values, gain=None):
    _, length, model = values.shape
    extra = [] if gain is None else [gain.reshape(1, model)]
    return pl.pallas_call(
        functools.partial(rows_kernel, gain is not None),
        grid=(length // BLOCK,),
        in_specs=[pl.BlockSpec((GROUP, BLOCK, model), lambda t: (0, t, 0))]
        + [pl.BlockSpec((1, model), lambda t: (0, 0))] * len(extra),
        out_specs=pl.BlockSpec((BLOCK * GROUP, model), lambda t: (t, 0)),
        out_shape=jax.ShapeDtypeStruct((length * GROUP, model), BF16),
        scratch_shapes=[pltpu.VMEM((model // LANES, BLOCK * GROUP, LANES), F32)],
        compiler_params=params(),
        cost_estimate=cost(8 * GROUP * length * model, 4 * GROUP * length * model),
        name="interleave",
    )(values, *extra)


class Peers:
    def __init__(self, size):
        self.size, self.half = size, size // 2
        self.member, self.copy = lax.axis_index("fsdp"), lax.axis_index("rep")
        row, column = lax.div(self.member, 2), lax.rem(self.member, 2)
        self.spot = row * (1 - column) + (size - 1 - row) * column
        side = lax.rem(self.copy, 2)
        self.core = (self.member, self.copy - side + (1 - side))
        self.across = (self.member, lax.rem(self.copy + 2, COPIES))
        self.ring = ((self.at(1), self.copy), (self.at(-1), self.copy))

    def at(self, offset):
        spot = lax.rem(self.spot + (offset + self.size), self.size)
        second = lax.div(spot, self.half)
        return 2 * spot * (1 - second) + (2 * (self.size - 1 - spot) + 1) * second

    def meet(self):
        barrier = pltpu.get_barrier_semaphore()
        peers = (*self.ring, self.core, self.across)
        for peer in peers:
            pl.semaphore_signal(barrier, inc=1, device_id=peer, device_id_type=pl.DeviceIdType.MESH)
        pl.semaphore_wait(barrier, len(peers))


def remote(source, target, sems, index, peer):
    return pltpu.make_async_remote_copy(
        src_ref=source,
        dst_ref=target,
        send_sem=sems[0].at[index],
        recv_sem=sems[1].at[index],
        device_id=peer,
        device_id_type=pl.DeviceIdType.MESH,
    )


def gather_kernel(
    size, entry_ref, few_ref, own_refs, whole_ref, gate_ref, all_ref, copies_refs, inner_ref, local, ring_sems, few_sems, rep_sems
):
    peers = Peers(size)
    half = peers.half
    rows, few_rows = inner_ref.shape[0] // 2, few_ref.shape[0] // 2
    keep = []
    for f in range(size):
        for side, target in enumerate((inner_ref, gate_ref)):
            source = ((side * size + f) * COPIES + peers.copy) * LANES
            keep.append(
                pltpu.make_async_copy(
                    entry_ref.at[:, pl.ds(pl.multiple_of(source, LANES), LANES)],
                    target.at[:, pl.ds(f * LANES, LANES)],
                    local.at[len(keep)],
                )
            )
    for copy in keep:
        copy.start()
    peers.meet()
    for copy in keep:
        copy.wait()

    sent = []

    def start(*copy):
        moving = remote(*copy)
        moving.start()
        sent.append(moving)

    for i, (own, copies) in enumerate(zip(own_refs, copies_refs)):
        start(own, copies.at[2], rep_sems, (i, 0), peers.across)
        start(own, copies.at[1], rep_sems, (i, 1), peers.core)

    def chunk(ref, c, step, n):
        return ref.at[pl.ds(c * n, n), :]

    def owner(way, step):
        return peers.at(-step if way == 0 else step)

    def come(way, step, c):
        piece = chunk(whole_ref.at[owner(way, step)], c, step, rows)
        remote(piece, piece, ring_sems, (way, step - 1, c), peers.ring[way]).wait_recv()

    def few_piece(way, step, last):
        columns = pl.ds(pl.multiple_of(owner(way, step) * LANES, LANES), LANES)
        return all_ref.at[pl.ds(way * few_rows if last else 0, few_rows * (1 if last else 2)), columns]

    def few_come(way, step):
        piece = few_piece(way, step, step == half)
        remote(piece, piece, few_sems, (way, step - 1), peers.ring[way]).wait_recv()

    for step in range(1, half + 1):
        last = step == half
        for way in range(2):
            if step > 1:
                few_come(way, step - 1)
            target = few_piece(way, step - 1, last)
            source = few_ref if step == 1 else target
            start(source, target, few_sems, (way, step - 1), peers.ring[way])
        for c in range(2):
            for way in range(2):
                if last and c != way:
                    continue
                if step > 1:
                    come(way, step - 1, c)
                target = chunk(whole_ref.at[owner(way, step - 1)], c, step, rows)
                source = chunk(inner_ref, c, step, rows) if step == 1 else target
                start(source, target, ring_sems, (way, step - 1, c), peers.ring[way])
        if step == 1:
            mine = pl.ds(pl.multiple_of(peers.member * LANES, LANES), LANES)
            keep = [
                pltpu.make_async_copy(inner_ref, whole_ref.at[peers.member], local.at[0]),
                pltpu.make_async_copy(few_ref, all_ref.at[:, mine], local.at[1]),
            ]
            for i, (own, copies) in enumerate(zip(own_refs, copies_refs)):
                keep.append(pltpu.make_async_copy(own, copies.at[0], local.at[2 + i]))
            for copy in keep:
                copy.start()
    for i, copies in enumerate(copies_refs):
        remote(copies.at[2], copies.at[2], rep_sems, (i, 0), peers.across).wait_recv()
        start(copies.at[2], copies.at[3], rep_sems, (i, 2), peers.core)
    for way in range(2):
        come(way, half - 1, 1 - way)
        come(way, half, way)
        few_come(way, half)
    for i, copies in enumerate(copies_refs):
        remote(copies.at[1], copies.at[1], rep_sems, (i, 1), peers.core).wait_recv()
        remote(copies.at[3], copies.at[3], rep_sems, (i, 2), peers.core).wait_recv()
    for moving in sent:
        moving.wait_send()
    for copy in keep:
        copy.wait()


def gather_all(size, entry, few, own):
    anywhere = pl.BlockSpec(memory_space=pl.ANY)
    count, half = len(own), size // 2
    shard = (entry.shape[0], size * LANES)

    def kernel(*refs):
        entry_ref, few_ref = refs[:2]
        own_refs = refs[2 : 2 + count]
        whole_ref, gate_ref, all_ref = refs[2 + count : 5 + count]
        copies_refs = refs[5 + count : 5 + 2 * count]
        inner_ref, local, *sems = refs[5 + 2 * count :]
        pairs = [sems[i : i + 2] for i in range(0, 6, 2)]
        gather_kernel(
            size, entry_ref, few_ref, own_refs, whole_ref, gate_ref, all_ref, copies_refs, inner_ref, local, *pairs
        )

    ring_sems = pltpu.SemaphoreType.DMA((2, half, 2))
    few_sems = pltpu.SemaphoreType.DMA((2, half))
    rep_sems = pltpu.SemaphoreType.DMA((count, 3))
    outs = [
        jax.ShapeDtypeStruct((size,) + shard, entry.dtype),
        jax.ShapeDtypeStruct(shard, entry.dtype),
        jax.ShapeDtypeStruct((few.shape[0], size * LANES), few.dtype),
    ] + [jax.ShapeDtypeStruct((COPIES,) + o.shape, o.dtype) for o in own]
    return pl.pallas_call(
        kernel,
        in_specs=[anywhere] * (2 + count),
        out_specs=[anywhere] * (3 + count),
        out_shape=outs,
        scratch_shapes=[pltpu.VMEM(shard, entry.dtype), pltpu.SemaphoreType.DMA((2 * size,))]
        + [ring_sems] * 2
        + [few_sems] * 2
        + [rep_sems] * 2,
        compiler_params=pltpu.CompilerParams(collective_id=1, has_side_effects=True),
        cost_estimate=cost(0, 4 * size * shard[0] * shard[1]),
        name="gather_all",
    )(entry, few, *own)


def scatter_kernel(
    size, grads_ref, small_ref, parts_ref, pieces_ref, small_pieces_ref, normed_ref,
    held, small_held, pair, far_out, far_in, ring_send, ring_recv, few_send, few_recv, rep_send, rep_recv, norm_send, norm_recv,
):
    peers = Peers(size)
    half = peers.half
    rows, few_rows = grads_ref.shape[1] // 2, small_ref.shape[1] // 2
    ring_sems, few_sems = (ring_send, ring_recv), (few_send, few_recv)
    rep_sems, norm_sems = (rep_send, rep_recv), (norm_send, norm_recv)
    peers.meet()
    sent = []

    def start(*copy):
        moving = remote(*copy)
        moving.start()
        sent.append(moving)

    def of_chunk(c):
        return pl.ds(c * rows, rows)

    def of_few(way):
        return pl.ds(way * few_rows, few_rows)

    def owner(way, step):
        away = half + 1 - step
        return peers.at(away if way == 0 else -away)

    def come(way, step, c):
        piece = held.at[way, step - 1, of_chunk(c), :]
        remote(piece, piece, ring_sems, (way, step - 1, c), peers.ring[way]).wait_recv()
        return piece

    def few_come(way, step):
        piece = small_held.at[way, step - 1]
        piece = piece.at[of_few(way), :] if step == 1 else piece
        remote(piece, piece, few_sems, (way, step - 1), peers.ring[way]).wait_recv()

    for way in range(2):
        start(
            grads_ref.at[owner(way, 1), of_chunk(way), :], held.at[way, 0, of_chunk(way), :],
            ring_sems, (way, 0, way), peers.ring[way],
        )
        start(
            small_ref.at[owner(way, 1), of_few(way), :], small_held.at[way, 0, of_few(way), :],
            few_sems, (way, 0), peers.ring[way],
        )
    for i in range(2):
        start(parts_ref.at[1 + 2 * i], pair.at[i], norm_sems, i, peers.core)
    for i in range(2):
        remote(pair.at[i], pair.at[i], norm_sems, i, peers.core).wait_recv()
    far_out[...] = (parts_ref[2].astype(F32) + pair[1].astype(F32)).astype(BF16)
    start(far_out, far_in, norm_sems, 2, peers.across)
    normed_ref[...] = parts_ref[0].astype(F32) + pair[0].astype(F32)

    for step in range(2, half + 1):
        for c in range(2):
            for way in range(2):
                block = owner(way, step)
                target = held.at[way, step - 1, of_chunk(c), :]
                if step == 2 and c != way:
                    source = grads_ref.at[block, of_chunk(c), :]
                else:
                    source = come(way, step - 1, c)
                    source[...] = (
                        grads_ref[block, of_chunk(c), :].astype(F32) + source[...].astype(F32)
                    ).astype(BF16)
                start(source, target, ring_sems, (way, step - 1, c), peers.ring[way])
        for way in range(2):
            block = owner(way, step)
            few_come(way, step - 1)
            source = small_held.at[way, step - 2]
            if step == 2:
                there, rest = of_few(way), of_few(1 - way)
                source[rest, :] = small_ref[block, rest, :]
            else:
                there = pl.ds(0, 2 * few_rows)
            source[there, :] = (
                small_ref[block, there, :].astype(F32) + source[there, :].astype(F32)
            ).astype(BF16)
            start(source, small_held.at[way, step - 1], few_sems, (way, step - 1), peers.ring[way])

    for c in range(2):
        at = of_chunk(c)
        for way in range(2):
            come(way, half, c)
        total = grads_ref[peers.member, at, :].astype(F32)
        for way in range(2):
            total = total + held[way, half - 1, at, :].astype(F32)
        pieces_ref[0, at, :] = total.astype(BF16)
        start(pieces_ref.at[0, at, :], pieces_ref.at[2, at, :], rep_sems, (c, 0), peers.across)
        start(pieces_ref.at[0, at, :], pieces_ref.at[1, at, :], rep_sems, (c, 1), peers.core)
    for way in range(2):
        few_come(way, half)
    total = small_ref[peers.member].astype(F32)
    for way in range(2):
        total = total + small_held[way, half - 1].astype(F32)
    small_pieces_ref[0] = total.astype(BF16)
    start(small_pieces_ref.at[0], small_pieces_ref.at[2], rep_sems, (2, 0), peers.across)
    start(small_pieces_ref.at[0], small_pieces_ref.at[1], rep_sems, (2, 1), peers.core)

    remote(far_in, far_in, norm_sems, 2, peers.across).wait_recv()
    normed_ref[...] = normed_ref[...] + far_in[...].astype(F32)

    def views(index):
        if index == 2:
            return [small_pieces_ref.at[k] for k in range(COPIES)]
        return [pieces_ref.at[k, of_chunk(index), :] for k in range(COPIES)]

    for index in range(3):
        view = views(index)
        remote(view[2], view[2], rep_sems, (index, 0), peers.across).wait_recv()
        start(view[2], view[3], rep_sems, (index, 2), peers.core)
    for index in range(3):
        view = views(index)
        remote(view[1], view[1], rep_sems, (index, 1), peers.core).wait_recv()
        remote(view[3], view[3], rep_sems, (index, 2), peers.core).wait_recv()
    for moving in sent:
        moving.wait_send()


def scatter_all(size, grads, small, parts):
    inside = pl.BlockSpec(memory_space=pltpu.VMEM)
    half = size // 2
    dma = pltpu.SemaphoreType.DMA
    return pl.pallas_call(
        functools.partial(scatter_kernel, size),
        in_specs=[inside] * 3,
        out_specs=[inside] * 3,
        out_shape=[
            jax.ShapeDtypeStruct((COPIES,) + grads.shape[1:], BF16),
            jax.ShapeDtypeStruct((COPIES,) + small.shape[1:], BF16),
            jax.ShapeDtypeStruct(parts.shape[1:], F32),
        ],
        scratch_shapes=[
            pltpu.VMEM((2, half) + grads.shape[1:], BF16),
            pltpu.VMEM((2, half) + small.shape[1:], BF16),
            pltpu.VMEM((2,) + parts.shape[1:], BF16),
            pltpu.VMEM(parts.shape[1:], BF16),
            pltpu.VMEM(parts.shape[1:], BF16),
        ]
        + [dma((2, half, 2))] * 2
        + [dma((2, half))] * 2
        + [dma((3, 3))] * 2
        + [dma((3,))] * 2,
        compiler_params=pltpu.CompilerParams(
            collective_id=2, has_side_effects=True, vmem_limit_bytes=VMEM_LIMIT
        ),
        cost_estimate=cost(0, 4 * grads.size),
        name="scatter_all",
    )(grads, small, parts)


def spread(coefs, nstate):
    terms = []
    for _ in range(3):
        term = coefs.astype(BF16)
        terms.append(term)
        coefs = coefs - term.astype(F32)
    joined = jnp.concatenate(terms, axis=1)
    return jnp.pad(joined, ((0, 0), (0, LANES - joined.shape[1])))


def spreader(nstate):
    row = lax.broadcasted_iota(jnp.int32, (LANES, 2 * nstate * LANES), 0)
    tile = lax.broadcasted_iota(jnp.int32, (LANES, 2 * nstate * LANES), 1) // LANES
    return ((row % (2 * nstate) == tile) & (row < 6 * nstate)).astype(BF16)


def folder(nstate):
    tile = lax.broadcasted_iota(jnp.int32, (2 * nstate * LANES, LANES), 0) // LANES
    column = lax.broadcasted_iota(jnp.int32, (2 * nstate * LANES, LANES), 1)
    return (tile == column).astype(BF16)


def tiled(value, width):
    return jnp.concatenate([value] * (width // LANES), axis=1)


def at_time(t):
    return pl.ds(pl.multiple_of(t * GROUP, GROUP), GROUP)


def scan_kernel(
    nstate, chunk, pre_ref, act_ref, coef_ref, spread_ref, keep_ref, rate_ref, row_ref, held_ref, *refs
):
    out_ref, step_ref, start_ref, carry_ref, wide = refs[-5:]
    width = pre_ref.shape[1]

    @pl.when(pl.program_id(0) == 0)
    def _():
        carry_ref[...] = held_ref[...]

    start_ref[0] = carry_ref[...]
    wide[...] = jnp.dot(coef_ref[...], spread_ref[...], preferred_element_type=F32)
    pre = pre_ref[...] + row_ref[0:1]
    step_ref[...] = jnp.maximum(pre, 0.0) + jnp.log1p(jnp.exp(-jnp.abs(pre)))
    for c in range(width // chunk):
        cols = slice(c * chunk, (c + 1) * chunk)

        def advance(t, states):
            at = at_time(t)
            step, act = step_ref[at, cols], act_ref[at, cols]
            drive = jnp.where(tiled(keep_ref[at, :], chunk) > 0.5, step, FAR)
            inflow = step * act
            total = row_ref[1:2, cols] * act
            now = []
            for n in range(nstate):
                write = tiled(wide[at, n * LANES : (n + 1) * LANES], chunk)
                read = tiled(wide[at, (nstate + n) * LANES : (nstate + n + 1) * LANES], chunk)
                state = jnp.exp2(drive * rate_ref[n, :, cols]) * states[n] + write * inflow
                total = total + read * state
                now.append(state)
            out_ref[at, cols] = total
            return tuple(now)

        start = tuple(carry_ref[n, :, cols] for n in range(nstate))
        states = lax.fori_loop(0, BLOCK, advance, start, unroll=4)
        for n in range(nstate):
            carry_ref[n, :, cols] = states[n]


def scan_forward(pre, act, coef, spread_by, keep, rate, rows, held, before, first, count):
    total, width = pre.shape
    nstate = rate.shape[0]
    size = BLOCK * GROUP
    tile = pl.BlockSpec((size, width), lambda t: (first + t, 0))
    thin = pl.BlockSpec((size, LANES), lambda t: (first + t, 0))
    state = pl.BlockSpec((nstate, GROUP, width), lambda t: (0, 0, 0))
    work = count * size * width * nstate
    return pl.pallas_call(
        functools.partial(scan_kernel, nstate, 256),
        grid=(count,),
        in_specs=[
            tile,
            tile,
            thin,
            pl.BlockSpec(spread_by.shape, lambda t: (0, 0)),
            thin,
            state,
            pl.BlockSpec((8, width), lambda t: (0, 0)),
            state,
        ]
        + [pl.BlockSpec(memory_space=pl.ANY)] * len(before),
        out_specs=[
            tile,
            tile,
            pl.BlockSpec((1, nstate, GROUP, width), lambda t: (first + t, 0, 0, 0)),
            state,
        ],
        out_shape=[
            jax.ShapeDtypeStruct((total, width), F32),
            jax.ShapeDtypeStruct((total, width), F32),
            jax.ShapeDtypeStruct((total // size, nstate, GROUP, width), F32),
            jax.ShapeDtypeStruct((nstate, GROUP, width), F32),
        ],
        scratch_shapes=[pltpu.VMEM((size, 2 * nstate * LANES), F32)],
        input_output_aliases={8 + i: i for i in range(len(before))},
        compiler_params=params(),
        cost_estimate=cost(16 * work, 16 * count * size * width),
        name="scan_forward",
    )(pre, act, coef, spread_by, keep, rate, rows, held, *before)


class Guests:
    def __init__(self, size, parts, totals, held, sems):
        self.peers = Peers(size)
        self.parts, self.totals, self.held, self.sems = parts, totals, held, sems

    def rows(self, which, c):
        half = self.parts[which].shape[1] // 2
        return pl.ds(c * half, half)

    def copy(self, which, way, step, c, source=None):
        target = self.held[which].at[way, step - 1, self.rows(which, c), :]
        index = (which, way, step - 1, c)
        source = target if source is None else source
        return remote(source, target, self.sems, index, self.peers.ring[way])

    def chunks(self, way, step):
        return (way,) if step == 1 else (0, 1)

    def own(self, which, way, step, c):
        away = self.peers.half + 1 - step
        block = self.peers.at(away if way == 0 else -away)
        return self.parts[which].at[block, self.rows(which, c), :]

    def source(self, which, way, step, c):
        own = self.own(which, way, step, c)
        if step == 1 or c not in self.chunks(way, step - 1):
            return own
        self.copy(which, way, step - 1, c).wait_recv()
        there = self.held[which].at[way, step - 2, self.rows(which, c), :]
        there[...] = (own[...].astype(F32) + there[...].astype(F32)).astype(BF16)
        return there

    def tick(self, number):
        which, step = number % 2, number // 2 + 1
        for c in range(2):
            for way in range(2):
                if c in self.chunks(way, step):
                    self.copy(which, way, step, c, self.source(which, way, step, c)).start()

    def finish(self):
        last = self.peers.half
        for which in range(2):
            for c in range(2):
                total = self.own(which, 0, last + 1, c)[...].astype(F32)
                for way in range(2):
                    self.copy(which, way, last, c).wait_recv()
                    there = self.held[which].at[way, last - 1, self.rows(which, c), :]
                    total = total + there[...].astype(F32)
                self.totals[which][self.rows(which, c), :] = total.astype(BF16)
        for which in range(2):
            for step in range(1, last + 1):
                for way in range(2):
                    for c in self.chunks(way, step):
                        self.copy(which, way, step, c).wait_send()


def scan_back_kernel(
    nstate, chunk, rings, pre_ref, step_ref, act_ref, grad_ref, coef_ref, spread_ref, fold_ref, keep_ref, rate_ref,
    row_ref, start_ref, *refs,
):
    wide, states_all, decays, parts, sizes = refs[-5:]
    width = pre_ref.shape[1]
    step_now = pl.program_id(0)
    if rings:
        first_ref, second_ref = refs[:2]
        pre_grad_ref, direct_ref, coef_grad_ref, carry_ref, sums_ref = refs[2:7]
        guest = Guests(rings, (first_ref, second_ref), refs[7:9], refs[9:11], refs[11:13])
        for tick in range(2 * guest.peers.half):

            @pl.when(step_now == tick)
            def _(tick=tick):
                if tick == 0:
                    guest.peers.meet()
                guest.tick(tick)

    else:
        pre_grad_ref, direct_ref, coef_grad_ref, carry_ref, sums_ref = refs[-10:-5]

    @pl.when(step_now == 0)
    def _():
        carry_ref[...] = jnp.zeros_like(carry_ref)
        sums_ref[...] = jnp.zeros_like(sums_ref)

    wide[...] = jnp.dot(coef_ref[...], spread_ref[...], preferred_element_type=F32)

    def fold(value):
        total = value[:, :LANES]
        for k in range(1, chunk // LANES):
            total = total + value[:, k * LANES : (k + 1) * LANES]
        return total

    for c in range(width // chunk):
        cols = slice(c * chunk, (c + 1) * chunk)

        def advance(t, states):
            at = at_time(t)
            step = step_ref[at, cols]
            drive = jnp.where(tiled(keep_ref[at, :], chunk) > 0.5, step, FAR)
            inflow = step * act_ref[at, cols]
            now = []
            for n in range(nstate):
                write = tiled(wide[at, n * LANES : (n + 1) * LANES], chunk)
                decay = jnp.exp2(drive * rate_ref[n, :, cols])
                decays[t, n] = decay
                states_all[t, n] = states[n]
                now.append(decay * states[n] + write * inflow)
            return tuple(now)

        start = tuple(start_ref[0, n, :, cols] for n in range(nstate))
        states = lax.fori_loop(0, BLOCK, advance, start, unroll=2)
        for n in range(nstate):
            states_all[BLOCK, n] = states[n]

        def retreat(i, carry):
            t = BLOCK - 1 - i
            at = at_time(t)
            step, act, grad = step_ref[at, cols], act_ref[at, cols], grad_ref[at, cols]
            inflow = step * act
            size = jnp.zeros_like(step)
            direct = jnp.zeros_like(step)
            now = []
            for n in range(nstate):
                tile_w = slice(n * LANES, (n + 1) * LANES)
                tile_r = slice((nstate + n) * LANES, (nstate + n + 1) * LANES)
                state_grad = tiled(wide[at, tile_r], chunk) * grad + carry[n]
                passed = decays[t, n] * state_grad
                through = passed * states_all[t, n]
                size = size + rate_ref[n, :, cols] * through
                direct = direct + state_grad * tiled(wide[at, tile_w], chunk)
                sums_ref[n, :, cols] += step * through
                write_part = fold(state_grad * inflow)
                read_part = fold(grad * states_all[t + 1, n])
                if c == 0:
                    parts[at, tile_w] = write_part
                    parts[at, tile_r] = read_part
                else:
                    parts[at, tile_w] += write_part
                    parts[at, tile_r] += read_part
                now.append(passed)
            sizes[at, cols] = LN2 * size + act * direct
            direct_ref[at, cols] = step * direct + row_ref[1:2, cols] * grad
            sums_ref[nstate, :, cols] += grad * act
            return tuple(now)

        start = tuple(carry_ref[n, :, cols] for n in range(nstate))
        carry = lax.fori_loop(0, BLOCK, retreat, start, unroll=2)
        for n in range(nstate):
            carry_ref[n, :, cols] = carry[n]

    pre_grad = sizes[...] * sigmoid(pre_ref[...] + row_ref[0:1])
    pre_grad_ref[...] = pre_grad.astype(BF16)
    total = pre_grad[:GROUP]
    for t in range(1, BLOCK):
        total = total + pre_grad[t * GROUP : (t + 1) * GROUP]
    sums_ref[nstate + 1] += total
    high = parts[...].astype(BF16)
    low = (parts[...] - high.astype(F32)).astype(BF16)
    coef_grad_ref[...] = jnp.dot(high, fold_ref[...], preferred_element_type=F32) + jnp.dot(
        low, fold_ref[...], preferred_element_type=F32
    )
    if rings:

        @pl.when(step_now == pl.num_programs(0) - 1)
        def _():
            guest.finish()


def scan_backward(
    pre, step, act, grad, coef, spread_by, fold_by, keep, rate, rows, starts, rings, wgrads
):
    total, width = pre.shape
    nstate = rate.shape[0]
    size = BLOCK * GROUP
    chunk = 256
    count = total // size
    tile = pl.BlockSpec((size, width), lambda t: (count - 1 - t, 0))
    thin = pl.BlockSpec((size, LANES), lambda t: (count - 1 - t, 0))
    state = pl.BlockSpec((nstate, GROUP, width), lambda t: (0, 0, 0))
    tally = pl.BlockSpec((nstate + 2, GROUP, width), lambda t: (0, 0, 0))
    work = count * size * width * nstate
    inside = pl.BlockSpec(memory_space=pltpu.VMEM)
    half = rings // 2
    guests = [jax.ShapeDtypeStruct(w.shape[1:], BF16) for w in wgrads]
    sems = [pltpu.SemaphoreType.DMA((2, 2, half, 2))] * 2 if rings else []
    return pl.pallas_call(
        functools.partial(scan_back_kernel, nstate, chunk, rings),
        grid=(count,),
        in_specs=[
            tile,
            tile,
            tile,
            tile,
            thin,
            pl.BlockSpec(spread_by.shape, lambda t: (0, 0)),
            pl.BlockSpec(fold_by.shape, lambda t: (0, 0)),
            thin,
            state,
            pl.BlockSpec((8, width), lambda t: (0, 0)),
            pl.BlockSpec((1, nstate, GROUP, width), lambda t: (count - 1 - t, 0, 0, 0)),
        ]
        + [inside] * len(wgrads),
        out_specs=[tile, tile, thin, state, tally] + [inside] * len(wgrads),
        out_shape=[
            jax.ShapeDtypeStruct((total, width), BF16),
            jax.ShapeDtypeStruct((total, width), F32),
            jax.ShapeDtypeStruct((total, LANES), F32),
            jax.ShapeDtypeStruct((nstate, GROUP, width), F32),
            jax.ShapeDtypeStruct((nstate + 2, GROUP, width), F32),
        ]
        + guests,
        scratch_shapes=[pltpu.VMEM((2, half) + w.shape[1:], BF16) for w in wgrads]
        + sems
        + [
            pltpu.VMEM((size, 2 * nstate * LANES), F32),
            pltpu.VMEM((BLOCK + 1, nstate, GROUP, chunk), F32),
            pltpu.VMEM((BLOCK, nstate, GROUP, chunk), F32),
            pltpu.VMEM((size, 2 * nstate * LANES), F32),
            pltpu.VMEM((size, width), F32),
        ],
        compiler_params=pltpu.CompilerParams(
            collective_id=3, has_side_effects=True, vmem_limit_bytes=VMEM_LIMIT
        )
        if rings
        else params(),
        cost_estimate=cost(40 * work, 24 * count * size * width),
        name="scan_backward",
    )(pre, step, act, grad, coef, spread_by, fold_by, keep, rate, rows, starts, *wgrads)


def spread_columns_kernel(copy_ref, *refs):
    pieces, weight_ref, out_ref, gain_ref = refs[:4], refs[4], refs[-2], refs[-1]
    part = pieces[0].shape[1]

    @pl.when(pl.program_id(0) == 0)
    def _():
        gain_ref[...] = jnp.zeros_like(gain_ref)

    total = gain_ref[...]
    for k, piece in enumerate(pieces):
        at = pl.ds(pl.multiple_of((copy_ref[0] ^ k) * part, part), part)
        value = piece[...].astype(F32)
        out_ref[:, at] = value
        total = total + value * weight_ref[:, at].astype(F32)
    gain_ref[...] = total


def spread_columns(copy, pieces, weight, side, before=None):
    rows, width = pieces[0].shape
    part = LANES
    shares = width // part
    block = pl.BlockSpec((rows, COPIES * part), lambda f, copy: (0, side * shares + f))
    piece = pl.BlockSpec((rows, part), lambda f, copy: (0, f))
    extra = [] if before is None else [before]
    return pl.pallas_call(
        spread_columns_kernel,
        grid_spec=pltpu.PrefetchScalarGridSpec(
            num_scalar_prefetch=1,
            grid=(shares,),
            in_specs=[piece] * 4 + [block] + [pl.BlockSpec(memory_space=pl.ANY)] * len(extra),
            out_specs=[block, pl.BlockSpec((rows, part), lambda f, copy: (0, 0))],
        ),
        out_shape=[
            jax.ShapeDtypeStruct(weight.shape, F32),
            jax.ShapeDtypeStruct((rows, part), F32),
        ],
        input_output_aliases={6: 0} if extra else {},
        compiler_params=params(),
        cost_estimate=cost(4 * rows * width, 20 * rows * width),
        name="spread_columns",
    )(copy, *pieces, weight, *extra)


def spread_rows_kernel(copy_ref, *refs):
    pieces, out_ref = refs[:4], refs[4]
    part = pieces[0].shape[0]
    for k, piece in enumerate(pieces):
        at = pl.ds(pl.multiple_of((copy_ref[0] ^ k) * part, part), part)
        out_ref[at, :] = piece[...].astype(F32)


def spread_rows(copy, pieces):
    part, columns = pieces[0].shape
    tile = 512
    return pl.pallas_call(
        spread_rows_kernel,
        grid_spec=pltpu.PrefetchScalarGridSpec(
            num_scalar_prefetch=1,
            grid=(columns // tile,),
            in_specs=[pl.BlockSpec((part, tile), lambda c, copy: (0, c))] * 4,
            out_specs=pl.BlockSpec((COPIES * part, tile), lambda c, copy: (0, c)),
        ),
        out_shape=jax.ShapeDtypeStruct((COPIES * part, columns), F32),
        compiler_params=params(),
        cost_estimate=cost(4 * part * columns, 24 * part * columns),
        name="spread_rows",
    )(copy, *pieces)


def on_device(
    tokens, segment_ids, out_grad, norm_gain, in_proj, conv_weight, conv_bias, x_proj,
    step_proj, step_bias, decay_log, skip_gain, out_proj, *, fsdp,
):
    ring = Ring(fsdp)
    copy = lax.axis_index("rep")
    batches, length, model = tokens.shape
    total = COPIES * batches * length
    slab = in_proj.shape[0]
    share = out_proj.shape[0]
    part = share // COPIES
    width = fsdp * part
    rank, nstate = step_proj.shape[1], decay_log.shape[1]
    taps_n = conv_weight.shape[1]
    gains_n = slab // part

    def mine(value):
        return lax.dynamic_slice_in_dim(value, copy * part, part, 0)

    copy_index = copy.astype(jnp.int32).reshape(1)
    aligned = part % LANES == 0
    if not aligned:
        entry = lax.dynamic_index_in_dim(
            in_proj.reshape(slab, 2, fsdp, COPIES, part), copy, 3, keepdims=False
        )
        inner_shard, gate_shard = (entry[:, i].reshape(slab, width) for i in range(2))
    few = jnp.concatenate(
        [
            mine(x_proj).T,
            mine(step_proj).T,
            mine(conv_weight).T,
            mine(conv_bias)[None],
            mine(step_bias)[None],
            mine(decay_log).T,
            mine(skip_gain)[None],
            norm_gain.reshape(gains_n, part),
        ],
        axis=0,
    )
    few = jnp.pad(few, ((0, -few.shape[0] % 16), (0, 0)))
    small_ring = ring.half == 4
    own = [tokens, out_grad, segment_ids[:, 0, :]]
    if small_ring and aligned:
        inner_in, gate_shard, few_all, *copies = gather_all(fsdp, in_proj, few, own)
        few_all = few_all.astype(F32)
    else:
        gathers = [Gather(ring, inner_shard), Gather(ring, few)]
        for gather in gathers:
            gather.rest()
        inner_in, few_all = (gather.whole for gather in gathers)
        few_all = jnp.moveaxis(few_all, 0, 1).reshape(-1, width).astype(F32)
        copies = [jnp.stack(rep_gather(value)) for value in own]
    inner_in, out_shard = lax.optimization_barrier((inner_in, mine(out_proj)))
    gate_gather = Gather(ring, gate_shard)
    out_gather = Gather(ring, out_shard)
    inner_in = inner_in.reshape(model, width)
    values, cotangent, segments = (c.reshape((GROUP,) + c.shape[2:]) for c in copies)

    sizes = [rank + 2 * nstate, rank, taps_n, 1, 1, nstate, 1, gains_n]
    pieces, start = [], 0
    for size in sizes:
        pieces.append(few_all[start : start + size])
        start += size
    select, stride, taps, shift_bias, size_bias, decay, skip, gain = pieces
    select, stride = select.astype(BF16), stride.astype(BF16)
    gain = jnp.moveaxis(gain.reshape(gains_n, fsdp, part), 0, 1).reshape(model)

    def masks_of(segments):
        masks = []
        for shift in range(1, taps_n):
            earlier = jnp.pad(segments, ((0, 0), (shift, 0)), constant_values=-1)[:, :length]
            masks.append((earlier == segments).astype(F32).T.reshape(total, 1))
        return jnp.broadcast_to(jnp.stack(masks), (taps_n - 1, total, LANES))

    def small_terms():
        tap_rows = jnp.concatenate(
            [taps, shift_bias, jnp.zeros((7 - taps_n, width), F32)]
        )
        side_rows = jnp.concatenate(
            [size_bias, skip, jnp.zeros((6, width), F32)]
        )
        decay_rate = -jnp.exp(decay)
        rate = jnp.broadcast_to((decay_rate * LOG2E)[:, None, :], (nstate, GROUP, width))
        return tap_rows, side_rows, decay_rate, rate, masks_of(segments), spreader(nstate), folder(nstate)

    tap_rows, side_rows, decay_rate, rate, masks, spread_by, fold_by = small_terms()
    normed = interleave(values, gain)
    keep = masks[0]

    state0 = jnp.zeros((nstate, GROUP, width), F32)
    blocks = length // BLOCK
    store = {}

    def g1():
        inner = dot(normed, inner_in, 1, 0)
        return (inner,) + tuple(conv_forward(inner, masks, tap_rows))

    def g2():
        part_sums = dot(store["act_low"], select, 1, 1)
        return sum_near(by_copy(part_sums))

    def g3():
        projected = to_time(sum_far(store["half_sums"]).reshape(total, -1))
        store["step_low"] = projected[:, :rank].astype(BF16)
        store["coef"] = spread(projected[:, rank:], nstate)
        store["pre"] = dot(store["step_low"], stride, 1, 0)
        return store["step_low"], store["coef"], store["pre"], forward_part(0, (), state0)

    def forward_part(first, before, held):
        return tuple(
            scan_forward(
                store["pre"], store["act"], store["coef"], spread_by, keep, rate, side_rows,
                held, before, first, blocks // 2,
            )
        )

    def g4():
        out = store["scan"]
        return forward_part(blocks // 2, out[:3], out[3])

    movers = [gate_gather] if small_ring else []
    ((store["inner"], store["act"], store["act_low"]),) = slot(1, movers, g1)
    (store["half_sums"],) = slot(2, movers, g2)
    ((store["step_low"], store["coef"], store["pre"], store["scan"]),) = slot(3, movers, g3)
    (store["scan"],) = slot(4, movers, g4)
    if not small_ring:
        gate_gather.rest()
    readout, step, starts, _ = store["scan"]
    gate_in = gate_gather.whole.reshape(model, width)

    def o1():
        return dot(normed, gate_in, 1, 0)

    def o2():
        return gate_forward(readout, store["gate"])

    def o3():
        return dot(gated, cotangent, 0, 0).astype(BF16).reshape(fsdp, part, model)

    movers = [out_gather] if small_ring else []
    (store["gate"],) = slot(1, movers, o1)
    (gated, gated_natural), cotangent = slot(2, movers, o2, lambda: interleave(cotangent))
    (out_wgrad,) = slot(3, movers, o3)
    slot(4, movers)
    if not small_ring:
        out_gather.rest()
    out_w = out_gather.whole.reshape(width, model)
    gate, inner, act, act_low = (store[k] for k in ("gate", "inner", "act", "act_low"))
    pre, coef, step_low = store["pre"], store["coef"], store["step_low"]

    fused = small_ring and aligned
    def r1():
        return gate_backward(dot(cotangent, out_w, 1, 1), readout, gate)

    read_grad, gate_grad, gate_grad_natural = r1()

    gate_wgrad = dot(normed, gate_grad, 0, 0).astype(BF16).reshape(fsdp, slab, width)
    wgrads = [out_wgrad, gate_wgrad] if fused else []
    pre_low, direct, coef_part, _, sums, *totals = scan_backward(
        pre, step, act, read_grad, coef, spread_by, fold_by, keep, rate, side_rows, starts,
        fsdp if fused else 0, wgrads,
    )
    if not fused:
        scatters = [Scatter(ring, out_wgrad), Scatter(ring, gate_wgrad)]
        for scatter in scatters:
            scatter.rest()
        totals = [scatter.total.astype(BF16) for scatter in scatters]
    low_part = dot(pre_low, stride, 1, 1)
    proj_part = jnp.concatenate([low_part, coef_part[:, : 2 * nstate]], axis=1)
    gated_natural, gate_grad_natural = after(pre_low, gated_natural, gate_grad_natural)

    def norm_gate_part():
        return dot(gate_grad_natural, gate_in, 1, 1)

    def out_part():
        return by_copy(dot(gated_natural, out_w, 1, 0).astype(BF16))

    def proj_sums():
        return sum_near(by_copy(to_sequence(proj_part)))

    half_sums, out_parts, norm_gate, out_pieces = slot(
        3, [], proj_sums, out_part, norm_gate_part, lambda: rep_gather(totals[0])
    )

    def conv_part():
        proj_low = sum_far(half_sums).reshape(total, -1).astype(BF16)
        act_grad = direct + dot(to_time(proj_low), select, 1, 0)
        inner_grad, inner_grad_natural, conv_sums = conv_backward(inner, act_grad, masks, tap_rows)
        inner_wgrad = dot(normed, inner_grad, 0, 0).astype(BF16).reshape(fsdp, slab, width)
        small = jnp.concatenate(
            [
                dot(proj_low, act_low, 0, 0),
                dot(step_low, pre_low, 0, 0),
                conv_sums[: taps_n + 1],
                jnp.sum(sums[nstate + 1 :], axis=1),
                decay_rate * jnp.sum(sums[:nstate], axis=1),
                jnp.sum(sums[nstate : nstate + 1], axis=1),
            ],
            axis=0,
        )
        small = jnp.pad(small, ((0, -small.shape[0] % 16), (0, 0))).astype(BF16)
        small = jnp.moveaxis(small.reshape(-1, fsdp, part), 1, 0)
        return inner_grad_natural, inner_wgrad, small

    (inner_grad_natural, inner_wgrad, small), (out_near, out_far) = slot(
        4, [], conv_part, lambda: rep_scatter_near(out_parts)
    )

    grads = dot(inner_grad_natural, inner_in, 1, 1) + norm_gate
    norm_parts = by_copy(grads.astype(BF16))

    def finish_out():
        summed = rep_scatter_far(out_near, out_far)
        return (tokens.astype(F32) + summed.reshape(tokens.shape)).astype(BF16)

    gate_pieces = rep_gather(totals[1])

    def place_gate():
        if not aligned:
            return gate_pieces
        return spread_columns(copy_index, gate_pieces, in_proj, 1)

    def place_out():
        if aligned:
            return spread_rows(copy_index, out_pieces)
        return jnp.stack(out_pieces)[jnp.arange(COPIES) ^ copy].reshape(share, model).astype(F32)

    gate_placed, out_all, block_out = place_gate(), place_out(), finish_out()
    if small_ring and aligned:
        inner_pieces, small_pieces, normed_sum = scatter_all(fsdp, inner_wgrad, small, norm_parts)
        inner_pieces = [inner_pieces[k] for k in range(COPIES)]
        small_pieces = [small_pieces[k] for k in range(COPIES)]
    else:
        near, far = rep_scatter_near(norm_parts)
        normed_sum = rep_scatter_far(near, far)
        scatters = [Scatter(ring, inner_wgrad), Scatter(ring, small)]
        for scatter in scatters:
            scatter.rest()
        inner_pieces, small_pieces = (rep_gather(s.total.astype(BF16)) for s in scatters)

    def finish_tokens():
        normed_grad = normed_sum.reshape(tokens.shape)
        own = tokens.astype(F32)
        own_scale = lax.rsqrt(jnp.mean(own * own, axis=-1, keepdims=True) + EPS)
        scaled = normed_grad * gain
        lean = jnp.mean(scaled * own, axis=-1, keepdims=True)
        return (
            out_grad.astype(F32) + own_scale * scaled - own * (own_scale**3) * lean
        ).astype(BF16)

    input_grad = finish_tokens()

    order = jnp.arange(COPIES) ^ copy
    if aligned:
        entry_all, gain_inner = spread_columns(
            copy_index, inner_pieces, in_proj, 0, gate_placed[0]
        )
        gain_sum = jnp.sum(gain_inner + gate_placed[1], axis=1)
    else:
        halves = jnp.stack([jnp.stack(inner_pieces), jnp.stack(gate_placed)])[:, order]
        halves = halves.reshape(2, COPIES, slab, fsdp, part).astype(F32)
        entry_all = jnp.transpose(halves, (2, 0, 3, 1, 4)).reshape(slab, -1)
        gain_sum = jnp.sum(entry_all * in_proj.astype(F32), axis=1)
    gain_grad = gain_sum / norm_gain.astype(F32)
    small_all = jnp.stack(small_pieces)[order].astype(F32)
    small_all = jnp.moveaxis(small_all, 0, 1).reshape(-1, share)
    out, start = [], 0
    for size in sizes[:-1]:
        out.append(small_all[start : start + size])
        start += size
    select_g, stride_g, taps_g, shift_g, size_g, decay_g, skip_g = out
    return (
        block_out,
        input_grad,
        gain_grad,
        entry_all,
        taps_g.T,
        shift_g[0],
        select_g.T,
        stride_g.T,
        size_g[0],
        decay_g.T,
        skip_g[0],
        out_all,
    )


def solution(mesh):
    tokens = P(None, ("fsdp", "rep"), None)
    rows, row = P("fsdp", None), P("fsdp")
    return jax.shard_map(
        functools.partial(on_device, fsdp=mesh.shape["fsdp"]),
        mesh=mesh,
        in_specs=(tokens, tokens, tokens, row, rows, rows, row, rows, rows, row, rows, row, rows),
        out_specs=(tokens, tokens, row, rows, rows, row, rows, rows, row, rows, row, rows),
        check_vma=False,
    )
```

```python
import functools

import jax
import jax.numpy as jnp
from jax import lax
from jax.experimental import pallas as pl
from jax.experimental.pallas import tpu as pltpu
from jax.sharding import PartitionSpec as P

EPS = 1e-05
BLOCK = 16
LANES = 128
GROUP = 8
COPIES = 4
LOG2E = 1.4426950408889634
LN2 = 0.6931471805599453
FAR = 1e30
F32 = jnp.float32
BF16 = jnp.bfloat16
VMEM_LIMIT = 56 * 1024 * 1024


def dot(left, right, left_dim, right_dim):
    return lax.dot_general(
        left, right, (((left_dim,), (right_dim,)), ((), ())), preferred_element_type=F32
    )


def params():
    return pltpu.CompilerParams(vmem_limit_bytes=VMEM_LIMIT)


def cost(flops, moved):
    return pl.CostEstimate(flops=int(flops), bytes_accessed=int(moved), transcendentals=0)


def blank(shape, dtype):
    return pl.pallas_call(
        lambda ref: None,
        out_shape=jax.ShapeDtypeStruct(shape, dtype),
        out_specs=pl.BlockSpec(memory_space=pl.ANY),
        name="blank",
    )()


def ring_order(size):
    half = size // 2
    return [2 * p if p < half else 2 * (size - 1 - p) + 1 for p in range(size)]


class Ring:
    def __init__(self, size):
        order = ring_order(size)
        place = [0] * size
        for spot, member in enumerate(order):
            place[member] = spot
        self.size, self.half = size, size // 2
        self.order = jnp.array(order, jnp.int32)
        self.spot = jnp.array(place, jnp.int32)[lax.axis_index("fsdp")]
        self.above = [(order[p], order[(p + 1) % size]) for p in range(size)]
        self.below = [(order[p], order[(p - 1) % size]) for p in range(size)]

    def member(self, offset):
        return self.order[(self.spot + offset + self.size) % self.size]

    def up(self, value):
        return lax.ppermute(value, "fsdp", self.above)

    def down(self, value):
        return lax.ppermute(value, "fsdp", self.below)


class Gather:
    def __init__(self, ring, shard):
        self.ring, self.cut = ring, shard.shape[0] // 2
        self.whole = blank((ring.size,) + shard.shape, shard.dtype)
        self.held = (shard, shard)
        self.put(shard, 0)

    def put(self, piece, offset, start=0):
        at = (self.ring.member(offset), jnp.int32(start), jnp.int32(0))
        self.whole = lax.dynamic_update_slice(self.whole, piece[None], at)

    def step(self, number):
        low, high = self.held
        if number == self.ring.half:
            low, high = low[: self.cut], high[self.cut :]
        return self.ring.up(low), self.ring.down(high)

    def take(self, number, got):
        self.held = got
        last = number == self.ring.half
        self.put(got[0], -number)
        self.put(got[1], number, self.cut if last else 0)

    def rest(self):
        def body(number, state):
            whole, low, high = state
            low, high = self.ring.up(low), self.ring.down(high)
            self.whole = whole
            self.put(low, -number)
            self.put(high, number)
            return self.whole, low, high

        self.whole, low, high = lax.fori_loop(1, self.ring.half, body, (self.whole,) + self.held)
        self.held = (low, high)
        self.take(self.ring.half, self.step(self.ring.half))


class Scatter:
    def __init__(self, ring, parts):
        self.ring, self.parts, self.cut = ring, parts, parts.shape[1] // 2
        far = self.own(ring.half)
        self.sent = (far[: self.cut], far[self.cut :])
        self.total = None

    def own(self, offset):
        return lax.dynamic_index_in_dim(self.parts, self.ring.member(offset), 0, keepdims=False)

    def step(self, number):
        return self.ring.up(self.sent[0]), self.ring.down(self.sent[1])

    def take(self, number, got):
        left = self.ring.half - number
        low, high = got
        near_low, near_high = self.own(left), self.own(-left)
        if number == 1:
            low = jnp.concatenate([low, jnp.zeros_like(near_low[self.cut :])])
            high = jnp.concatenate([jnp.zeros_like(near_high[: self.cut]), high])
        if left == 0:
            self.total = near_low.astype(F32) + low.astype(F32) + high.astype(F32)
        else:
            self.sent = (self.add(near_low, low), self.add(near_high, high))

    def add(self, near, got):
        return (near.astype(F32) + got.astype(F32)).astype(near.dtype)

    def rest(self):
        self.take(1, self.step(1))

        def body(number, sent):
            left = self.ring.half - number
            low, high = self.ring.up(sent[0]), self.ring.down(sent[1])
            return self.add(self.own(left), low), self.add(self.own(-left), high)

        self.sent = lax.fori_loop(2, self.ring.half, body, self.sent)
        self.take(self.ring.half, self.step(self.ring.half))


def after(value, *held):
    return lax.optimization_barrier((value, held))[1]


def slot(number, movers, *work):
    moved = tuple(m.step(number) for m in movers)
    done = tuple(w() for w in work)
    moved, done = lax.optimization_barrier((moved, done))
    for mover, got in zip(movers, moved):
        mover.take(number, got)
    return done


def swap(value, bit):
    return lax.ppermute(value, "rep", [(r, r ^ bit) for r in range(COPIES)])


def rep_gather(value):
    across = swap(value, 2)
    return [value, swap(value, 1), across, swap(across, 1)]


def rep_scatter_near(parts):
    pair = swap(jnp.stack([parts[1], parts[3]]), 1)
    near = parts[0].astype(F32) + pair[0].astype(F32)
    far = parts[2].astype(F32) + pair[1].astype(F32)
    return near, far.astype(parts.dtype)


def rep_scatter_far(near, far):
    return near + swap(far, 2).astype(F32)


def sum_near(parts):
    pair = swap(jnp.stack([parts[1], parts[3]]), 1)
    mine = jnp.stack([parts[0], parts[2]]) + pair
    return mine + swap(jnp.stack([mine[1], mine[0]]), 2)


def sum_far(mine):
    next_to = swap(mine, 1)
    return jnp.stack([mine[0], next_to[0], mine[1], next_to[1]])


def to_time(value):
    return jnp.swapaxes(value.reshape(GROUP, -1, value.shape[-1]), 0, 1).reshape(value.shape)


def to_sequence(value):
    return jnp.swapaxes(value.reshape(-1, GROUP, value.shape[-1]), 0, 1).reshape(value.shape)


def by_copy(value):
    return value.reshape(COPIES, -1, value.shape[-1])


def sigmoid(value):
    return 1.0 / (1.0 + jnp.exp(-value))


def later(value, shift):
    rows = shift * GROUP
    return jnp.concatenate([jnp.zeros_like(value[:rows]), value[:-rows]], axis=0)


def sooner(value, shift):
    rows = shift * GROUP
    return jnp.concatenate([value[rows:], jnp.zeros_like(value[:rows])], axis=0)


def conv_of(inner, masks, taps):
    total = taps[4:5] + taps[3:4] * inner
    for shift in range(1, 4):
        total = total + taps[3 - shift : 4 - shift] * (later(inner, shift) * masks[shift - 1])
    return total


def by_sequence(held, out_ref, value):
    length = value.shape[0] // GROUP
    held[...] = value
    for s in range(GROUP):
        out_ref[s * length : (s + 1) * length, :] = held[
            pl.ds(s, length, stride=GROUP), :
        ].astype(out_ref.dtype)


def conv_kernel(inner_ref, masks_ref, taps_ref, act_ref, low_ref):
    value = conv_of(inner_ref[...], masks_ref, taps_ref[...])
    act = value * sigmoid(value)
    act_ref[...] = act
    low_ref[...] = act.astype(BF16)


def conv_forward(inner, masks, taps):
    rows, width = inner.shape
    tile = pl.BlockSpec((rows, LANES), lambda c: (0, c))
    return pl.pallas_call(
        conv_kernel,
        grid=(width // LANES,),
        in_specs=[
            tile,
            pl.BlockSpec((3, rows, LANES), lambda c: (0, 0, 0)),
            pl.BlockSpec((8, LANES), lambda c: (0, c)),
        ],
        out_specs=[tile, tile],
        out_shape=[
            jax.ShapeDtypeStruct((rows, width), F32),
            jax.ShapeDtypeStruct((rows, width), BF16),
        ],
        compiler_params=params(),
        cost_estimate=cost(30 * rows * width, 10 * rows * width),
        name="conv_forward",
    )(inner, masks, taps)


def conv_back_kernel(inner_ref, grad_ref, masks_ref, taps_ref, out_ref, natural_ref, sums_ref, held):
    inner, taps = inner_ref[...], taps_ref[...]
    value = conv_of(inner, masks_ref, taps)
    gate = sigmoid(value)
    grad = grad_ref[...] * (gate * (1.0 + value * (1.0 - gate)))
    total = taps[3:4] * grad
    sums = [None] * 4 + [jnp.sum(grad, axis=0, keepdims=True)]
    sums[3] = jnp.sum(grad * inner, axis=0, keepdims=True)
    for shift in range(1, 4):
        masked = grad * masks_ref[shift - 1]
        total = total + taps[3 - shift : 4 - shift] * sooner(masked, shift)
        sums[3 - shift] = jnp.sum(masked * later(inner, shift), axis=0, keepdims=True)
    out_ref[...] = total.astype(BF16)
    by_sequence(held, natural_ref, total)
    sums_ref[...] = jnp.concatenate(sums + [jnp.zeros((3, inner.shape[1]), F32)], axis=0)


def conv_backward(inner, grad, masks, taps):
    rows, width = inner.shape
    tile = pl.BlockSpec((rows, LANES), lambda c: (0, c))
    few = pl.BlockSpec((8, LANES), lambda c: (0, c))
    return pl.pallas_call(
        conv_back_kernel,
        grid=(width // LANES,),
        in_specs=[tile, tile, pl.BlockSpec((3, rows, LANES), lambda c: (0, 0, 0)), few],
        out_specs=[tile, tile, few],
        out_shape=[
            jax.ShapeDtypeStruct((rows, width), BF16),
            jax.ShapeDtypeStruct((rows, width), BF16),
            jax.ShapeDtypeStruct((8, width), F32),
        ],
        scratch_shapes=[pltpu.VMEM((rows, LANES), F32)],
        compiler_params=params(),
        cost_estimate=cost(60 * rows * width, 10 * rows * width),
        name="conv_backward",
    )(inner, grad, masks, taps)


def gate_kernel(readout_ref, gate_ref, out_ref, natural_ref, held):
    gate = gate_ref[...]
    gated = readout_ref[...] * (gate * sigmoid(gate))
    out_ref[...] = gated.astype(BF16)
    by_sequence(held, natural_ref, gated)


def gate_forward(readout, gate):
    rows, width = gate.shape
    tile = pl.BlockSpec((rows, LANES), lambda c: (0, c))
    return pl.pallas_call(
        gate_kernel,
        grid=(width // LANES,),
        in_specs=[tile] * 2,
        out_specs=[tile] * 2,
        out_shape=[jax.ShapeDtypeStruct((rows, width), BF16)] * 2,
        scratch_shapes=[pltpu.VMEM((rows, LANES), F32)],
        compiler_params=params(),
        cost_estimate=cost(20 * rows * width, 12 * rows * width),
        name="gate_forward",
    )(readout, gate)


def gate_back_kernel(grad_ref, readout_ref, gate_ref, read_ref, out_ref, natural_ref, held):
    gate, grad = gate_ref[...], grad_ref[...]
    sig = sigmoid(gate)
    read_ref[...] = grad * (gate * sig)
    gate_grad = grad * readout_ref[...] * (sig * (1.0 + gate * (1.0 - sig)))
    out_ref[...] = gate_grad.astype(BF16)
    by_sequence(held, natural_ref, gate_grad)


def gate_backward(grad, readout, gate):
    rows, width = gate.shape
    tile = pl.BlockSpec((rows, LANES), lambda c: (0, c))
    return pl.pallas_call(
        gate_back_kernel,
        grid=(width // LANES,),
        in_specs=[tile] * 3,
        out_specs=[tile] * 3,
        out_shape=[jax.ShapeDtypeStruct((rows, width), F32)]
        + [jax.ShapeDtypeStruct((rows, width), BF16)] * 2,
        scratch_shapes=[pltpu.VMEM((rows, LANES), F32)],
        compiler_params=params(),
        cost_estimate=cost(20 * rows * width, 20 * rows * width),
        name="gate_backward",
    )(grad, readout, gate)


def rows_kernel(scaled, *refs):
    values_ref, out_ref, held = refs[0], refs[-2], refs[-1]
    for s in range(GROUP):
        value = values_ref[s].astype(F32)
        if scaled:
            square = jnp.mean(value * value, axis=-1, keepdims=True)
            value = value * lax.rsqrt(square + EPS) * refs[1][...]
        for k in range(held.shape[0]):
            held[k, pl.ds(s, value.shape[0], stride=GROUP), :] = value[
                :, k * LANES : (k + 1) * LANES
            ]
    for k in range(held.shape[0]):
        out_ref[:, k * LANES : (k + 1) * LANES] = held[k].astype(BF16)


def interleave(values, gain=None):
    _, length, model = values.shape
    extra = [] if gain is None else [gain.reshape(1, model)]
    return pl.pallas_call(
        functools.partial(rows_kernel, gain is not None),
        grid=(length // BLOCK,),
        in_specs=[pl.BlockSpec((GROUP, BLOCK, model), lambda t: (0, t, 0))]
        + [pl.BlockSpec((1, model), lambda t: (0, 0))] * len(extra),
        out_specs=pl.BlockSpec((BLOCK * GROUP, model), lambda t: (t, 0)),
        out_shape=jax.ShapeDtypeStruct((length * GROUP, model), BF16),
        scratch_shapes=[pltpu.VMEM((model // LANES, BLOCK * GROUP, LANES), F32)],
        compiler_params=params(),
        cost_estimate=cost(8 * GROUP * length * model, 4 * GROUP * length * model),
        name="interleave",
    )(values, *extra)


class Peers:
    def __init__(self, size):
        self.size, self.half = size, size // 2
        self.member, self.copy = lax.axis_index("fsdp"), lax.axis_index("rep")
        row, column = lax.div(self.member, 2), lax.rem(self.member, 2)
        self.spot = row * (1 - column) + (size - 1 - row) * column
        side = lax.rem(self.copy, 2)
        self.core = (self.member, self.copy - side + (1 - side))
        self.across = (self.member, lax.rem(self.copy + 2, COPIES))
        self.ring = ((self.at(1), self.copy), (self.at(-1), self.copy))

    def at(self, offset):
        spot = lax.rem(self.spot + (offset + self.size), self.size)
        second = lax.div(spot, self.half)
        return 2 * spot * (1 - second) + (2 * (self.size - 1 - spot) + 1) * second

    def meet(self):
        barrier = pltpu.get_barrier_semaphore()
        peers = (*self.ring, self.core, self.across)
        for peer in peers:
            pl.semaphore_signal(barrier, inc=1, device_id=peer, device_id_type=pl.DeviceIdType.MESH)
        pl.semaphore_wait(barrier, len(peers))


def remote(source, target, sems, index, peer):
    return pltpu.make_async_remote_copy(
        src_ref=source,
        dst_ref=target,
        send_sem=sems[0].at[index],
        recv_sem=sems[1].at[index],
        device_id=peer,
        device_id_type=pl.DeviceIdType.MESH,
    )


def scatter_kernel(
    size, grads_ref, small_ref, parts_ref, pieces_ref, small_pieces_ref, normed_ref,
    held, small_held, pair, far_out, far_in, ring_send, ring_recv, few_send, few_recv, rep_send, rep_recv, norm_send, norm_recv,
):
    peers = Peers(size)
    half = peers.half
    rows, few_rows = grads_ref.shape[1] // 2, small_ref.shape[1] // 2
    ring_sems, few_sems = (ring_send, ring_recv), (few_send, few_recv)
    rep_sems, norm_sems = (rep_send, rep_recv), (norm_send, norm_recv)
    peers.meet()
    sent = []

    def start(*copy):
        moving = remote(*copy)
        moving.start()
        sent.append(moving)

    def of_chunk(c):
        return pl.ds(c * rows, rows)

    def of_few(way):
        return pl.ds(way * few_rows, few_rows)

    def owner(way, step):
        away = half + 1 - step
        return peers.at(away if way == 0 else -away)

    def come(way, step, c):
        piece = held.at[way, step - 1, of_chunk(c), :]
        remote(piece, piece, ring_sems, (way, step - 1, c), peers.ring[way]).wait_recv()
        return piece

    def few_come(way, step):
        piece = small_held.at[way, step - 1]
        piece = piece.at[of_few(way), :] if step == 1 else piece
        remote(piece, piece, few_sems, (way, step - 1), peers.ring[way]).wait_recv()

    for way in range(2):
        start(
            grads_ref.at[owner(way, 1), of_chunk(way), :], held.at[way, 0, of_chunk(way), :],
            ring_sems, (way, 0, way), peers.ring[way],
        )
        start(
            small_ref.at[owner(way, 1), of_few(way), :], small_held.at[way, 0, of_few(way), :],
            few_sems, (way, 0), peers.ring[way],
        )
    for i in range(2):
        start(parts_ref.at[1 + 2 * i], pair.at[i], norm_sems, i, peers.core)
    for i in range(2):
        remote(pair.at[i], pair.at[i], norm_sems, i, peers.core).wait_recv()
    far_out[...] = (parts_ref[2].astype(F32) + pair[1].astype(F32)).astype(BF16)
    start(far_out, far_in, norm_sems, 2, peers.across)
    normed_ref[...] = parts_ref[0].astype(F32) + pair[0].astype(F32)

    for step in range(2, half + 1):
        for c in range(2):
            for way in range(2):
                block = owner(way, step)
                target = held.at[way, step - 1, of_chunk(c), :]
                if step == 2 and c != way:
                    source = grads_ref.at[block, of_chunk(c), :]
                else:
                    source = come(way, step - 1, c)
                    source[...] = (
                        grads_ref[block, of_chunk(c), :].astype(F32) + source[...].astype(F32)
                    ).astype(BF16)
                start(source, target, ring_sems, (way, step - 1, c), peers.ring[way])
        for way in range(2):
            block = owner(way, step)
            few_come(way, step - 1)
            source = small_held.at[way, step - 2]
            if step == 2:
                there, rest = of_few(way), of_few(1 - way)
                source[rest, :] = small_ref[block, rest, :]
            else:
                there = pl.ds(0, 2 * few_rows)
            source[there, :] = (
                small_ref[block, there, :].astype(F32) + source[there, :].astype(F32)
            ).astype(BF16)
            start(source, small_held.at[way, step - 1], few_sems, (way, step - 1), peers.ring[way])

    for c in range(2):
        at = of_chunk(c)
        for way in range(2):
            come(way, half, c)
        total = grads_ref[peers.member, at, :].astype(F32)
        for way in range(2):
            total = total + held[way, half - 1, at, :].astype(F32)
        pieces_ref[0, at, :] = total.astype(BF16)
        start(pieces_ref.at[0, at, :], pieces_ref.at[2, at, :], rep_sems, (c, 0), peers.across)
        start(pieces_ref.at[0, at, :], pieces_ref.at[1, at, :], rep_sems, (c, 1), peers.core)
    for way in range(2):
        few_come(way, half)
    total = small_ref[peers.member].astype(F32)
    for way in range(2):
        total = total + small_held[way, half - 1].astype(F32)
    small_pieces_ref[0] = total.astype(BF16)
    start(small_pieces_ref.at[0], small_pieces_ref.at[2], rep_sems, (2, 0), peers.across)
    start(small_pieces_ref.at[0], small_pieces_ref.at[1], rep_sems, (2, 1), peers.core)

    remote(far_in, far_in, norm_sems, 2, peers.across).wait_recv()
    normed_ref[...] = normed_ref[...] + far_in[...].astype(F32)

    def views(index):
        if index == 2:
            return [small_pieces_ref.at[k] for k in range(COPIES)]
        return [pieces_ref.at[k, of_chunk(index), :] for k in range(COPIES)]

    for index in range(3):
        view = views(index)
        remote(view[2], view[2], rep_sems, (index, 0), peers.across).wait_recv()
        start(view[2], view[3], rep_sems, (index, 2), peers.core)
    for index in range(3):
        view = views(index)
        remote(view[1], view[1], rep_sems, (index, 1), peers.core).wait_recv()
        remote(view[3], view[3], rep_sems, (index, 2), peers.core).wait_recv()
    for moving in sent:
        moving.wait_send()


def scatter_all(size, grads, small, parts):
    inside = pl.BlockSpec(memory_space=pltpu.VMEM)
    half = size // 2
    dma = pltpu.SemaphoreType.DMA
    return pl.pallas_call(
        functools.partial(scatter_kernel, size),
        in_specs=[inside] * 3,
        out_specs=[inside] * 3,
        out_shape=[
            jax.ShapeDtypeStruct((COPIES,) + grads.shape[1:], BF16),
            jax.ShapeDtypeStruct((COPIES,) + small.shape[1:], BF16),
            jax.ShapeDtypeStruct(parts.shape[1:], F32),
        ],
        scratch_shapes=[
            pltpu.VMEM((2, half) + grads.shape[1:], BF16),
            pltpu.VMEM((2, half) + small.shape[1:], BF16),
            pltpu.VMEM((2,) + parts.shape[1:], BF16),
            pltpu.VMEM(parts.shape[1:], BF16),
            pltpu.VMEM(parts.shape[1:], BF16),
        ]
        + [dma((2, half, 2))] * 2
        + [dma((2, half))] * 2
        + [dma((3, 3))] * 2
        + [dma((3,))] * 2,
        compiler_params=pltpu.CompilerParams(
            collective_id=2, has_side_effects=True, vmem_limit_bytes=VMEM_LIMIT
        ),
        cost_estimate=cost(0, 4 * grads.size),
        name="scatter_all",
    )(grads, small, parts)


def spread(coefs, nstate):
    terms = []
    for _ in range(3):
        term = coefs.astype(BF16)
        terms.append(term)
        coefs = coefs - term.astype(F32)
    joined = jnp.concatenate(terms, axis=1)
    return jnp.pad(joined, ((0, 0), (0, LANES - joined.shape[1])))


def spreader(nstate):
    row = lax.broadcasted_iota(jnp.int32, (LANES, 2 * nstate * LANES), 0)
    tile = lax.broadcasted_iota(jnp.int32, (LANES, 2 * nstate * LANES), 1) // LANES
    return ((row % (2 * nstate) == tile) & (row < 6 * nstate)).astype(BF16)


def folder(nstate):
    tile = lax.broadcasted_iota(jnp.int32, (2 * nstate * LANES, LANES), 0) // LANES
    column = lax.broadcasted_iota(jnp.int32, (2 * nstate * LANES, LANES), 1)
    return (tile == column).astype(BF16)


def tiled(value, width):
    return jnp.concatenate([value] * (width // LANES), axis=1)


def at_time(t):
    return pl.ds(pl.multiple_of(t * GROUP, GROUP), GROUP)


def scan_kernel(
    nstate, chunk, pre_ref, act_ref, coef_ref, spread_ref, keep_ref, rate_ref, row_ref,
    out_ref, step_ref, start_ref, carry_ref, wide,
):
    width = pre_ref.shape[1]

    @pl.when(pl.program_id(0) == 0)
    def _():
        carry_ref[...] = jnp.zeros_like(carry_ref)

    start_ref[0] = carry_ref[...]
    wide[...] = jnp.dot(coef_ref[...], spread_ref[...], preferred_element_type=F32)
    pre = pre_ref[...] + row_ref[0:1]
    step_ref[...] = jnp.maximum(pre, 0.0) + jnp.log1p(jnp.exp(-jnp.abs(pre)))
    for c in range(width // chunk):
        cols = slice(c * chunk, (c + 1) * chunk)

        def advance(t, states):
            at = at_time(t)
            step, act = step_ref[at, cols], act_ref[at, cols]
            drive = jnp.where(tiled(keep_ref[at, :], chunk) > 0.5, step, FAR)
            inflow = step * act
            total = row_ref[1:2, cols] * act
            now = []
            for n in range(nstate):
                write = tiled(wide[at, n * LANES : (n + 1) * LANES], chunk)
                read = tiled(wide[at, (nstate + n) * LANES : (nstate + n + 1) * LANES], chunk)
                state = jnp.exp2(drive * rate_ref[n, :, cols]) * states[n] + write * inflow
                total = total + read * state
                now.append(state)
            out_ref[at, cols] = total
            return tuple(now)

        start = tuple(carry_ref[n, :, cols] for n in range(nstate))
        states = lax.fori_loop(0, BLOCK, advance, start, unroll=4)
        for n in range(nstate):
            carry_ref[n, :, cols] = states[n]


def scan_forward(pre, act, coef, spread_by, keep, rate, rows):
    total, width = pre.shape
    nstate = rate.shape[0]
    size = BLOCK * GROUP
    tile = pl.BlockSpec((size, width), lambda t: (t, 0))
    thin = pl.BlockSpec((size, LANES), lambda t: (t, 0))
    state = pl.BlockSpec((nstate, GROUP, width), lambda t: (0, 0, 0))
    count = total // size
    work = total * width * nstate
    return pl.pallas_call(
        functools.partial(scan_kernel, nstate, 256),
        grid=(count,),
        in_specs=[
            tile,
            tile,
            thin,
            pl.BlockSpec(spread_by.shape, lambda t: (0, 0)),
            thin,
            state,
            pl.BlockSpec((8, width), lambda t: (0, 0)),
        ],
        out_specs=[
            tile,
            tile,
            pl.BlockSpec((1, nstate, GROUP, width), lambda t: (t, 0, 0, 0)),
        ],
        out_shape=[
            jax.ShapeDtypeStruct((total, width), F32),
            jax.ShapeDtypeStruct((total, width), F32),
            jax.ShapeDtypeStruct((total // size, nstate, GROUP, width), F32),
        ],
        scratch_shapes=[
            pltpu.VMEM((nstate, GROUP, width), F32),
            pltpu.VMEM((size, 2 * nstate * LANES), F32),
        ],
        compiler_params=params(),
        cost_estimate=cost(16 * work, 16 * count * size * width),
        name="scan_forward",
    )(pre, act, coef, spread_by, keep, rate, rows)


class Shares:
    def __init__(self, peers, shards, wholes, sems):
        self.peers, self.shards, self.wholes, self.sems = peers, shards, wholes, sems
        self.sent = []

    def place(self, which, member, c):
        rows = self.shards[which].shape[0]
        start = pl.multiple_of(member * rows + c * (rows // 2), rows // 2)
        return self.wholes[which].at[pl.ds(start, rows // 2), :]

    def owner(self, way, step):
        return self.peers.at(-step if way == 0 else step)

    def chunks(self, way, step):
        return (way,) if step == self.peers.half else (0, 1)

    def come(self, which, way, step, c):
        there = self.place(which, self.owner(way, step), c)
        remote(there, there, self.sems, (which, way, step - 1, c), self.peers.ring[way]).wait_recv()

    def step(self, which, step):
        for c in range(2):
            for way in range(2):
                if c not in self.chunks(way, step):
                    continue
                target = self.place(which, self.owner(way, step - 1), c)
                source = target
                if step == 1:
                    rows = self.shards[which].shape[0] // 2
                    source = self.shards[which].at[pl.ds(c * rows, rows), :]
                else:
                    self.come(which, way, step - 1, c)
                index = (which, way, step - 1, c)
                remote(source, target, self.sems, index, self.peers.ring[way]).start()

    def finish(self, which):
        half = self.peers.half
        for way in range(2):
            self.come(which, way, half - 1, 1 - way)
            self.come(which, way, half, way)

    def sent_all(self):
        for which in range(len(self.shards)):
            for step in range(1, self.peers.half + 1):
                for way in range(2):
                    for c in self.chunks(way, step):
                        place = self.place(which, self.owner(way, step - 1), c)
                        index = (which, way, step - 1, c)
                        remote(place, place, self.sems, index, self.peers.ring[way]).wait_send()


def softplus(value):
    return jnp.maximum(value, 0.0) + jnp.log1p(jnp.exp(-jnp.abs(value)))


def forward_kernel(
    size, rank, nstate,
    entry, few, tokens, out_grad, segments, out_proj,
    few_out, masks_out, rate_out, spread_out, fold_out, normed_out, cotangent_out, tokens_all, grads_all, segments_all,
    w_in_out, inner_out, act_out, low_out, step_low_out, coef_out, step_out, start_out, gate_out, readout_out,
    gated_out, natural_out, gate_w_out, out_w_out,
    few_all, small, masks, rate, spread_by, fold_by, normed, stage, cotangent, held, seg, inner_shard, gate_shard, w_in,
    inner, act, low, part, nat, got_near, to_across, got_across, shared, step_low, coef, wide, pre, step, readout,
    carry, start_at, gate, gated, natural, gate_w,
    local, start_sems, gate_sems, own_sems, entry_sems, stage_sems, out_sems, seg_sems,
    ring_send, ring_recv, few_send, few_recv, rep_send, rep_recv, near_send, near_recv,
):
    peers = Peers(size)
    total, width = normed.shape[0], w_in.shape[1]
    pad = 3 * GROUP
    chunk = 256
    rows = 64
    length = total // GROUP
    batches = GROUP // COPIES
    half = peers.half
    side_rows = total // COPIES
    saved = []

    def save(source, target):
        copy = pltpu.make_async_copy(source, target, local.at[len(saved)])
        copy.start()
        saved.append(copy)

    picks = []
    for side_of, target in enumerate((inner_shard, gate_shard)):
        for f in range(size):
            source = ((side_of * size + f) * COPIES + peers.copy) * LANES
            picks.append(
                pltpu.make_async_copy(
                    entry.at[:, pl.ds(pl.multiple_of(source, LANES), LANES)],
                    target.at[:, pl.ds(f * LANES, LANES)],
                    entry_sems.at[len(picks)],
                )
            )
    for pick in picks:
        pick.start()
    peers.meet()
    sent = []

    def send(*copy):
        moving = remote(*copy)
        moving.start()
        sent.append(moving)

    rep_sems = (rep_send, rep_recv)

    def of_copy(ref, k):
        return ref.at[k] if ref is segments_all else ref.at[pl.ds(k * batches, batches)]

    def exchange(i, own, everyone):
        send(own, of_copy(everyone, 2), rep_sems, (i, 0), peers.across)
        send(own, of_copy(everyone, 1), rep_sems, (i, 1), peers.core)
        copy = pltpu.make_async_copy(own, of_copy(everyone, 0), own_sems.at[3 + i])
        copy.start()
        return copy

    def pass_on(i, everyone):
        far = of_copy(everyone, 2)
        remote(far, far, rep_sems, (i, 0), peers.across).wait_recv()
        send(far, of_copy(everyone, 3), rep_sems, (i, 2), peers.core)

    def exchanged(i, everyone, copy):
        copy.wait()
        for k, which in ((1, 1), (3, 2)):
            there = of_copy(everyone, k)
            remote(there, there, rep_sems, (i, which), peers.core).wait_recv()

    out_rows = out_proj.shape[0] // COPIES
    out_shard = out_proj.at[pl.ds(pl.multiple_of(peers.copy * out_rows, out_rows), out_rows), :]
    ring = Shares(
        peers, (inner_shard, gate_shard, out_shard), (w_in, gate_w, out_w_out), (ring_send, ring_recv),
    )
    gate_rows = gate_shard.shape[0]
    shard_rows = pl.ds(pl.multiple_of(peers.member * gate_rows, gate_rows), gate_rows)
    own_rows = pl.ds(pl.multiple_of(peers.member * out_rows, out_rows), out_rows)
    own_columns = pl.ds(pl.multiple_of(peers.member * LANES, LANES), LANES)

    few_sems = (few_send, few_recv)
    few_rows = few.shape[0] // 2

    def few_place(way, number, split):
        columns = pl.ds(pl.multiple_of(ring.owner(way, number) * LANES, LANES), LANES)
        place = pl.ds(way * few_rows, few_rows) if split else pl.ds(0, 2 * few_rows)
        return few_all.at[place, columns]

    def few_come(way, number):
        there = few_place(way, number, number == half)
        remote(there, there, few_sems, (way, number - 1), peers.ring[way]).wait_recv()

    def few_step(number):
        for way in range(2):
            if number > 1:
                few_come(way, number - 1)
            target = few_place(way, number - 1, number == half)
            source = few if number == 1 else target
            send(source, target, few_sems, (way, number - 1), peers.ring[way])

    few_step(1)
    own_tokens = exchange(0, tokens, tokens_all)
    own_segments = exchange(2, segments, segments_all)
    own = [
        pltpu.make_async_copy(few, few_all.at[:, own_columns], own_sems.at[0]),
        pltpu.make_async_copy(out_shard, out_w_out.at[own_rows, :], own_sems.at[1]),
    ]
    for copy in own:
        copy.start()
    for pick in picks[:size]:
        pick.wait()
    ring.step(0, 1)
    for pick in picks[size:]:
        pick.wait()
    own_shards = [
        pltpu.make_async_copy(inner_shard, w_in.at[shard_rows, :], own_sems.at[6]),
        pltpu.make_async_copy(gate_shard, gate_w.at[shard_rows, :], own_sems.at[2]),
    ]
    for copy in own_shards:
        copy.start()

    wide_shape, thin_shape = spread_by.shape, fold_by.shape
    tile = lax.broadcasted_iota(jnp.int32, wide_shape, 1) // LANES
    row = lax.broadcasted_iota(jnp.int32, wide_shape, 0)
    spread_by[...] = jnp.where(
        (lax.rem(row, 2 * nstate) == tile) & (row < 6 * nstate), 1.0, 0.0
    ).astype(BF16)
    tile = lax.broadcasted_iota(jnp.int32, thin_shape, 0) // LANES
    column = lax.broadcasted_iota(jnp.int32, thin_shape, 1)
    fold_by[...] = jnp.where(tile == column, 1.0, 0.0).astype(BF16)
    save(spread_by, spread_out)
    save(fold_by, fold_out)

    few_step(2)
    pass_on(2, segments_all)
    few_step(3)
    ring.step(0, 2)
    few_step(4)
    exchanged(2, segments_all, own_segments)
    numbers = pltpu.make_async_copy(segments_all, seg, seg_sems.at[0])
    numbers.start()
    for way in range(2):
        few_come(way, half - 1) if half < 2 else None
        few_come(way, half)
    own[0].wait()
    numbers.wait()

    numbers = jnp.concatenate([seg[k] for k in range(COPIES)], axis=0).astype(F32)
    lane = lax.broadcasted_iota(jnp.int32, (total, LANES), 1)
    time = lax.broadcasted_iota(jnp.int32, (total, LANES), 0) // GROUP
    picked = jnp.where(lane == time, jnp.concatenate([numbers] * length, axis=0), 0.0).astype(BF16)
    numbers = jnp.dot(picked, jnp.ones((LANES, LANES), BF16), preferred_element_type=F32)
    for shift in range(1, 4):
        earlier = jnp.concatenate(
            [jnp.full((shift * GROUP, LANES), -1.0, F32), numbers[: -shift * GROUP]], axis=0
        )
        masks[shift - 1] = jnp.where(earlier == numbers, 1.0, 0.0)
    save(masks, masks_out)
    save(few_all, few_out)
    first_small = 2 * rank + 2 * nstate
    small[...] = few_all[first_small : first_small + small.shape[0], :].astype(F32)
    taps, bias_row, skip_row, gain_row = 0, 5, 6 + nstate, 7 + nstate
    for n in range(nstate):
        rate[n] = jnp.broadcast_to(-LOG2E * jnp.exp(small[6 + n : 7 + n, :]), (GROUP, width))
    save(rate, rate_out)

    def fetch(source, t, slot):
        return pltpu.make_async_copy(
            source.at[:, pl.ds(pl.multiple_of(t * BLOCK, BLOCK), BLOCK), :], stage.at[slot], stage_sems.at[slot]
        )

    def weave(slot, scaled):
        for s in range(GROUP):
            value = stage[slot, s].astype(F32)
            if scaled:
                square = jnp.mean(value * value, axis=-1, keepdims=True)
                value = value * lax.rsqrt(square + EPS)
            for k in range(held.shape[0]):
                tile = value[:, k * LANES : (k + 1) * LANES]
                if scaled:
                    at = gain_row + k % 2
                    tile = tile * small[at : at + 1, (k // 2) * LANES : (k // 2 + 1) * LANES]
                held[k, pl.ds(s, BLOCK, stride=GROUP), :] = tile

    block_rows = BLOCK * GROUP
    blocks = total // block_rows

    def block_of(t):
        return pl.ds(pl.multiple_of(t * block_rows, block_rows), block_rows)

    pass_on(0, tokens_all)
    own_grads = exchange(1, out_grad, grads_all)
    ring.step(0, 3)
    exchanged(0, tokens_all, own_tokens)
    fetch(tokens_all, 0, 0).start()

    @pl.loop(0, blocks)
    def _(t):
        slot = lax.rem(t, 2)

        @pl.when(t + 1 < blocks)
        def _():
            fetch(tokens_all, t + 1, 1 - slot).start()

        @pl.when(t == blocks - 2)
        def _():
            ring.step(0, 4)
            ring.step(1, 1)

        fetch(tokens_all, t, slot).wait()
        weave(slot, True)
        for k in range(held.shape[0]):
            normed[block_of(t), k * LANES : (k + 1) * LANES] = held[k].astype(BF16)

    save(normed, normed_out)
    for copy in own_shards:
        copy.wait()
    ring.finish(0)
    save(w_in, w_in_out)

    def cotangent_out_of(t, slot):
        return pltpu.make_async_copy(cotangent.at[slot], cotangent_out.at[block_of(t), :], out_sems.at[slot])

    def weave_grads(first, count):
        fetch(grads_all, first, first % 2).start()

        @pl.loop(first, first + count)
        def _(t):
            slot = lax.rem(t, 2)

            @pl.when(t + 1 < first + count)
            def _():
                fetch(grads_all, t + 1, 1 - slot).start()

            @pl.when(t >= 2)
            def _():
                cotangent_out_of(t - 2, slot).wait()

            fetch(grads_all, t, slot).wait()
            weave(slot, False)
            for k in range(held.shape[0]):
                cotangent[slot, :, k * LANES : (k + 1) * LANES] = held[k].astype(BF16)
            cotangent_out_of(t, slot).start()

    inner[0:pad, :] = jnp.zeros((pad, width), F32)
    part[...] = jnp.zeros_like(part)

    @pl.loop(0, width // chunk)
    def _(c):
        cols = pl.ds(pl.multiple_of(c * chunk, chunk), chunk)
        inner[pad:, cols] = jnp.dot(normed[...], w_in[:, cols], preferred_element_type=F32)

        @pl.when(c == 1)
        def _():
            ring.step(2, 1)

        tap = [small[taps + i : taps + i + 1, cols] for i in range(5)]

        @pl.loop(0, total // rows)
        def _(i):
            start = pl.multiple_of(i * rows, rows)
            value = tap[4] + tap[3] * inner[pl.ds(pad + start, rows), cols]
            for shift in range(1, 4):
                mask = tiled(masks[shift - 1, pl.ds(start, rows), :], chunk)
                before = inner[pl.ds(pad - shift * GROUP + start, rows), cols]
                value = value + tap[3 - shift] * (before * mask)
            here = value * sigmoid(value)
            act[pl.ds(start, rows), cols] = here
            low[pl.ds(start, rows), cols] = here.astype(BF16)

        for j in range(2):
            part[j] += lax.dot_general(
                low[:, cols], few_all[j * LANES : (j + 1) * LANES, cols], (((1,), (1,)), ((), ())),
                preferred_element_type=F32,
            )

    save(inner.at[pl.ds(pad, total), :], inner_out)
    save(act, act_out)
    save(low, low_out)

    near = (near_send, near_recv)
    for j in range(2):
        for s in range(GROUP):
            nat[j, s * length : (s + 1) * length, :] = part[j, pl.ds(s, length, stride=GROUP), :]
    sends = []

    def start(source, target, index, peer):
        copy = remote(source, target, near, index, peer)
        copy.start()
        sends.append(copy)

    def come(target, index, peer):
        remote(target, target, near, index, peer).wait_recv()

    for i in range(2):
        start(nat.at[:, pl.ds((2 * i + 1) * side_rows, side_rows), :], got_near.at[i], i, peers.core)
    ring.step(1, 2)
    pass_on(1, grads_all)
    for i in range(2):
        come(got_near.at[i], i, peers.core)
    to_across[...] = nat[:, 2 * side_rows : 3 * side_rows, :] + got_near[1]
    start(to_across, got_across, 2, peers.across)
    exchanged(1, grads_all, own_grads)
    weave_grads(0, blocks // 2)
    ring.step(2, 2)
    come(got_across, 2, peers.across)
    mine = nat[:, :side_rows, :] + got_near[0] + got_across[...]
    shared[0, 0] = mine[0].astype(BF16)
    lane = lax.broadcasted_iota(jnp.int32, (side_rows, LANES), 1)
    rest, terms = jnp.where(lane < 2 * nstate, mine[1], 0.0), jnp.zeros((side_rows, LANES), F32)
    for i in range(3):
        term = rest.astype(BF16).astype(F32)
        rest = rest - term
        terms = terms + (pltpu.roll(term, 2 * nstate * i, 1) if i else term)
    shared[0, 1] = terms.astype(BF16)
    start(shared.at[0], shared.at[2], 3, peers.across)
    start(shared.at[0], shared.at[1], 4, peers.core)
    weave_grads(blocks // 2, blocks // 2)
    come(shared.at[2], 3, peers.across)
    start(shared.at[2], shared.at[3], 5, peers.core)
    come(shared.at[1], 4, peers.core)
    come(shared.at[3], 5, peers.core)
    for copy in sends:
        copy.wait_send()
    for k in range(COPIES):
        for b in range(batches):
            for j in range(2):
                part[j, pl.ds(k * batches + b, length, stride=GROUP), :] = shared[
                    k, j, b * length : (b + 1) * length, :
                ].astype(F32)
    step_low[...] = part[0].astype(BF16)
    coef[...] = part[1].astype(BF16)
    save(step_low, step_low_out)
    save(coef, coef_out)

    stride = few_all[rank + 2 * nstate : 2 * rank + 2 * nstate, :]
    side_bias = small[bias_row : bias_row + 1, :]
    carry[...] = jnp.zeros_like(carry)

    def keep_start(t, slot):
        return pltpu.make_async_copy(start_at.at[slot], start_out.at[t], start_sems.at[slot])

    @pl.loop(0, blocks)
    def _(t):
        for tick, which, number in ((0, 1, 3), (2, 2, 3), (4, 1, 4), (6, 2, 4)):

            @pl.when(t == tick)
            def _(which=which, number=number):
                ring.step(which, number)

        base = pl.multiple_of(t * block_rows, block_rows)
        these = block_of(t)
        wide[...] = jnp.dot(coef[these, :], spread_by[...], preferred_element_type=F32)
        pre[...] = jnp.dot(step_low[these, :], stride, preferred_element_type=F32)
        for i in range(BLOCK // 2):
            sub = slice(i * 2 * GROUP, (i + 1) * 2 * GROUP)
            step[pl.ds(base + i * 2 * GROUP, 2 * GROUP), :] = softplus(pre[sub, :] + side_bias)
        slot = lax.rem(t, 2)

        @pl.when(t >= 2)
        def _():
            keep_start(t - 2, slot).wait()

        start_at[slot] = carry[...]
        keep_start(t, slot).start()
        for c in range(width // chunk):
            cols = slice(c * chunk, (c + 1) * chunk)

            def advance(i, states):
                at = pl.ds(pl.multiple_of(base + i * GROUP, GROUP), GROUP)
                here = at_time(i)
                step_t, act_t = step[at, cols], act[at, cols]
                drive = jnp.where(tiled(masks[0, at, :], chunk) > 0.5, step_t, FAR)
                inflow = step_t * act_t
                out = small[skip_row : skip_row + 1, cols] * act_t
                now = []
                for n in range(nstate):
                    write = tiled(wide[here, n * LANES : (n + 1) * LANES], chunk)
                    read = tiled(wide[here, (nstate + n) * LANES : (nstate + n + 1) * LANES], chunk)
                    state = jnp.exp2(drive * rate[n, :, cols]) * states[n] + write * inflow
                    out = out + read * state
                    now.append(state)
                readout[at, cols] = out
                return tuple(now)

            states = lax.fori_loop(
                0, BLOCK, advance, tuple(carry[n, :, cols] for n in range(nstate)), unroll=4
            )
            for n in range(nstate):
                carry[n, :, cols] = states[n]

    save(step, step_out)
    save(readout, readout_out)

    ring.finish(1)
    save(gate_w, gate_w_out)

    def keep_gate(c, slot):
        cols = pl.ds(pl.multiple_of(c * chunk, chunk), chunk)
        return pltpu.make_async_copy(gate.at[slot], gate_out.at[:, cols], gate_sems.at[slot])

    @pl.loop(0, width // chunk)
    def _(c):
        cols = pl.ds(pl.multiple_of(c * chunk, chunk), chunk)
        slot = lax.rem(c, 2)

        @pl.when(c >= 2)
        def _():
            keep_gate(c - 2, slot).wait()

        gate[slot] = jnp.dot(normed[...], gate_w[:, cols], preferred_element_type=F32)
        keep_gate(c, slot).start()

        @pl.loop(0, total // rows)
        def _(i):
            at = pl.ds(pl.multiple_of(i * rows, rows), rows)
            here = gate[slot, at, :]
            value = readout[at, cols] * (here * sigmoid(here))
            gated[at, cols] = value.astype(BF16)
            for k in range(chunk // LANES):
                nat[k, at, :] = value[:, k * LANES : (k + 1) * LANES]

        for k in range(chunk // LANES):
            for s in range(GROUP):
                natural[s * length : (s + 1) * length, pl.ds(pl.multiple_of(c * chunk + k * LANES, LANES), LANES)] = nat[
                    k, pl.ds(s, length, stride=GROUP), :
                ].astype(BF16)

    save(gated, gated_out)
    save(natural, natural_out)
    own[1].wait()
    ring.finish(2)
    ring.sent_all()
    for moving in sent:
        moving.wait_send()
    for slot in range(2):
        keep_start(blocks - 2 + slot, slot).wait()
        keep_gate(width // chunk - 2 + slot, slot).wait()
        cotangent_out_of(blocks - 2 + slot, slot).wait()
    for copy in saved:
        copy.wait()


def forward(size, rank, nstate, entry, few, tokens, out_grad, segments, out_proj):
    batches, length, model = tokens.shape
    total = COPIES * batches * length
    slab, width = entry.shape[0], size * LANES
    blocks = length // BLOCK
    anywhere = pl.BlockSpec(memory_space=pl.ANY)
    half = size // 2
    dma = pltpu.SemaphoreType.DMA
    shape = jax.ShapeDtypeStruct
    full, low = shape((total, width), F32), shape((total, width), BF16)
    thin = shape((total, LANES), BF16)
    rows = shape((total, model), BF16)
    weights = shape((size * slab, width), BF16)
    few_all = shape((few.shape[0], width), BF16)
    masks = shape((3, total, LANES), F32)
    state = shape((nstate, GROUP, width), F32)
    spread_by = shape((LANES, 2 * nstate * LANES), BF16)
    fold_by = shape((2 * nstate * LANES, LANES), BF16)
    outs = dict(
        few=few_all,
        masks=masks,
        rate=state,
        spread_by=spread_by,
        fold_by=fold_by,
        normed=rows,
        cotangent=rows,
        tokens_all=shape((GROUP, length, model), BF16),
        grads_all=shape((GROUP, length, model), BF16),
        segments_all=shape((COPIES,) + segments.shape, segments.dtype),
        inner_in=weights,
        inner=full,
        act=full,
        act_low=low,
        step_low=thin,
        coef=thin,
        step=full,
        starts=shape((blocks,) + state.shape, F32),
        gate=full,
        readout=full,
        gated=low,
        gated_natural=low,
        gate_in=weights,
        out_w=shape((size * out_proj.shape[0] // COPIES, model), BF16),
    )
    quarter = total // COPIES
    scratch = [
        few_all,
        shape((few.shape[0] - 2 * rank - 2 * nstate, width), F32),
        masks,
        state,
        spread_by,
        fold_by,
        rows,
        shape((2, GROUP, BLOCK, model), BF16),
        shape((2, BLOCK * GROUP, model), BF16),
        shape((model // LANES, BLOCK * GROUP, LANES), F32),
        shape((COPIES,) + segments.shape, segments.dtype),
        shape((slab, width), BF16),
        shape((slab, width), BF16),
        weights,
        shape((total + 3 * GROUP, width), F32),
        full,
        low,
        shape((2, total, LANES), F32),
        shape((2, total, LANES), F32),
        shape((2, 2, quarter, LANES), F32),
        shape((2, quarter, LANES), F32),
        shape((2, quarter, LANES), F32),
        shape((COPIES, 2, quarter, LANES), BF16),
        thin,
        thin,
        shape((BLOCK * GROUP, 2 * nstate * LANES), F32),
        shape((BLOCK * GROUP, width), F32),
        full,
        full,
        state,
        shape((2,) + state.shape, F32),
        shape((2, total, 256), F32),
        low,
        low,
        weights,
    ]
    sems = [(20,), (2,), (2,), (7,), (2 * size,), (2,), (2,), (1,)]
    sems += [(3, 2, half, 2)] * 2 + [(2, half)] * 2 + [(3, 3)] * 2 + [(6,)] * 2
    results = pl.pallas_call(
        functools.partial(forward_kernel, size, rank, nstate),
        in_specs=[anywhere] * 6,
        out_specs=[anywhere] * len(outs),
        out_shape=list(outs.values()),
        scratch_shapes=[pltpu.VMEM(x.shape, x.dtype) for x in scratch] + [dma(n) for n in sems],
        compiler_params=pltpu.CompilerParams(
            collective_id=4, has_side_effects=True, vmem_limit_bytes=62 * 1024 * 1024
        ),
        cost_estimate=cost(8 * total * width * model, 100 * total * width),
        name="forward",
    )(entry, few, tokens, out_grad, segments, out_proj)
    return dict(zip(outs, results))


class Guests:
    def __init__(self, size, parts, totals, held, sems):
        self.peers = Peers(size)
        self.parts, self.totals, self.held, self.sems = parts, totals, held, sems

    def rows(self, which, c):
        half = self.parts[which].shape[1] // 2
        return pl.ds(c * half, half)

    def copy(self, which, way, step, c, source=None):
        target = self.held[which].at[way, step - 1, self.rows(which, c), :]
        index = (which, way, step - 1, c)
        source = target if source is None else source
        return remote(source, target, self.sems, index, self.peers.ring[way])

    def chunks(self, way, step):
        return (way,) if step == 1 else (0, 1)

    def own(self, which, way, step, c):
        away = self.peers.half + 1 - step
        block = self.peers.at(away if way == 0 else -away)
        return self.parts[which].at[block, self.rows(which, c), :]

    def source(self, which, way, step, c):
        own = self.own(which, way, step, c)
        if step == 1 or c not in self.chunks(way, step - 1):
            return own
        self.copy(which, way, step - 1, c).wait_recv()
        there = self.held[which].at[way, step - 2, self.rows(which, c), :]
        there[...] = (own[...].astype(F32) + there[...].astype(F32)).astype(BF16)
        return there

    def tick(self, number):
        which, step = number % 2, number // 2 + 1
        for c in range(2):
            for way in range(2):
                if c in self.chunks(way, step):
                    self.copy(which, way, step, c, self.source(which, way, step, c)).start()

    def finish(self):
        last = self.peers.half
        for which in range(2):
            for c in range(2):
                total = self.own(which, 0, last + 1, c)[...].astype(F32)
                for way in range(2):
                    self.copy(which, way, last, c).wait_recv()
                    there = self.held[which].at[way, last - 1, self.rows(which, c), :]
                    total = total + there[...].astype(F32)
                self.totals[which][self.rows(which, c), :] = total.astype(BF16)
        for which in range(2):
            for step in range(1, last + 1):
                for way in range(2):
                    for c in self.chunks(way, step):
                        self.copy(which, way, step, c).wait_send()


def scan_back_kernel(
    nstate, chunk, rings, step_ref, act_ref, grad_ref, coef_ref, spread_ref, fold_ref, keep_ref, rate_ref,
    row_ref, start_ref, *refs,
):
    wide, states_all, decays, parts, sizes = refs[-5:]
    width = step_ref.shape[1]
    step_now = pl.program_id(0)
    if rings:
        first_ref, second_ref = refs[:2]
        pre_grad_ref, direct_ref, coef_grad_ref, carry_ref, sums_ref = refs[2:7]
        guest = Guests(rings, (first_ref, second_ref), refs[7:9], refs[9:11], refs[11:13])
        for tick in range(2 * guest.peers.half):

            @pl.when(step_now == tick)
            def _(tick=tick):
                if tick == 0:
                    guest.peers.meet()
                guest.tick(tick)

    else:
        pre_grad_ref, direct_ref, coef_grad_ref, carry_ref, sums_ref = refs[-10:-5]

    @pl.when(step_now == 0)
    def _():
        carry_ref[...] = jnp.zeros_like(carry_ref)
        sums_ref[...] = jnp.zeros_like(sums_ref)

    wide[...] = jnp.dot(coef_ref[...], spread_ref[...], preferred_element_type=F32)

    def fold(value):
        total = value[:, :LANES]
        for k in range(1, chunk // LANES):
            total = total + value[:, k * LANES : (k + 1) * LANES]
        return total

    for c in range(width // chunk):
        cols = slice(c * chunk, (c + 1) * chunk)

        def advance(t, states):
            at = at_time(t)
            step = step_ref[at, cols]
            drive = jnp.where(tiled(keep_ref[at, :], chunk) > 0.5, step, FAR)
            inflow = step * act_ref[at, cols]
            now = []
            for n in range(nstate):
                write = tiled(wide[at, n * LANES : (n + 1) * LANES], chunk)
                decay = jnp.exp2(drive * rate_ref[n, :, cols])
                decays[t, n] = decay
                states_all[t, n] = states[n]
                now.append(decay * states[n] + write * inflow)
            return tuple(now)

        start = tuple(start_ref[0, n, :, cols] for n in range(nstate))
        states = lax.fori_loop(0, BLOCK, advance, start, unroll=2)
        for n in range(nstate):
            states_all[BLOCK, n] = states[n]

        def retreat(i, carry):
            t = BLOCK - 1 - i
            at = at_time(t)
            step, act, grad = step_ref[at, cols], act_ref[at, cols], grad_ref[at, cols]
            inflow = step * act
            size = jnp.zeros_like(step)
            direct = jnp.zeros_like(step)
            now = []
            for n in range(nstate):
                tile_w = slice(n * LANES, (n + 1) * LANES)
                tile_r = slice((nstate + n) * LANES, (nstate + n + 1) * LANES)
                state_grad = tiled(wide[at, tile_r], chunk) * grad + carry[n]
                passed = decays[t, n] * state_grad
                through = passed * states_all[t, n]
                size = size + rate_ref[n, :, cols] * through
                direct = direct + state_grad * tiled(wide[at, tile_w], chunk)
                sums_ref[n, :, cols] += step * through
                write_part = fold(state_grad * inflow)
                read_part = fold(grad * states_all[t + 1, n])
                if c == 0:
                    parts[at, tile_w] = write_part
                    parts[at, tile_r] = read_part
                else:
                    parts[at, tile_w] += write_part
                    parts[at, tile_r] += read_part
                now.append(passed)
            sizes[at, cols] = LN2 * size + act * direct
            direct_ref[at, cols] = step * direct + row_ref[1:2, cols] * grad
            sums_ref[nstate, :, cols] += grad * act
            return tuple(now)

        start = tuple(carry_ref[n, :, cols] for n in range(nstate))
        carry = lax.fori_loop(0, BLOCK, retreat, start, unroll=2)
        for n in range(nstate):
            carry_ref[n, :, cols] = carry[n]

    step = step_ref[...]
    series = step * (1.0 - step * (0.5 - step * (1.0 / 6.0)))
    pre_grad = sizes[...] * jnp.where(step < 0.01, series, 1.0 - jnp.exp(-step))
    pre_grad_ref[...] = pre_grad.astype(BF16)
    total = pre_grad[:GROUP]
    for t in range(1, BLOCK):
        total = total + pre_grad[t * GROUP : (t + 1) * GROUP]
    sums_ref[nstate + 1] += total
    high = parts[...].astype(BF16)
    low = (parts[...] - high.astype(F32)).astype(BF16)
    coef_grad_ref[...] = jnp.dot(high, fold_ref[...], preferred_element_type=F32) + jnp.dot(
        low, fold_ref[...], preferred_element_type=F32
    )
    if rings:

        @pl.when(step_now == pl.num_programs(0) - 1)
        def _():
            guest.finish()


def scan_backward(
    step, act, grad, coef, spread_by, fold_by, keep, rate, rows, starts, rings, wgrads
):
    total, width = step.shape
    nstate = rate.shape[0]
    size = BLOCK * GROUP
    chunk = 256
    count = total // size
    tile = pl.BlockSpec((size, width), lambda t: (count - 1 - t, 0))
    thin = pl.BlockSpec((size, LANES), lambda t: (count - 1 - t, 0))
    state = pl.BlockSpec((nstate, GROUP, width), lambda t: (0, 0, 0))
    tally = pl.BlockSpec((nstate + 2, GROUP, width), lambda t: (0, 0, 0))
    work = count * size * width * nstate
    inside = pl.BlockSpec(memory_space=pltpu.VMEM)
    half = rings // 2
    guests = [jax.ShapeDtypeStruct(w.shape[1:], BF16) for w in wgrads]
    sems = [pltpu.SemaphoreType.DMA((2, 2, half, 2))] * 2 if rings else []
    return pl.pallas_call(
        functools.partial(scan_back_kernel, nstate, chunk, rings),
        grid=(count,),
        in_specs=[
            tile,
            tile,
            tile,
            thin,
            pl.BlockSpec(spread_by.shape, lambda t: (0, 0)),
            pl.BlockSpec(fold_by.shape, lambda t: (0, 0)),
            thin,
            state,
            pl.BlockSpec((8, width), lambda t: (0, 0)),
            pl.BlockSpec((1, nstate, GROUP, width), lambda t: (count - 1 - t, 0, 0, 0)),
        ]
        + [inside] * len(wgrads),
        out_specs=[tile, tile, thin, state, tally] + [inside] * len(wgrads),
        out_shape=[
            jax.ShapeDtypeStruct((total, width), BF16),
            jax.ShapeDtypeStruct((total, width), F32),
            jax.ShapeDtypeStruct((total, LANES), F32),
            jax.ShapeDtypeStruct((nstate, GROUP, width), F32),
            jax.ShapeDtypeStruct((nstate + 2, GROUP, width), F32),
        ]
        + guests,
        scratch_shapes=[pltpu.VMEM((2, half) + w.shape[1:], BF16) for w in wgrads]
        + sems
        + [
            pltpu.VMEM((size, 2 * nstate * LANES), F32),
            pltpu.VMEM((BLOCK + 1, nstate, GROUP, chunk), F32),
            pltpu.VMEM((BLOCK, nstate, GROUP, chunk), F32),
            pltpu.VMEM((size, 2 * nstate * LANES), F32),
            pltpu.VMEM((size, width), F32),
        ],
        compiler_params=pltpu.CompilerParams(
            collective_id=3, has_side_effects=True, vmem_limit_bytes=VMEM_LIMIT
        )
        if rings
        else params(),
        cost_estimate=cost(40 * work, 24 * count * size * width),
        name="scan_backward",
    )(step, act, grad, coef, spread_by, fold_by, keep, rate, rows, starts, *wgrads)


def spread_columns_kernel(copy_ref, *refs):
    pieces, weight_ref, out_ref, gain_ref = refs[:4], refs[4], refs[-2], refs[-1]
    part = pieces[0].shape[1]

    @pl.when(pl.program_id(0) == 0)
    def _():
        gain_ref[...] = jnp.zeros_like(gain_ref)

    total = gain_ref[...]
    for k, piece in enumerate(pieces):
        at = pl.ds(pl.multiple_of((copy_ref[0] ^ k) * part, part), part)
        value = piece[...].astype(F32)
        out_ref[:, at] = value
        total = total + value * weight_ref[:, at].astype(F32)
    gain_ref[...] = total


def spread_columns(copy, pieces, weight, side, before=None):
    rows, width = pieces[0].shape
    part = LANES
    shares = width // part
    block = pl.BlockSpec((rows, COPIES * part), lambda f, copy: (0, side * shares + f))
    piece = pl.BlockSpec((rows, part), lambda f, copy: (0, f))
    extra = [] if before is None else [before]
    return pl.pallas_call(
        spread_columns_kernel,
        grid_spec=pltpu.PrefetchScalarGridSpec(
            num_scalar_prefetch=1,
            grid=(shares,),
            in_specs=[piece] * 4 + [block] + [pl.BlockSpec(memory_space=pl.ANY)] * len(extra),
            out_specs=[block, pl.BlockSpec((rows, part), lambda f, copy: (0, 0))],
        ),
        out_shape=[
            jax.ShapeDtypeStruct(weight.shape, F32),
            jax.ShapeDtypeStruct((rows, part), F32),
        ],
        input_output_aliases={6: 0} if extra else {},
        compiler_params=params(),
        cost_estimate=cost(4 * rows * width, 20 * rows * width),
        name="spread_columns",
    )(copy, *pieces, weight, *extra)


def spread_rows_kernel(copy_ref, *refs):
    pieces, out_ref = refs[:4], refs[4]
    part = pieces[0].shape[0]
    for k, piece in enumerate(pieces):
        at = pl.ds(pl.multiple_of((copy_ref[0] ^ k) * part, part), part)
        out_ref[at, :] = piece[...].astype(F32)


def spread_rows(copy, pieces):
    part, columns = pieces[0].shape
    tile = 512
    return pl.pallas_call(
        spread_rows_kernel,
        grid_spec=pltpu.PrefetchScalarGridSpec(
            num_scalar_prefetch=1,
            grid=(columns // tile,),
            in_specs=[pl.BlockSpec((part, tile), lambda c, copy: (0, c))] * 4,
            out_specs=pl.BlockSpec((COPIES * part, tile), lambda c, copy: (0, c)),
        ),
        out_shape=jax.ShapeDtypeStruct((COPIES * part, columns), F32),
        compiler_params=params(),
        cost_estimate=cost(4 * part * columns, 24 * part * columns),
        name="spread_rows",
    )(copy, *pieces)


def on_device(
    tokens, segment_ids, out_grad, norm_gain, in_proj, conv_weight, conv_bias, x_proj,
    step_proj, step_bias, decay_log, skip_gain, out_proj, *, fsdp,
):
    ring = Ring(fsdp)
    copy = lax.axis_index("rep")
    batches, length, model = tokens.shape
    total = COPIES * batches * length
    slab = in_proj.shape[0]
    share = out_proj.shape[0]
    part = share // COPIES
    width = fsdp * part
    rank, nstate = step_proj.shape[1], decay_log.shape[1]
    taps_n = conv_weight.shape[1]
    gains_n = slab // part

    def mine(value):
        return lax.dynamic_slice_in_dim(value, copy * part, part, 0)

    copy_index = copy.astype(jnp.int32).reshape(1)
    aligned = part % LANES == 0
    if not aligned:
        entry = lax.dynamic_index_in_dim(
            in_proj.reshape(slab, 2, fsdp, COPIES, part), copy, 3, keepdims=False
        )
        inner_shard, gate_shard = (entry[:, i].reshape(slab, width) for i in range(2))
    few = jnp.concatenate(
        [
            mine(x_proj).T,
            mine(step_proj).T,
            mine(conv_weight).T,
            mine(conv_bias)[None],
            mine(step_bias)[None],
            mine(decay_log).T,
            mine(skip_gain)[None],
            norm_gain.reshape(gains_n, part),
        ],
        axis=0,
    )
    few = jnp.pad(few, ((0, -few.shape[0] % 16), (0, 0)))
    small_ring = ring.half == 4
    own = [tokens, out_grad, segment_ids[:, 0, :]]
    fused = small_ring and aligned
    if fused:
        out = forward(fsdp, rank, nstate, in_proj, few, *own, out_proj)
        few_all = out["few"].astype(F32)
    else:
        gathers = [Gather(ring, inner_shard), Gather(ring, few)]
        for gather in gathers:
            gather.rest()
        inner_in, few_all = (gather.whole for gather in gathers)
        few_all = jnp.moveaxis(few_all, 0, 1).reshape(-1, width).astype(F32)
        copies = [jnp.stack(rep_gather(value)) for value in own]
        inner_in = inner_in.reshape(model, width)
        values, cotangent, segments = (c.reshape((GROUP,) + c.shape[2:]) for c in copies)

    sizes = [rank + 2 * nstate, rank, taps_n, 1, 1, nstate, 1, gains_n]
    pieces, start = [], 0
    for size in sizes:
        pieces.append(few_all[start : start + size])
        start += size
    select, stride, taps, shift_bias, size_bias, decay, skip, gain = pieces
    select, stride = select.astype(BF16), stride.astype(BF16)
    gain = jnp.moveaxis(gain.reshape(gains_n, fsdp, part), 0, 1).reshape(model)

    def masks_of(segments):
        masks = []
        for shift in range(1, taps_n):
            earlier = jnp.pad(segments, ((0, 0), (shift, 0)), constant_values=-1)[:, :length]
            masks.append((earlier == segments).astype(F32).T.reshape(total, 1))
        return jnp.broadcast_to(jnp.stack(masks), (taps_n - 1, total, LANES))

    tap_rows = jnp.concatenate([taps, shift_bias, jnp.zeros((7 - taps_n, width), F32)])
    side_rows = jnp.concatenate([size_bias, skip, jnp.zeros((6, width), F32)])
    decay_rate = -jnp.exp(decay)

    if fused:
        (
            masks, rate, spread_by, fold_by, normed, cotangent, inner_in, inner, act, act_low, step_low, coef, step,
            starts, gate, readout, gated, gated_natural, gate_in, out_w,
        ) = (
            out[k]
            for k in (
                "masks", "rate", "spread_by", "fold_by", "normed", "cotangent", "inner_in", "inner", "act", "act_low",
                "step_low", "coef", "step", "starts", "gate", "readout", "gated", "gated_natural", "gate_in", "out_w",
            )
        )
    else:
        rate = jnp.broadcast_to((decay_rate * LOG2E)[:, None, :], (nstate, GROUP, width))
        masks, spread_by, fold_by = masks_of(segments), spreader(nstate), folder(nstate)
        normed, cotangent = interleave(values, gain), interleave(cotangent)
        gathers = [Gather(ring, gate_shard), Gather(ring, mine(out_proj))]
        for gather in gathers:
            gather.rest()
        gate_in = gathers[0].whole.reshape(model, width)
        out_w = gathers[1].whole.reshape(width, model)
        inner = dot(normed, inner_in, 1, 0)
        act, act_low = conv_forward(inner, masks, tap_rows)
        half_sums = sum_near(by_copy(to_sequence(dot(act_low, select, 1, 1))))
        projected = to_time(sum_far(half_sums).reshape(total, -1))
        step_low = projected[:, :rank].astype(BF16)
        coef = spread(projected[:, rank:], nstate)
        pre = dot(step_low, stride, 1, 0)
        readout, step, starts = scan_forward(pre, act, coef, spread_by, masks[0], rate, side_rows)
        gate = dot(normed, gate_in, 1, 0)
        gated, gated_natural = gate_forward(readout, gate)
    keep = masks[0]
    out_wgrad = dot(gated, cotangent, 0, 0).astype(BF16).reshape(fsdp, part, model)

    def r1():
        return gate_backward(dot(cotangent, out_w, 1, 1), readout, gate)

    read_grad, gate_grad, gate_grad_natural = r1()

    gate_wgrad = dot(normed, gate_grad, 0, 0).astype(BF16).reshape(fsdp, slab, width)
    wgrads = [out_wgrad, gate_wgrad] if fused else []
    pre_low, direct, coef_part, _, sums, *totals = scan_backward(
        step, act, read_grad, coef, spread_by, fold_by, keep, rate, side_rows, starts,
        fsdp if fused else 0, wgrads,
    )
    if not fused:
        scatters = [Scatter(ring, out_wgrad), Scatter(ring, gate_wgrad)]
        for scatter in scatters:
            scatter.rest()
        totals = [scatter.total.astype(BF16) for scatter in scatters]
    low_part = dot(pre_low, stride, 1, 1)
    proj_part = jnp.concatenate([low_part, coef_part[:, : 2 * nstate]], axis=1)
    gated_natural, gate_grad_natural = after(pre_low, gated_natural, gate_grad_natural)

    def norm_gate_part():
        return dot(gate_grad_natural, gate_in, 1, 1)

    def out_part():
        return by_copy(dot(gated_natural, out_w, 1, 0).astype(BF16))

    def proj_sums():
        return sum_near(by_copy(to_sequence(proj_part)))

    half_sums, out_parts, norm_gate, out_pieces = slot(
        3, [], proj_sums, out_part, norm_gate_part, lambda: rep_gather(totals[0])
    )

    def conv_part():
        proj_time = to_time(sum_far(half_sums).reshape(total, -1).astype(BF16))
        act_grad = direct + dot(proj_time, select, 1, 0)
        inner_grad, inner_grad_natural, conv_sums = conv_backward(inner, act_grad, masks, tap_rows)
        inner_wgrad = dot(normed, inner_grad, 0, 0).astype(BF16).reshape(fsdp, slab, width)
        small = jnp.concatenate(
            [
                dot(proj_time, act_low, 0, 0),
                dot(step_low, pre_low, 0, 0),
                conv_sums[: taps_n + 1],
                jnp.sum(sums[nstate + 1 :], axis=1),
                decay_rate * jnp.sum(sums[:nstate], axis=1),
                jnp.sum(sums[nstate : nstate + 1], axis=1),
            ],
            axis=0,
        )
        small = jnp.pad(small, ((0, -small.shape[0] % 16), (0, 0))).astype(BF16)
        small = jnp.moveaxis(small.reshape(-1, fsdp, part), 1, 0)
        return inner_grad_natural, inner_wgrad, small

    (inner_grad_natural, inner_wgrad, small), (out_near, out_far) = slot(
        4, [], conv_part, lambda: rep_scatter_near(out_parts)
    )

    grads = dot(inner_grad_natural, inner_in, 1, 1) + norm_gate
    norm_parts = by_copy(grads.astype(BF16))

    def finish_out():
        summed = rep_scatter_far(out_near, out_far)
        return (tokens.astype(F32) + summed.reshape(tokens.shape)).astype(BF16)

    gate_pieces = rep_gather(totals[1])

    def place_gate():
        if not aligned:
            return gate_pieces
        return spread_columns(copy_index, gate_pieces, in_proj, 1)

    def place_out():
        if aligned:
            return spread_rows(copy_index, out_pieces)
        return jnp.stack(out_pieces)[jnp.arange(COPIES) ^ copy].reshape(share, model).astype(F32)

    gate_placed, out_all, block_out = place_gate(), place_out(), finish_out()
    if small_ring and aligned:
        inner_pieces, small_pieces, normed_sum = scatter_all(fsdp, inner_wgrad, small, norm_parts)
        inner_pieces = [inner_pieces[k] for k in range(COPIES)]
        small_pieces = [small_pieces[k] for k in range(COPIES)]
    else:
        near, far = rep_scatter_near(norm_parts)
        normed_sum = rep_scatter_far(near, far)
        scatters = [Scatter(ring, inner_wgrad), Scatter(ring, small)]
        for scatter in scatters:
            scatter.rest()
        inner_pieces, small_pieces = (rep_gather(s.total.astype(BF16)) for s in scatters)

    def finish_tokens():
        normed_grad = normed_sum.reshape(tokens.shape)
        own = tokens.astype(F32)
        own_scale = lax.rsqrt(jnp.mean(own * own, axis=-1, keepdims=True) + EPS)
        scaled = normed_grad * gain
        lean = jnp.mean(scaled * own, axis=-1, keepdims=True)
        return (
            out_grad.astype(F32) + own_scale * scaled - own * (own_scale**3) * lean
        ).astype(BF16)

    input_grad = finish_tokens()

    order = jnp.arange(COPIES) ^ copy
    if aligned:
        entry_all, gain_inner = spread_columns(
            copy_index, inner_pieces, in_proj, 0, gate_placed[0]
        )
        gain_sum = jnp.sum(gain_inner + gate_placed[1], axis=1)
    else:
        halves = jnp.stack([jnp.stack(inner_pieces), jnp.stack(gate_placed)])[:, order]
        halves = halves.reshape(2, COPIES, slab, fsdp, part).astype(F32)
        entry_all = jnp.transpose(halves, (2, 0, 3, 1, 4)).reshape(slab, -1)
        gain_sum = jnp.sum(entry_all * in_proj.astype(F32), axis=1)
    gain_grad = gain_sum / norm_gain.astype(F32)
    small_all = jnp.stack(small_pieces)[order].astype(F32)
    small_all = jnp.moveaxis(small_all, 0, 1).reshape(-1, share)
    out, start = [], 0
    for size in sizes[:-1]:
        out.append(small_all[start : start + size])
        start += size
    select_g, stride_g, taps_g, shift_g, size_g, decay_g, skip_g = out
    return (
        block_out,
        input_grad,
        gain_grad,
        entry_all,
        taps_g.T,
        shift_g[0],
        select_g.T,
        stride_g.T,
        size_g[0],
        decay_g.T,
        skip_g[0],
        out_all,
    )


def solution(mesh):
    tokens = P(None, ("fsdp", "rep"), None)
    rows, row = P("fsdp", None), P("fsdp")
    return jax.shard_map(
        functools.partial(on_device, fsdp=mesh.shape["fsdp"]),
        mesh=mesh,
        in_specs=(tokens, tokens, tokens, row, rows, rows, row, rows, rows, row, rows, row, rows),
        out_specs=(tokens, tokens, row, rows, rows, row, rows, rows, row, rows, row, rows),
        check_vma=False,
    )
```

```python
import functools

import jax
import jax.numpy as jnp
from jax import lax
from jax.experimental import pallas as pl
from jax.experimental.pallas import tpu as pltpu
from jax.sharding import PartitionSpec as P

EPS = 1e-05
BLOCK = 16
LANES = 128
GROUP = 8
COPIES = 4
LOG2E = 1.4426950408889634
LN2 = 0.6931471805599453
FAR = 1e30
F32 = jnp.float32
BF16 = jnp.bfloat16
VMEM_LIMIT = 56 * 1024 * 1024


def dot(left, right, left_dim, right_dim):
    return lax.dot_general(
        left, right, (((left_dim,), (right_dim,)), ((), ())), preferred_element_type=F32
    )


def params():
    return pltpu.CompilerParams(vmem_limit_bytes=VMEM_LIMIT)


def cost(flops, moved):
    return pl.CostEstimate(flops=int(flops), bytes_accessed=int(moved), transcendentals=0)


def blank(shape, dtype):
    return pl.pallas_call(
        lambda ref: None,
        out_shape=jax.ShapeDtypeStruct(shape, dtype),
        out_specs=pl.BlockSpec(memory_space=pl.ANY),
        name="blank",
    )()


def ring_order(size):
    half = size // 2
    return [2 * p if p < half else 2 * (size - 1 - p) + 1 for p in range(size)]


class Ring:
    def __init__(self, size):
        order = ring_order(size)
        place = [0] * size
        for spot, member in enumerate(order):
            place[member] = spot
        self.size, self.half = size, size // 2
        self.order = jnp.array(order, jnp.int32)
        self.spot = jnp.array(place, jnp.int32)[lax.axis_index("fsdp")]
        self.above = [(order[p], order[(p + 1) % size]) for p in range(size)]
        self.below = [(order[p], order[(p - 1) % size]) for p in range(size)]

    def member(self, offset):
        return self.order[(self.spot + offset + self.size) % self.size]

    def up(self, value):
        return lax.ppermute(value, "fsdp", self.above)

    def down(self, value):
        return lax.ppermute(value, "fsdp", self.below)


class Gather:
    def __init__(self, ring, shard):
        self.ring, self.cut = ring, shard.shape[0] // 2
        self.whole = blank((ring.size,) + shard.shape, shard.dtype)
        self.held = (shard, shard)
        self.put(shard, 0)

    def put(self, piece, offset, start=0):
        at = (self.ring.member(offset), jnp.int32(start), jnp.int32(0))
        self.whole = lax.dynamic_update_slice(self.whole, piece[None], at)

    def step(self, number):
        low, high = self.held
        if number == self.ring.half:
            low, high = low[: self.cut], high[self.cut :]
        return self.ring.up(low), self.ring.down(high)

    def take(self, number, got):
        self.held = got
        last = number == self.ring.half
        self.put(got[0], -number)
        self.put(got[1], number, self.cut if last else 0)

    def rest(self):
        def body(number, state):
            whole, low, high = state
            low, high = self.ring.up(low), self.ring.down(high)
            self.whole = whole
            self.put(low, -number)
            self.put(high, number)
            return self.whole, low, high

        self.whole, low, high = lax.fori_loop(1, self.ring.half, body, (self.whole,) + self.held)
        self.held = (low, high)
        self.take(self.ring.half, self.step(self.ring.half))


class Scatter:
    def __init__(self, ring, parts):
        self.ring, self.parts, self.cut = ring, parts, parts.shape[1] // 2
        far = self.own(ring.half)
        self.sent = (far[: self.cut], far[self.cut :])
        self.total = None

    def own(self, offset):
        return lax.dynamic_index_in_dim(self.parts, self.ring.member(offset), 0, keepdims=False)

    def step(self, number):
        return self.ring.up(self.sent[0]), self.ring.down(self.sent[1])

    def take(self, number, got):
        left = self.ring.half - number
        low, high = got
        near_low, near_high = self.own(left), self.own(-left)
        if number == 1:
            low = jnp.concatenate([low, jnp.zeros_like(near_low[self.cut :])])
            high = jnp.concatenate([jnp.zeros_like(near_high[: self.cut]), high])
        if left == 0:
            self.total = near_low.astype(F32) + low.astype(F32) + high.astype(F32)
        else:
            self.sent = (self.add(near_low, low), self.add(near_high, high))

    def add(self, near, got):
        return (near.astype(F32) + got.astype(F32)).astype(near.dtype)

    def rest(self):
        self.take(1, self.step(1))

        def body(number, sent):
            left = self.ring.half - number
            low, high = self.ring.up(sent[0]), self.ring.down(sent[1])
            return self.add(self.own(left), low), self.add(self.own(-left), high)

        self.sent = lax.fori_loop(2, self.ring.half, body, self.sent)
        self.take(self.ring.half, self.step(self.ring.half))


def swap(value, bit):
    return lax.ppermute(value, "rep", [(r, r ^ bit) for r in range(COPIES)])


def rep_gather(value):
    across = swap(value, 2)
    return [value, swap(value, 1), across, swap(across, 1)]


def rep_scatter_near(parts):
    pair = swap(jnp.stack([parts[1], parts[3]]), 1)
    near = parts[0].astype(F32) + pair[0].astype(F32)
    far = parts[2].astype(F32) + pair[1].astype(F32)
    return near, far.astype(parts.dtype)


def rep_scatter_far(near, far):
    return near + swap(far, 2).astype(F32)


def sum_near(parts):
    pair = swap(jnp.stack([parts[1], parts[3]]), 1)
    mine = jnp.stack([parts[0], parts[2]]) + pair
    return mine + swap(jnp.stack([mine[1], mine[0]]), 2)


def sum_far(mine):
    next_to = swap(mine, 1)
    return jnp.stack([mine[0], next_to[0], mine[1], next_to[1]])


def to_time(value):
    return jnp.swapaxes(value.reshape(GROUP, -1, value.shape[-1]), 0, 1).reshape(value.shape)


def to_sequence(value):
    return jnp.swapaxes(value.reshape(-1, GROUP, value.shape[-1]), 0, 1).reshape(value.shape)


def by_copy(value):
    return value.reshape(COPIES, -1, value.shape[-1])


def sigmoid(value):
    return 1.0 / (1.0 + jnp.exp(-value))


def later(value, shift):
    rows = shift * GROUP
    return jnp.concatenate([jnp.zeros_like(value[:rows]), value[:-rows]], axis=0)


def sooner(value, shift):
    rows = shift * GROUP
    return jnp.concatenate([value[rows:], jnp.zeros_like(value[:rows])], axis=0)


def conv_of(inner, masks, taps):
    total = taps[4:5] + taps[3:4] * inner
    for shift in range(1, 4):
        total = total + taps[3 - shift : 4 - shift] * (later(inner, shift) * masks[shift - 1])
    return total


def by_sequence(held, out_ref, value):
    length = value.shape[0] // GROUP
    held[...] = value
    for s in range(GROUP):
        out_ref[s * length : (s + 1) * length, :] = held[
            pl.ds(s, length, stride=GROUP), :
        ].astype(out_ref.dtype)


def conv_kernel(inner_ref, masks_ref, taps_ref, act_ref, low_ref):
    value = conv_of(inner_ref[...], masks_ref, taps_ref[...])
    act = value * sigmoid(value)
    act_ref[...] = act
    low_ref[...] = act.astype(BF16)


def conv_forward(inner, masks, taps):
    rows, width = inner.shape
    tile = pl.BlockSpec((rows, LANES), lambda c: (0, c))
    return pl.pallas_call(
        conv_kernel,
        grid=(width // LANES,),
        in_specs=[
            tile,
            pl.BlockSpec((3, rows, LANES), lambda c: (0, 0, 0)),
            pl.BlockSpec((8, LANES), lambda c: (0, c)),
        ],
        out_specs=[tile, tile],
        out_shape=[
            jax.ShapeDtypeStruct((rows, width), F32),
            jax.ShapeDtypeStruct((rows, width), BF16),
        ],
        compiler_params=params(),
        cost_estimate=cost(30 * rows * width, 10 * rows * width),
        name="conv_forward",
    )(inner, masks, taps)


def conv_back_kernel(inner_ref, grad_ref, masks_ref, taps_ref, out_ref, natural_ref, sums_ref, held):
    inner, taps = inner_ref[...], taps_ref[...]
    value = conv_of(inner, masks_ref, taps)
    gate = sigmoid(value)
    grad = grad_ref[...] * (gate * (1.0 + value * (1.0 - gate)))
    total = taps[3:4] * grad
    sums = [None] * 4 + [jnp.sum(grad, axis=0, keepdims=True)]
    sums[3] = jnp.sum(grad * inner, axis=0, keepdims=True)
    for shift in range(1, 4):
        masked = grad * masks_ref[shift - 1]
        total = total + taps[3 - shift : 4 - shift] * sooner(masked, shift)
        sums[3 - shift] = jnp.sum(masked * later(inner, shift), axis=0, keepdims=True)
    out_ref[...] = total.astype(BF16)
    by_sequence(held, natural_ref, total)
    sums_ref[...] = jnp.concatenate(sums + [jnp.zeros((3, inner.shape[1]), F32)], axis=0)


def conv_backward(inner, grad, masks, taps):
    rows, width = inner.shape
    tile = pl.BlockSpec((rows, LANES), lambda c: (0, c))
    few = pl.BlockSpec((8, LANES), lambda c: (0, c))
    return pl.pallas_call(
        conv_back_kernel,
        grid=(width // LANES,),
        in_specs=[tile, tile, pl.BlockSpec((3, rows, LANES), lambda c: (0, 0, 0)), few],
        out_specs=[tile, tile, few],
        out_shape=[
            jax.ShapeDtypeStruct((rows, width), BF16),
            jax.ShapeDtypeStruct((rows, width), BF16),
            jax.ShapeDtypeStruct((8, width), F32),
        ],
        scratch_shapes=[pltpu.VMEM((rows, LANES), F32)],
        compiler_params=params(),
        cost_estimate=cost(60 * rows * width, 10 * rows * width),
        name="conv_backward",
    )(inner, grad, masks, taps)


def gate_kernel(readout_ref, gate_ref, out_ref, natural_ref, held):
    gate = gate_ref[...]
    gated = readout_ref[...] * (gate * sigmoid(gate))
    out_ref[...] = gated.astype(BF16)
    by_sequence(held, natural_ref, gated)


def gate_forward(readout, gate):
    rows, width = gate.shape
    tile = pl.BlockSpec((rows, LANES), lambda c: (0, c))
    return pl.pallas_call(
        gate_kernel,
        grid=(width // LANES,),
        in_specs=[tile] * 2,
        out_specs=[tile] * 2,
        out_shape=[jax.ShapeDtypeStruct((rows, width), BF16)] * 2,
        scratch_shapes=[pltpu.VMEM((rows, LANES), F32)],
        compiler_params=params(),
        cost_estimate=cost(20 * rows * width, 12 * rows * width),
        name="gate_forward",
    )(readout, gate)


def gate_back_kernel(grad_ref, readout_ref, gate_ref, read_ref, out_ref, natural_ref, held):
    gate, grad = gate_ref[...], grad_ref[...]
    sig = sigmoid(gate)
    read_ref[...] = grad * (gate * sig)
    gate_grad = grad * readout_ref[...] * (sig * (1.0 + gate * (1.0 - sig)))
    out_ref[...] = gate_grad.astype(BF16)
    by_sequence(held, natural_ref, gate_grad)


def gate_backward(grad, readout, gate):
    rows, width = gate.shape
    tile = pl.BlockSpec((rows, LANES), lambda c: (0, c))
    return pl.pallas_call(
        gate_back_kernel,
        grid=(width // LANES,),
        in_specs=[tile] * 3,
        out_specs=[tile] * 3,
        out_shape=[jax.ShapeDtypeStruct((rows, width), F32)]
        + [jax.ShapeDtypeStruct((rows, width), BF16)] * 2,
        scratch_shapes=[pltpu.VMEM((rows, LANES), F32)],
        compiler_params=params(),
        cost_estimate=cost(20 * rows * width, 20 * rows * width),
        name="gate_backward",
    )(grad, readout, gate)


def rows_kernel(scaled, *refs):
    values_ref, out_ref, held = refs[0], refs[-2], refs[-1]
    for s in range(GROUP):
        value = values_ref[s].astype(F32)
        if scaled:
            square = jnp.mean(value * value, axis=-1, keepdims=True)
            value = value * lax.rsqrt(square + EPS) * refs[1][...]
        for k in range(held.shape[0]):
            held[k, pl.ds(s, value.shape[0], stride=GROUP), :] = value[
                :, k * LANES : (k + 1) * LANES
            ]
    for k in range(held.shape[0]):
        out_ref[:, k * LANES : (k + 1) * LANES] = held[k].astype(BF16)


def interleave(values, gain=None):
    _, length, model = values.shape
    extra = [] if gain is None else [gain.reshape(1, model)]
    return pl.pallas_call(
        functools.partial(rows_kernel, gain is not None),
        grid=(length // BLOCK,),
        in_specs=[pl.BlockSpec((GROUP, BLOCK, model), lambda t: (0, t, 0))]
        + [pl.BlockSpec((1, model), lambda t: (0, 0))] * len(extra),
        out_specs=pl.BlockSpec((BLOCK * GROUP, model), lambda t: (t, 0)),
        out_shape=jax.ShapeDtypeStruct((length * GROUP, model), BF16),
        scratch_shapes=[pltpu.VMEM((model // LANES, BLOCK * GROUP, LANES), F32)],
        compiler_params=params(),
        cost_estimate=cost(8 * GROUP * length * model, 4 * GROUP * length * model),
        name="interleave",
    )(values, *extra)


class Peers:
    def __init__(self, size):
        self.size, self.half = size, size // 2
        self.member, self.copy = lax.axis_index("fsdp"), lax.axis_index("rep")
        row, column = lax.div(self.member, 2), lax.rem(self.member, 2)
        self.spot = row * (1 - column) + (size - 1 - row) * column
        side = lax.rem(self.copy, 2)
        self.core = (self.member, self.copy - side + (1 - side))
        self.across = (self.member, lax.rem(self.copy + 2, COPIES))
        self.ring = ((self.at(1), self.copy), (self.at(-1), self.copy))

    def at(self, offset):
        spot = lax.rem(self.spot + (offset + self.size), self.size)
        second = lax.div(spot, self.half)
        return 2 * spot * (1 - second) + (2 * (self.size - 1 - spot) + 1) * second

    def meet(self):
        barrier = pltpu.get_barrier_semaphore()
        peers = (*self.ring, self.core, self.across)
        for peer in peers:
            pl.semaphore_signal(barrier, inc=1, device_id=peer, device_id_type=pl.DeviceIdType.MESH)
        pl.semaphore_wait(barrier, len(peers))


def remote(source, target, sems, index, peer):
    return pltpu.make_async_remote_copy(
        src_ref=source,
        dst_ref=target,
        send_sem=sems[0].at[index],
        recv_sem=sems[1].at[index],
        device_id=peer,
        device_id_type=pl.DeviceIdType.MESH,
    )


def spread(coefs, nstate):
    terms = []
    for _ in range(3):
        term = coefs.astype(BF16)
        terms.append(term)
        coefs = coefs - term.astype(F32)
    joined = jnp.concatenate(terms, axis=1)
    return jnp.pad(joined, ((0, 0), (0, LANES - joined.shape[1])))


def spreader(nstate):
    row = lax.broadcasted_iota(jnp.int32, (LANES, 2 * nstate * LANES), 0)
    tile = lax.broadcasted_iota(jnp.int32, (LANES, 2 * nstate * LANES), 1) // LANES
    return ((row % (2 * nstate) == tile) & (row < 6 * nstate)).astype(BF16)


def folder(nstate):
    tile = lax.broadcasted_iota(jnp.int32, (2 * nstate * LANES, LANES), 0) // LANES
    column = lax.broadcasted_iota(jnp.int32, (2 * nstate * LANES, LANES), 1)
    return (tile == column).astype(BF16)


def tiled(value, width):
    return jnp.concatenate([value] * (width // LANES), axis=1)


def at_time(t):
    return pl.ds(pl.multiple_of(t * GROUP, GROUP), GROUP)


def scan_kernel(
    nstate, chunk, pre_ref, act_ref, coef_ref, spread_ref, keep_ref, rate_ref, row_ref,
    out_ref, step_ref, start_ref, carry_ref, wide,
):
    width = pre_ref.shape[1]

    @pl.when(pl.program_id(0) == 0)
    def _():
        carry_ref[...] = jnp.zeros_like(carry_ref)

    start_ref[0] = carry_ref[...]
    wide[...] = jnp.dot(coef_ref[...], spread_ref[...], preferred_element_type=F32)
    pre = pre_ref[...] + row_ref[0:1]
    step_ref[...] = jnp.maximum(pre, 0.0) + jnp.log1p(jnp.exp(-jnp.abs(pre)))
    for c in range(width // chunk):
        cols = slice(c * chunk, (c + 1) * chunk)

        def advance(t, states):
            at = at_time(t)
            step, act = step_ref[at, cols], act_ref[at, cols]
            drive = jnp.where(tiled(keep_ref[at, :], chunk) > 0.5, step, FAR)
            inflow = step * act
            total = row_ref[1:2, cols] * act
            now = []
            for n in range(nstate):
                write = tiled(wide[at, n * LANES : (n + 1) * LANES], chunk)
                read = tiled(wide[at, (nstate + n) * LANES : (nstate + n + 1) * LANES], chunk)
                state = jnp.exp2(drive * rate_ref[n, :, cols]) * states[n] + write * inflow
                total = total + read * state
                now.append(state)
            out_ref[at, cols] = total
            return tuple(now)

        start = tuple(carry_ref[n, :, cols] for n in range(nstate))
        states = lax.fori_loop(0, BLOCK, advance, start, unroll=4)
        for n in range(nstate):
            carry_ref[n, :, cols] = states[n]


def scan_forward(pre, act, coef, spread_by, keep, rate, rows):
    total, width = pre.shape
    nstate = rate.shape[0]
    size = BLOCK * GROUP
    tile = pl.BlockSpec((size, width), lambda t: (t, 0))
    thin = pl.BlockSpec((size, LANES), lambda t: (t, 0))
    state = pl.BlockSpec((nstate, GROUP, width), lambda t: (0, 0, 0))
    count = total // size
    work = total * width * nstate
    return pl.pallas_call(
        functools.partial(scan_kernel, nstate, 256),
        grid=(count,),
        in_specs=[
            tile,
            tile,
            thin,
            pl.BlockSpec(spread_by.shape, lambda t: (0, 0)),
            thin,
            state,
            pl.BlockSpec((8, width), lambda t: (0, 0)),
        ],
        out_specs=[
            tile,
            tile,
            pl.BlockSpec((1, nstate, GROUP, width), lambda t: (t, 0, 0, 0)),
        ],
        out_shape=[
            jax.ShapeDtypeStruct((total, width), F32),
            jax.ShapeDtypeStruct((total, width), F32),
            jax.ShapeDtypeStruct((total // size, nstate, GROUP, width), F32),
        ],
        scratch_shapes=[
            pltpu.VMEM((nstate, GROUP, width), F32),
            pltpu.VMEM((size, 2 * nstate * LANES), F32),
        ],
        compiler_params=params(),
        cost_estimate=cost(16 * work, 16 * count * size * width),
        name="scan_forward",
    )(pre, act, coef, spread_by, keep, rate, rows)


class Shares:
    def __init__(self, peers, shards, wholes, sems):
        self.peers, self.shards, self.wholes, self.sems = peers, shards, wholes, sems
        self.sent = []

    def place(self, which, member, c):
        rows = self.shards[which].shape[0]
        start = pl.multiple_of(member * rows + c * (rows // 2), rows // 2)
        return self.wholes[which].at[pl.ds(start, rows // 2), :]

    def owner(self, way, step):
        return self.peers.at(-step if way == 0 else step)

    def chunks(self, way, step):
        return (way,) if step == self.peers.half else (0, 1)

    def come(self, which, way, step, c):
        there = self.place(which, self.owner(way, step), c)
        remote(there, there, self.sems, (which, way, step - 1, c), self.peers.ring[way]).wait_recv()

    def step(self, which, step):
        for c in range(2):
            for way in range(2):
                if c not in self.chunks(way, step):
                    continue
                target = self.place(which, self.owner(way, step - 1), c)
                source = target
                if step == 1:
                    rows = self.shards[which].shape[0] // 2
                    source = self.shards[which].at[pl.ds(c * rows, rows), :]
                else:
                    self.come(which, way, step - 1, c)
                index = (which, way, step - 1, c)
                remote(source, target, self.sems, index, self.peers.ring[way]).start()

    def finish(self, which):
        half = self.peers.half
        for way in range(2):
            self.come(which, way, half - 1, 1 - way)
            self.come(which, way, half, way)

    def sent_all(self):
        for which in range(len(self.shards)):
            for step in range(1, self.peers.half + 1):
                for way in range(2):
                    for c in self.chunks(way, step):
                        place = self.place(which, self.owner(way, step - 1), c)
                        index = (which, way, step - 1, c)
                        remote(place, place, self.sems, index, self.peers.ring[way]).wait_send()


def softplus(value):
    return jnp.maximum(value, 0.0) + jnp.log1p(jnp.exp(-jnp.abs(value)))


def forward_kernel(
    size, rank, nstate,
    entry, few, tokens, out_grad, segments, out_proj,
    few_out, masks_out, rate_out, spread_out, fold_out, normed_out, cotangent_out, tokens_all, grads_all, segments_all,
    w_in_out, inner_out, act_out, low_out, step_low_out, coef_out, step_out, start_out, gate_out, readout_out,
    gated_out, natural_out, gate_w_out, out_w_out,
    few_all, small, masks, rate, spread_by, fold_by, normed, stage, cotangent, held, seg, inner_shard, gate_shard, w_in,
    inner, act, low, part, nat, got_near, to_across, got_across, shared, step_low, coef, wide, pre, step, readout,
    carry, start_at, gate, gated, natural, gate_w,
    local, start_sems, gate_sems, own_sems, entry_sems, stage_sems, out_sems, seg_sems,
    ring_send, ring_recv, few_send, few_recv, rep_send, rep_recv, near_send, near_recv,
):
    peers = Peers(size)
    total, width = normed.shape[0], w_in.shape[1]
    pad = 3 * GROUP
    chunk = 256
    rows = 64
    length = total // GROUP
    batches = GROUP // COPIES
    half = peers.half
    side_rows = total // COPIES
    saved = []

    def save(source, target):
        copy = pltpu.make_async_copy(source, target, local.at[len(saved)])
        copy.start()
        saved.append(copy)

    picks = []
    for side_of, target in enumerate((inner_shard, gate_shard)):
        for f in range(size):
            source = ((side_of * size + f) * COPIES + peers.copy) * LANES
            picks.append(
                pltpu.make_async_copy(
                    entry.at[:, pl.ds(pl.multiple_of(source, LANES), LANES)],
                    target.at[:, pl.ds(f * LANES, LANES)],
                    entry_sems.at[len(picks)],
                )
            )
    for pick in picks:
        pick.start()
    peers.meet()
    sent = []

    def send(*copy):
        moving = remote(*copy)
        moving.start()
        sent.append(moving)

    rep_sems = (rep_send, rep_recv)

    def of_copy(ref, k):
        return ref.at[k] if ref is segments_all else ref.at[pl.ds(k * batches, batches)]

    def exchange(i, own, everyone):
        send(own, of_copy(everyone, 2), rep_sems, (i, 0), peers.across)
        send(own, of_copy(everyone, 1), rep_sems, (i, 1), peers.core)
        copy = pltpu.make_async_copy(own, of_copy(everyone, 0), own_sems.at[3 + i])
        copy.start()
        return copy

    def pass_on(i, everyone):
        far = of_copy(everyone, 2)
        remote(far, far, rep_sems, (i, 0), peers.across).wait_recv()
        send(far, of_copy(everyone, 3), rep_sems, (i, 2), peers.core)

    def exchanged(i, everyone, copy):
        copy.wait()
        for k, which in ((1, 1), (3, 2)):
            there = of_copy(everyone, k)
            remote(there, there, rep_sems, (i, which), peers.core).wait_recv()

    out_rows = out_proj.shape[0] // COPIES
    out_shard = out_proj.at[pl.ds(pl.multiple_of(peers.copy * out_rows, out_rows), out_rows), :]
    ring = Shares(
        peers, (inner_shard, gate_shard, out_shard), (w_in, gate_w, out_w_out), (ring_send, ring_recv),
    )
    gate_rows = gate_shard.shape[0]
    shard_rows = pl.ds(pl.multiple_of(peers.member * gate_rows, gate_rows), gate_rows)
    own_rows = pl.ds(pl.multiple_of(peers.member * out_rows, out_rows), out_rows)
    own_columns = pl.ds(pl.multiple_of(peers.member * LANES, LANES), LANES)

    few_sems = (few_send, few_recv)
    few_rows = few.shape[0] // 2

    def few_place(way, number, split):
        columns = pl.ds(pl.multiple_of(ring.owner(way, number) * LANES, LANES), LANES)
        place = pl.ds(way * few_rows, few_rows) if split else pl.ds(0, 2 * few_rows)
        return few_all.at[place, columns]

    def few_come(way, number):
        there = few_place(way, number, number == half)
        remote(there, there, few_sems, (way, number - 1), peers.ring[way]).wait_recv()

    def few_step(number):
        for way in range(2):
            if number > 1:
                few_come(way, number - 1)
            target = few_place(way, number - 1, number == half)
            source = few if number == 1 else target
            send(source, target, few_sems, (way, number - 1), peers.ring[way])

    few_step(1)
    own_tokens = exchange(0, tokens, tokens_all)
    own_segments = exchange(2, segments, segments_all)
    own = [
        pltpu.make_async_copy(few, few_all.at[:, own_columns], own_sems.at[0]),
        pltpu.make_async_copy(out_shard, out_w_out.at[own_rows, :], own_sems.at[1]),
    ]
    for copy in own:
        copy.start()
    for pick in picks[:size]:
        pick.wait()
    ring.step(0, 1)
    for pick in picks[size:]:
        pick.wait()
    own_shards = [
        pltpu.make_async_copy(inner_shard, w_in.at[shard_rows, :], own_sems.at[6]),
        pltpu.make_async_copy(gate_shard, gate_w.at[shard_rows, :], own_sems.at[2]),
    ]
    for copy in own_shards:
        copy.start()

    wide_shape, thin_shape = spread_by.shape, fold_by.shape
    tile = lax.broadcasted_iota(jnp.int32, wide_shape, 1) // LANES
    row = lax.broadcasted_iota(jnp.int32, wide_shape, 0)
    spread_by[...] = jnp.where(
        (lax.rem(row, 2 * nstate) == tile) & (row < 6 * nstate), 1.0, 0.0
    ).astype(BF16)
    tile = lax.broadcasted_iota(jnp.int32, thin_shape, 0) // LANES
    column = lax.broadcasted_iota(jnp.int32, thin_shape, 1)
    fold_by[...] = jnp.where(tile == column, 1.0, 0.0).astype(BF16)
    save(spread_by, spread_out)
    save(fold_by, fold_out)

    few_step(2)
    pass_on(2, segments_all)
    few_step(3)
    ring.step(0, 2)
    few_step(4)
    exchanged(2, segments_all, own_segments)
    numbers = pltpu.make_async_copy(segments_all, seg, seg_sems.at[0])
    numbers.start()
    for way in range(2):
        few_come(way, half - 1) if half < 2 else None
        few_come(way, half)
    own[0].wait()
    numbers.wait()

    numbers = jnp.concatenate([seg[k] for k in range(COPIES)], axis=0).astype(F32)
    lane = lax.broadcasted_iota(jnp.int32, (total, LANES), 1)
    time = lax.broadcasted_iota(jnp.int32, (total, LANES), 0) // GROUP
    picked = jnp.where(lane == time, jnp.concatenate([numbers] * length, axis=0), 0.0).astype(BF16)
    numbers = jnp.dot(picked, jnp.ones((LANES, LANES), BF16), preferred_element_type=F32)
    for shift in range(1, 4):
        earlier = jnp.concatenate(
            [jnp.full((shift * GROUP, LANES), -1.0, F32), numbers[: -shift * GROUP]], axis=0
        )
        masks[shift - 1] = jnp.where(earlier == numbers, 1.0, 0.0)
    save(masks, masks_out)
    save(few_all, few_out)
    first_small = 2 * rank + 2 * nstate
    small[...] = few_all[first_small : first_small + small.shape[0], :].astype(F32)
    taps, bias_row, skip_row, gain_row = 0, 5, 6 + nstate, 7 + nstate
    for n in range(nstate):
        rate[n] = jnp.broadcast_to(-LOG2E * jnp.exp(small[6 + n : 7 + n, :]), (GROUP, width))
    save(rate, rate_out)

    def fetch(source, t, slot):
        return pltpu.make_async_copy(
            source.at[:, pl.ds(pl.multiple_of(t * BLOCK, BLOCK), BLOCK), :], stage.at[slot], stage_sems.at[slot]
        )

    def weave(slot, scaled):
        for s in range(GROUP):
            value = stage[slot, s].astype(F32)
            if scaled:
                square = jnp.mean(value * value, axis=-1, keepdims=True)
                value = value * lax.rsqrt(square + EPS)
            for k in range(held.shape[0]):
                tile = value[:, k * LANES : (k + 1) * LANES]
                if scaled:
                    at = gain_row + k % 2
                    tile = tile * small[at : at + 1, (k // 2) * LANES : (k // 2 + 1) * LANES]
                held[k, pl.ds(s, BLOCK, stride=GROUP), :] = tile

    block_rows = BLOCK * GROUP
    blocks = total // block_rows

    def block_of(t):
        return pl.ds(pl.multiple_of(t * block_rows, block_rows), block_rows)

    pass_on(0, tokens_all)
    own_grads = exchange(1, out_grad, grads_all)
    ring.step(0, 3)
    exchanged(0, tokens_all, own_tokens)
    fetch(tokens_all, 0, 0).start()

    @pl.loop(0, blocks)
    def _(t):
        slot = lax.rem(t, 2)

        @pl.when(t + 1 < blocks)
        def _():
            fetch(tokens_all, t + 1, 1 - slot).start()

        @pl.when(t == blocks - 2)
        def _():
            ring.step(0, 4)
            ring.step(1, 1)

        fetch(tokens_all, t, slot).wait()
        weave(slot, True)
        for k in range(held.shape[0]):
            normed[block_of(t), k * LANES : (k + 1) * LANES] = held[k].astype(BF16)

    save(normed, normed_out)
    for copy in own_shards:
        copy.wait()
    ring.finish(0)
    save(w_in, w_in_out)

    def cotangent_out_of(t, slot):
        return pltpu.make_async_copy(cotangent.at[slot], cotangent_out.at[block_of(t), :], out_sems.at[slot])

    def weave_grads(first, count):
        fetch(grads_all, first, first % 2).start()

        @pl.loop(first, first + count)
        def _(t):
            slot = lax.rem(t, 2)

            @pl.when(t + 1 < first + count)
            def _():
                fetch(grads_all, t + 1, 1 - slot).start()

            @pl.when(t >= 2)
            def _():
                cotangent_out_of(t - 2, slot).wait()

            fetch(grads_all, t, slot).wait()
            weave(slot, False)
            for k in range(held.shape[0]):
                cotangent[slot, :, k * LANES : (k + 1) * LANES] = held[k].astype(BF16)
            cotangent_out_of(t, slot).start()

    inner[0:pad, :] = jnp.zeros((pad, width), F32)
    part[...] = jnp.zeros_like(part)

    @pl.loop(0, width // chunk)
    def _(c):
        cols = pl.ds(pl.multiple_of(c * chunk, chunk), chunk)
        inner[pad:, cols] = jnp.dot(normed[...], w_in[:, cols], preferred_element_type=F32)

        @pl.when(c == 1)
        def _():
            ring.step(2, 1)

        tap = [small[taps + i : taps + i + 1, cols] for i in range(5)]

        @pl.loop(0, total // rows)
        def _(i):
            start = pl.multiple_of(i * rows, rows)
            value = tap[4] + tap[3] * inner[pl.ds(pad + start, rows), cols]
            for shift in range(1, 4):
                mask = tiled(masks[shift - 1, pl.ds(start, rows), :], chunk)
                before = inner[pl.ds(pad - shift * GROUP + start, rows), cols]
                value = value + tap[3 - shift] * (before * mask)
            here = value * sigmoid(value)
            act[pl.ds(start, rows), cols] = here
            low[pl.ds(start, rows), cols] = here.astype(BF16)

        for j in range(2):
            part[j] += lax.dot_general(
                low[:, cols], few_all[j * LANES : (j + 1) * LANES, cols], (((1,), (1,)), ((), ())),
                preferred_element_type=F32,
            )

    save(inner.at[pl.ds(pad, total), :], inner_out)
    save(act, act_out)
    save(low, low_out)

    near = (near_send, near_recv)
    for j in range(2):
        for s in range(GROUP):
            nat[j, s * length : (s + 1) * length, :] = part[j, pl.ds(s, length, stride=GROUP), :]
    sends = []

    def start(source, target, index, peer):
        copy = remote(source, target, near, index, peer)
        copy.start()
        sends.append(copy)

    def come(target, index, peer):
        remote(target, target, near, index, peer).wait_recv()

    for i in range(2):
        start(nat.at[:, pl.ds((2 * i + 1) * side_rows, side_rows), :], got_near.at[i], i, peers.core)
    ring.step(1, 2)
    pass_on(1, grads_all)
    for i in range(2):
        come(got_near.at[i], i, peers.core)
    to_across[...] = nat[:, 2 * side_rows : 3 * side_rows, :] + got_near[1]
    start(to_across, got_across, 2, peers.across)
    exchanged(1, grads_all, own_grads)
    weave_grads(0, blocks // 2)
    ring.step(2, 2)
    come(got_across, 2, peers.across)
    mine = nat[:, :side_rows, :] + got_near[0] + got_across[...]
    shared[0, 0] = mine[0].astype(BF16)
    lane = lax.broadcasted_iota(jnp.int32, (side_rows, LANES), 1)
    rest, terms = jnp.where(lane < 2 * nstate, mine[1], 0.0), jnp.zeros((side_rows, LANES), F32)
    for i in range(3):
        term = rest.astype(BF16).astype(F32)
        rest = rest - term
        terms = terms + (pltpu.roll(term, 2 * nstate * i, 1) if i else term)
    shared[0, 1] = terms.astype(BF16)
    start(shared.at[0], shared.at[2], 3, peers.across)
    start(shared.at[0], shared.at[1], 4, peers.core)
    weave_grads(blocks // 2, blocks // 2)
    come(shared.at[2], 3, peers.across)
    start(shared.at[2], shared.at[3], 5, peers.core)
    come(shared.at[1], 4, peers.core)
    come(shared.at[3], 5, peers.core)
    for copy in sends:
        copy.wait_send()
    for k in range(COPIES):
        for b in range(batches):
            for j in range(2):
                part[j, pl.ds(k * batches + b, length, stride=GROUP), :] = shared[
                    k, j, b * length : (b + 1) * length, :
                ].astype(F32)
    step_low[...] = part[0].astype(BF16)
    coef[...] = part[1].astype(BF16)
    save(step_low, step_low_out)
    save(coef, coef_out)

    stride = few_all[rank + 2 * nstate : 2 * rank + 2 * nstate, :]
    side_bias = small[bias_row : bias_row + 1, :]
    carry[...] = jnp.zeros_like(carry)

    def keep_start(t, slot):
        return pltpu.make_async_copy(start_at.at[slot], start_out.at[t], start_sems.at[slot])

    @pl.loop(0, blocks)
    def _(t):
        for tick, which, number in ((0, 1, 3), (2, 2, 3), (4, 1, 4), (6, 2, 4)):

            @pl.when(t == tick)
            def _(which=which, number=number):
                ring.step(which, number)

        base = pl.multiple_of(t * block_rows, block_rows)
        these = block_of(t)
        wide[...] = jnp.dot(coef[these, :], spread_by[...], preferred_element_type=F32)
        pre[...] = jnp.dot(step_low[these, :], stride, preferred_element_type=F32)
        for i in range(BLOCK // 2):
            sub = slice(i * 2 * GROUP, (i + 1) * 2 * GROUP)
            step[pl.ds(base + i * 2 * GROUP, 2 * GROUP), :] = softplus(pre[sub, :] + side_bias)
        slot = lax.rem(t, 2)

        @pl.when(t >= 2)
        def _():
            keep_start(t - 2, slot).wait()

        start_at[slot] = carry[...]
        keep_start(t, slot).start()
        for c in range(width // chunk):
            cols = slice(c * chunk, (c + 1) * chunk)

            def advance(i, states):
                at = pl.ds(pl.multiple_of(base + i * GROUP, GROUP), GROUP)
                here = at_time(i)
                step_t, act_t = step[at, cols], act[at, cols]
                drive = jnp.where(tiled(masks[0, at, :], chunk) > 0.5, step_t, FAR)
                inflow = step_t * act_t
                out = small[skip_row : skip_row + 1, cols] * act_t
                now = []
                for n in range(nstate):
                    write = tiled(wide[here, n * LANES : (n + 1) * LANES], chunk)
                    read = tiled(wide[here, (nstate + n) * LANES : (nstate + n + 1) * LANES], chunk)
                    state = jnp.exp2(drive * rate[n, :, cols]) * states[n] + write * inflow
                    out = out + read * state
                    now.append(state)
                readout[at, cols] = out
                return tuple(now)

            states = lax.fori_loop(
                0, BLOCK, advance, tuple(carry[n, :, cols] for n in range(nstate)), unroll=4
            )
            for n in range(nstate):
                carry[n, :, cols] = states[n]

    save(step, step_out)
    save(readout, readout_out)

    ring.finish(1)
    save(gate_w, gate_w_out)

    def keep_gate(c, slot):
        cols = pl.ds(pl.multiple_of(c * chunk, chunk), chunk)
        return pltpu.make_async_copy(gate.at[slot], gate_out.at[:, cols], gate_sems.at[slot])

    @pl.loop(0, width // chunk)
    def _(c):
        cols = pl.ds(pl.multiple_of(c * chunk, chunk), chunk)
        slot = lax.rem(c, 2)

        @pl.when(c >= 2)
        def _():
            keep_gate(c - 2, slot).wait()

        gate[slot] = jnp.dot(normed[...], gate_w[:, cols], preferred_element_type=F32)
        keep_gate(c, slot).start()

        @pl.loop(0, total // rows)
        def _(i):
            at = pl.ds(pl.multiple_of(i * rows, rows), rows)
            here = gate[slot, at, :]
            value = readout[at, cols] * (here * sigmoid(here))
            gated[at, cols] = value.astype(BF16)
            for k in range(chunk // LANES):
                nat[k, at, :] = value[:, k * LANES : (k + 1) * LANES]

        for k in range(chunk // LANES):
            for s in range(GROUP):
                natural[s * length : (s + 1) * length, pl.ds(pl.multiple_of(c * chunk + k * LANES, LANES), LANES)] = nat[
                    k, pl.ds(s, length, stride=GROUP), :
                ].astype(BF16)

    save(gated, gated_out)
    save(natural, natural_out)
    own[1].wait()
    ring.finish(2)
    ring.sent_all()
    for moving in sent:
        moving.wait_send()
    for slot in range(2):
        keep_start(blocks - 2 + slot, slot).wait()
        keep_gate(width // chunk - 2 + slot, slot).wait()
        cotangent_out_of(blocks - 2 + slot, slot).wait()
    for copy in saved:
        copy.wait()


def forward(size, rank, nstate, entry, few, tokens, out_grad, segments, out_proj):
    batches, length, model = tokens.shape
    total = COPIES * batches * length
    slab, width = entry.shape[0], size * LANES
    blocks = length // BLOCK
    anywhere = pl.BlockSpec(memory_space=pl.ANY)
    half = size // 2
    dma = pltpu.SemaphoreType.DMA
    shape = jax.ShapeDtypeStruct
    full, low = shape((total, width), F32), shape((total, width), BF16)
    thin = shape((total, LANES), BF16)
    rows = shape((total, model), BF16)
    weights = shape((size * slab, width), BF16)
    few_all = shape((few.shape[0], width), BF16)
    masks = shape((3, total, LANES), F32)
    state = shape((nstate, GROUP, width), F32)
    spread_by = shape((LANES, 2 * nstate * LANES), BF16)
    fold_by = shape((2 * nstate * LANES, LANES), BF16)
    outs = dict(
        few=few_all,
        masks=masks,
        rate=state,
        spread_by=spread_by,
        fold_by=fold_by,
        normed=rows,
        cotangent=rows,
        tokens_all=shape((GROUP, length, model), BF16),
        grads_all=shape((GROUP, length, model), BF16),
        segments_all=shape((COPIES,) + segments.shape, segments.dtype),
        inner_in=weights,
        inner=full,
        act=full,
        act_low=low,
        step_low=thin,
        coef=thin,
        step=full,
        starts=shape((blocks,) + state.shape, F32),
        gate=full,
        readout=full,
        gated=low,
        gated_natural=low,
        gate_in=weights,
        out_w=shape((size * out_proj.shape[0] // COPIES, model), BF16),
    )
    quarter = total // COPIES
    scratch = [
        few_all,
        shape((few.shape[0] - 2 * rank - 2 * nstate, width), F32),
        masks,
        state,
        spread_by,
        fold_by,
        rows,
        shape((2, GROUP, BLOCK, model), BF16),
        shape((2, BLOCK * GROUP, model), BF16),
        shape((model // LANES, BLOCK * GROUP, LANES), F32),
        shape((COPIES,) + segments.shape, segments.dtype),
        shape((slab, width), BF16),
        shape((slab, width), BF16),
        weights,
        shape((total + 3 * GROUP, width), F32),
        full,
        low,
        shape((2, total, LANES), F32),
        shape((2, total, LANES), F32),
        shape((2, 2, quarter, LANES), F32),
        shape((2, quarter, LANES), F32),
        shape((2, quarter, LANES), F32),
        shape((COPIES, 2, quarter, LANES), BF16),
        thin,
        thin,
        shape((BLOCK * GROUP, 2 * nstate * LANES), F32),
        shape((BLOCK * GROUP, width), F32),
        full,
        full,
        state,
        shape((2,) + state.shape, F32),
        shape((2, total, 256), F32),
        low,
        low,
        weights,
    ]
    sems = [(20,), (2,), (2,), (7,), (2 * size,), (2,), (2,), (1,)]
    sems += [(3, 2, half, 2)] * 2 + [(2, half)] * 2 + [(3, 3)] * 2 + [(6,)] * 2
    results = pl.pallas_call(
        functools.partial(forward_kernel, size, rank, nstate),
        in_specs=[anywhere] * 6,
        out_specs=[anywhere] * len(outs),
        out_shape=list(outs.values()),
        scratch_shapes=[pltpu.VMEM(x.shape, x.dtype) for x in scratch] + [dma(n) for n in sems],
        compiler_params=pltpu.CompilerParams(
            collective_id=4, has_side_effects=True, vmem_limit_bytes=62 * 1024 * 1024
        ),
        cost_estimate=cost(8 * total * width * model, 100 * total * width),
        name="forward",
    )(entry, few, tokens, out_grad, segments, out_proj)
    return dict(zip(outs, results))


class Guests:
    def __init__(self, size, parts, totals, held, sems):
        self.peers = Peers(size)
        self.parts, self.totals, self.held, self.sems = parts, totals, held, sems

    def rows(self, which, c):
        half = self.parts[which].shape[1] // 2
        return pl.ds(c * half, half)

    def copy(self, which, way, step, c, source=None):
        target = self.held[which].at[way, step - 1, self.rows(which, c), :]
        index = (which, way, step - 1, c)
        source = target if source is None else source
        return remote(source, target, self.sems, index, self.peers.ring[way])

    def chunks(self, way, step):
        return (way,) if step == 1 else (0, 1)

    def own(self, which, way, step, c):
        away = self.peers.half + 1 - step
        block = self.peers.at(away if way == 0 else -away)
        return self.parts[which].at[block, self.rows(which, c), :]

    def source(self, which, way, step, c):
        own = self.own(which, way, step, c)
        if step == 1 or c not in self.chunks(way, step - 1):
            return own
        self.copy(which, way, step - 1, c).wait_recv()
        there = self.held[which].at[way, step - 2, self.rows(which, c), :]
        there[...] = (own[...].astype(F32) + there[...].astype(F32)).astype(BF16)
        return there

    def tick(self, number):
        which, step = number % 2, number // 2 + 1
        for c in range(2):
            for way in range(2):
                if c in self.chunks(way, step):
                    self.copy(which, way, step, c, self.source(which, way, step, c)).start()

    def finish(self):
        last = self.peers.half
        for which in range(2):
            for c in range(2):
                total = self.own(which, 0, last + 1, c)[...].astype(F32)
                for way in range(2):
                    self.copy(which, way, last, c).wait_recv()
                    there = self.held[which].at[way, last - 1, self.rows(which, c), :]
                    total = total + there[...].astype(F32)
                self.totals[which][self.rows(which, c), :] = total.astype(BF16)
        for which in range(2):
            for step in range(1, last + 1):
                for way in range(2):
                    for c in self.chunks(way, step):
                        self.copy(which, way, step, c).wait_send()


def scan_back_kernel(
    nstate, chunk, rings, step_ref, act_ref, grad_ref, coef_ref, spread_ref, fold_ref, keep_ref, rate_ref,
    row_ref, start_ref, *refs,
):
    wide, states_all, decays, parts, sizes = refs[-5:]
    width = step_ref.shape[1]
    step_now = pl.program_id(0)
    if rings:
        first_ref, second_ref = refs[:2]
        pre_grad_ref, direct_ref, coef_grad_ref, carry_ref, sums_ref = refs[2:7]
        guest = Guests(rings, (first_ref, second_ref), refs[7:9], refs[9:11], refs[11:13])
        for tick in range(2 * guest.peers.half):

            @pl.when(step_now == tick)
            def _(tick=tick):
                if tick == 0:
                    guest.peers.meet()
                guest.tick(tick)

    else:
        pre_grad_ref, direct_ref, coef_grad_ref, carry_ref, sums_ref = refs[-10:-5]

    @pl.when(step_now == 0)
    def _():
        carry_ref[...] = jnp.zeros_like(carry_ref)
        sums_ref[...] = jnp.zeros_like(sums_ref)

    wide[...] = jnp.dot(coef_ref[...], spread_ref[...], preferred_element_type=F32)

    def fold(value):
        total = value[:, :LANES]
        for k in range(1, chunk // LANES):
            total = total + value[:, k * LANES : (k + 1) * LANES]
        return total

    for c in range(width // chunk):
        cols = slice(c * chunk, (c + 1) * chunk)

        def advance(t, states):
            at = at_time(t)
            step = step_ref[at, cols]
            drive = jnp.where(tiled(keep_ref[at, :], chunk) > 0.5, step, FAR)
            inflow = step * act_ref[at, cols]
            now = []
            for n in range(nstate):
                write = tiled(wide[at, n * LANES : (n + 1) * LANES], chunk)
                decay = jnp.exp2(drive * rate_ref[n, :, cols])
                decays[t, n] = decay
                states_all[t, n] = states[n]
                now.append(decay * states[n] + write * inflow)
            return tuple(now)

        start = tuple(start_ref[0, n, :, cols] for n in range(nstate))
        states = lax.fori_loop(0, BLOCK, advance, start, unroll=2)
        for n in range(nstate):
            states_all[BLOCK, n] = states[n]

        def retreat(i, carry):
            t = BLOCK - 1 - i
            at = at_time(t)
            step, act, grad = step_ref[at, cols], act_ref[at, cols], grad_ref[at, cols]
            inflow = step * act
            size = jnp.zeros_like(step)
            direct = jnp.zeros_like(step)
            now = []
            for n in range(nstate):
                tile_w = slice(n * LANES, (n + 1) * LANES)
                tile_r = slice((nstate + n) * LANES, (nstate + n + 1) * LANES)
                state_grad = tiled(wide[at, tile_r], chunk) * grad + carry[n]
                passed = decays[t, n] * state_grad
                through = passed * states_all[t, n]
                size = size + rate_ref[n, :, cols] * through
                direct = direct + state_grad * tiled(wide[at, tile_w], chunk)
                sums_ref[n, :, cols] += step * through
                write_part = fold(state_grad * inflow)
                read_part = fold(grad * states_all[t + 1, n])
                if c == 0:
                    parts[at, tile_w] = write_part
                    parts[at, tile_r] = read_part
                else:
                    parts[at, tile_w] += write_part
                    parts[at, tile_r] += read_part
                now.append(passed)
            sizes[at, cols] = LN2 * size + act * direct
            direct_ref[at, cols] = step * direct + row_ref[1:2, cols] * grad
            sums_ref[nstate, :, cols] += grad * act
            return tuple(now)

        start = tuple(carry_ref[n, :, cols] for n in range(nstate))
        carry = lax.fori_loop(0, BLOCK, retreat, start, unroll=2)
        for n in range(nstate):
            carry_ref[n, :, cols] = carry[n]

    step = step_ref[...]
    series = step * (1.0 - step * (0.5 - step * (1.0 / 6.0)))
    pre_grad = sizes[...] * jnp.where(step < 0.01, series, 1.0 - jnp.exp(-step))
    pre_grad_ref[...] = pre_grad.astype(BF16)
    total = pre_grad[:GROUP]
    for t in range(1, BLOCK):
        total = total + pre_grad[t * GROUP : (t + 1) * GROUP]
    sums_ref[nstate + 1] += total
    high = parts[...].astype(BF16)
    low = (parts[...] - high.astype(F32)).astype(BF16)
    coef_grad_ref[...] = jnp.dot(high, fold_ref[...], preferred_element_type=F32) + jnp.dot(
        low, fold_ref[...], preferred_element_type=F32
    )
    if rings:

        @pl.when(step_now == pl.num_programs(0) - 1)
        def _():
            guest.finish()


def scan_backward(
    step, act, grad, coef, spread_by, fold_by, keep, rate, rows, starts, rings, wgrads
):
    total, width = step.shape
    nstate = rate.shape[0]
    size = BLOCK * GROUP
    chunk = 256
    count = total // size
    tile = pl.BlockSpec((size, width), lambda t: (count - 1 - t, 0))
    thin = pl.BlockSpec((size, LANES), lambda t: (count - 1 - t, 0))
    state = pl.BlockSpec((nstate, GROUP, width), lambda t: (0, 0, 0))
    tally = pl.BlockSpec((nstate + 2, GROUP, width), lambda t: (0, 0, 0))
    work = count * size * width * nstate
    inside = pl.BlockSpec(memory_space=pltpu.VMEM)
    half = rings // 2
    guests = [jax.ShapeDtypeStruct(w.shape[1:], BF16) for w in wgrads]
    sems = [pltpu.SemaphoreType.DMA((2, 2, half, 2))] * 2 if rings else []
    return pl.pallas_call(
        functools.partial(scan_back_kernel, nstate, chunk, rings),
        grid=(count,),
        in_specs=[
            tile,
            tile,
            tile,
            thin,
            pl.BlockSpec(spread_by.shape, lambda t: (0, 0)),
            pl.BlockSpec(fold_by.shape, lambda t: (0, 0)),
            thin,
            state,
            pl.BlockSpec((8, width), lambda t: (0, 0)),
            pl.BlockSpec((1, nstate, GROUP, width), lambda t: (count - 1 - t, 0, 0, 0)),
        ]
        + [inside] * len(wgrads),
        out_specs=[tile, tile, thin, state, tally] + [inside] * len(wgrads),
        out_shape=[
            jax.ShapeDtypeStruct((total, width), BF16),
            jax.ShapeDtypeStruct((total, width), F32),
            jax.ShapeDtypeStruct((total, LANES), F32),
            jax.ShapeDtypeStruct((nstate, GROUP, width), F32),
            jax.ShapeDtypeStruct((nstate + 2, GROUP, width), F32),
        ]
        + guests,
        scratch_shapes=[pltpu.VMEM((2, half) + w.shape[1:], BF16) for w in wgrads]
        + sems
        + [
            pltpu.VMEM((size, 2 * nstate * LANES), F32),
            pltpu.VMEM((BLOCK + 1, nstate, GROUP, chunk), F32),
            pltpu.VMEM((BLOCK, nstate, GROUP, chunk), F32),
            pltpu.VMEM((size, 2 * nstate * LANES), F32),
            pltpu.VMEM((size, width), F32),
        ],
        compiler_params=pltpu.CompilerParams(
            collective_id=3, has_side_effects=True, vmem_limit_bytes=VMEM_LIMIT
        )
        if rings
        else params(),
        cost_estimate=cost(40 * work, 24 * count * size * width),
        name="scan_backward",
    )(step, act, grad, coef, spread_by, fold_by, keep, rate, rows, starts, *wgrads)


def finish_kernel(
    size, rank, nstate,
    pre_low_in, coef_in, direct_in, inner_in, act_low_in, step_low_in, masks_in, few_in, normed_in, w_inner, w_gate,
    gate_grad_in, gated_in, w_out, sums_in, out_total, gate_total,
    inner_pieces, gate_pieces, out_pieces, small_pieces, out_sum, norm_sum,
    pre_low, part, nat, got_near, to_across, got_across, shared, low_grad, act_low, step_low, masks, few, normed, gate_grad,
    gated, inner, direct, grad, wgrad, held, small, small_low, small_held, out_w, out_parts,
    out_pair, norm_pair, out_far, norm_far, w_tiles, total_at, sums,
    load_sems, tile_sems, w_sems, near_send, near_recv, pair_send, pair_recv, ring_send, ring_recv, few_send, few_recv,
    piece_send, piece_recv, own_sems,
):
    peers = Peers(size)
    half = peers.half
    total, width = pre_low.shape
    model = normed.shape[1]
    length = total // GROUP
    batches = GROUP // COPIES
    quarter = total // COPIES
    chunk, rows, pad = 256, 64, 3 * GROUP
    tiles = width // chunk
    slab = held.shape[2]
    sent, loads = [], {}

    def load(name, source, target):
        loads[name] = pltpu.make_async_copy(source, target, load_sems.at[len(loads)])
        loads[name].start()

    def send(*copy):
        moving = remote(*copy)
        moving.start()
        sent.append(moving)

    def tile_copies(c, slot):
        cols = slice(c * chunk, (c + 1) * chunk)
        return [
            pltpu.make_async_copy(inner_in.at[:, cols], inner.at[slot, pl.ds(pad, total), :], tile_sems.at[0, slot]),
            pltpu.make_async_copy(direct_in.at[:, cols], direct.at[slot], tile_sems.at[1, slot]),
        ]

    load("pre", pre_low_in, pre_low)
    load("few", few_in, few)
    load("coef", coef_in, part.at[1])
    load("step", step_low_in, step_low)
    load("gated", gated_in, gated)
    load("out_w", w_out, out_w)
    load("act", act_low_in, act_low)
    load("masks", masks_in, masks.at[:, pl.ds(0, total), :])
    load("normed", normed_in, normed)
    load("sums", sums_in, sums)
    load("gate", gate_grad_in, gate_grad)
    for copy in tile_copies(0, 0):
        copy.start()
    peers.meet()

    near = (near_send, near_recv)

    def come(target, index, peer):
        remote(target, target, near, index, peer).wait_recv()

    first_stride = rank + 2 * nstate
    loads["pre"].wait()
    loads["few"].wait()
    part[0] = lax.dot_general(
        pre_low[...], few[first_stride : first_stride + rank, :], (((1,), (1,)), ((), ())),
        preferred_element_type=F32,
    )
    loads["coef"].wait()
    for j in range(2):
        for s in range(GROUP):
            nat[j, s * length : (s + 1) * length, :] = part[j, pl.ds(s, length, stride=GROUP), :]
    for i in range(2):
        send(nat.at[:, pl.ds((2 * i + 1) * quarter, quarter), :], got_near.at[i], near, i, peers.core)
    near_sends = list(sent)
    loads["step"].wait()
    small[first_stride : first_stride + rank, :] = lax.dot_general(
        step_low[...], pre_low[...], (((0,), (0,)), ((), ())), preferred_element_type=F32
    )
    for i in range(2):
        come(got_near.at[i], i, peers.core)
    to_across[...] = nat[:, 2 * quarter : 3 * quarter, :] + got_near[1]
    send(to_across, got_across, near, 2, peers.across)
    loads["gated"].wait()
    loads["out_w"].wait()

    def out_tiles(first, count):
        @pl.loop(first, first + count)
        def _(c):
            cols = pl.ds(pl.multiple_of(c * chunk, chunk), chunk)
            out_parts[:, cols] = jnp.dot(gated[...], out_w[:, cols], preferred_element_type=F32).astype(BF16)

    out_tiles(0, model // chunk // 2)
    come(got_across, 2, peers.across)
    mine = nat[:, :quarter, :] + got_near[0] + got_across[...]
    for j in range(2):
        shared[0, j] = mine[j].astype(BF16)
    send(shared.at[0], shared.at[2], near, 3, peers.across)
    send(shared.at[0], shared.at[1], near, 4, peers.core)
    out_tiles(model // chunk // 2, model // chunk // 2)
    come(shared.at[2], 3, peers.across)
    send(shared.at[2], shared.at[3], near, 5, peers.core)
    come(shared.at[1], 4, peers.core)
    come(shared.at[3], 5, peers.core)
    for copy in near_sends:
        copy.wait_send()
    for k in range(COPIES):
        for b in range(batches):
            for j in range(2):
                part[j, pl.ds(k * batches + b, length, stride=GROUP), :] = shared[
                    k, j, b * length : (b + 1) * length, :
                ].astype(F32)
    for j in range(2):
        low_grad[j] = part[j].astype(BF16)

    pair_sems, piece_sems = (pair_send, pair_recv), (piece_send, piece_recv)
    keeps = []

    def of_copy(ref, k):
        return ref.at[pl.ds(k * quarter, quarter), :]

    def exchange(index, parts, pair):
        for i in range(2):
            send(of_copy(parts, 2 * i + 1), pair.at[i], pair_sems, 3 * index + i, peers.core)

    def exchange_far(index, parts, pair, far):
        for i in range(2):
            remote(pair.at[i], pair.at[i], pair_sems, 3 * index + i, peers.core).wait_recv()
        there = of_copy(parts, 2)
        there[...] = (there[...].astype(F32) + pair[1].astype(F32)).astype(BF16)
        send(there, far, pair_sems, 3 * index + 2, peers.across)

    def exchanged(index, parts, pair, far):
        remote(far, far, pair_sems, 3 * index + 2, peers.across).wait_recv()
        return of_copy(parts, 0)[...].astype(F32) + pair[0].astype(F32) + far[...].astype(F32)

    def give(index, own, pieces):
        keeps.append(pltpu.make_async_copy(own, pieces[0], own_sems.at[index]))
        keeps[-1].start()
        send(own, pieces[2], piece_sems, (index, 0), peers.across)
        send(own, pieces[1], piece_sems, (index, 1), peers.core)

    def pass_on(index, pieces):
        remote(pieces[2], pieces[2], piece_sems, (index, 0), peers.across).wait_recv()
        send(pieces[2], pieces[3], piece_sems, (index, 2), peers.core)

    def given(index, pieces):
        for k, which in ((1, 1), (3, 2)):
            remote(pieces[k], pieces[k], piece_sems, (index, which), peers.core).wait_recv()

    def every(ref, *at):
        return [ref.at[(k, *at)] for k in range(COPIES)]

    exchange(0, out_parts, out_pair)
    give(0, out_total, every(out_pieces))
    give(1, gate_total, every(gate_pieces))

    loads["act"].wait()
    for j, n in ((0, rank), (1, 2 * nstate)):
        weights = lax.dot_general(
            low_grad[j], act_low[...], (((0,), (0,)), ((), ())), preferred_element_type=F32
        )
        small[j * rank : j * rank + n, :] = weights[:n]

    inner_grad, natural = gated, pre_low
    loads["masks"].wait()
    loads["normed"].wait()
    masks[:, total:, :] = jnp.zeros((3, pad, LANES), F32)
    grad[total:, :] = jnp.zeros((pad, chunk), F32)
    for slot in range(2):
        inner[slot, :pad, :] = jnp.zeros((pad, chunk), F32)
    first_tap = first_stride + rank
    ring_sems, few_sems = (ring_send, ring_recv), (few_send, few_recv)

    def block_rows(member, part_of=None):
        start = pl.multiple_of(member * slab, slab)
        if part_of is None:
            return pl.ds(start, slab)
        return pl.ds(start + part_of * (slab // 2), slab // 2)

    def owner(way, step):
        away = half + 1 - step
        return peers.at(away if way == 0 else -away)

    def landing(way, step, c):
        there = held.at[way, step - 1, :, slice(c * chunk, (c + 1) * chunk)]
        return there.at[pl.ds(way * (slab // 2), slab // 2), :] if step == 1 else there

    def arrive(way, step, c):
        there = landing(way, step, c)
        remote(there, there, ring_sems, (way, step - 1, c), peers.ring[way]).wait_recv()

    def ring_step(step, c):
        cols = slice(c * chunk, (c + 1) * chunk)
        for way in range(2):
            member = owner(way, step)
            if step == 1:
                source = wgrad.at[block_rows(member, way), cols]
            else:
                arrive(way, step - 1, c)
                source = held.at[way, step - 2, :, cols]
                if step == 2:
                    here, other = (slice(w * (slab // 2), (w + 1) * (slab // 2)) for w in (way, 1 - way))
                    source[other, :] = wgrad[block_rows(member, 1 - way), cols]
                    source[here, :] = (
                        source[here, :].astype(F32) + wgrad[block_rows(member, way), cols].astype(F32)
                    ).astype(BF16)
                else:
                    source[...] = (
                        source[...].astype(F32) + wgrad[block_rows(member), cols].astype(F32)
                    ).astype(BF16)
            send(source, landing(way, step, c), ring_sems, (way, step - 1, c), peers.ring[way])

    def fold_rows(value):
        out = value[:GROUP]
        for i in range(1, rows // GROUP):
            out = out + value[i * GROUP : (i + 1) * GROUP]
        return out

    for c in range(tiles):
        cols, slot = slice(c * chunk, (c + 1) * chunk), c % 2
        if c + 1 < tiles:
            for copy in tile_copies(c + 1, 1 - slot):
                copy.start()
        for copy in tile_copies(c, slot):
            copy.wait()
        here, there = inner.at[slot], direct.at[slot]
        there[...] += jnp.dot(low_grad[0], few[:rank, cols], preferred_element_type=F32) + jnp.dot(
            low_grad[1], few[rank : rank + LANES, cols], preferred_element_type=F32
        )
        tap = [few[first_tap : first_tap + 16, cols].astype(F32)[i : i + 1] for i in range(5)]

        def back(i, tallies):
            start = pl.multiple_of(i * rows, rows)
            at = pl.ds(start, rows)
            now = here[pl.ds(pad + start, rows), :]
            earlier = [
                here[pl.ds(pad - shift * GROUP + start, rows), :] * tiled(masks[shift - 1, at, :], chunk)
                for shift in range(1, 4)
            ]
            value = tap[4] + tap[3] * now
            for shift in range(1, 4):
                value = value + tap[3 - shift] * earlier[shift - 1]
            sig = sigmoid(value)
            flow = there[at, :] * (sig * (1.0 + value * (1.0 - sig)))
            grad[at, :] = flow
            terms = [flow * e for e in earlier[::-1]] + [flow * now, flow]
            return tuple(tally + fold_rows(term) for tally, term in zip(tallies, terms))

        zero = jnp.zeros((GROUP, chunk), F32)
        tallies = lax.fori_loop(0, total // rows, back, (zero,) * 5)
        for i, tally in enumerate(tallies):
            small[first_tap + i : first_tap + i + 1, cols] = jnp.sum(tally, axis=0, keepdims=True)

        @pl.loop(0, total // rows)
        def _(i):
            start = pl.multiple_of(i * rows, rows)
            at = pl.ds(start, rows)
            value = tap[3] * grad[at, :]
            for shift in range(1, 4):
                after_it = pl.ds(start + shift * GROUP, rows)
                value = value + tap[3 - shift] * (
                    grad[after_it, :] * tiled(masks[shift - 1, after_it, :], chunk)
                )
            inner_grad[at, cols] = value.astype(BF16)
            for k in range(chunk // LANES):
                nat[k, at, :] = value[:, k * LANES : (k + 1) * LANES]

        for k in range(chunk // LANES):
            lanes = slice(c * chunk + k * LANES, c * chunk + (k + 1) * LANES)
            for s in range(GROUP):
                natural[s * length : (s + 1) * length, lanes] = nat[
                    k, pl.ds(s, length, stride=GROUP), :
                ].astype(BF16)
        wgrad[:, cols] = lax.dot_general(
            normed[...], inner_grad[:, cols], (((0,), (0,)), ((), ())), preferred_element_type=F32
        ).astype(BF16)
        ring_step(1, c)
        if c == 1:
            exchange_far(0, out_parts, out_pair, out_far)
        if c >= 2:
            ring_step(2, c - 2)

    loads["sums"].wait()
    at = first_tap + 5
    small[at : at + 1, :] = jnp.sum(sums[nstate + 1], axis=0, keepdims=True)
    decays = few[first_tap : first_tap + 32, :].astype(F32)
    for n in range(nstate):
        small[at + 1 + n : at + 2 + n, :] = -jnp.exp(decays[6 + n : 7 + n]) * jnp.sum(
            sums[n], axis=0, keepdims=True
        )
    at = at + 1 + nstate
    small[at : at + 1, :] = jnp.sum(sums[nstate], axis=0, keepdims=True)
    small[at + 1 :, :] = jnp.zeros((small.shape[0] - at - 1, width), F32)
    small_low[...] = small[...].astype(BF16)
    few_half = small.shape[0] // 2

    def few_columns(member):
        return pl.ds(pl.multiple_of(member * LANES, LANES), LANES)

    def few_landing(way, step):
        there = small_held.at[way, step - 1]
        return there.at[pl.ds(way * few_half, few_half), :] if step == 1 else there

    def few_arrive(way, step):
        there = few_landing(way, step)
        remote(there, there, few_sems, (way, step - 1), peers.ring[way]).wait_recv()

    def few_step(step):
        for way in range(2):
            columns = few_columns(owner(way, step))
            here, other = (slice(w * few_half, (w + 1) * few_half) for w in (way, 1 - way))
            if step == 1:
                source = small_low.at[pl.ds(way * few_half, few_half), columns]
            else:
                few_arrive(way, step - 1)
                source = small_held.at[way, step - 2]
                if step == 2:
                    source[other, :] = small_low[other, columns]
                    source[here, :] = (
                        source[here, :].astype(F32) + small_low[here, columns].astype(F32)
                    ).astype(BF16)
                else:
                    source[...] = (source[...].astype(F32) + small_low[:, columns].astype(F32)).astype(BF16)
            send(source, few_landing(way, step), few_sems, (way, step - 1), peers.ring[way])

    loads["gate"].wait()
    norm_parts = out_w

    def w_copies(n, slot):
        these = pl.ds(pl.multiple_of(n * chunk, chunk), chunk)
        return [
            pltpu.make_async_copy(w.at[these, :], w_tiles.at[slot, i], w_sems.at[i, slot])
            for i, w in enumerate((w_inner, w_gate))
        ]

    w_count = model // chunk

    def norm_tiles(first, count):
        @pl.loop(first, first + count)
        def _(n):
            slot = lax.rem(n, 2)

            @pl.when(n + 1 < w_count)
            def _():
                for copy in w_copies(n + 1, 1 - slot):
                    copy.start()

            for copy in w_copies(n, slot):
                copy.wait()
            nt = (((1,), (1,)), ((), ()))
            value = lax.dot_general(natural[...], w_tiles[slot, 0], nt, preferred_element_type=F32)
            value += lax.dot_general(gate_grad[...], w_tiles[slot, 1], nt, preferred_element_type=F32)
            norm_parts[:, pl.ds(pl.multiple_of(n * chunk, chunk), chunk)] = value.astype(BF16)

    few_step(1)
    for copy in w_copies(0, 0):
        copy.start()
    for i in range(2):
        norm_tiles(i, 1)
        ring_step(2, 2 + i)
    few_step(2)
    for i in range(4):
        norm_tiles(2 + i, 1)
        ring_step(3, i)
    few_step(3)
    norm_tiles(6, w_count - 6)
    exchange(1, norm_parts, norm_pair)
    ring_step(4, 0)
    ring_step(4, 1)
    exchange_far(1, norm_parts, norm_pair, norm_far)
    ring_step(4, 2)
    ring_step(4, 3)
    few_step(4)
    for index, pieces in ((0, out_pieces), (1, gate_pieces)):
        pass_on(index, every(pieces))
    out_sum[...] = exchanged(0, out_parts, out_pair, out_far)

    def cols_of(c):
        return slice(c * chunk, (c + 1) * chunk)

    def inner_views(c):
        return [inner_pieces.at[k, :, cols_of(c)] for k in range(COPIES)]

    own_block = block_rows(peers.member)
    for c in range(tiles):
        for way in range(2):
            arrive(way, half, c)
        value = wgrad[own_block, cols_of(c)].astype(F32)
        for way in range(2):
            value = value + held[way, half - 1, :, cols_of(c)].astype(F32)
        total_at[:, cols_of(c)] = value.astype(BF16)
        give(3 + c, total_at.at[:, cols_of(c)], inner_views(c))
    for way in range(2):
        few_arrive(way, half)
    value = small_low[:, few_columns(peers.member)].astype(F32)
    for way in range(2):
        value = value + small_held[way, half - 1].astype(F32)
    small_total = small_pieces.at[0]
    small_total[...] = value.astype(BF16)
    send(small_total, small_pieces.at[2], piece_sems, (2, 0), peers.across)
    send(small_total, small_pieces.at[1], piece_sems, (2, 1), peers.core)
    norm_sum[...] = exchanged(1, norm_parts, norm_pair, norm_far)
    for c in range(tiles):
        pass_on(3 + c, inner_views(c))
    pass_on(2, every(small_pieces))
    for index, pieces in ((0, every(out_pieces)), (1, every(gate_pieces)), (2, every(small_pieces))):
        given(index, pieces)
    for c in range(tiles):
        given(3 + c, inner_views(c))
    for copy in keeps:
        copy.wait()
    for moving in sent[len(near_sends) :]:
        moving.wait_send()


def finish(size, rank, nstate, arrays, small_rows):
    (pre_low, coef, direct, inner, act_low, step_low, masks, few, normed) = arrays[:9]
    total, width = pre_low.shape
    model = normed.shape[1]
    out_total, gate_total = arrays[-2:]
    slab = gate_total.shape[0]
    quarter, half = total // COPIES, size // 2
    inside, anywhere = pl.BlockSpec(memory_space=pltpu.VMEM), pl.BlockSpec(memory_space=pl.ANY)
    shape, dma = jax.ShapeDtypeStruct, pltpu.SemaphoreType.DMA
    low = shape((total, width), BF16)
    wide = shape((total, model), BF16)
    pair = shape((2, quarter, model), BF16)
    far = shape((quarter, model), BF16)
    sums = arrays[-3]
    padded = total + 3 * GROUP
    scratch = [
        low,
        shape((2, total, LANES), F32),
        shape((2, total, LANES), F32),
        shape((2, 2, quarter, LANES), F32),
        shape((2, quarter, LANES), F32),
        shape((2, quarter, LANES), F32),
        shape((COPIES, 2, quarter, LANES), BF16),
        shape((2, total, LANES), BF16),
        low,
        shape(step_low.shape, BF16),
        shape((3, padded, LANES), F32),
        shape(few.shape, BF16),
        wide,
        low,
        low,
        shape((2, padded, 256), F32),
        shape((2, total, 256), F32),
        shape((padded, 256), F32),
        shape((size * slab, width), BF16),
        shape((2, half, slab, width), BF16),
        shape((small_rows, width), F32),
        shape((small_rows, width), BF16),
        shape((2, half, small_rows, LANES), BF16),
        shape((max(width, total), model), BF16),
        wide,
        pair,
        pair,
        far,
        far,
        shape((2, 2, 256, width), BF16),
        shape((slab, width), BF16),
        shape(sums.shape, F32),
    ]
    tiles = width // 256
    sems = [(11,), (2, 2), (2, 2)] + [(6,)] * 2 + [(6,)] * 2 + [(2, half, tiles)] * 2 + [(2, half)] * 2
    sems += [(3 + tiles, 3)] * 2 + [(3 + tiles,)]
    return pl.pallas_call(
        functools.partial(finish_kernel, size, rank, nstate),
        in_specs=[anywhere] * len(arrays),
        out_specs=[anywhere] * 3 + [inside] * 3,
        out_shape=[
            shape((COPIES, slab, width), BF16),
            shape((COPIES, slab, width), BF16),
            shape((COPIES,) + out_total.shape, BF16),
            shape((COPIES, small_rows, LANES), BF16),
            shape((quarter, model), F32),
            shape((quarter, model), F32),
        ],
        scratch_shapes=[pltpu.VMEM(x.shape, x.dtype) for x in scratch] + [dma(n) for n in sems],
        compiler_params=pltpu.CompilerParams(
            collective_id=2, has_side_effects=True, vmem_limit_bytes=62 * 1024 * 1024
        ),
        cost_estimate=cost(10 * total * width * model, 100 * total * width),
        name="finish",
    )(*arrays)


def spread_columns_kernel(copy_ref, *refs):
    pieces, weight_ref, out_ref, gain_ref = refs[:4], refs[4], refs[-2], refs[-1]
    part = pieces[0].shape[1]

    @pl.when(pl.program_id(0) == 0)
    def _():
        gain_ref[...] = jnp.zeros_like(gain_ref)

    total = gain_ref[...]
    for k, piece in enumerate(pieces):
        at = pl.ds(pl.multiple_of((copy_ref[0] ^ k) * part, part), part)
        value = piece[...].astype(F32)
        out_ref[:, at] = value
        total = total + value * weight_ref[:, at].astype(F32)
    gain_ref[...] = total


def spread_columns(copy, pieces, weight, side, before=None):
    rows, width = pieces[0].shape
    part = LANES
    shares = width // part
    block = pl.BlockSpec((rows, COPIES * part), lambda f, copy: (0, side * shares + f))
    piece = pl.BlockSpec((rows, part), lambda f, copy: (0, f))
    extra = [] if before is None else [before]
    return pl.pallas_call(
        spread_columns_kernel,
        grid_spec=pltpu.PrefetchScalarGridSpec(
            num_scalar_prefetch=1,
            grid=(shares,),
            in_specs=[piece] * 4 + [block] + [pl.BlockSpec(memory_space=pl.ANY)] * len(extra),
            out_specs=[block, pl.BlockSpec((rows, part), lambda f, copy: (0, 0))],
        ),
        out_shape=[
            jax.ShapeDtypeStruct(weight.shape, F32),
            jax.ShapeDtypeStruct((rows, part), F32),
        ],
        input_output_aliases={6: 0} if extra else {},
        compiler_params=params(),
        cost_estimate=cost(4 * rows * width, 20 * rows * width),
        name="spread_columns",
    )(copy, *pieces, weight, *extra)


def spread_rows_kernel(copy_ref, *refs):
    pieces, out_ref = refs[:4], refs[4]
    part = pieces[0].shape[0]
    for k, piece in enumerate(pieces):
        at = pl.ds(pl.multiple_of((copy_ref[0] ^ k) * part, part), part)
        out_ref[at, :] = piece[...].astype(F32)


def spread_rows(copy, pieces):
    part, columns = pieces[0].shape
    tile = 512
    return pl.pallas_call(
        spread_rows_kernel,
        grid_spec=pltpu.PrefetchScalarGridSpec(
            num_scalar_prefetch=1,
            grid=(columns // tile,),
            in_specs=[pl.BlockSpec((part, tile), lambda c, copy: (0, c))] * 4,
            out_specs=pl.BlockSpec((COPIES * part, tile), lambda c, copy: (0, c)),
        ),
        out_shape=jax.ShapeDtypeStruct((COPIES * part, columns), F32),
        compiler_params=params(),
        cost_estimate=cost(4 * part * columns, 24 * part * columns),
        name="spread_rows",
    )(copy, *pieces)


def on_device(
    tokens, segment_ids, out_grad, norm_gain, in_proj, conv_weight, conv_bias, x_proj,
    step_proj, step_bias, decay_log, skip_gain, out_proj, *, fsdp,
):
    ring = Ring(fsdp)
    copy = lax.axis_index("rep")
    batches, length, model = tokens.shape
    total = COPIES * batches * length
    slab = in_proj.shape[0]
    share = out_proj.shape[0]
    part = share // COPIES
    width = fsdp * part
    rank, nstate = step_proj.shape[1], decay_log.shape[1]
    taps_n = conv_weight.shape[1]
    gains_n = slab // part

    def mine(value):
        return lax.dynamic_slice_in_dim(value, copy * part, part, 0)

    copy_index = copy.astype(jnp.int32).reshape(1)
    aligned = part % LANES == 0
    if not aligned:
        entry = lax.dynamic_index_in_dim(
            in_proj.reshape(slab, 2, fsdp, COPIES, part), copy, 3, keepdims=False
        )
        inner_shard, gate_shard = (entry[:, i].reshape(slab, width) for i in range(2))
    few = jnp.concatenate(
        [
            mine(x_proj).T,
            mine(step_proj).T,
            mine(conv_weight).T,
            mine(conv_bias)[None],
            mine(step_bias)[None],
            mine(decay_log).T,
            mine(skip_gain)[None],
            norm_gain.reshape(gains_n, part),
        ],
        axis=0,
    )
    few = jnp.pad(few, ((0, -few.shape[0] % 16), (0, 0)))
    small_ring = ring.half == 4
    own = [tokens, out_grad, segment_ids[:, 0, :]]
    fused = small_ring and aligned
    if fused:
        out = forward(fsdp, rank, nstate, in_proj, few, *own, out_proj)
        few_all = out["few"].astype(F32)
    else:
        gathers = [Gather(ring, inner_shard), Gather(ring, few)]
        for gather in gathers:
            gather.rest()
        inner_in, few_all = (gather.whole for gather in gathers)
        few_all = jnp.moveaxis(few_all, 0, 1).reshape(-1, width).astype(F32)
        copies = [jnp.stack(rep_gather(value)) for value in own]
        inner_in = inner_in.reshape(model, width)
        values, cotangent, segments = (c.reshape((GROUP,) + c.shape[2:]) for c in copies)

    sizes = [rank + 2 * nstate, rank, taps_n, 1, 1, nstate, 1, gains_n]
    pieces, start = [], 0
    for size in sizes:
        pieces.append(few_all[start : start + size])
        start += size
    select, stride, taps, shift_bias, size_bias, decay, skip, gain = pieces
    select, stride = select.astype(BF16), stride.astype(BF16)
    gain = jnp.moveaxis(gain.reshape(gains_n, fsdp, part), 0, 1).reshape(model)

    def masks_of(segments):
        masks = []
        for shift in range(1, taps_n):
            earlier = jnp.pad(segments, ((0, 0), (shift, 0)), constant_values=-1)[:, :length]
            masks.append((earlier == segments).astype(F32).T.reshape(total, 1))
        return jnp.broadcast_to(jnp.stack(masks), (taps_n - 1, total, LANES))

    tap_rows = jnp.concatenate([taps, shift_bias, jnp.zeros((7 - taps_n, width), F32)])
    side_rows = jnp.concatenate([size_bias, skip, jnp.zeros((6, width), F32)])
    decay_rate = -jnp.exp(decay)

    if fused:
        (
            masks, rate, spread_by, fold_by, normed, cotangent, inner_in, inner, act, act_low, step_low, coef, step,
            starts, gate, readout, gated, gated_natural, gate_in, out_w,
        ) = (
            out[k]
            for k in (
                "masks", "rate", "spread_by", "fold_by", "normed", "cotangent", "inner_in", "inner", "act", "act_low",
                "step_low", "coef", "step", "starts", "gate", "readout", "gated", "gated_natural", "gate_in", "out_w",
            )
        )
    else:
        rate = jnp.broadcast_to((decay_rate * LOG2E)[:, None, :], (nstate, GROUP, width))
        masks, spread_by, fold_by = masks_of(segments), spreader(nstate), folder(nstate)
        normed, cotangent = interleave(values, gain), interleave(cotangent)
        gathers = [Gather(ring, gate_shard), Gather(ring, mine(out_proj))]
        for gather in gathers:
            gather.rest()
        gate_in = gathers[0].whole.reshape(model, width)
        out_w = gathers[1].whole.reshape(width, model)
        inner = dot(normed, inner_in, 1, 0)
        act, act_low = conv_forward(inner, masks, tap_rows)
        half_sums = sum_near(by_copy(to_sequence(dot(act_low, select, 1, 1))))
        projected = to_time(sum_far(half_sums).reshape(total, -1))
        step_low = projected[:, :rank].astype(BF16)
        coef = spread(projected[:, rank:], nstate)
        pre = dot(step_low, stride, 1, 0)
        readout, step, starts = scan_forward(pre, act, coef, spread_by, masks[0], rate, side_rows)
        gate = dot(normed, gate_in, 1, 0)
        gated, gated_natural = gate_forward(readout, gate)
    keep = masks[0]
    out_wgrad = dot(gated, cotangent, 0, 0).astype(BF16).reshape(fsdp, part, model)

    def r1():
        return gate_backward(dot(cotangent, out_w, 1, 1), readout, gate)

    read_grad, gate_grad, gate_grad_natural = r1()

    gate_wgrad = dot(normed, gate_grad, 0, 0).astype(BF16).reshape(fsdp, slab, width)
    wgrads = [out_wgrad, gate_wgrad] if fused else []
    pre_low, direct, coef_part, _, sums, *totals = scan_backward(
        step, act, read_grad, coef, spread_by, fold_by, keep, rate, side_rows, starts,
        fsdp if fused else 0, wgrads,
    )
    if not fused:
        scatters = [Scatter(ring, out_wgrad), Scatter(ring, gate_wgrad)]
        for scatter in scatters:
            scatter.rest()
        totals = [scatter.total.astype(BF16) for scatter in scatters]
    small_rows = few.shape[0]
    if fused:
        inner_pieces, gate_pieces, out_pieces, small_pieces, out_sum, normed_sum = finish(
            fsdp, rank, nstate,
            (
                pre_low, coef_part, direct, inner, act_low, step_low, masks, out["few"], normed, inner_in, gate_in,
                gate_grad_natural, gated_natural, out_w, sums, *totals,
            ),
            small_rows,
        )
        inner_pieces, gate_pieces, out_pieces, small_pieces = (
            [value[k] for k in range(COPIES)]
            for value in (inner_pieces, gate_pieces, out_pieces, small_pieces)
        )
    else:
        low_part = dot(pre_low, stride, 1, 1)
        proj_part = jnp.concatenate([low_part, coef_part[:, : 2 * nstate]], axis=1)
        half_sums = sum_near(by_copy(to_sequence(proj_part)))
        proj_time = to_time(sum_far(half_sums).reshape(total, -1).astype(BF16))
        act_grad = direct + dot(proj_time, select, 1, 0)
        inner_grad, inner_grad_natural, conv_sums = conv_backward(inner, act_grad, masks, tap_rows)
        inner_wgrad = dot(normed, inner_grad, 0, 0).astype(BF16).reshape(fsdp, slab, width)
        small = jnp.concatenate(
            [
                dot(proj_time, act_low, 0, 0),
                dot(step_low, pre_low, 0, 0),
                conv_sums[: taps_n + 1],
                jnp.sum(sums[nstate + 1 :], axis=1),
                decay_rate * jnp.sum(sums[:nstate], axis=1),
                jnp.sum(sums[nstate : nstate + 1], axis=1),
            ],
            axis=0,
        )
        small = jnp.pad(small, ((0, small_rows - small.shape[0]), (0, 0))).astype(BF16)
        small = jnp.moveaxis(small.reshape(-1, fsdp, part), 1, 0)
        grads = dot(inner_grad_natural, inner_in, 1, 1) + dot(gate_grad_natural, gate_in, 1, 1)
        sums_of = []
        for parts in (dot(gated_natural, out_w, 1, 0), grads):
            sums_of.append(rep_scatter_far(*rep_scatter_near(by_copy(parts.astype(BF16)))))
        out_sum, normed_sum = sums_of
        scatters = [Scatter(ring, inner_wgrad), Scatter(ring, small)]
        for scatter in scatters:
            scatter.rest()
        totals = [scatter.total.astype(BF16) for scatter in scatters] + totals
        inner_pieces, small_pieces, out_pieces, gate_pieces = (rep_gather(t) for t in totals)

    block_out = (tokens.astype(F32) + out_sum.reshape(tokens.shape)).astype(BF16)
    normed_grad = normed_sum.reshape(tokens.shape)
    own_values = tokens.astype(F32)
    own_scale = lax.rsqrt(jnp.mean(own_values * own_values, axis=-1, keepdims=True) + EPS)
    scaled = normed_grad * gain
    lean = jnp.mean(scaled * own_values, axis=-1, keepdims=True)
    input_grad = (
        out_grad.astype(F32) + own_scale * scaled - own_values * (own_scale**3) * lean
    ).astype(BF16)

    order = jnp.arange(COPIES) ^ copy
    if aligned:
        out_all = spread_rows(copy_index, out_pieces)
        entry_half, gain_gate = spread_columns(copy_index, gate_pieces, in_proj, 1)
        entry_all, gain_inner = spread_columns(copy_index, inner_pieces, in_proj, 0, entry_half)
        gain_sum = jnp.sum(gain_inner + gain_gate, axis=1)
    else:
        out_all = jnp.stack(out_pieces)[order].reshape(share, model).astype(F32)
        halves = jnp.stack([jnp.stack(inner_pieces), jnp.stack(gate_pieces)])[:, order]
        halves = halves.reshape(2, COPIES, slab, fsdp, part).astype(F32)
        entry_all = jnp.transpose(halves, (2, 0, 3, 1, 4)).reshape(slab, -1)
        gain_sum = jnp.sum(entry_all * in_proj.astype(F32), axis=1)
    gain_grad = gain_sum / norm_gain.astype(F32)
    small_all = jnp.stack(small_pieces)[order].astype(F32)
    small_all = jnp.moveaxis(small_all, 0, 1).reshape(-1, share)
    out, start = [], 0
    for size in sizes[:-1]:
        out.append(small_all[start : start + size])
        start += size
    select_g, stride_g, taps_g, shift_g, size_g, decay_g, skip_g = out
    return (
        block_out,
        input_grad,
        gain_grad,
        entry_all,
        taps_g.T,
        shift_g[0],
        select_g.T,
        stride_g.T,
        size_g[0],
        decay_g.T,
        skip_g[0],
        out_all,
    )


def solution(mesh):
    tokens = P(None, ("fsdp", "rep"), None)
    rows, row = P("fsdp", None), P("fsdp")
    return jax.shard_map(
        functools.partial(on_device, fsdp=mesh.shape["fsdp"]),
        mesh=mesh,
        in_specs=(tokens, tokens, tokens, row, rows, rows, row, rows, rows, row, rows, row, rows),
        out_specs=(tokens, tokens, row, rows, rows, row, rows, rows, row, rows, row, rows),
        check_vma=False,
    )
```

```python
import functools

import jax
import jax.numpy as jnp
from jax import lax
from jax.experimental import pallas as pl
from jax.experimental.pallas import tpu as pltpu
from jax.sharding import PartitionSpec as P

EPS = 1e-05
BLOCK = 16
LANES = 128
GROUP = 8
COPIES = 4
LOG2E = 1.4426950408889634
LN2 = 0.6931471805599453
FAR = 1e30
F32 = jnp.float32
BF16 = jnp.bfloat16
VMEM_LIMIT = 56 * 1024 * 1024


def dot(left, right, left_dim, right_dim):
    return lax.dot_general(
        left, right, (((left_dim,), (right_dim,)), ((), ())), preferred_element_type=F32
    )


def params():
    return pltpu.CompilerParams(vmem_limit_bytes=VMEM_LIMIT)


def cost(flops, moved):
    return pl.CostEstimate(flops=int(flops), bytes_accessed=int(moved), transcendentals=0)


def blank(shape, dtype):
    return pl.pallas_call(
        lambda ref: None,
        out_shape=jax.ShapeDtypeStruct(shape, dtype),
        out_specs=pl.BlockSpec(memory_space=pl.ANY),
        name="blank",
    )()


def ring_order(size):
    half = size // 2
    return [2 * p if p < half else 2 * (size - 1 - p) + 1 for p in range(size)]


class Ring:
    def __init__(self, size):
        order = ring_order(size)
        place = [0] * size
        for spot, member in enumerate(order):
            place[member] = spot
        self.size, self.half = size, size // 2
        self.order = jnp.array(order, jnp.int32)
        self.spot = jnp.array(place, jnp.int32)[lax.axis_index("fsdp")]
        self.above = [(order[p], order[(p + 1) % size]) for p in range(size)]
        self.below = [(order[p], order[(p - 1) % size]) for p in range(size)]

    def member(self, offset):
        return self.order[(self.spot + offset + self.size) % self.size]

    def up(self, value):
        return lax.ppermute(value, "fsdp", self.above)

    def down(self, value):
        return lax.ppermute(value, "fsdp", self.below)


class Gather:
    def __init__(self, ring, shard):
        self.ring, self.cut = ring, shard.shape[0] // 2
        self.whole = blank((ring.size,) + shard.shape, shard.dtype)
        self.held = (shard, shard)
        self.put(shard, 0)

    def put(self, piece, offset, start=0):
        at = (self.ring.member(offset), jnp.int32(start), jnp.int32(0))
        self.whole = lax.dynamic_update_slice(self.whole, piece[None], at)

    def step(self, number):
        low, high = self.held
        if number == self.ring.half:
            low, high = low[: self.cut], high[self.cut :]
        return self.ring.up(low), self.ring.down(high)

    def take(self, number, got):
        self.held = got
        last = number == self.ring.half
        self.put(got[0], -number)
        self.put(got[1], number, self.cut if last else 0)

    def rest(self):
        def body(number, state):
            whole, low, high = state
            low, high = self.ring.up(low), self.ring.down(high)
            self.whole = whole
            self.put(low, -number)
            self.put(high, number)
            return self.whole, low, high

        self.whole, low, high = lax.fori_loop(1, self.ring.half, body, (self.whole,) + self.held)
        self.held = (low, high)
        self.take(self.ring.half, self.step(self.ring.half))


class Scatter:
    def __init__(self, ring, parts):
        self.ring, self.parts, self.cut = ring, parts, parts.shape[1] // 2
        far = self.own(ring.half)
        self.sent = (far[: self.cut], far[self.cut :])
        self.total = None

    def own(self, offset):
        return lax.dynamic_index_in_dim(self.parts, self.ring.member(offset), 0, keepdims=False)

    def step(self, number):
        return self.ring.up(self.sent[0]), self.ring.down(self.sent[1])

    def take(self, number, got):
        left = self.ring.half - number
        low, high = got
        near_low, near_high = self.own(left), self.own(-left)
        if number == 1:
            low = jnp.concatenate([low, jnp.zeros_like(near_low[self.cut :])])
            high = jnp.concatenate([jnp.zeros_like(near_high[: self.cut]), high])
        if left == 0:
            self.total = near_low.astype(F32) + low.astype(F32) + high.astype(F32)
        else:
            self.sent = (self.add(near_low, low), self.add(near_high, high))

    def add(self, near, got):
        return (near.astype(F32) + got.astype(F32)).astype(near.dtype)

    def rest(self):
        self.take(1, self.step(1))

        def body(number, sent):
            left = self.ring.half - number
            low, high = self.ring.up(sent[0]), self.ring.down(sent[1])
            return self.add(self.own(left), low), self.add(self.own(-left), high)

        self.sent = lax.fori_loop(2, self.ring.half, body, self.sent)
        self.take(self.ring.half, self.step(self.ring.half))


def swap(value, bit):
    return lax.ppermute(value, "rep", [(r, r ^ bit) for r in range(COPIES)])


def rep_gather(value):
    across = swap(value, 2)
    return [value, swap(value, 1), across, swap(across, 1)]


def rep_scatter_near(parts):
    pair = swap(jnp.stack([parts[1], parts[3]]), 1)
    near = parts[0].astype(F32) + pair[0].astype(F32)
    far = parts[2].astype(F32) + pair[1].astype(F32)
    return near, far.astype(parts.dtype)


def rep_scatter_far(near, far):
    return near + swap(far, 2).astype(F32)


def sum_near(parts):
    pair = swap(jnp.stack([parts[1], parts[3]]), 1)
    mine = jnp.stack([parts[0], parts[2]]) + pair
    return mine + swap(jnp.stack([mine[1], mine[0]]), 2)


def sum_far(mine):
    next_to = swap(mine, 1)
    return jnp.stack([mine[0], next_to[0], mine[1], next_to[1]])


def to_time(value):
    return jnp.swapaxes(value.reshape(GROUP, -1, value.shape[-1]), 0, 1).reshape(value.shape)


def to_sequence(value):
    return jnp.swapaxes(value.reshape(-1, GROUP, value.shape[-1]), 0, 1).reshape(value.shape)


def by_copy(value):
    return value.reshape(COPIES, -1, value.shape[-1])


def sigmoid(value):
    return 1.0 / (1.0 + jnp.exp(-value))


def later(value, shift):
    rows = shift * GROUP
    return jnp.concatenate([jnp.zeros_like(value[:rows]), value[:-rows]], axis=0)


def sooner(value, shift):
    rows = shift * GROUP
    return jnp.concatenate([value[rows:], jnp.zeros_like(value[:rows])], axis=0)


def conv_of(inner, masks, taps):
    total = taps[4:5] + taps[3:4] * inner
    for shift in range(1, 4):
        total = total + taps[3 - shift : 4 - shift] * (later(inner, shift) * masks[shift - 1])
    return total


def by_sequence(held, out_ref, value):
    length = value.shape[0] // GROUP
    held[...] = value
    for s in range(GROUP):
        out_ref[s * length : (s + 1) * length, :] = held[
            pl.ds(s, length, stride=GROUP), :
        ].astype(out_ref.dtype)


def conv_kernel(inner_ref, masks_ref, taps_ref, act_ref, low_ref):
    value = conv_of(inner_ref[...], masks_ref, taps_ref[...])
    act = value * sigmoid(value)
    act_ref[...] = act
    low_ref[...] = act.astype(BF16)


def conv_forward(inner, masks, taps):
    rows, width = inner.shape
    tile = pl.BlockSpec((rows, LANES), lambda c: (0, c))
    return pl.pallas_call(
        conv_kernel,
        grid=(width // LANES,),
        in_specs=[
            tile,
            pl.BlockSpec((3, rows, LANES), lambda c: (0, 0, 0)),
            pl.BlockSpec((8, LANES), lambda c: (0, c)),
        ],
        out_specs=[tile, tile],
        out_shape=[
            jax.ShapeDtypeStruct((rows, width), F32),
            jax.ShapeDtypeStruct((rows, width), BF16),
        ],
        compiler_params=params(),
        cost_estimate=cost(30 * rows * width, 10 * rows * width),
        name="conv_forward",
    )(inner, masks, taps)


def conv_back_kernel(inner_ref, grad_ref, masks_ref, taps_ref, out_ref, natural_ref, sums_ref, held):
    inner, taps = inner_ref[...], taps_ref[...]
    value = conv_of(inner, masks_ref, taps)
    gate = sigmoid(value)
    grad = grad_ref[...] * (gate * (1.0 + value * (1.0 - gate)))
    total = taps[3:4] * grad
    sums = [None] * 4 + [jnp.sum(grad, axis=0, keepdims=True)]
    sums[3] = jnp.sum(grad * inner, axis=0, keepdims=True)
    for shift in range(1, 4):
        masked = grad * masks_ref[shift - 1]
        total = total + taps[3 - shift : 4 - shift] * sooner(masked, shift)
        sums[3 - shift] = jnp.sum(masked * later(inner, shift), axis=0, keepdims=True)
    out_ref[...] = total.astype(BF16)
    by_sequence(held, natural_ref, total)
    sums_ref[...] = jnp.concatenate(sums + [jnp.zeros((3, inner.shape[1]), F32)], axis=0)


def conv_backward(inner, grad, masks, taps):
    rows, width = inner.shape
    tile = pl.BlockSpec((rows, LANES), lambda c: (0, c))
    few = pl.BlockSpec((8, LANES), lambda c: (0, c))
    return pl.pallas_call(
        conv_back_kernel,
        grid=(width // LANES,),
        in_specs=[tile, tile, pl.BlockSpec((3, rows, LANES), lambda c: (0, 0, 0)), few],
        out_specs=[tile, tile, few],
        out_shape=[
            jax.ShapeDtypeStruct((rows, width), BF16),
            jax.ShapeDtypeStruct((rows, width), BF16),
            jax.ShapeDtypeStruct((8, width), F32),
        ],
        scratch_shapes=[pltpu.VMEM((rows, LANES), F32)],
        compiler_params=params(),
        cost_estimate=cost(60 * rows * width, 10 * rows * width),
        name="conv_backward",
    )(inner, grad, masks, taps)


def gate_kernel(readout_ref, gate_ref, out_ref, natural_ref, held):
    gate = gate_ref[...]
    gated = readout_ref[...] * (gate * sigmoid(gate))
    out_ref[...] = gated.astype(BF16)
    by_sequence(held, natural_ref, gated)


def gate_forward(readout, gate):
    rows, width = gate.shape
    tile = pl.BlockSpec((rows, LANES), lambda c: (0, c))
    return pl.pallas_call(
        gate_kernel,
        grid=(width // LANES,),
        in_specs=[tile] * 2,
        out_specs=[tile] * 2,
        out_shape=[jax.ShapeDtypeStruct((rows, width), BF16)] * 2,
        scratch_shapes=[pltpu.VMEM((rows, LANES), F32)],
        compiler_params=params(),
        cost_estimate=cost(20 * rows * width, 12 * rows * width),
        name="gate_forward",
    )(readout, gate)


def gate_back_kernel(grad_ref, readout_ref, gate_ref, read_ref, out_ref, natural_ref, held):
    gate, grad = gate_ref[...], grad_ref[...]
    sig = sigmoid(gate)
    read_ref[...] = grad * (gate * sig)
    gate_grad = grad * readout_ref[...] * (sig * (1.0 + gate * (1.0 - sig)))
    out_ref[...] = gate_grad.astype(BF16)
    by_sequence(held, natural_ref, gate_grad)


def gate_backward(grad, readout, gate):
    rows, width = gate.shape
    tile = pl.BlockSpec((rows, LANES), lambda c: (0, c))
    return pl.pallas_call(
        gate_back_kernel,
        grid=(width // LANES,),
        in_specs=[tile] * 3,
        out_specs=[tile] * 3,
        out_shape=[jax.ShapeDtypeStruct((rows, width), F32)]
        + [jax.ShapeDtypeStruct((rows, width), BF16)] * 2,
        scratch_shapes=[pltpu.VMEM((rows, LANES), F32)],
        compiler_params=params(),
        cost_estimate=cost(20 * rows * width, 20 * rows * width),
        name="gate_backward",
    )(grad, readout, gate)


def rows_kernel(scaled, *refs):
    values_ref, out_ref, held = refs[0], refs[-2], refs[-1]
    for s in range(GROUP):
        value = values_ref[s].astype(F32)
        if scaled:
            square = jnp.mean(value * value, axis=-1, keepdims=True)
            value = value * lax.rsqrt(square + EPS) * refs[1][...]
        for k in range(held.shape[0]):
            held[k, pl.ds(s, value.shape[0], stride=GROUP), :] = value[
                :, k * LANES : (k + 1) * LANES
            ]
    for k in range(held.shape[0]):
        out_ref[:, k * LANES : (k + 1) * LANES] = held[k].astype(BF16)


def interleave(values, gain=None):
    _, length, model = values.shape
    extra = [] if gain is None else [gain.reshape(1, model)]
    return pl.pallas_call(
        functools.partial(rows_kernel, gain is not None),
        grid=(length // BLOCK,),
        in_specs=[pl.BlockSpec((GROUP, BLOCK, model), lambda t: (0, t, 0))]
        + [pl.BlockSpec((1, model), lambda t: (0, 0))] * len(extra),
        out_specs=pl.BlockSpec((BLOCK * GROUP, model), lambda t: (t, 0)),
        out_shape=jax.ShapeDtypeStruct((length * GROUP, model), BF16),
        scratch_shapes=[pltpu.VMEM((model // LANES, BLOCK * GROUP, LANES), F32)],
        compiler_params=params(),
        cost_estimate=cost(8 * GROUP * length * model, 4 * GROUP * length * model),
        name="interleave",
    )(values, *extra)


class Peers:
    def __init__(self, size):
        self.size, self.half = size, size // 2
        self.member, self.copy = lax.axis_index("fsdp"), lax.axis_index("rep")
        row, column = lax.div(self.member, 2), lax.rem(self.member, 2)
        self.spot = row * (1 - column) + (size - 1 - row) * column
        side = lax.rem(self.copy, 2)
        self.core = (self.member, self.copy - side + (1 - side))
        self.across = (self.member, lax.rem(self.copy + 2, COPIES))
        self.ring = ((self.at(1), self.copy), (self.at(-1), self.copy))

    def at(self, offset):
        spot = lax.rem(self.spot + (offset + self.size), self.size)
        second = lax.div(spot, self.half)
        return 2 * spot * (1 - second) + (2 * (self.size - 1 - spot) + 1) * second

    def meet(self):
        barrier = pltpu.get_barrier_semaphore()
        peers = (*self.ring, self.core, self.across)
        for peer in peers:
            pl.semaphore_signal(barrier, inc=1, device_id=peer, device_id_type=pl.DeviceIdType.MESH)
        pl.semaphore_wait(barrier, len(peers))


def remote(source, target, sems, index, peer):
    return pltpu.make_async_remote_copy(
        src_ref=source,
        dst_ref=target,
        send_sem=sems[0].at[index],
        recv_sem=sems[1].at[index],
        device_id=peer,
        device_id_type=pl.DeviceIdType.MESH,
    )


def spread(coefs, nstate):
    terms = []
    for _ in range(3):
        term = coefs.astype(BF16)
        terms.append(term)
        coefs = coefs - term.astype(F32)
    joined = jnp.concatenate(terms, axis=1)
    return jnp.pad(joined, ((0, 0), (0, LANES - joined.shape[1])))


def spreader(nstate):
    row = lax.broadcasted_iota(jnp.int32, (LANES, 2 * nstate * LANES), 0)
    tile = lax.broadcasted_iota(jnp.int32, (LANES, 2 * nstate * LANES), 1) // LANES
    return ((row % (2 * nstate) == tile) & (row < 6 * nstate)).astype(BF16)


def folder(nstate):
    tile = lax.broadcasted_iota(jnp.int32, (2 * nstate * LANES, LANES), 0) // LANES
    column = lax.broadcasted_iota(jnp.int32, (2 * nstate * LANES, LANES), 1)
    return (tile == column).astype(BF16)


def tiled(value, width):
    return jnp.concatenate([value] * (width // LANES), axis=1)


def at_time(t):
    return pl.ds(pl.multiple_of(t * GROUP, GROUP), GROUP)


def scan_kernel(
    nstate, chunk, pre_ref, act_ref, coef_ref, spread_ref, keep_ref, rate_ref, row_ref,
    out_ref, step_ref, start_ref, carry_ref, wide,
):
    width = pre_ref.shape[1]

    @pl.when(pl.program_id(0) == 0)
    def _():
        carry_ref[...] = jnp.zeros_like(carry_ref)

    start_ref[0] = carry_ref[...]
    wide[...] = jnp.dot(coef_ref[...], spread_ref[...], preferred_element_type=F32)
    pre = pre_ref[...] + row_ref[0:1]
    step_ref[...] = jnp.maximum(pre, 0.0) + jnp.log1p(jnp.exp(-jnp.abs(pre)))
    for c in range(width // chunk):
        cols = slice(c * chunk, (c + 1) * chunk)

        def advance(t, states):
            at = at_time(t)
            step, act = step_ref[at, cols], act_ref[at, cols]
            drive = jnp.where(tiled(keep_ref[at, :], chunk) > 0.5, step, FAR)
            inflow = step * act
            total = row_ref[1:2, cols] * act
            now = []
            for n in range(nstate):
                write = tiled(wide[at, n * LANES : (n + 1) * LANES], chunk)
                read = tiled(wide[at, (nstate + n) * LANES : (nstate + n + 1) * LANES], chunk)
                state = jnp.exp2(drive * rate_ref[n, :, cols]) * states[n] + write * inflow
                total = total + read * state
                now.append(state)
            out_ref[at, cols] = total
            return tuple(now)

        start = tuple(carry_ref[n, :, cols] for n in range(nstate))
        states = lax.fori_loop(0, BLOCK, advance, start, unroll=4)
        for n in range(nstate):
            carry_ref[n, :, cols] = states[n]


def scan_forward(pre, act, coef, spread_by, keep, rate, rows):
    total, width = pre.shape
    nstate = rate.shape[0]
    size = BLOCK * GROUP
    tile = pl.BlockSpec((size, width), lambda t: (t, 0))
    thin = pl.BlockSpec((size, LANES), lambda t: (t, 0))
    state = pl.BlockSpec((nstate, GROUP, width), lambda t: (0, 0, 0))
    count = total // size
    work = total * width * nstate
    return pl.pallas_call(
        functools.partial(scan_kernel, nstate, 256),
        grid=(count,),
        in_specs=[
            tile,
            tile,
            thin,
            pl.BlockSpec(spread_by.shape, lambda t: (0, 0)),
            thin,
            state,
            pl.BlockSpec((8, width), lambda t: (0, 0)),
        ],
        out_specs=[
            tile,
            tile,
            pl.BlockSpec((1, nstate, GROUP, width), lambda t: (t, 0, 0, 0)),
        ],
        out_shape=[
            jax.ShapeDtypeStruct((total, width), F32),
            jax.ShapeDtypeStruct((total, width), F32),
            jax.ShapeDtypeStruct((total // size, nstate, GROUP, width), F32),
        ],
        scratch_shapes=[
            pltpu.VMEM((nstate, GROUP, width), F32),
            pltpu.VMEM((size, 2 * nstate * LANES), F32),
        ],
        compiler_params=params(),
        cost_estimate=cost(16 * work, 16 * count * size * width),
        name="scan_forward",
    )(pre, act, coef, spread_by, keep, rate, rows)


class Shares:
    def __init__(self, peers, shards, wholes, sems):
        self.peers, self.shards, self.wholes, self.sems = peers, shards, wholes, sems
        self.sent = []

    def place(self, which, member, c):
        rows = self.shards[which].shape[0]
        start = pl.multiple_of(member * rows + c * (rows // 2), rows // 2)
        return self.wholes[which].at[pl.ds(start, rows // 2), :]

    def owner(self, way, step):
        return self.peers.at(-step if way == 0 else step)

    def chunks(self, way, step):
        return (way,) if step == self.peers.half else (0, 1)

    def come(self, which, way, step, c):
        there = self.place(which, self.owner(way, step), c)
        remote(there, there, self.sems, (which, way, step - 1, c), self.peers.ring[way]).wait_recv()

    def step(self, which, step):
        for c in range(2):
            for way in range(2):
                if c not in self.chunks(way, step):
                    continue
                target = self.place(which, self.owner(way, step - 1), c)
                source = target
                if step == 1:
                    rows = self.shards[which].shape[0] // 2
                    source = self.shards[which].at[pl.ds(c * rows, rows), :]
                else:
                    self.come(which, way, step - 1, c)
                index = (which, way, step - 1, c)
                remote(source, target, self.sems, index, self.peers.ring[way]).start()

    def finish(self, which):
        half = self.peers.half
        for way in range(2):
            self.come(which, way, half - 1, 1 - way)
            self.come(which, way, half, way)

    def sent_all(self):
        for which in range(len(self.shards)):
            for step in range(1, self.peers.half + 1):
                for way in range(2):
                    for c in self.chunks(way, step):
                        place = self.place(which, self.owner(way, step - 1), c)
                        index = (which, way, step - 1, c)
                        remote(place, place, self.sems, index, self.peers.ring[way]).wait_send()


def softplus(value):
    return jnp.maximum(value, 0.0) + jnp.log1p(jnp.exp(-jnp.abs(value)))


def forward_kernel(
    size, rank, nstate,
    entry, few, tokens, out_grad, segments, out_proj,
    few_out, masks_out, rate_out, spread_out, fold_out, normed_out, cotangent_out, tokens_all, grads_all, segments_all,
    w_in_out, inner_out, act_out, low_out, step_low_out, coef_out, step_out, start_out, gate_out, readout_out,
    gated_out, natural_out, gate_w_out, out_w_out,
    few_all, small, masks, rate, spread_by, fold_by, normed, stage, cotangent, held, seg, inner_shard, gate_shard, w_in,
    inner, act, low, part, nat, got_near, to_across, got_across, shared, step_low, coef, wide, pre, step, readout,
    carry, start_at, gate, gated, natural, gate_w,
    local, start_sems, gate_sems, own_sems, entry_sems, stage_sems, out_sems, seg_sems,
    ring_send, ring_recv, few_send, few_recv, rep_send, rep_recv, near_send, near_recv,
):
    peers = Peers(size)
    total, width = normed.shape[0], w_in.shape[1]
    pad = 3 * GROUP
    chunk = 256
    rows = 64
    length = total // GROUP
    batches = GROUP // COPIES
    half = peers.half
    side_rows = total // COPIES
    saved = []

    def save(source, target):
        copy = pltpu.make_async_copy(source, target, local.at[len(saved)])
        copy.start()
        saved.append(copy)

    picks = []
    for side_of, target in enumerate((inner_shard, gate_shard)):
        for f in range(size):
            source = ((side_of * size + f) * COPIES + peers.copy) * LANES
            picks.append(
                pltpu.make_async_copy(
                    entry.at[:, pl.ds(pl.multiple_of(source, LANES), LANES)],
                    target.at[:, pl.ds(f * LANES, LANES)],
                    entry_sems.at[len(picks)],
                )
            )
    for pick in picks:
        pick.start()
    peers.meet()
    sent = []

    def send(*copy):
        moving = remote(*copy)
        moving.start()
        sent.append(moving)

    rep_sems = (rep_send, rep_recv)

    def of_copy(ref, k):
        return ref.at[k] if ref is segments_all else ref.at[pl.ds(k * batches, batches)]

    def exchange(i, own, everyone):
        send(own, of_copy(everyone, 2), rep_sems, (i, 0), peers.across)
        send(own, of_copy(everyone, 1), rep_sems, (i, 1), peers.core)
        copy = pltpu.make_async_copy(own, of_copy(everyone, 0), own_sems.at[3 + i])
        copy.start()
        return copy

    def pass_on(i, everyone):
        far = of_copy(everyone, 2)
        remote(far, far, rep_sems, (i, 0), peers.across).wait_recv()
        send(far, of_copy(everyone, 3), rep_sems, (i, 2), peers.core)

    def exchanged(i, everyone, copy):
        copy.wait()
        for k, which in ((1, 1), (3, 2)):
            there = of_copy(everyone, k)
            remote(there, there, rep_sems, (i, which), peers.core).wait_recv()

    out_rows = out_proj.shape[0] // COPIES
    out_shard = out_proj.at[pl.ds(pl.multiple_of(peers.copy * out_rows, out_rows), out_rows), :]
    ring = Shares(
        peers, (inner_shard, gate_shard, out_shard), (w_in, gate_w, out_w_out), (ring_send, ring_recv),
    )
    gate_rows = gate_shard.shape[0]
    shard_rows = pl.ds(pl.multiple_of(peers.member * gate_rows, gate_rows), gate_rows)
    own_rows = pl.ds(pl.multiple_of(peers.member * out_rows, out_rows), out_rows)
    own_columns = pl.ds(pl.multiple_of(peers.member * LANES, LANES), LANES)

    few_sems = (few_send, few_recv)
    few_rows = few.shape[0] // 2

    def few_place(way, number, split):
        columns = pl.ds(pl.multiple_of(ring.owner(way, number) * LANES, LANES), LANES)
        place = pl.ds(way * few_rows, few_rows) if split else pl.ds(0, 2 * few_rows)
        return few_all.at[place, columns]

    def few_come(way, number):
        there = few_place(way, number, number == half)
        remote(there, there, few_sems, (way, number - 1), peers.ring[way]).wait_recv()

    def few_step(number):
        for way in range(2):
            if number > 1:
                few_come(way, number - 1)
            target = few_place(way, number - 1, number == half)
            source = few if number == 1 else target
            send(source, target, few_sems, (way, number - 1), peers.ring[way])

    few_step(1)
    own_tokens = exchange(0, tokens, tokens_all)
    own_segments = exchange(2, segments, segments_all)
    own = [
        pltpu.make_async_copy(few, few_all.at[:, own_columns], own_sems.at[0]),
        pltpu.make_async_copy(out_shard, out_w_out.at[own_rows, :], own_sems.at[1]),
    ]
    for copy in own:
        copy.start()
    for pick in picks[:size]:
        pick.wait()
    ring.step(0, 1)
    for pick in picks[size:]:
        pick.wait()
    own_shards = [
        pltpu.make_async_copy(inner_shard, w_in.at[shard_rows, :], own_sems.at[6]),
        pltpu.make_async_copy(gate_shard, gate_w.at[shard_rows, :], own_sems.at[2]),
    ]
    for copy in own_shards:
        copy.start()

    wide_shape, thin_shape = spread_by.shape, fold_by.shape
    tile = lax.broadcasted_iota(jnp.int32, wide_shape, 1) // LANES
    row = lax.broadcasted_iota(jnp.int32, wide_shape, 0)
    spread_by[...] = jnp.where(
        (lax.rem(row, 2 * nstate) == tile) & (row < 6 * nstate), 1.0, 0.0
    ).astype(BF16)
    tile = lax.broadcasted_iota(jnp.int32, thin_shape, 0) // LANES
    column = lax.broadcasted_iota(jnp.int32, thin_shape, 1)
    fold_by[...] = jnp.where(tile == column, 1.0, 0.0).astype(BF16)
    save(spread_by, spread_out)
    save(fold_by, fold_out)

    few_step(2)
    pass_on(2, segments_all)
    few_step(3)
    ring.step(0, 2)
    few_step(4)
    exchanged(2, segments_all, own_segments)
    numbers = pltpu.make_async_copy(segments_all, seg, seg_sems.at[0])
    numbers.start()
    for way in range(2):
        few_come(way, half - 1) if half < 2 else None
        few_come(way, half)
    own[0].wait()
    numbers.wait()

    numbers = jnp.concatenate([seg[k] for k in range(COPIES)], axis=0).astype(F32)
    lane = lax.broadcasted_iota(jnp.int32, (total, LANES), 1)
    time = lax.broadcasted_iota(jnp.int32, (total, LANES), 0) // GROUP
    picked = jnp.where(lane == time, jnp.concatenate([numbers] * length, axis=0), 0.0).astype(BF16)
    numbers = jnp.dot(picked, jnp.ones((LANES, LANES), BF16), preferred_element_type=F32)
    for shift in range(1, 4):
        earlier = jnp.concatenate(
            [jnp.full((shift * GROUP, LANES), -1.0, F32), numbers[: -shift * GROUP]], axis=0
        )
        masks[shift - 1] = jnp.where(earlier == numbers, 1.0, 0.0)
    save(masks, masks_out)
    save(few_all, few_out)
    first_small = 2 * rank + 2 * nstate
    small[...] = few_all[first_small : first_small + small.shape[0], :].astype(F32)
    taps, bias_row, skip_row, gain_row = 0, 5, 6 + nstate, 7 + nstate
    for n in range(nstate):
        rate[n] = jnp.broadcast_to(-LOG2E * jnp.exp(small[6 + n : 7 + n, :]), (GROUP, width))
    save(rate, rate_out)

    def fetch(source, t, slot):
        return pltpu.make_async_copy(
            source.at[:, pl.ds(pl.multiple_of(t * BLOCK, BLOCK), BLOCK), :], stage.at[slot], stage_sems.at[slot]
        )

    def weave(slot, scaled):
        for s in range(GROUP):
            value = stage[slot, s].astype(F32)
            if scaled:
                square = jnp.mean(value * value, axis=-1, keepdims=True)
                value = value * lax.rsqrt(square + EPS)
            for k in range(held.shape[0]):
                tile = value[:, k * LANES : (k + 1) * LANES]
                if scaled:
                    at = gain_row + k % 2
                    tile = tile * small[at : at + 1, (k // 2) * LANES : (k // 2 + 1) * LANES]
                held[k, pl.ds(s, BLOCK, stride=GROUP), :] = tile

    block_rows = BLOCK * GROUP
    blocks = total // block_rows

    def block_of(t):
        return pl.ds(pl.multiple_of(t * block_rows, block_rows), block_rows)

    pass_on(0, tokens_all)
    own_grads = exchange(1, out_grad, grads_all)
    ring.step(0, 3)
    exchanged(0, tokens_all, own_tokens)
    fetch(tokens_all, 0, 0).start()

    @pl.loop(0, blocks)
    def _(t):
        slot = lax.rem(t, 2)

        @pl.when(t + 1 < blocks)
        def _():
            fetch(tokens_all, t + 1, 1 - slot).start()

        @pl.when(t == blocks - 2)
        def _():
            ring.step(0, 4)
            ring.step(1, 1)

        fetch(tokens_all, t, slot).wait()
        weave(slot, True)
        for k in range(held.shape[0]):
            normed[block_of(t), k * LANES : (k + 1) * LANES] = held[k].astype(BF16)

    save(normed, normed_out)
    for copy in own_shards:
        copy.wait()
    ring.finish(0)
    save(w_in, w_in_out)

    def cotangent_out_of(t, slot):
        return pltpu.make_async_copy(cotangent.at[slot], cotangent_out.at[block_of(t), :], out_sems.at[slot])

    def weave_grads(first, count):
        fetch(grads_all, first, first % 2).start()

        @pl.loop(first, first + count)
        def _(t):
            slot = lax.rem(t, 2)

            @pl.when(t + 1 < first + count)
            def _():
                fetch(grads_all, t + 1, 1 - slot).start()

            @pl.when(t >= 2)
            def _():
                cotangent_out_of(t - 2, slot).wait()

            fetch(grads_all, t, slot).wait()
            weave(slot, False)
            for k in range(held.shape[0]):
                cotangent[slot, :, k * LANES : (k + 1) * LANES] = held[k].astype(BF16)
            cotangent_out_of(t, slot).start()

    inner[0:pad, :] = jnp.zeros((pad, width), F32)
    part[...] = jnp.zeros_like(part)

    @pl.loop(0, width // chunk)
    def _(c):
        cols = pl.ds(pl.multiple_of(c * chunk, chunk), chunk)
        inner[pad:, cols] = jnp.dot(normed[...], w_in[:, cols], preferred_element_type=F32)

        @pl.when(c == 1)
        def _():
            ring.step(2, 1)

        tap = [small[taps + i : taps + i + 1, cols] for i in range(5)]

        @pl.loop(0, total // rows)
        def _(i):
            start = pl.multiple_of(i * rows, rows)
            value = tap[4] + tap[3] * inner[pl.ds(pad + start, rows), cols]
            for shift in range(1, 4):
                mask = tiled(masks[shift - 1, pl.ds(start, rows), :], chunk)
                before = inner[pl.ds(pad - shift * GROUP + start, rows), cols]
                value = value + tap[3 - shift] * (before * mask)
            here = value * sigmoid(value)
            act[pl.ds(start, rows), cols] = here
            low[pl.ds(start, rows), cols] = here.astype(BF16)

        for j in range(2):
            part[j] += lax.dot_general(
                low[:, cols], few_all[j * LANES : (j + 1) * LANES, cols], (((1,), (1,)), ((), ())),
                preferred_element_type=F32,
            )

    save(inner.at[pl.ds(pad, total), :], inner_out)
    save(act, act_out)
    save(low, low_out)

    near = (near_send, near_recv)
    for j in range(2):
        for s in range(GROUP):
            nat[j, s * length : (s + 1) * length, :] = part[j, pl.ds(s, length, stride=GROUP), :]
    sends = []

    def start(source, target, index, peer):
        copy = remote(source, target, near, index, peer)
        copy.start()
        sends.append(copy)

    def come(target, index, peer):
        remote(target, target, near, index, peer).wait_recv()

    for i in range(2):
        start(nat.at[:, pl.ds((2 * i + 1) * side_rows, side_rows), :], got_near.at[i], i, peers.core)
    ring.step(1, 2)
    pass_on(1, grads_all)
    for i in range(2):
        come(got_near.at[i], i, peers.core)
    to_across[...] = nat[:, 2 * side_rows : 3 * side_rows, :] + got_near[1]
    start(to_across, got_across, 2, peers.across)
    exchanged(1, grads_all, own_grads)
    weave_grads(0, blocks // 2)
    ring.step(2, 2)
    come(got_across, 2, peers.across)
    mine = nat[:, :side_rows, :] + got_near[0] + got_across[...]
    shared[0, 0] = mine[0].astype(BF16)
    lane = lax.broadcasted_iota(jnp.int32, (side_rows, LANES), 1)
    rest, terms = jnp.where(lane < 2 * nstate, mine[1], 0.0), jnp.zeros((side_rows, LANES), F32)
    for i in range(3):
        term = rest.astype(BF16).astype(F32)
        rest = rest - term
        terms = terms + (pltpu.roll(term, 2 * nstate * i, 1) if i else term)
    shared[0, 1] = terms.astype(BF16)
    start(shared.at[0], shared.at[2], 3, peers.across)
    start(shared.at[0], shared.at[1], 4, peers.core)
    weave_grads(blocks // 2, blocks // 2)
    come(shared.at[2], 3, peers.across)
    start(shared.at[2], shared.at[3], 5, peers.core)
    come(shared.at[1], 4, peers.core)
    come(shared.at[3], 5, peers.core)
    for copy in sends:
        copy.wait_send()
    for k in range(COPIES):
        for b in range(batches):
            for j in range(2):
                part[j, pl.ds(k * batches + b, length, stride=GROUP), :] = shared[
                    k, j, b * length : (b + 1) * length, :
                ].astype(F32)
    step_low[...] = part[0].astype(BF16)
    coef[...] = part[1].astype(BF16)
    save(step_low, step_low_out)
    save(coef, coef_out)

    stride = few_all[rank + 2 * nstate : 2 * rank + 2 * nstate, :]
    side_bias = small[bias_row : bias_row + 1, :]
    carry[...] = jnp.zeros_like(carry)

    def keep_start(t, slot):
        return pltpu.make_async_copy(start_at.at[slot], start_out.at[t], start_sems.at[slot])

    @pl.loop(0, blocks)
    def _(t):
        for tick, which, number in ((0, 1, 3), (2, 2, 3), (4, 1, 4), (6, 2, 4)):

            @pl.when(t == tick)
            def _(which=which, number=number):
                ring.step(which, number)

        base = pl.multiple_of(t * block_rows, block_rows)
        these = block_of(t)
        wide[...] = jnp.dot(coef[these, :], spread_by[...], preferred_element_type=F32)
        pre[...] = jnp.dot(step_low[these, :], stride, preferred_element_type=F32)
        for i in range(BLOCK // 2):
            sub = slice(i * 2 * GROUP, (i + 1) * 2 * GROUP)
            step[pl.ds(base + i * 2 * GROUP, 2 * GROUP), :] = softplus(pre[sub, :] + side_bias)
        slot = lax.rem(t, 2)

        @pl.when(t >= 2)
        def _():
            keep_start(t - 2, slot).wait()

        start_at[slot] = carry[...]
        keep_start(t, slot).start()
        for c in range(width // chunk):
            cols = slice(c * chunk, (c + 1) * chunk)

            def advance(i, states):
                at = pl.ds(pl.multiple_of(base + i * GROUP, GROUP), GROUP)
                here = at_time(i)
                step_t, act_t = step[at, cols], act[at, cols]
                drive = jnp.where(tiled(masks[0, at, :], chunk) > 0.5, step_t, FAR)
                inflow = step_t * act_t
                out = small[skip_row : skip_row + 1, cols] * act_t
                now = []
                for n in range(nstate):
                    write = tiled(wide[here, n * LANES : (n + 1) * LANES], chunk)
                    read = tiled(wide[here, (nstate + n) * LANES : (nstate + n + 1) * LANES], chunk)
                    state = jnp.exp2(drive * rate[n, :, cols]) * states[n] + write * inflow
                    out = out + read * state
                    now.append(state)
                readout[at, cols] = out
                return tuple(now)

            states = lax.fori_loop(
                0, BLOCK, advance, tuple(carry[n, :, cols] for n in range(nstate)), unroll=4
            )
            for n in range(nstate):
                carry[n, :, cols] = states[n]

    save(step, step_out)
    save(readout, readout_out)

    ring.finish(1)
    save(gate_w, gate_w_out)

    def keep_gate(c, slot):
        cols = pl.ds(pl.multiple_of(c * chunk, chunk), chunk)
        return pltpu.make_async_copy(gate.at[slot], gate_out.at[:, cols], gate_sems.at[slot])

    @pl.loop(0, width // chunk)
    def _(c):
        cols = pl.ds(pl.multiple_of(c * chunk, chunk), chunk)
        slot = lax.rem(c, 2)

        @pl.when(c >= 2)
        def _():
            keep_gate(c - 2, slot).wait()

        gate[slot] = jnp.dot(normed[...], gate_w[:, cols], preferred_element_type=F32)
        keep_gate(c, slot).start()

        @pl.loop(0, total // rows)
        def _(i):
            at = pl.ds(pl.multiple_of(i * rows, rows), rows)
            here = gate[slot, at, :]
            value = readout[at, cols] * (here * sigmoid(here))
            gated[at, cols] = value.astype(BF16)
            for k in range(chunk // LANES):
                nat[k, at, :] = value[:, k * LANES : (k + 1) * LANES]

        for k in range(chunk // LANES):
            for s in range(GROUP):
                natural[s * length : (s + 1) * length, pl.ds(pl.multiple_of(c * chunk + k * LANES, LANES), LANES)] = nat[
                    k, pl.ds(s, length, stride=GROUP), :
                ].astype(BF16)

    save(gated, gated_out)
    save(natural, natural_out)
    own[1].wait()
    ring.finish(2)
    ring.sent_all()
    for moving in sent:
        moving.wait_send()
    for slot in range(2):
        keep_start(blocks - 2 + slot, slot).wait()
        keep_gate(width // chunk - 2 + slot, slot).wait()
        cotangent_out_of(blocks - 2 + slot, slot).wait()
    for copy in saved:
        copy.wait()


def forward(size, rank, nstate, entry, few, tokens, out_grad, segments, out_proj):
    batches, length, model = tokens.shape
    total = COPIES * batches * length
    slab, width = entry.shape[0], size * LANES
    blocks = length // BLOCK
    anywhere = pl.BlockSpec(memory_space=pl.ANY)
    half = size // 2
    dma = pltpu.SemaphoreType.DMA
    shape = jax.ShapeDtypeStruct
    full, low = shape((total, width), F32), shape((total, width), BF16)
    thin = shape((total, LANES), BF16)
    rows = shape((total, model), BF16)
    weights = shape((size * slab, width), BF16)
    few_all = shape((few.shape[0], width), BF16)
    masks = shape((3, total, LANES), F32)
    state = shape((nstate, GROUP, width), F32)
    spread_by = shape((LANES, 2 * nstate * LANES), BF16)
    fold_by = shape((2 * nstate * LANES, LANES), BF16)
    outs = dict(
        few=few_all,
        masks=masks,
        rate=state,
        spread_by=spread_by,
        fold_by=fold_by,
        normed=rows,
        cotangent=rows,
        tokens_all=shape((GROUP, length, model), BF16),
        grads_all=shape((GROUP, length, model), BF16),
        segments_all=shape((COPIES,) + segments.shape, segments.dtype),
        inner_in=weights,
        inner=full,
        act=full,
        act_low=low,
        step_low=thin,
        coef=thin,
        step=full,
        starts=shape((blocks,) + state.shape, F32),
        gate=full,
        readout=full,
        gated=low,
        gated_natural=low,
        gate_in=weights,
        out_w=shape((size * out_proj.shape[0] // COPIES, model), BF16),
    )
    quarter = total // COPIES
    scratch = [
        few_all,
        shape((few.shape[0] - 2 * rank - 2 * nstate, width), F32),
        masks,
        state,
        spread_by,
        fold_by,
        rows,
        shape((2, GROUP, BLOCK, model), BF16),
        shape((2, BLOCK * GROUP, model), BF16),
        shape((model // LANES, BLOCK * GROUP, LANES), F32),
        shape((COPIES,) + segments.shape, segments.dtype),
        shape((slab, width), BF16),
        shape((slab, width), BF16),
        weights,
        shape((total + 3 * GROUP, width), F32),
        full,
        low,
        shape((2, total, LANES), F32),
        shape((2, total, LANES), F32),
        shape((2, 2, quarter, LANES), F32),
        shape((2, quarter, LANES), F32),
        shape((2, quarter, LANES), F32),
        shape((COPIES, 2, quarter, LANES), BF16),
        thin,
        thin,
        shape((BLOCK * GROUP, 2 * nstate * LANES), F32),
        shape((BLOCK * GROUP, width), F32),
        full,
        full,
        state,
        shape((2,) + state.shape, F32),
        shape((2, total, 256), F32),
        low,
        low,
        weights,
    ]
    sems = [(20,), (2,), (2,), (7,), (2 * size,), (2,), (2,), (1,)]
    sems += [(3, 2, half, 2)] * 2 + [(2, half)] * 2 + [(3, 3)] * 2 + [(6,)] * 2
    results = pl.pallas_call(
        functools.partial(forward_kernel, size, rank, nstate),
        in_specs=[anywhere] * 6,
        out_specs=[anywhere] * len(outs),
        out_shape=list(outs.values()),
        scratch_shapes=[pltpu.VMEM(x.shape, x.dtype) for x in scratch] + [dma(n) for n in sems],
        compiler_params=pltpu.CompilerParams(
            collective_id=4, has_side_effects=True, vmem_limit_bytes=62 * 1024 * 1024
        ),
        cost_estimate=cost(8 * total * width * model, 100 * total * width),
        name="forward",
    )(entry, few, tokens, out_grad, segments, out_proj)
    return dict(zip(outs, results))


class Guests:
    def __init__(self, peers, parts, totals, held, sems):
        self.peers = peers
        self.parts, self.totals, self.held, self.sems = parts, totals, held, sems

    def rows(self, which, c):
        half = self.parts[which].shape[1] // 2
        return pl.ds(c * half, half)

    def copy(self, which, way, step, c, source=None):
        target = self.held[which].at[way, step - 1, self.rows(which, c), :]
        index = (which, way, step - 1, c)
        source = target if source is None else source
        return remote(source, target, self.sems, index, self.peers.ring[way])

    def chunks(self, way, step):
        return (way,) if step == 1 else (0, 1)

    def own(self, which, way, step, c):
        away = self.peers.half + 1 - step
        block = self.peers.at(away if way == 0 else -away)
        return self.parts[which].at[block, self.rows(which, c), :]

    def source(self, which, way, step, c):
        own = self.own(which, way, step, c)
        if step == 1 or c not in self.chunks(way, step - 1):
            return own
        self.copy(which, way, step - 1, c).wait_recv()
        there = self.held[which].at[way, step - 2, self.rows(which, c), :]
        there[...] = (own[...].astype(F32) + there[...].astype(F32)).astype(BF16)
        return there

    def step(self, which, step):
        for c in range(2):
            for way in range(2):
                if c in self.chunks(way, step):
                    self.copy(which, way, step, c, self.source(which, way, step, c)).start()

    def finish(self):
        last = self.peers.half
        for which in range(2):
            for c in range(2):
                total = self.own(which, 0, last + 1, c)[...].astype(F32)
                for way in range(2):
                    self.copy(which, way, last, c).wait_recv()
                    there = self.held[which].at[way, last - 1, self.rows(which, c), :]
                    total = total + there[...].astype(F32)
                self.totals[which][self.rows(which, c), :] = total.astype(BF16)
        for which in range(2):
            for step in range(1, last + 1):
                for way in range(2):
                    for c in self.chunks(way, step):
                        self.copy(which, way, step, c).wait_send()


def scan_back_kernel(
    nstate, chunk, step_ref, act_ref, grad_ref, coef_ref, spread_ref, fold_ref, keep_ref, rate_ref,
    row_ref, start_ref, *refs,
):
    wide, states_all, decays, parts, sizes = refs[-5:]
    width = step_ref.shape[1]
    step_now = pl.program_id(0)
    pre_grad_ref, direct_ref, coef_grad_ref, carry_ref, sums_ref = refs[-10:-5]

    @pl.when(step_now == 0)
    def _():
        carry_ref[...] = jnp.zeros_like(carry_ref)
        sums_ref[...] = jnp.zeros_like(sums_ref)

    wide[...] = jnp.dot(coef_ref[...], spread_ref[...], preferred_element_type=F32)

    def fold(value):
        total = value[:, :LANES]
        for k in range(1, chunk // LANES):
            total = total + value[:, k * LANES : (k + 1) * LANES]
        return total

    for c in range(width // chunk):
        cols = slice(c * chunk, (c + 1) * chunk)

        def advance(t, states):
            at = at_time(t)
            step = step_ref[at, cols]
            drive = jnp.where(tiled(keep_ref[at, :], chunk) > 0.5, step, FAR)
            inflow = step * act_ref[at, cols]
            now = []
            for n in range(nstate):
                write = tiled(wide[at, n * LANES : (n + 1) * LANES], chunk)
                decay = jnp.exp2(drive * rate_ref[n, :, cols])
                decays[t, n] = decay
                states_all[t, n] = states[n]
                now.append(decay * states[n] + write * inflow)
            return tuple(now)

        start = tuple(start_ref[0, n, :, cols] for n in range(nstate))
        states = lax.fori_loop(0, BLOCK, advance, start, unroll=2)
        for n in range(nstate):
            states_all[BLOCK, n] = states[n]

        def retreat(i, carry):
            t = BLOCK - 1 - i
            at = at_time(t)
            step, act, grad = step_ref[at, cols], act_ref[at, cols], grad_ref[at, cols]
            inflow = step * act
            size = jnp.zeros_like(step)
            direct = jnp.zeros_like(step)
            now = []
            for n in range(nstate):
                tile_w = slice(n * LANES, (n + 1) * LANES)
                tile_r = slice((nstate + n) * LANES, (nstate + n + 1) * LANES)
                state_grad = tiled(wide[at, tile_r], chunk) * grad + carry[n]
                passed = decays[t, n] * state_grad
                through = passed * states_all[t, n]
                size = size + rate_ref[n, :, cols] * through
                direct = direct + state_grad * tiled(wide[at, tile_w], chunk)
                sums_ref[n, :, cols] += step * through
                write_part = fold(state_grad * inflow)
                read_part = fold(grad * states_all[t + 1, n])
                if c == 0:
                    parts[at, tile_w] = write_part
                    parts[at, tile_r] = read_part
                else:
                    parts[at, tile_w] += write_part
                    parts[at, tile_r] += read_part
                now.append(passed)
            sizes[at, cols] = LN2 * size + act * direct
            direct_ref[at, cols] = step * direct + row_ref[1:2, cols] * grad
            sums_ref[nstate, :, cols] += grad * act
            return tuple(now)

        start = tuple(carry_ref[n, :, cols] for n in range(nstate))
        carry = lax.fori_loop(0, BLOCK, retreat, start, unroll=2)
        for n in range(nstate):
            carry_ref[n, :, cols] = carry[n]

    step = step_ref[...]
    series = step * (1.0 - step * (0.5 - step * (1.0 / 6.0)))
    pre_grad = sizes[...] * jnp.where(step < 0.01, series, 1.0 - jnp.exp(-step))
    pre_grad_ref[...] = pre_grad.astype(BF16)
    total = pre_grad[:GROUP]
    for t in range(1, BLOCK):
        total = total + pre_grad[t * GROUP : (t + 1) * GROUP]
    sums_ref[nstate + 1] += total
    high = parts[...].astype(BF16)
    low = (parts[...] - high.astype(F32)).astype(BF16)
    coef_grad_ref[...] = jnp.dot(high, fold_ref[...], preferred_element_type=F32) + jnp.dot(
        low, fold_ref[...], preferred_element_type=F32
    )


def scan_backward(
    step, act, grad, coef, spread_by, fold_by, keep, rate, rows, starts
):
    total, width = step.shape
    nstate = rate.shape[0]
    size = BLOCK * GROUP
    chunk = 256
    count = total // size
    tile = pl.BlockSpec((size, width), lambda t: (count - 1 - t, 0))
    thin = pl.BlockSpec((size, LANES), lambda t: (count - 1 - t, 0))
    state = pl.BlockSpec((nstate, GROUP, width), lambda t: (0, 0, 0))
    tally = pl.BlockSpec((nstate + 2, GROUP, width), lambda t: (0, 0, 0))
    work = count * size * width * nstate
    return pl.pallas_call(
        functools.partial(scan_back_kernel, nstate, chunk),
        grid=(count,),
        in_specs=[
            tile,
            tile,
            tile,
            thin,
            pl.BlockSpec(spread_by.shape, lambda t: (0, 0)),
            pl.BlockSpec(fold_by.shape, lambda t: (0, 0)),
            thin,
            state,
            pl.BlockSpec((8, width), lambda t: (0, 0)),
            pl.BlockSpec((1, nstate, GROUP, width), lambda t: (count - 1 - t, 0, 0, 0)),
        ],
        out_specs=[tile, tile, thin, state, tally],
        out_shape=[
            jax.ShapeDtypeStruct((total, width), BF16),
            jax.ShapeDtypeStruct((total, width), F32),
            jax.ShapeDtypeStruct((total, LANES), F32),
            jax.ShapeDtypeStruct((nstate, GROUP, width), F32),
            jax.ShapeDtypeStruct((nstate + 2, GROUP, width), F32),
        ],
        scratch_shapes=[
            pltpu.VMEM((size, 2 * nstate * LANES), F32),
            pltpu.VMEM((BLOCK + 1, nstate, GROUP, chunk), F32),
            pltpu.VMEM((BLOCK, nstate, GROUP, chunk), F32),
            pltpu.VMEM((size, 2 * nstate * LANES), F32),
            pltpu.VMEM((size, width), F32),
        ],
        compiler_params=params(),
        cost_estimate=cost(40 * work, 24 * count * size * width),
        name="scan_backward",
    )(step, act, grad, coef, spread_by, fold_by, keep, rate, rows, starts)


def backward_kernel(
    size, nstate, rank,
    gated_in, cotangent_in, w_out, readout_in, gate_in, normed_in, step_in, act_in, coef_in, starts_in, masks_in, rate_in,
    spread_in, fold_in, few_in,
    natural_out, pre_low_out, direct_out, coef_grad_out, sums_out, out_total, gate_total,
    gated, cotangent, out_w, normed, out_wgrad, gate_wgrad, out_held, gate_held, gate_grad, natural, grad, nat,
    step_at, act_at, start_at, wide, states_all, decays, parts, sizes, sums, carry, coef, spread_by, fold_by, rate, keep, few,
    coef_grad,
    load_sems, tile_sems, block_sems, save_sems, block_saves, ring_send, ring_recv,
):
    peers = Peers(size)
    total, width = gated.shape
    model = normed.shape[1]
    length = total // GROUP
    chunk, rows = 256, 64
    block_rows = BLOCK * GROUP
    blocks = total // block_rows
    loads, saved = {}, []

    def load(name, source, target):
        loads[name] = pltpu.make_async_copy(source, target, load_sems.at[len(loads)])
        loads[name].start()

    def save(source, target):
        saved.append(pltpu.make_async_copy(source, target, save_sems.at[len(saved)]))
        saved[-1].start()

    first_small = 2 * rank + 2 * nstate
    load("gated", gated_in, gated)
    load("cotangent", cotangent_in, cotangent)
    load("out_w", w_out, out_w)
    load("normed", normed_in, normed)
    load("coef", coef_in, coef)
    load("spread", spread_in, spread_by)
    load("fold", fold_in, fold_by)
    load("rate", rate_in, rate)
    load("keep", masks_in.at[0], keep)
    load("few", few_in.at[pl.ds(first_small, few.shape[0]), :], few)

    def tile_copies(c, slot):
        cols = pl.ds(pl.multiple_of(c * chunk, chunk), chunk)
        there = pl.ds(pl.multiple_of(slot * total, total), total)
        return [
            pltpu.make_async_copy(gate_in.at[:, cols], decays.at[there, :], tile_sems.at[0, slot]),
            pltpu.make_async_copy(readout_in.at[:, cols], states_all.at[there, :], tile_sems.at[1, slot]),
        ]

    for copy in tile_copies(0, 0):
        copy.start()
    peers.meet()
    ring = Guests(
        peers, (out_wgrad, gate_wgrad), None, (out_held, gate_held), (ring_send, ring_recv)
    )
    loads["gated"].wait()
    loads["cotangent"].wait()
    tn = (((0,), (0,)), ((), ()))
    nt = (((1,), (1,)), ((), ()))

    @pl.loop(0, model // chunk)
    def _(c):
        cols = pl.ds(pl.multiple_of(c * chunk, chunk), chunk)
        value = lax.dot_general(gated[...], cotangent[:, cols], tn, preferred_element_type=F32)
        out_wgrad[:, :, cols] = value.astype(BF16).reshape(size, -1, chunk)

    ring.step(0, 1)
    loads["out_w"].wait()

    @pl.loop(0, width // chunk)
    def _(c):
        cols = pl.ds(pl.multiple_of(c * chunk, chunk), chunk)
        slot = lax.rem(c, 2)

        @pl.when(c + 1 < width // chunk)
        def _():
            for copy in tile_copies(c + 1, 1 - slot):
                copy.start()

        @pl.when(c == 2)
        def _():
            ring.step(0, 2)

        grad[:, cols] = lax.dot_general(cotangent[...], out_w[cols, :], nt, preferred_element_type=F32)
        for copy in tile_copies(c, slot):
            copy.wait()

        @pl.loop(0, total // rows)
        def _(i):
            start = pl.multiple_of(i * rows, rows)
            at = pl.ds(start, rows)
            there = pl.ds(pl.multiple_of(slot * total + start, rows), rows)
            gate, readout, value = decays[there, :], states_all[there, :], grad[at, cols]
            sig = sigmoid(gate)
            grad[at, cols] = value * (gate * sig)
            value = value * readout * (sig * (1.0 + gate * (1.0 - sig)))
            gate_grad[at, cols] = value.astype(BF16)
            for k in range(chunk // LANES):
                nat[k, at, :] = value[:, k * LANES : (k + 1) * LANES]

        for k in range(chunk // LANES):
            lanes = pl.ds(pl.multiple_of(c * chunk + k * LANES, LANES), LANES)
            for s in range(GROUP):
                natural[s * length : (s + 1) * length, lanes] = nat[
                    k, pl.ds(s, length, stride=GROUP), :
                ].astype(BF16)

    save(natural, natural_out)

    def block_copies(t, slot):
        these = pl.ds(pl.multiple_of(t * block_rows, block_rows), block_rows)
        return [
            pltpu.make_async_copy(step_in.at[these, :], step_at.at[slot], block_sems.at[0, slot]),
            pltpu.make_async_copy(act_in.at[these, :], act_at.at[slot], block_sems.at[1, slot]),
            pltpu.make_async_copy(starts_in.at[t], start_at.at[slot], block_sems.at[2, slot]),
        ]

    for copy in block_copies(blocks - 1, (blocks - 1) % 2):
        copy.start()
    loads["normed"].wait()

    @pl.loop(0, width // chunk)
    def _(c):
        cols = pl.ds(pl.multiple_of(c * chunk, chunk), chunk)
        value = lax.dot_general(normed[...], gate_grad[:, cols], tn, preferred_element_type=F32)
        gate_wgrad[:, :, cols] = value.astype(BF16).reshape(size, -1, chunk)

    ring.step(1, 1)
    for name in ("coef", "spread", "fold", "rate", "keep", "few"):
        loads[name].wait()
    pre_low = gated
    skip_at = 6 + nstate
    skip_row = few[...].astype(F32)[skip_at : skip_at + 1]
    carry[...] = jnp.zeros_like(carry)
    sums[...] = jnp.zeros_like(sums)

    def fold(value):
        out = value[:, :LANES]
        for k in range(1, chunk // LANES):
            out = out + value[:, k * LANES : (k + 1) * LANES]
        return out

    def block_keeps(t):
        these = pl.ds(pl.multiple_of(t * block_rows, block_rows), block_rows)
        return [
            pltpu.make_async_copy(pre_low.at[these, :], pre_low_out.at[these, :], block_saves.at[0, t]),
            pltpu.make_async_copy(grad.at[these, :], direct_out.at[these, :], block_saves.at[1, t]),
        ]

    @pl.loop(0, blocks)
    def _(turn):
        t = blocks - 1 - turn
        slot = lax.rem(t, 2)
        for tick, which, number in ((0, 0, 3), (1, 1, 2), (3, 0, 4), (4, 1, 3), (6, 1, 4)):

            @pl.when(turn == tick)
            def _(which=which, number=number):
                ring.step(which, number)

        @pl.when(t > 0)
        def _():
            for copy in block_copies(t - 1, 1 - slot):
                copy.start()

        base = pl.multiple_of(t * block_rows, block_rows)
        these = pl.ds(base, block_rows)
        wide[...] = jnp.dot(coef[these, :], spread_by[...], preferred_element_type=F32)
        for copy in block_copies(t, slot):
            copy.wait()

        for c in range(width // chunk):
            cols = slice(c * chunk, (c + 1) * chunk)

            def entry(i, n):
                return pl.ds(pl.multiple_of((i * nstate + n) * GROUP, GROUP), GROUP)

            def advance(i, states):
                here = at_time(i)
                at = pl.ds(pl.multiple_of(base + i * GROUP, GROUP), GROUP)
                step = step_at[slot, here, cols]
                drive = jnp.where(tiled(keep[at, :], chunk) > 0.5, step, FAR)
                inflow = step * act_at[slot, here, cols]
                now = []
                for n in range(nstate):
                    write = tiled(wide[here, n * LANES : (n + 1) * LANES], chunk)
                    decay = jnp.exp2(drive * rate[n, :, cols])
                    decays[entry(i, n), :] = decay
                    states_all[entry(i, n), :] = states[n]
                    now.append(decay * states[n] + write * inflow)
                return tuple(now)

            start = tuple(start_at[slot, n, :, cols] for n in range(nstate))
            states = lax.fori_loop(0, BLOCK, advance, start, unroll=2)
            for n in range(nstate):
                states_all[entry(BLOCK, n), :] = states[n]

            def retreat(i, carried):
                i = BLOCK - 1 - i
                here = at_time(i)
                at = pl.ds(pl.multiple_of(base + i * GROUP, GROUP), GROUP)
                step, act, flow = step_at[slot, here, cols], act_at[slot, here, cols], grad[at, cols]
                inflow = step * act
                size_grad, direct = jnp.zeros_like(step), jnp.zeros_like(step)
                now = []
                for n in range(nstate):
                    tile_w = slice(n * LANES, (n + 1) * LANES)
                    tile_r = slice((nstate + n) * LANES, (nstate + n + 1) * LANES)
                    state_grad = tiled(wide[here, tile_r], chunk) * flow + carried[n]
                    passed = decays[entry(i, n), :] * state_grad
                    through = passed * states_all[entry(i, n), :]
                    size_grad = size_grad + rate[n, :, cols] * through
                    direct = direct + state_grad * tiled(wide[here, tile_w], chunk)
                    sums[n, :, cols] += step * through
                    write_part = fold(state_grad * inflow)
                    read_part = fold(flow * states_all[entry(i + 1, n), :])
                    if c == 0:
                        parts[here, tile_w] = write_part
                        parts[here, tile_r] = read_part
                    else:
                        parts[here, tile_w] += write_part
                        parts[here, tile_r] += read_part
                    now.append(passed)
                sizes[here, cols] = LN2 * size_grad + act * direct
                grad[at, cols] = step * direct + skip_row[:, cols] * flow
                sums[nstate, :, cols] += flow * act
                return tuple(now)

            start = tuple(carry[n, :, cols] for n in range(nstate))
            carried = lax.fori_loop(0, BLOCK, retreat, start, unroll=2)
            for n in range(nstate):
                carry[n, :, cols] = carried[n]

        step = step_at[slot]
        series = step * (1.0 - step * (0.5 - step * (1.0 / 6.0)))
        pre_grad = sizes[...] * jnp.where(step < 0.01, series, 1.0 - jnp.exp(-step))
        pre_low[these, :] = pre_grad.astype(BF16)
        tally = pre_grad[:GROUP]
        for i in range(1, BLOCK):
            tally = tally + pre_grad[i * GROUP : (i + 1) * GROUP]
        sums[nstate + 1] += tally
        high = parts[...].astype(BF16)
        low = (parts[...] - high.astype(F32)).astype(BF16)
        coef_grad[these, :] = jnp.dot(high, fold_by[...], preferred_element_type=F32) + jnp.dot(
            low, fold_by[...], preferred_element_type=F32
        )
        for copy in block_keeps(t):
            copy.start()

    save(coef_grad, coef_grad_out)
    save(sums, sums_out)
    ring.totals = (out_total, gate_total)
    ring.finish()
    for t in range(blocks):
        for copy in block_keeps(t):
            copy.wait()
    for copy in saved:
        copy.wait()


def backward(size, nstate, rank, arrays):
    gated, cotangent, w_out, readout, gate, normed, step, act, coef, starts, masks, rate, spread_by, fold_by, few = arrays
    total, width = gated.shape
    model = normed.shape[1]
    inside, anywhere = pl.BlockSpec(memory_space=pltpu.VMEM), pl.BlockSpec(memory_space=pl.ANY)
    shape, dma = jax.ShapeDtypeStruct, pltpu.SemaphoreType.DMA
    low, rows, full = shape((total, width), BF16), shape((total, model), BF16), shape((total, width), F32)
    out_unit, gate_unit = (width // size, model), (model // size, width)
    half = size // 2
    block = shape((2, BLOCK * GROUP, width), F32)
    state = shape((nstate, GROUP, width), F32)
    tally = shape((nstate + 2, GROUP, width), F32)
    wide = shape((BLOCK * GROUP, 2 * nstate * LANES), F32)
    thin = shape((total, LANES), F32)
    scratch = [
        low,
        rows,
        shape(w_out.shape, BF16),
        rows,
        shape((size,) + out_unit, BF16),
        shape((size,) + gate_unit, BF16),
        shape((2, half) + out_unit, BF16),
        shape((2, half) + gate_unit, BF16),
        low,
        low,
        full,
        shape((2, total, LANES), F32),
        block,
        block,
        shape((2,) + state.shape, F32),
        wide,
        shape(((BLOCK + 1) * nstate * GROUP, 256), F32),
        shape((BLOCK * nstate * GROUP, 256), F32),
        wide,
        shape((BLOCK * GROUP, width), F32),
        tally,
        state,
        shape(coef.shape, BF16),
        shape(spread_by.shape, BF16),
        shape(fold_by.shape, BF16),
        state,
        thin,
        shape((few.shape[0] - 2 * rank - 2 * nstate, width), BF16),
        thin,
    ]
    blocks = total // (BLOCK * GROUP)
    sems = [(10,), (2, 2), (3, 2), (3,), (2, blocks), (2, 2, half, 2), (2, 2, half, 2)]
    return pl.pallas_call(
        functools.partial(backward_kernel, size, nstate, rank),
        in_specs=[anywhere] * len(arrays),
        out_specs=[anywhere] * 5 + [inside] * 2,
        out_shape=[low, low, full, thin, tally, shape(out_unit, BF16), shape(gate_unit, BF16)],
        scratch_shapes=[pltpu.VMEM(x.shape, x.dtype) for x in scratch] + [dma(n) for n in sems],
        compiler_params=pltpu.CompilerParams(
            collective_id=3, has_side_effects=True, vmem_limit_bytes=62 * 1024 * 1024
        ),
        cost_estimate=cost(6 * total * width * model, 200 * total * width),
        name="backward",
    )(*arrays)


def finish_kernel(
    size, rank, nstate,
    pre_low_in, coef_in, direct_in, inner_in, act_low_in, step_low_in, masks_in, few_in, normed_in, w_inner, w_gate,
    gate_grad_in, gated_in, w_out, sums_in, out_total, gate_total,
    inner_pieces, gate_pieces, out_pieces, small_pieces, out_sum, norm_sum,
    pre_low, part, nat, got_near, to_across, got_across, shared, low_grad, act_low, step_low, masks, few, normed, gate_grad,
    gated, inner, direct, grad, wgrad, held, small, small_low, small_held, out_w, out_parts,
    out_pair, norm_pair, out_far, norm_far, w_tiles, total_at, sums,
    load_sems, tile_sems, w_sems, near_send, near_recv, pair_send, pair_recv, ring_send, ring_recv, few_send, few_recv,
    piece_send, piece_recv, own_sems,
):
    peers = Peers(size)
    half = peers.half
    total, width = pre_low.shape
    model = normed.shape[1]
    length = total // GROUP
    batches = GROUP // COPIES
    quarter = total // COPIES
    chunk, rows, pad = 256, 64, 3 * GROUP
    tiles = width // chunk
    slab = held.shape[2]
    sent, loads = [], {}

    def load(name, source, target):
        loads[name] = pltpu.make_async_copy(source, target, load_sems.at[len(loads)])
        loads[name].start()

    def send(*copy):
        moving = remote(*copy)
        moving.start()
        sent.append(moving)

    def tile_copies(c, slot):
        cols = slice(c * chunk, (c + 1) * chunk)
        return [
            pltpu.make_async_copy(inner_in.at[:, cols], inner.at[slot, pl.ds(pad, total), :], tile_sems.at[0, slot]),
            pltpu.make_async_copy(direct_in.at[:, cols], direct.at[slot], tile_sems.at[1, slot]),
        ]

    load("pre", pre_low_in, pre_low)
    load("few", few_in, few)
    load("coef", coef_in, part.at[1])
    load("step", step_low_in, step_low)
    load("gated", gated_in, gated)
    load("out_w", w_out, out_w)
    load("act", act_low_in, act_low)
    load("masks", masks_in, masks.at[:, pl.ds(0, total), :])
    load("normed", normed_in, normed)
    load("sums", sums_in, sums)
    load("gate", gate_grad_in, gate_grad)
    for copy in tile_copies(0, 0):
        copy.start()
    peers.meet()

    near = (near_send, near_recv)

    def come(target, index, peer):
        remote(target, target, near, index, peer).wait_recv()

    first_stride = rank + 2 * nstate
    loads["pre"].wait()
    loads["few"].wait()
    part[0] = lax.dot_general(
        pre_low[...], few[first_stride : first_stride + rank, :], (((1,), (1,)), ((), ())),
        preferred_element_type=F32,
    )
    loads["coef"].wait()
    for j in range(2):
        for s in range(GROUP):
            nat[j, s * length : (s + 1) * length, :] = part[j, pl.ds(s, length, stride=GROUP), :]
    for i in range(2):
        send(nat.at[:, pl.ds((2 * i + 1) * quarter, quarter), :], got_near.at[i], near, i, peers.core)
    near_sends = list(sent)
    loads["step"].wait()
    small[first_stride : first_stride + rank, :] = lax.dot_general(
        step_low[...], pre_low[...], (((0,), (0,)), ((), ())), preferred_element_type=F32
    )
    for i in range(2):
        come(got_near.at[i], i, peers.core)
    to_across[...] = nat[:, 2 * quarter : 3 * quarter, :] + got_near[1]
    send(to_across, got_across, near, 2, peers.across)
    loads["gated"].wait()
    loads["out_w"].wait()

    def out_tiles(first, count):
        @pl.loop(first, first + count)
        def _(c):
            cols = pl.ds(pl.multiple_of(c * chunk, chunk), chunk)
            out_parts[:, cols] = jnp.dot(gated[...], out_w[:, cols], preferred_element_type=F32).astype(BF16)

    out_tiles(0, model // chunk // 2)
    come(got_across, 2, peers.across)
    mine = nat[:, :quarter, :] + got_near[0] + got_across[...]
    for j in range(2):
        shared[0, j] = mine[j].astype(BF16)
    send(shared.at[0], shared.at[2], near, 3, peers.across)
    send(shared.at[0], shared.at[1], near, 4, peers.core)
    out_tiles(model // chunk // 2, model // chunk // 2)
    come(shared.at[2], 3, peers.across)
    send(shared.at[2], shared.at[3], near, 5, peers.core)
    come(shared.at[1], 4, peers.core)
    come(shared.at[3], 5, peers.core)
    for copy in near_sends:
        copy.wait_send()
    for k in range(COPIES):
        for b in range(batches):
            for j in range(2):
                part[j, pl.ds(k * batches + b, length, stride=GROUP), :] = shared[
                    k, j, b * length : (b + 1) * length, :
                ].astype(F32)
    for j in range(2):
        low_grad[j] = part[j].astype(BF16)

    pair_sems, piece_sems = (pair_send, pair_recv), (piece_send, piece_recv)
    keeps = []

    def of_copy(ref, k):
        return ref.at[pl.ds(k * quarter, quarter), :]

    def exchange(index, parts, pair):
        for i in range(2):
            send(of_copy(parts, 2 * i + 1), pair.at[i], pair_sems, 3 * index + i, peers.core)

    def exchange_far(index, parts, pair, far):
        for i in range(2):
            remote(pair.at[i], pair.at[i], pair_sems, 3 * index + i, peers.core).wait_recv()
        there = of_copy(parts, 2)
        there[...] = (there[...].astype(F32) + pair[1].astype(F32)).astype(BF16)
        send(there, far, pair_sems, 3 * index + 2, peers.across)

    def exchanged(index, parts, pair, far):
        remote(far, far, pair_sems, 3 * index + 2, peers.across).wait_recv()
        return of_copy(parts, 0)[...].astype(F32) + pair[0].astype(F32) + far[...].astype(F32)

    def give(index, own, pieces):
        keeps.append(pltpu.make_async_copy(own, pieces[0], own_sems.at[index]))
        keeps[-1].start()
        send(own, pieces[2], piece_sems, (index, 0), peers.across)
        send(own, pieces[1], piece_sems, (index, 1), peers.core)

    def pass_on(index, pieces):
        remote(pieces[2], pieces[2], piece_sems, (index, 0), peers.across).wait_recv()
        send(pieces[2], pieces[3], piece_sems, (index, 2), peers.core)

    def given(index, pieces):
        for k, which in ((1, 1), (3, 2)):
            remote(pieces[k], pieces[k], piece_sems, (index, which), peers.core).wait_recv()

    def every(ref, *at):
        return [ref.at[(k, *at)] for k in range(COPIES)]

    exchange(0, out_parts, out_pair)
    give(0, out_total, every(out_pieces))
    give(1, gate_total, every(gate_pieces))

    loads["act"].wait()
    for j, n in ((0, rank), (1, 2 * nstate)):
        weights = lax.dot_general(
            low_grad[j], act_low[...], (((0,), (0,)), ((), ())), preferred_element_type=F32
        )
        small[j * rank : j * rank + n, :] = weights[:n]

    inner_grad, natural = gated, pre_low
    loads["masks"].wait()
    loads["normed"].wait()
    masks[:, total:, :] = jnp.zeros((3, pad, LANES), F32)
    grad[total:, :] = jnp.zeros((pad, chunk), F32)
    for slot in range(2):
        inner[slot, :pad, :] = jnp.zeros((pad, chunk), F32)
    first_tap = first_stride + rank
    ring_sems, few_sems = (ring_send, ring_recv), (few_send, few_recv)

    def block_rows(member, part_of=None):
        start = pl.multiple_of(member * slab, slab)
        if part_of is None:
            return pl.ds(start, slab)
        return pl.ds(start + part_of * (slab // 2), slab // 2)

    def owner(way, step):
        away = half + 1 - step
        return peers.at(away if way == 0 else -away)

    def landing(way, step, c):
        there = held.at[way, step - 1, :, slice(c * chunk, (c + 1) * chunk)]
        return there.at[pl.ds(way * (slab // 2), slab // 2), :] if step == 1 else there

    def arrive(way, step, c):
        there = landing(way, step, c)
        remote(there, there, ring_sems, (way, step - 1, c), peers.ring[way]).wait_recv()

    def ring_step(step, c):
        cols = slice(c * chunk, (c + 1) * chunk)
        for way in range(2):
            member = owner(way, step)
            if step == 1:
                source = wgrad.at[block_rows(member, way), cols]
            else:
                arrive(way, step - 1, c)
                source = held.at[way, step - 2, :, cols]
                if step == 2:
                    here, other = (slice(w * (slab // 2), (w + 1) * (slab // 2)) for w in (way, 1 - way))
                    source[other, :] = wgrad[block_rows(member, 1 - way), cols]
                    source[here, :] = (
                        source[here, :].astype(F32) + wgrad[block_rows(member, way), cols].astype(F32)
                    ).astype(BF16)
                else:
                    source[...] = (
                        source[...].astype(F32) + wgrad[block_rows(member), cols].astype(F32)
                    ).astype(BF16)
            send(source, landing(way, step, c), ring_sems, (way, step - 1, c), peers.ring[way])

    def fold_rows(value):
        out = value[:GROUP]
        for i in range(1, rows // GROUP):
            out = out + value[i * GROUP : (i + 1) * GROUP]
        return out

    for c in range(tiles):
        cols, slot = slice(c * chunk, (c + 1) * chunk), c % 2
        if c + 1 < tiles:
            for copy in tile_copies(c + 1, 1 - slot):
                copy.start()
        for copy in tile_copies(c, slot):
            copy.wait()
        here, there = inner.at[slot], direct.at[slot]
        there[...] += jnp.dot(low_grad[0], few[:rank, cols], preferred_element_type=F32) + jnp.dot(
            low_grad[1], few[rank : rank + LANES, cols], preferred_element_type=F32
        )
        tap = [few[first_tap : first_tap + 16, cols].astype(F32)[i : i + 1] for i in range(5)]

        def back(i, tallies):
            start = pl.multiple_of(i * rows, rows)
            at = pl.ds(start, rows)
            now = here[pl.ds(pad + start, rows), :]
            earlier = [
                here[pl.ds(pad - shift * GROUP + start, rows), :] * tiled(masks[shift - 1, at, :], chunk)
                for shift in range(1, 4)
            ]
            value = tap[4] + tap[3] * now
            for shift in range(1, 4):
                value = value + tap[3 - shift] * earlier[shift - 1]
            sig = sigmoid(value)
            flow = there[at, :] * (sig * (1.0 + value * (1.0 - sig)))
            grad[at, :] = flow
            terms = [flow * e for e in earlier[::-1]] + [flow * now, flow]
            return tuple(tally + fold_rows(term) for tally, term in zip(tallies, terms))

        zero = jnp.zeros((GROUP, chunk), F32)
        tallies = lax.fori_loop(0, total // rows, back, (zero,) * 5)
        for i, tally in enumerate(tallies):
            small[first_tap + i : first_tap + i + 1, cols] = jnp.sum(tally, axis=0, keepdims=True)

        @pl.loop(0, total // rows)
        def _(i):
            start = pl.multiple_of(i * rows, rows)
            at = pl.ds(start, rows)
            value = tap[3] * grad[at, :]
            for shift in range(1, 4):
                after_it = pl.ds(start + shift * GROUP, rows)
                value = value + tap[3 - shift] * (
                    grad[after_it, :] * tiled(masks[shift - 1, after_it, :], chunk)
                )
            inner_grad[at, cols] = value.astype(BF16)
            for k in range(chunk // LANES):
                nat[k, at, :] = value[:, k * LANES : (k + 1) * LANES]

        for k in range(chunk // LANES):
            lanes = slice(c * chunk + k * LANES, c * chunk + (k + 1) * LANES)
            for s in range(GROUP):
                natural[s * length : (s + 1) * length, lanes] = nat[
                    k, pl.ds(s, length, stride=GROUP), :
                ].astype(BF16)
        wgrad[:, cols] = lax.dot_general(
            normed[...], inner_grad[:, cols], (((0,), (0,)), ((), ())), preferred_element_type=F32
        ).astype(BF16)
        ring_step(1, c)
        if c == 1:
            exchange_far(0, out_parts, out_pair, out_far)
        if c >= 2:
            ring_step(2, c - 2)

    loads["sums"].wait()
    at = first_tap + 5
    small[at : at + 1, :] = jnp.sum(sums[nstate + 1], axis=0, keepdims=True)
    decays = few[first_tap : first_tap + 32, :].astype(F32)
    for n in range(nstate):
        small[at + 1 + n : at + 2 + n, :] = -jnp.exp(decays[6 + n : 7 + n]) * jnp.sum(
            sums[n], axis=0, keepdims=True
        )
    at = at + 1 + nstate
    small[at : at + 1, :] = jnp.sum(sums[nstate], axis=0, keepdims=True)
    small[at + 1 :, :] = jnp.zeros((small.shape[0] - at - 1, width), F32)
    small_low[...] = small[...].astype(BF16)
    few_half = small.shape[0] // 2

    def few_columns(member):
        return pl.ds(pl.multiple_of(member * LANES, LANES), LANES)

    def few_landing(way, step):
        there = small_held.at[way, step - 1]
        return there.at[pl.ds(way * few_half, few_half), :] if step == 1 else there

    def few_arrive(way, step):
        there = few_landing(way, step)
        remote(there, there, few_sems, (way, step - 1), peers.ring[way]).wait_recv()

    def few_step(step):
        for way in range(2):
            columns = few_columns(owner(way, step))
            here, other = (slice(w * few_half, (w + 1) * few_half) for w in (way, 1 - way))
            if step == 1:
                source = small_low.at[pl.ds(way * few_half, few_half), columns]
            else:
                few_arrive(way, step - 1)
                source = small_held.at[way, step - 2]
                if step == 2:
                    source[other, :] = small_low[other, columns]
                    source[here, :] = (
                        source[here, :].astype(F32) + small_low[here, columns].astype(F32)
                    ).astype(BF16)
                else:
                    source[...] = (source[...].astype(F32) + small_low[:, columns].astype(F32)).astype(BF16)
            send(source, few_landing(way, step), few_sems, (way, step - 1), peers.ring[way])

    loads["gate"].wait()
    norm_parts = out_w

    def w_copies(n, slot):
        these = pl.ds(pl.multiple_of(n * chunk, chunk), chunk)
        return [
            pltpu.make_async_copy(w.at[these, :], w_tiles.at[slot, i], w_sems.at[i, slot])
            for i, w in enumerate((w_inner, w_gate))
        ]

    w_count = model // chunk

    def norm_tiles(first, count):
        @pl.loop(first, first + count)
        def _(n):
            slot = lax.rem(n, 2)

            @pl.when(n + 1 < w_count)
            def _():
                for copy in w_copies(n + 1, 1 - slot):
                    copy.start()

            for copy in w_copies(n, slot):
                copy.wait()
            nt = (((1,), (1,)), ((), ()))
            value = lax.dot_general(natural[...], w_tiles[slot, 0], nt, preferred_element_type=F32)
            value += lax.dot_general(gate_grad[...], w_tiles[slot, 1], nt, preferred_element_type=F32)
            norm_parts[:, pl.ds(pl.multiple_of(n * chunk, chunk), chunk)] = value.astype(BF16)

    few_step(1)
    for copy in w_copies(0, 0):
        copy.start()
    for i in range(2):
        norm_tiles(i, 1)
        ring_step(2, 2 + i)
    few_step(2)
    for i in range(4):
        norm_tiles(2 + i, 1)
        ring_step(3, i)
    few_step(3)
    norm_tiles(6, w_count - 6)
    own_rows = block_rows(peers.member)
    owns = [
        pltpu.make_async_copy(w_inner.at[own_rows, :], w_tiles.at[0, 0], w_sems.at[0, 0]),
        pltpu.make_async_copy(w_gate.at[own_rows, :], w_tiles.at[0, 1], w_sems.at[1, 0]),
        pltpu.make_async_copy(gate_total, w_tiles.at[1, 0], w_sems.at[0, 1]),
    ]
    for copy in owns:
        copy.start()
    exchange(1, norm_parts, norm_pair)
    ring_step(4, 0)
    ring_step(4, 1)
    exchange_far(1, norm_parts, norm_pair, norm_far)
    ring_step(4, 2)
    ring_step(4, 3)
    few_step(4)
    for index, pieces in ((0, out_pieces), (1, gate_pieces)):
        pass_on(index, every(pieces))
    out_sum[...] = exchanged(0, out_parts, out_pair, out_far)

    def cols_of(c):
        return slice(c * chunk, (c + 1) * chunk)

    def inner_views(c):
        return [inner_pieces.at[k, :, cols_of(c)] for k in range(COPIES)]

    own_block = block_rows(peers.member)
    for c in range(tiles):
        for way in range(2):
            arrive(way, half, c)
        value = wgrad[own_block, cols_of(c)].astype(F32)
        for way in range(2):
            value = value + held[way, half - 1, :, cols_of(c)].astype(F32)
        total_at[:, cols_of(c)] = value.astype(BF16)
        give(3 + c, total_at.at[:, cols_of(c)], inner_views(c))
    for way in range(2):
        few_arrive(way, half)
    value = small_low[:, few_columns(peers.member)].astype(F32)
    for way in range(2):
        value = value + small_held[way, half - 1].astype(F32)
    small_total = small_pieces.at[0]
    small_total[...] = value.astype(BF16)
    for copy in owns:
        copy.wait()
    value = total_at[...].astype(F32) * w_tiles[0, 0].astype(F32)
    value = value + w_tiles[1, 0].astype(F32) * w_tiles[0, 1].astype(F32)
    high = value.astype(BF16)
    low = (value - high.astype(F32)).astype(BF16)
    ones = jnp.ones((GROUP, width), BF16)
    nt = (((1,), (1,)), ((), ()))
    value = lax.dot_general(ones, high, nt, preferred_element_type=F32) + lax.dot_general(
        ones, low, nt, preferred_element_type=F32
    )
    gain_at = first_tap + 7 + nstate
    last = small_total[gain_at - gain_at % 16 :, :].astype(F32)
    line = lax.broadcasted_iota(jnp.int32, last.shape, 0) + (gain_at - gain_at % 16)
    for i in range(slab // LANES):
        last = jnp.where(line == gain_at + i, value[0:1, i * LANES : (i + 1) * LANES], last)
    small_total[gain_at - gain_at % 16 :, :] = last.astype(BF16)
    send(small_total, small_pieces.at[2], piece_sems, (2, 0), peers.across)
    send(small_total, small_pieces.at[1], piece_sems, (2, 1), peers.core)
    norm_sum[...] = exchanged(1, norm_parts, norm_pair, norm_far)
    for c in range(tiles):
        pass_on(3 + c, inner_views(c))
    pass_on(2, every(small_pieces))
    for index, pieces in ((0, every(out_pieces)), (1, every(gate_pieces)), (2, every(small_pieces))):
        given(index, pieces)
    for c in range(tiles):
        given(3 + c, inner_views(c))
    for copy in keeps:
        copy.wait()
    for moving in sent[len(near_sends) :]:
        moving.wait_send()


def finish(size, rank, nstate, arrays, small_rows):
    (pre_low, coef, direct, inner, act_low, step_low, masks, few, normed) = arrays[:9]
    total, width = pre_low.shape
    model = normed.shape[1]
    out_total, gate_total = arrays[-2:]
    slab = gate_total.shape[0]
    quarter, half = total // COPIES, size // 2
    inside, anywhere = pl.BlockSpec(memory_space=pltpu.VMEM), pl.BlockSpec(memory_space=pl.ANY)
    shape, dma = jax.ShapeDtypeStruct, pltpu.SemaphoreType.DMA
    low = shape((total, width), BF16)
    wide = shape((total, model), BF16)
    pair = shape((2, quarter, model), BF16)
    far = shape((quarter, model), BF16)
    sums = arrays[-3]
    padded = total + 3 * GROUP
    scratch = [
        low,
        shape((2, total, LANES), F32),
        shape((2, total, LANES), F32),
        shape((2, 2, quarter, LANES), F32),
        shape((2, quarter, LANES), F32),
        shape((2, quarter, LANES), F32),
        shape((COPIES, 2, quarter, LANES), BF16),
        shape((2, total, LANES), BF16),
        low,
        shape(step_low.shape, BF16),
        shape((3, padded, LANES), F32),
        shape(few.shape, BF16),
        wide,
        low,
        low,
        shape((2, padded, 256), F32),
        shape((2, total, 256), F32),
        shape((padded, 256), F32),
        shape((size * slab, width), BF16),
        shape((2, half, slab, width), BF16),
        shape((small_rows, width), F32),
        shape((small_rows, width), BF16),
        shape((2, half, small_rows, LANES), BF16),
        shape((max(width, total), model), BF16),
        wide,
        pair,
        pair,
        far,
        far,
        shape((2, 2, 256, width), BF16),
        shape((slab, width), BF16),
        shape(sums.shape, F32),
    ]
    tiles = width // 256
    sems = [(11,), (2, 2), (2, 2)] + [(6,)] * 2 + [(6,)] * 2 + [(2, half, tiles)] * 2 + [(2, half)] * 2
    sems += [(3 + tiles, 3)] * 2 + [(3 + tiles,)]
    return pl.pallas_call(
        functools.partial(finish_kernel, size, rank, nstate),
        in_specs=[anywhere] * len(arrays),
        out_specs=[anywhere] * 3 + [inside] * 3,
        out_shape=[
            shape((COPIES, slab, width), BF16),
            shape((COPIES, slab, width), BF16),
            shape((COPIES,) + out_total.shape, BF16),
            shape((COPIES, small_rows, LANES), BF16),
            shape((quarter, model), F32),
            shape((quarter, model), F32),
        ],
        scratch_shapes=[pltpu.VMEM(x.shape, x.dtype) for x in scratch] + [dma(n) for n in sems],
        compiler_params=pltpu.CompilerParams(
            collective_id=2, has_side_effects=True, vmem_limit_bytes=62 * 1024 * 1024
        ),
        cost_estimate=cost(10 * total * width * model, 100 * total * width),
        name="finish",
    )(*arrays)


def place_kernel(
    sizes, copy_ref, inner_ref, gate_ref, out_ref, small_ref, out_sum_ref, norm_ref, tokens_ref, grads_ref, few_ref,
    entry_ref, out_proj_ref, select_ref, stride_ref, taps_ref, decay_ref, rows_ref, block_out_ref, input_grad_ref,
):
    copy = copy_ref[0]
    width = inner_ref.shape[2]
    for k in range(COPIES):
        for side, ref in enumerate((inner_ref, gate_ref)):
            for f in range(width // LANES):
                start = (side * (width // LANES) + f) * COPIES * LANES + (copy ^ k) * LANES
                entry_ref[:, pl.ds(pl.multiple_of(start, LANES), LANES)] = ref[
                    k, :, f * LANES : (f + 1) * LANES
                ].astype(F32)
        out_proj_ref[copy ^ k] = out_ref[k].astype(F32)

    @pl.when(pl.program_id(0) == 0)
    def _():
        for k in range(COPIES):
            piece = small_ref[k].astype(F32)
            at = pl.ds(pl.multiple_of((copy ^ k) * LANES, LANES), LANES)
            stride_ref[at, :] = piece[sizes[0] : sizes[0] + sizes[1]].T
            start = 0
            for size, ref in zip(sizes, (select_ref, None, taps_ref, None, None, decay_ref)):
                if ref is not None:
                    ref[:, at] = piece[start : start + size]
                start += size
            first = start - start % 8
            low_row = sizes[0] + sizes[1]
            rows_ref[:, at] = jnp.concatenate(
                [piece[low_row : low_row + 8], piece[first : first + 8]], axis=0
            )

    tokens = tokens_ref[...].astype(F32)
    block_out_ref[...] = (tokens + out_sum_ref[...]).astype(BF16)
    gains = few_ref[...].astype(F32)
    start = sum(sizes) - (sizes[0] + sizes[1])
    gain = jnp.concatenate(
        [
            gains[start + i : start + i + 1, f * LANES : (f + 1) * LANES]
            for f in range(width // LANES)
            for i in range(tokens.shape[1] // width)
        ],
        axis=1,
    )
    scale = lax.rsqrt(jnp.mean(tokens * tokens, axis=-1, keepdims=True) + EPS)
    scaled = norm_ref[...] * gain
    lean = jnp.mean(scaled * tokens, axis=-1, keepdims=True)
    input_grad_ref[...] = (
        grads_ref[...].astype(F32) + scale * scaled - tokens * (scale * scale * scale) * lean
    ).astype(BF16)


def place(copy, sizes, inner, gate, out, small, out_sum, norm_sum, tokens, grads, few):
    steps = 4
    _, slab, width = inner.shape
    part, model = out.shape[1:]
    rows = tokens.shape[0]
    share = COPIES * LANES

    def cut_rows(total, columns):
        return pl.BlockSpec((total // steps, columns), lambda i, copy: (i, 0))

    def pieces(total, columns):
        return pl.BlockSpec((COPIES, total // steps, columns), lambda i, copy: (0, i, 0))

    def fixed(*shape):
        return pl.BlockSpec(shape, lambda i, copy: (0,) * len(shape))

    first = sizes[0] + sizes[1]
    last = few.shape[0] - first
    shape = jax.ShapeDtypeStruct
    narrow = [(sizes[0], share), (share, sizes[1]), (sizes[2], share), (sizes[5], share)]
    token_rows = cut_rows(rows, model)
    return pl.pallas_call(
        functools.partial(place_kernel, sizes),
        grid_spec=pltpu.PrefetchScalarGridSpec(
            num_scalar_prefetch=1,
            grid=(steps,),
            in_specs=[pieces(slab, width)] * 2
            + [pieces(part, model), fixed(*small.shape)]
            + [token_rows] * 4
            + [pl.BlockSpec((last, width), lambda i, copy: (first // last, 0))],
            out_specs=[cut_rows(slab, 2 * COPIES * width), pieces(part, model)]
            + [fixed(*n) for n in narrow]
            + [fixed(16, share)]
            + [token_rows] * 2,
        ),
        out_shape=[
            shape((slab, 2 * COPIES * width), F32),
            shape(out.shape, F32),
        ]
        + [shape(n, F32) for n in narrow]
        + [shape((16, share), F32)]
        + [shape(tokens.shape, BF16)] * 2,
        compiler_params=params(),
        cost_estimate=cost(40 * rows * model, 20 * slab * width),
        name="place",
    )(copy, inner, gate, out, small, out_sum, norm_sum, tokens, grads, few)


def on_device(
    tokens, segment_ids, out_grad, norm_gain, in_proj, conv_weight, conv_bias, x_proj,
    step_proj, step_bias, decay_log, skip_gain, out_proj, *, fsdp,
):
    ring = Ring(fsdp)
    copy = lax.axis_index("rep")
    batches, length, model = tokens.shape
    total = COPIES * batches * length
    slab = in_proj.shape[0]
    share = out_proj.shape[0]
    part = share // COPIES
    width = fsdp * part
    rank, nstate = step_proj.shape[1], decay_log.shape[1]
    taps_n = conv_weight.shape[1]
    gains_n = slab // part

    def mine(value):
        return lax.dynamic_slice_in_dim(value, copy * part, part, 0)

    copy_index = copy.astype(jnp.int32).reshape(1)
    aligned = part % LANES == 0
    if not aligned:
        entry = lax.dynamic_index_in_dim(
            in_proj.reshape(slab, 2, fsdp, COPIES, part), copy, 3, keepdims=False
        )
        inner_shard, gate_shard = (entry[:, i].reshape(slab, width) for i in range(2))
    few = jnp.concatenate(
        [
            mine(x_proj).T,
            mine(step_proj).T,
            mine(conv_weight).T,
            mine(conv_bias)[None],
            mine(step_bias)[None],
            mine(decay_log).T,
            mine(skip_gain)[None],
            norm_gain.reshape(gains_n, part),
        ],
        axis=0,
    )
    few = jnp.pad(few, ((0, -few.shape[0] % 16), (0, 0)))
    small_ring = ring.half == 4
    own = [tokens, out_grad, segment_ids[:, 0, :]]
    fused = small_ring and aligned
    if fused:
        out = forward(fsdp, rank, nstate, in_proj, few, *own, out_proj)
        few_all = out["few"].astype(F32)
    else:
        gathers = [Gather(ring, inner_shard), Gather(ring, few)]
        for gather in gathers:
            gather.rest()
        inner_in, few_all = (gather.whole for gather in gathers)
        few_all = jnp.moveaxis(few_all, 0, 1).reshape(-1, width).astype(F32)
        copies = [jnp.stack(rep_gather(value)) for value in own]
        inner_in = inner_in.reshape(model, width)
        values, cotangent, segments = (c.reshape((GROUP,) + c.shape[2:]) for c in copies)

    sizes = [rank + 2 * nstate, rank, taps_n, 1, 1, nstate, 1, gains_n]
    pieces, start = [], 0
    for size in sizes:
        pieces.append(few_all[start : start + size])
        start += size
    select, stride, taps, shift_bias, size_bias, decay, skip, gain = pieces
    select, stride = select.astype(BF16), stride.astype(BF16)
    gain = jnp.moveaxis(gain.reshape(gains_n, fsdp, part), 0, 1).reshape(model)

    def masks_of(segments):
        masks = []
        for shift in range(1, taps_n):
            earlier = jnp.pad(segments, ((0, 0), (shift, 0)), constant_values=-1)[:, :length]
            masks.append((earlier == segments).astype(F32).T.reshape(total, 1))
        return jnp.broadcast_to(jnp.stack(masks), (taps_n - 1, total, LANES))

    tap_rows = jnp.concatenate([taps, shift_bias, jnp.zeros((7 - taps_n, width), F32)])
    side_rows = jnp.concatenate([size_bias, skip, jnp.zeros((6, width), F32)])
    decay_rate = -jnp.exp(decay)

    if fused:
        (
            masks, rate, spread_by, fold_by, normed, cotangent, inner_in, inner, act, act_low, step_low, coef, step,
            starts, gate, readout, gated, gated_natural, gate_in, out_w,
        ) = (
            out[k]
            for k in (
                "masks", "rate", "spread_by", "fold_by", "normed", "cotangent", "inner_in", "inner", "act", "act_low",
                "step_low", "coef", "step", "starts", "gate", "readout", "gated", "gated_natural", "gate_in", "out_w",
            )
        )
    else:
        rate = jnp.broadcast_to((decay_rate * LOG2E)[:, None, :], (nstate, GROUP, width))
        masks, spread_by, fold_by = masks_of(segments), spreader(nstate), folder(nstate)
        normed, cotangent = interleave(values, gain), interleave(cotangent)
        gathers = [Gather(ring, gate_shard), Gather(ring, mine(out_proj))]
        for gather in gathers:
            gather.rest()
        gate_in = gathers[0].whole.reshape(model, width)
        out_w = gathers[1].whole.reshape(width, model)
        inner = dot(normed, inner_in, 1, 0)
        act, act_low = conv_forward(inner, masks, tap_rows)
        half_sums = sum_near(by_copy(to_sequence(dot(act_low, select, 1, 1))))
        projected = to_time(sum_far(half_sums).reshape(total, -1))
        step_low = projected[:, :rank].astype(BF16)
        coef = spread(projected[:, rank:], nstate)
        pre = dot(step_low, stride, 1, 0)
        readout, step, starts = scan_forward(pre, act, coef, spread_by, masks[0], rate, side_rows)
        gate = dot(normed, gate_in, 1, 0)
        gated, gated_natural = gate_forward(readout, gate)
    if fused:
        gate_grad_natural, pre_low, direct, coef_part, sums, *totals = backward(
            fsdp, nstate, rank,
            (
                gated, cotangent, out_w, readout, gate, normed, step, act, coef, starts, masks, rate, spread_by, fold_by,
                out["few"],
            ),
        )
    else:
        out_wgrad = dot(gated, cotangent, 0, 0).astype(BF16).reshape(fsdp, part, model)
        read_grad, gate_grad, gate_grad_natural = gate_backward(dot(cotangent, out_w, 1, 1), readout, gate)
        gate_wgrad = dot(normed, gate_grad, 0, 0).astype(BF16).reshape(fsdp, slab, width)
        pre_low, direct, coef_part, _, sums = scan_backward(
            step, act, read_grad, coef, spread_by, fold_by, masks[0], rate, side_rows, starts
        )
        scatters = [Scatter(ring, out_wgrad), Scatter(ring, gate_wgrad)]
        for scatter in scatters:
            scatter.rest()
        totals = [scatter.total.astype(BF16) for scatter in scatters]
    small_rows = few.shape[0]
    if fused:
        inner_pieces, gate_pieces, out_pieces, small_pieces, out_sum, normed_sum = finish(
            fsdp, rank, nstate,
            (
                pre_low, coef_part, direct, inner, act_low, step_low, masks, out["few"], normed, inner_in, gate_in,
                gate_grad_natural, gated_natural, out_w, sums, *totals,
            ),
            small_rows,
        )
        flat = (batches * length, model)
        entry_all, out_all, select_g, stride_g, taps_g, decay_g, rows_g, block_out, input_grad = place(
            copy_index, sizes[:-1], inner_pieces, gate_pieces, out_pieces, small_pieces, out_sum, normed_sum,
            tokens.reshape(flat), out_grad.reshape(flat), out["few"],
        )
        gain_at = sum(sizes[:-1])
        gain_sum = jnp.sum(small_pieces[:, gain_at : gain_at + gains_n].astype(F32), axis=0).reshape(slab)
        return (
            block_out.reshape(tokens.shape),
            input_grad.reshape(tokens.shape),
            gain_sum / norm_gain.astype(F32),
            entry_all,
            taps_g.T,
            rows_g[taps_n],
            select_g.T,
            stride_g,
            rows_g[taps_n + 1],
            decay_g.T,
            rows_g[8 + (gain_at - 1) % 8],
            out_all.reshape(share, model),
        )
    else:
        low_part = dot(pre_low, stride, 1, 1)
        proj_part = jnp.concatenate([low_part, coef_part[:, : 2 * nstate]], axis=1)
        half_sums = sum_near(by_copy(to_sequence(proj_part)))
        proj_time = to_time(sum_far(half_sums).reshape(total, -1).astype(BF16))
        act_grad = direct + dot(proj_time, select, 1, 0)
        inner_grad, inner_grad_natural, conv_sums = conv_backward(inner, act_grad, masks, tap_rows)
        inner_wgrad = dot(normed, inner_grad, 0, 0).astype(BF16).reshape(fsdp, slab, width)
        small = jnp.concatenate(
            [
                dot(proj_time, act_low, 0, 0),
                dot(step_low, pre_low, 0, 0),
                conv_sums[: taps_n + 1],
                jnp.sum(sums[nstate + 1 :], axis=1),
                decay_rate * jnp.sum(sums[:nstate], axis=1),
                jnp.sum(sums[nstate : nstate + 1], axis=1),
            ],
            axis=0,
        )
        small = jnp.pad(small, ((0, small_rows - small.shape[0]), (0, 0))).astype(BF16)
        small = jnp.moveaxis(small.reshape(-1, fsdp, part), 1, 0)
        grads = dot(inner_grad_natural, inner_in, 1, 1) + dot(gate_grad_natural, gate_in, 1, 1)
        sums_of = []
        for parts in (dot(gated_natural, out_w, 1, 0), grads):
            sums_of.append(rep_scatter_far(*rep_scatter_near(by_copy(parts.astype(BF16)))))
        out_sum, normed_sum = sums_of
        scatters = [Scatter(ring, inner_wgrad), Scatter(ring, small)]
        for scatter in scatters:
            scatter.rest()
        totals = [scatter.total.astype(BF16) for scatter in scatters] + totals
        inner_pieces, small_pieces, out_pieces, gate_pieces = (rep_gather(t) for t in totals)

    block_out = (tokens.astype(F32) + out_sum.reshape(tokens.shape)).astype(BF16)
    normed_grad = normed_sum.reshape(tokens.shape)
    own_values = tokens.astype(F32)
    own_scale = lax.rsqrt(jnp.mean(own_values * own_values, axis=-1, keepdims=True) + EPS)
    scaled = normed_grad * gain
    lean = jnp.mean(scaled * own_values, axis=-1, keepdims=True)
    input_grad = (
        out_grad.astype(F32) + own_scale * scaled - own_values * (own_scale**3) * lean
    ).astype(BF16)

    order = jnp.arange(COPIES) ^ copy
    out_all = jnp.stack(out_pieces)[order].reshape(share, model).astype(F32)
    halves = jnp.stack([jnp.stack(inner_pieces), jnp.stack(gate_pieces)])[:, order]
    halves = halves.reshape(2, COPIES, slab, fsdp, part).astype(F32)
    entry_all = jnp.transpose(halves, (2, 0, 3, 1, 4)).reshape(slab, -1)
    gain_sum = jnp.sum(entry_all * in_proj.astype(F32), axis=1)
    gain_grad = gain_sum / norm_gain.astype(F32)
    small_all = jnp.stack(small_pieces)[order].astype(F32)
    small_all = jnp.moveaxis(small_all, 0, 1).reshape(-1, share)
    out, start = [], 0
    for size in sizes[:-1]:
        out.append(small_all[start : start + size])
        start += size
    select_g, stride_g, taps_g, shift_g, size_g, decay_g, skip_g = out
    return (
        block_out,
        input_grad,
        gain_grad,
        entry_all,
        taps_g.T,
        shift_g[0],
        select_g.T,
        stride_g.T,
        size_g[0],
        decay_g.T,
        skip_g[0],
        out_all,
    )


def solution(mesh):
    tokens = P(None, ("fsdp", "rep"), None)
    rows, row = P("fsdp", None), P("fsdp")
    return jax.shard_map(
        functools.partial(on_device, fsdp=mesh.shape["fsdp"]),
        mesh=mesh,
        in_specs=(tokens, tokens, tokens, row, rows, rows, row, rows, rows, row, rows, row, rows),
        out_specs=(tokens, tokens, row, rows, rows, row, rows, rows, row, rows, row, rows),
        check_vma=False,
    )
```

```python
import functools

import jax
import jax.numpy as jnp
from jax import lax
from jax.experimental import pallas as pl
from jax.experimental.pallas import tpu as pltpu
from jax.sharding import PartitionSpec as P

EPS = 1e-05
BLOCK = 16
LANES = 128
GROUP = 8
COPIES = 4
LOG2E = 1.4426950408889634
LN2 = 0.6931471805599453
FAR = 1e30
F32 = jnp.float32
BF16 = jnp.bfloat16
VMEM_LIMIT = 56 * 1024 * 1024


def dot(left, right, left_dim, right_dim):
    return lax.dot_general(
        left, right, (((left_dim,), (right_dim,)), ((), ())), preferred_element_type=F32
    )


def params():
    return pltpu.CompilerParams(vmem_limit_bytes=VMEM_LIMIT)


def cost(flops, moved):
    return pl.CostEstimate(flops=int(flops), bytes_accessed=int(moved), transcendentals=0)


def blank(shape, dtype):
    return pl.pallas_call(
        lambda ref: None,
        out_shape=jax.ShapeDtypeStruct(shape, dtype),
        out_specs=pl.BlockSpec(memory_space=pl.ANY),
        name="blank",
    )()


def ring_order(size):
    half = size // 2
    return [2 * p if p < half else 2 * (size - 1 - p) + 1 for p in range(size)]


class Ring:
    def __init__(self, size):
        order = ring_order(size)
        place = [0] * size
        for spot, member in enumerate(order):
            place[member] = spot
        self.size, self.half = size, size // 2
        self.order = jnp.array(order, jnp.int32)
        self.spot = jnp.array(place, jnp.int32)[lax.axis_index("fsdp")]
        self.above = [(order[p], order[(p + 1) % size]) for p in range(size)]
        self.below = [(order[p], order[(p - 1) % size]) for p in range(size)]

    def member(self, offset):
        return self.order[(self.spot + offset + self.size) % self.size]

    def up(self, value):
        return lax.ppermute(value, "fsdp", self.above)

    def down(self, value):
        return lax.ppermute(value, "fsdp", self.below)


class Gather:
    def __init__(self, ring, shard):
        self.ring, self.cut = ring, shard.shape[0] // 2
        self.whole = blank((ring.size,) + shard.shape, shard.dtype)
        self.held = (shard, shard)
        self.put(shard, 0)

    def put(self, piece, offset, start=0):
        at = (self.ring.member(offset), jnp.int32(start), jnp.int32(0))
        self.whole = lax.dynamic_update_slice(self.whole, piece[None], at)

    def step(self, number):
        low, high = self.held
        if number == self.ring.half:
            low, high = low[: self.cut], high[self.cut :]
        return self.ring.up(low), self.ring.down(high)

    def take(self, number, got):
        self.held = got
        last = number == self.ring.half
        self.put(got[0], -number)
        self.put(got[1], number, self.cut if last else 0)

    def rest(self):
        def body(number, state):
            whole, low, high = state
            low, high = self.ring.up(low), self.ring.down(high)
            self.whole = whole
            self.put(low, -number)
            self.put(high, number)
            return self.whole, low, high

        self.whole, low, high = lax.fori_loop(1, self.ring.half, body, (self.whole,) + self.held)
        self.held = (low, high)
        self.take(self.ring.half, self.step(self.ring.half))


class Scatter:
    def __init__(self, ring, parts):
        self.ring, self.parts, self.cut = ring, parts, parts.shape[1] // 2
        far = self.own(ring.half)
        self.sent = (far[: self.cut], far[self.cut :])
        self.total = None

    def own(self, offset):
        return lax.dynamic_index_in_dim(self.parts, self.ring.member(offset), 0, keepdims=False)

    def step(self, number):
        return self.ring.up(self.sent[0]), self.ring.down(self.sent[1])

    def take(self, number, got):
        left = self.ring.half - number
        low, high = got
        near_low, near_high = self.own(left), self.own(-left)
        if number == 1:
            low = jnp.concatenate([low, jnp.zeros_like(near_low[self.cut :])])
            high = jnp.concatenate([jnp.zeros_like(near_high[: self.cut]), high])
        if left == 0:
            self.total = near_low.astype(F32) + low.astype(F32) + high.astype(F32)
        else:
            self.sent = (self.add(near_low, low), self.add(near_high, high))

    def add(self, near, got):
        return (near.astype(F32) + got.astype(F32)).astype(near.dtype)

    def rest(self):
        self.take(1, self.step(1))

        def body(number, sent):
            left = self.ring.half - number
            low, high = self.ring.up(sent[0]), self.ring.down(sent[1])
            return self.add(self.own(left), low), self.add(self.own(-left), high)

        self.sent = lax.fori_loop(2, self.ring.half, body, self.sent)
        self.take(self.ring.half, self.step(self.ring.half))


def swap(value, bit):
    return lax.ppermute(value, "rep", [(r, r ^ bit) for r in range(COPIES)])


def rep_gather(value):
    across = swap(value, 2)
    return [value, swap(value, 1), across, swap(across, 1)]


def rep_scatter_near(parts):
    pair = swap(jnp.stack([parts[1], parts[3]]), 1)
    near = parts[0].astype(F32) + pair[0].astype(F32)
    far = parts[2].astype(F32) + pair[1].astype(F32)
    return near, far.astype(parts.dtype)


def rep_scatter_far(near, far):
    return near + swap(far, 2).astype(F32)


def sum_near(parts):
    pair = swap(jnp.stack([parts[1], parts[3]]), 1)
    mine = jnp.stack([parts[0], parts[2]]) + pair
    return mine + swap(jnp.stack([mine[1], mine[0]]), 2)


def sum_far(mine):
    next_to = swap(mine, 1)
    return jnp.stack([mine[0], next_to[0], mine[1], next_to[1]])


def to_time(value):
    return jnp.swapaxes(value.reshape(GROUP, -1, value.shape[-1]), 0, 1).reshape(value.shape)


def to_sequence(value):
    return jnp.swapaxes(value.reshape(-1, GROUP, value.shape[-1]), 0, 1).reshape(value.shape)


def by_copy(value):
    return value.reshape(COPIES, -1, value.shape[-1])


def sigmoid(value):
    return 1.0 / (1.0 + jnp.exp(-value))


def later(value, shift):
    rows = shift * GROUP
    return jnp.concatenate([jnp.zeros_like(value[:rows]), value[:-rows]], axis=0)


def sooner(value, shift):
    rows = shift * GROUP
    return jnp.concatenate([value[rows:], jnp.zeros_like(value[:rows])], axis=0)


def conv_of(inner, masks, taps):
    total = taps[4:5] + taps[3:4] * inner
    for shift in range(1, 4):
        total = total + taps[3 - shift : 4 - shift] * (later(inner, shift) * masks[shift - 1])
    return total


def by_sequence(held, out_ref, value):
    length = value.shape[0] // GROUP
    held[...] = value
    for s in range(GROUP):
        out_ref[s * length : (s + 1) * length, :] = held[
            pl.ds(s, length, stride=GROUP), :
        ].astype(out_ref.dtype)


def conv_kernel(inner_ref, masks_ref, taps_ref, act_ref, low_ref):
    value = conv_of(inner_ref[...], masks_ref, taps_ref[...])
    act = value * sigmoid(value)
    act_ref[...] = act
    low_ref[...] = act.astype(BF16)


def conv_forward(inner, masks, taps):
    rows, width = inner.shape
    tile = pl.BlockSpec((rows, LANES), lambda c: (0, c))
    return pl.pallas_call(
        conv_kernel,
        grid=(width // LANES,),
        in_specs=[
            tile,
            pl.BlockSpec((3, rows, LANES), lambda c: (0, 0, 0)),
            pl.BlockSpec((8, LANES), lambda c: (0, c)),
        ],
        out_specs=[tile, tile],
        out_shape=[
            jax.ShapeDtypeStruct((rows, width), F32),
            jax.ShapeDtypeStruct((rows, width), BF16),
        ],
        compiler_params=params(),
        cost_estimate=cost(30 * rows * width, 10 * rows * width),
        name="conv_forward",
    )(inner, masks, taps)


def conv_back_kernel(inner_ref, grad_ref, masks_ref, taps_ref, out_ref, natural_ref, sums_ref, held):
    inner, taps = inner_ref[...], taps_ref[...]
    value = conv_of(inner, masks_ref, taps)
    gate = sigmoid(value)
    grad = grad_ref[...] * (gate * (1.0 + value * (1.0 - gate)))
    total = taps[3:4] * grad
    sums = [None] * 4 + [jnp.sum(grad, axis=0, keepdims=True)]
    sums[3] = jnp.sum(grad * inner, axis=0, keepdims=True)
    for shift in range(1, 4):
        masked = grad * masks_ref[shift - 1]
        total = total + taps[3 - shift : 4 - shift] * sooner(masked, shift)
        sums[3 - shift] = jnp.sum(masked * later(inner, shift), axis=0, keepdims=True)
    out_ref[...] = total.astype(BF16)
    by_sequence(held, natural_ref, total)
    sums_ref[...] = jnp.concatenate(sums + [jnp.zeros((3, inner.shape[1]), F32)], axis=0)


def conv_backward(inner, grad, masks, taps):
    rows, width = inner.shape
    tile = pl.BlockSpec((rows, LANES), lambda c: (0, c))
    few = pl.BlockSpec((8, LANES), lambda c: (0, c))
    return pl.pallas_call(
        conv_back_kernel,
        grid=(width // LANES,),
        in_specs=[tile, tile, pl.BlockSpec((3, rows, LANES), lambda c: (0, 0, 0)), few],
        out_specs=[tile, tile, few],
        out_shape=[
            jax.ShapeDtypeStruct((rows, width), BF16),
            jax.ShapeDtypeStruct((rows, width), BF16),
            jax.ShapeDtypeStruct((8, width), F32),
        ],
        scratch_shapes=[pltpu.VMEM((rows, LANES), F32)],
        compiler_params=params(),
        cost_estimate=cost(60 * rows * width, 10 * rows * width),
        name="conv_backward",
    )(inner, grad, masks, taps)


def gate_kernel(readout_ref, gate_ref, out_ref, natural_ref, held):
    gate = gate_ref[...]
    gated = readout_ref[...] * (gate * sigmoid(gate))
    out_ref[...] = gated.astype(BF16)
    by_sequence(held, natural_ref, gated)


def gate_forward(readout, gate):
    rows, width = gate.shape
    tile = pl.BlockSpec((rows, LANES), lambda c: (0, c))
    return pl.pallas_call(
        gate_kernel,
        grid=(width // LANES,),
        in_specs=[tile] * 2,
        out_specs=[tile] * 2,
        out_shape=[jax.ShapeDtypeStruct((rows, width), BF16)] * 2,
        scratch_shapes=[pltpu.VMEM((rows, LANES), F32)],
        compiler_params=params(),
        cost_estimate=cost(20 * rows * width, 12 * rows * width),
        name="gate_forward",
    )(readout, gate)


def gate_back_kernel(grad_ref, readout_ref, gate_ref, read_ref, out_ref, natural_ref, held):
    gate, grad = gate_ref[...], grad_ref[...]
    sig = sigmoid(gate)
    read_ref[...] = grad * (gate * sig)
    gate_grad = grad * readout_ref[...] * (sig * (1.0 + gate * (1.0 - sig)))
    out_ref[...] = gate_grad.astype(BF16)
    by_sequence(held, natural_ref, gate_grad)


def gate_backward(grad, readout, gate):
    rows, width = gate.shape
    tile = pl.BlockSpec((rows, LANES), lambda c: (0, c))
    return pl.pallas_call(
        gate_back_kernel,
        grid=(width // LANES,),
        in_specs=[tile] * 3,
        out_specs=[tile] * 3,
        out_shape=[jax.ShapeDtypeStruct((rows, width), F32)]
        + [jax.ShapeDtypeStruct((rows, width), BF16)] * 2,
        scratch_shapes=[pltpu.VMEM((rows, LANES), F32)],
        compiler_params=params(),
        cost_estimate=cost(20 * rows * width, 20 * rows * width),
        name="gate_backward",
    )(grad, readout, gate)


def rows_kernel(scaled, *refs):
    values_ref, out_ref, held = refs[0], refs[-2], refs[-1]
    for s in range(GROUP):
        value = values_ref[s].astype(F32)
        if scaled:
            square = jnp.mean(value * value, axis=-1, keepdims=True)
            value = value * lax.rsqrt(square + EPS) * refs[1][...]
        for k in range(held.shape[0]):
            held[k, pl.ds(s, value.shape[0], stride=GROUP), :] = value[
                :, k * LANES : (k + 1) * LANES
            ]
    for k in range(held.shape[0]):
        out_ref[:, k * LANES : (k + 1) * LANES] = held[k].astype(BF16)


def interleave(values, gain=None):
    _, length, model = values.shape
    extra = [] if gain is None else [gain.reshape(1, model)]
    return pl.pallas_call(
        functools.partial(rows_kernel, gain is not None),
        grid=(length // BLOCK,),
        in_specs=[pl.BlockSpec((GROUP, BLOCK, model), lambda t: (0, t, 0))]
        + [pl.BlockSpec((1, model), lambda t: (0, 0))] * len(extra),
        out_specs=pl.BlockSpec((BLOCK * GROUP, model), lambda t: (t, 0)),
        out_shape=jax.ShapeDtypeStruct((length * GROUP, model), BF16),
        scratch_shapes=[pltpu.VMEM((model // LANES, BLOCK * GROUP, LANES), F32)],
        compiler_params=params(),
        cost_estimate=cost(8 * GROUP * length * model, 4 * GROUP * length * model),
        name="interleave",
    )(values, *extra)


class Peers:
    def __init__(self, size):
        self.size, self.half = size, size // 2
        self.member, self.copy = lax.axis_index("fsdp"), lax.axis_index("rep")
        row, column = lax.div(self.member, 2), lax.rem(self.member, 2)
        self.spot = row * (1 - column) + (size - 1 - row) * column
        side = lax.rem(self.copy, 2)
        self.core = (self.member, self.copy - side + (1 - side))
        self.across = (self.member, lax.rem(self.copy + 2, COPIES))
        self.ring = ((self.at(1), self.copy), (self.at(-1), self.copy))

    def at(self, offset):
        spot = lax.rem(self.spot + (offset + self.size), self.size)
        second = lax.div(spot, self.half)
        return 2 * spot * (1 - second) + (2 * (self.size - 1 - spot) + 1) * second

    def meet(self):
        barrier = pltpu.get_barrier_semaphore()
        peers = (*self.ring, self.core, self.across)
        for peer in peers:
            pl.semaphore_signal(barrier, inc=1, device_id=peer, device_id_type=pl.DeviceIdType.MESH)
        pl.semaphore_wait(barrier, len(peers))


def remote(source, target, sems, index, peer):
    return pltpu.make_async_remote_copy(
        src_ref=source,
        dst_ref=target,
        send_sem=sems[0].at[index],
        recv_sem=sems[1].at[index],
        device_id=peer,
        device_id_type=pl.DeviceIdType.MESH,
    )


def spread(coefs, nstate):
    terms = []
    for _ in range(3):
        term = coefs.astype(BF16)
        terms.append(term)
        coefs = coefs - term.astype(F32)
    joined = jnp.concatenate(terms, axis=1)
    return jnp.pad(joined, ((0, 0), (0, LANES - joined.shape[1])))


def spreader(nstate):
    row = lax.broadcasted_iota(jnp.int32, (LANES, 2 * nstate * LANES), 0)
    tile = lax.broadcasted_iota(jnp.int32, (LANES, 2 * nstate * LANES), 1) // LANES
    return ((row % (2 * nstate) == tile) & (row < 6 * nstate)).astype(BF16)


def folder(nstate):
    tile = lax.broadcasted_iota(jnp.int32, (2 * nstate * LANES, LANES), 0) // LANES
    column = lax.broadcasted_iota(jnp.int32, (2 * nstate * LANES, LANES), 1)
    return (tile == column).astype(BF16)


def tiled(value, width):
    return jnp.concatenate([value] * (width // LANES), axis=1)


def at_time(t):
    return pl.ds(pl.multiple_of(t * GROUP, GROUP), GROUP)


def scan_kernel(
    nstate, chunk, pre_ref, act_ref, coef_ref, spread_ref, keep_ref, rate_ref, row_ref,
    out_ref, step_ref, start_ref, carry_ref, wide,
):
    width = pre_ref.shape[1]

    @pl.when(pl.program_id(0) == 0)
    def _():
        carry_ref[...] = jnp.zeros_like(carry_ref)

    start_ref[0] = carry_ref[...]
    wide[...] = jnp.dot(coef_ref[...], spread_ref[...], preferred_element_type=F32)
    pre = pre_ref[...] + row_ref[0:1]
    step_ref[...] = jnp.maximum(pre, 0.0) + jnp.log1p(jnp.exp(-jnp.abs(pre)))
    for c in range(width // chunk):
        cols = slice(c * chunk, (c + 1) * chunk)

        def advance(t, states):
            at = at_time(t)
            step, act = step_ref[at, cols], act_ref[at, cols]
            drive = jnp.where(tiled(keep_ref[at, :], chunk) > 0.5, step, FAR)
            inflow = step * act
            total = row_ref[1:2, cols] * act
            now = []
            for n in range(nstate):
                write = tiled(wide[at, n * LANES : (n + 1) * LANES], chunk)
                read = tiled(wide[at, (nstate + n) * LANES : (nstate + n + 1) * LANES], chunk)
                state = jnp.exp2(drive * rate_ref[n, :, cols]) * states[n] + write * inflow
                total = total + read * state
                now.append(state)
            out_ref[at, cols] = total
            return tuple(now)

        start = tuple(carry_ref[n, :, cols] for n in range(nstate))
        states = lax.fori_loop(0, BLOCK, advance, start, unroll=4)
        for n in range(nstate):
            carry_ref[n, :, cols] = states[n]


def scan_forward(pre, act, coef, spread_by, keep, rate, rows):
    total, width = pre.shape
    nstate = rate.shape[0]
    size = BLOCK * GROUP
    tile = pl.BlockSpec((size, width), lambda t: (t, 0))
    thin = pl.BlockSpec((size, LANES), lambda t: (t, 0))
    state = pl.BlockSpec((nstate, GROUP, width), lambda t: (0, 0, 0))
    count = total // size
    work = total * width * nstate
    return pl.pallas_call(
        functools.partial(scan_kernel, nstate, 256),
        grid=(count,),
        in_specs=[
            tile,
            tile,
            thin,
            pl.BlockSpec(spread_by.shape, lambda t: (0, 0)),
            thin,
            state,
            pl.BlockSpec((8, width), lambda t: (0, 0)),
        ],
        out_specs=[
            tile,
            tile,
            pl.BlockSpec((1, nstate, GROUP, width), lambda t: (t, 0, 0, 0)),
        ],
        out_shape=[
            jax.ShapeDtypeStruct((total, width), F32),
            jax.ShapeDtypeStruct((total, width), F32),
            jax.ShapeDtypeStruct((total // size, nstate, GROUP, width), F32),
        ],
        scratch_shapes=[
            pltpu.VMEM((nstate, GROUP, width), F32),
            pltpu.VMEM((size, 2 * nstate * LANES), F32),
        ],
        compiler_params=params(),
        cost_estimate=cost(16 * work, 16 * count * size * width),
        name="scan_forward",
    )(pre, act, coef, spread_by, keep, rate, rows)


def start_send(*copy):
    remote(*copy).start()


class Sends:
    def __init__(self):
        self.sent = []

    def __call__(self, *copy):
        moving = remote(*copy)
        moving.start()
        self.sent.append(moving)

    def wait(self):
        for moving in self.sent:
            moving.wait_send()
        self.sent = []


class Pieces:
    def __init__(self, peers, send, sems, own_sems, index, own, view, kept=True):
        self.peers, self.send, self.sems, self.own_sems = peers, send, sems, own_sems
        self.index, self.own, self.view, self.kept = index, own, view, kept

    def keep(self):
        return pltpu.make_async_copy(self.own(), self.view(0), self.own_sems.at[self.index])

    def give(self):
        if self.kept:
            self.keep().start()
        self.send(self.own(), self.view(2), self.sems, (self.index, 0), self.peers.across)
        self.send(self.own(), self.view(1), self.sems, (self.index, 1), self.peers.core)

    def pass_on(self):
        there = self.view(2)
        remote(there, there, self.sems, (self.index, 0), self.peers.across).wait_recv()
        self.send(there, self.view(3), self.sems, (self.index, 2), self.peers.core)

    def come(self):
        for k, which in ((1, 1), (3, 2)):
            there = self.view(k)
            remote(there, there, self.sems, (self.index, which), self.peers.core).wait_recv()
        if self.kept:
            self.keep().wait()

    def sent_all(self):
        for which, target in ((0, 2), (1, 1), (2, 3)):
            there = self.view(target)
            remote(there, there, self.sems, (self.index, which), self.peers.core).wait_send()


class Parts:
    def __init__(self, peers, send, sems, parts, near, far, rows):
        self.peers, self.send, self.sems = peers, send, sems
        self.parts, self.near, self.far, self.rows = parts, near, far, rows

    def block(self, k):
        return self.parts.at[pl.ds(k * self.rows, self.rows), :]

    def start(self):
        for i in range(2):
            self.send(self.block(2 * i + 1), self.near.at[i], self.sems, i, self.peers.core)

    def come_near(self):
        for i in range(2):
            there = self.near.at[i]
            remote(there, there, self.sems, i, self.peers.core).wait_recv()

    def go_far(self, here):
        there = self.block(2)
        there[...] = (there[...].astype(F32) + here[...].astype(F32)).astype(BF16)
        self.send(there, self.far, self.sems, 2, self.peers.across)

    def come(self):
        remote(self.far, self.far, self.sems, 2, self.peers.across).wait_recv()

    def sent_all(self):
        for i in range(2):
            there = self.near.at[i]
            remote(there, there, self.sems, i, self.peers.core).wait_send()
        remote(self.far, self.far, self.sems, 2, self.peers.across).wait_send()


class Shares:
    def __init__(self, peers, shards, wholes, sems):
        self.peers, self.shards, self.wholes, self.sems = peers, shards, wholes, sems
        self.sent = []

    def place(self, which, member, c):
        rows = self.shards[which].shape[0]
        start = pl.multiple_of(member * rows + c * (rows // 2), rows // 2)
        return self.wholes[which].at[pl.ds(start, rows // 2), :]

    def owner(self, way, step):
        return self.peers.at(-step if way == 0 else step)

    def chunks(self, way, step):
        return (way,) if step == self.peers.half else (0, 1)

    def come(self, which, way, step, c):
        there = self.place(which, self.owner(way, step), c)
        remote(there, there, self.sems, (which, way, step - 1, c), self.peers.ring[way]).wait_recv()

    def step(self, which, step):
        for c in range(2):
            for way in range(2):
                if c not in self.chunks(way, step):
                    continue
                target = self.place(which, self.owner(way, step - 1), c)
                source = target
                if step == 1:
                    rows = self.shards[which].shape[0] // 2
                    source = self.shards[which].at[pl.ds(c * rows, rows), :]
                else:
                    self.come(which, way, step - 1, c)
                index = (which, way, step - 1, c)
                remote(source, target, self.sems, index, self.peers.ring[way]).start()

    def finish(self, which):
        half = self.peers.half
        for way in range(2):
            self.come(which, way, half - 1, 1 - way)
            self.come(which, way, half, way)

    def sent_all(self):
        for which in range(len(self.shards)):
            for step in range(1, self.peers.half + 1):
                for way in range(2):
                    for c in self.chunks(way, step):
                        place = self.place(which, self.owner(way, step - 1), c)
                        index = (which, way, step - 1, c)
                        remote(place, place, self.sems, index, self.peers.ring[way]).wait_send()


def softplus(value):
    return jnp.maximum(value, 0.0) + jnp.log1p(jnp.exp(-jnp.abs(value)))


def forward_kernel(
    size, rank, nstate,
    entry, few, tokens, out_grad, segments, out_proj,
    few_out, masks_out, rate_out, spread_out, fold_out, normed_out, cotangent_out, tokens_all, grads_all, segments_all,
    w_in_out, inner_out, act_out, low_out, step_low_out, coef_out, step_out, states_out, gate_out, readout_out,
    gated_out, natural_out, gate_w_out, out_w_out,
    few_all, small, masks, rate, spread_by, fold_by, normed, stage, cotangent, held, seg, inner_shard, gate_shard, w_in,
    inner, act, low, part, nat, got_near, to_across, got_across, shared, step_low, coef, wide, pre, step, readout,
    carry, states_at, gate, gated, natural, gate_w,
    local, states_sems, gate_sems, own_sems, entry_sems, stage_sems, out_sems, seg_sems,
    ring_send, ring_recv, few_send, few_recv, rep_send, rep_recv, near_send, near_recv,
):
    peers = Peers(size)
    total, width = normed.shape[0], w_in.shape[1]
    pad = 3 * GROUP
    chunk = 256
    rows = 64
    length = total // GROUP
    batches = GROUP // COPIES
    half = peers.half
    side_rows = total // COPIES
    saved = []

    def save(source, target):
        copy = pltpu.make_async_copy(source, target, local.at[len(saved)])
        copy.start()
        saved.append(copy)

    picks = []
    for side_of, target in enumerate((inner_shard, gate_shard)):
        for f in range(size):
            source = ((side_of * size + f) * COPIES + peers.copy) * LANES
            picks.append(
                pltpu.make_async_copy(
                    entry.at[:, pl.ds(pl.multiple_of(source, LANES), LANES)],
                    target.at[:, pl.ds(f * LANES, LANES)],
                    entry_sems.at[len(picks)],
                )
            )
    for pick in picks:
        pick.start()
    peers.meet()
    sent = []

    def send(*copy):
        moving = remote(*copy)
        moving.start()
        sent.append(moving)

    rep_sems = (rep_send, rep_recv)

    def of_copy(ref, k):
        return ref.at[k] if ref is segments_all else ref.at[pl.ds(k * batches, batches)]

    def exchange(i, own, everyone):
        send(own, of_copy(everyone, 2), rep_sems, (i, 0), peers.across)
        send(own, of_copy(everyone, 1), rep_sems, (i, 1), peers.core)

    def pass_on(i, everyone):
        far = of_copy(everyone, 2)
        remote(far, far, rep_sems, (i, 0), peers.across).wait_recv()
        send(far, of_copy(everyone, 3), rep_sems, (i, 2), peers.core)

    def exchanged(i, everyone):
        for k, which in ((1, 1), (3, 2)):
            there = of_copy(everyone, k)
            remote(there, there, rep_sems, (i, which), peers.core).wait_recv()

    out_rows = out_proj.shape[0] // COPIES
    out_shard = out_proj.at[pl.ds(pl.multiple_of(peers.copy * out_rows, out_rows), out_rows), :]
    ring = Shares(
        peers, (inner_shard, gate_shard, out_shard), (w_in, gate_w, out_w_out), (ring_send, ring_recv),
    )
    gate_rows = gate_shard.shape[0]
    shard_rows = pl.ds(pl.multiple_of(peers.member * gate_rows, gate_rows), gate_rows)
    own_rows = pl.ds(pl.multiple_of(peers.member * out_rows, out_rows), out_rows)
    own_columns = pl.ds(pl.multiple_of(peers.member * LANES, LANES), LANES)

    few_sems = (few_send, few_recv)
    few_rows = few.shape[0] // 2

    def few_place(way, number, split):
        columns = pl.ds(pl.multiple_of(ring.owner(way, number) * LANES, LANES), LANES)
        place = pl.ds(way * few_rows, few_rows) if split else pl.ds(0, 2 * few_rows)
        return few_all.at[place, columns]

    def few_come(way, number):
        there = few_place(way, number, number == half)
        remote(there, there, few_sems, (way, number - 1), peers.ring[way]).wait_recv()

    def few_step(number):
        for way in range(2):
            if number > 1:
                few_come(way, number - 1)
            target = few_place(way, number - 1, number == half)
            source = few if number == 1 else target
            send(source, target, few_sems, (way, number - 1), peers.ring[way])

    few_step(1)
    exchange(2, segments, segments_all)
    exchange(0, tokens, tokens_all)
    own = [
        pltpu.make_async_copy(few, few_all.at[:, own_columns], own_sems.at[0]),
        pltpu.make_async_copy(out_shard, cotangent.at[1], own_sems.at[1]),
        pltpu.make_async_copy(segments, seg.at[0], own_sems.at[3]),
    ]
    for copy in own:
        copy.start()
    for pick in picks[:size]:
        pick.wait()
    ring.step(0, 1)
    own[1].wait()
    own_out = pltpu.make_async_copy(cotangent.at[1], out_w_out.at[own_rows, :], own_sems.at[4])
    own_out.start()
    for pick in picks[size:]:
        pick.wait()
    own_shards = [
        pltpu.make_async_copy(inner_shard, w_in.at[shard_rows, :], own_sems.at[6]),
        pltpu.make_async_copy(gate_shard, gate_w.at[shard_rows, :], own_sems.at[2]),
    ]
    for copy in own_shards:
        copy.start()

    wide_shape, thin_shape = spread_by.shape, fold_by.shape
    tile = lax.broadcasted_iota(jnp.int32, wide_shape, 1) // LANES
    row = lax.broadcasted_iota(jnp.int32, wide_shape, 0)
    spread_by[...] = jnp.where(
        (lax.rem(row, 2 * nstate) == tile) & (row < 6 * nstate), 1.0, 0.0
    ).astype(BF16)
    tile = lax.broadcasted_iota(jnp.int32, thin_shape, 0) // LANES
    column = lax.broadcasted_iota(jnp.int32, thin_shape, 1)
    fold_by[...] = jnp.where(tile == column, 1.0, 0.0).astype(BF16)
    save(spread_by, spread_out)
    save(fold_by, fold_out)

    few_step(2)
    pass_on(2, segments_all)
    few_step(3)
    ring.step(0, 2)
    few_step(4)
    exchanged(2, segments_all)
    others = pl.ds(1, COPIES - 1)
    numbers = pltpu.make_async_copy(segments_all.at[others], seg.at[others], seg_sems.at[0])
    numbers.start()
    for way in range(2):
        few_come(way, half - 1) if half < 2 else None
        few_come(way, half)
    own[0].wait()
    own[2].wait()
    numbers.wait()
    own_out.wait()

    numbers = jnp.concatenate([seg[k] for k in range(COPIES)], axis=0).astype(F32)
    lane = lax.broadcasted_iota(jnp.int32, (total, LANES), 1)
    time = lax.broadcasted_iota(jnp.int32, (total, LANES), 0) // GROUP
    picked = jnp.where(lane == time, jnp.concatenate([numbers] * length, axis=0), 0.0).astype(BF16)
    numbers = jnp.dot(picked, jnp.ones((LANES, LANES), BF16), preferred_element_type=F32)
    for shift in range(1, 4):
        earlier = jnp.concatenate(
            [jnp.full((shift * GROUP, LANES), -1.0, F32), numbers[: -shift * GROUP]], axis=0
        )
        masks[shift - 1] = jnp.where(earlier == numbers, 1.0, 0.0)
    save(masks, masks_out)
    save(few_all, few_out)
    first_small = 2 * rank + 2 * nstate
    small[...] = few_all[first_small : first_small + small.shape[0], :].astype(F32)
    taps, bias_row, skip_row, gain_row = 0, 5, 6 + nstate, 7 + nstate
    for n in range(nstate):
        rate[n] = jnp.broadcast_to(-LOG2E * jnp.exp(small[6 + n : 7 + n, :]), (GROUP, width))
    save(rate, rate_out)

    def fetch(own, everyone, t, slot):
        these = pl.ds(pl.multiple_of(t * BLOCK, BLOCK), BLOCK)
        others = pl.ds(batches, GROUP - batches)
        return [
            pltpu.make_async_copy(own.at[:, these, :], stage.at[slot, pl.ds(0, batches)], stage_sems.at[0, slot]),
            pltpu.make_async_copy(everyone.at[others, these, :], stage.at[slot, others], stage_sems.at[1, slot]),
        ]

    def fetch_start(*what):
        for copy in fetch(*what):
            copy.start()

    def fetch_wait(*what):
        for copy in fetch(*what):
            copy.wait()

    def weave(slot, scaled):
        for s in range(GROUP):
            value = stage[slot, s].astype(F32)
            if scaled:
                square = jnp.mean(value * value, axis=-1, keepdims=True)
                value = value * lax.rsqrt(square + EPS)
            for k in range(held.shape[0]):
                tile = value[:, k * LANES : (k + 1) * LANES]
                if scaled:
                    at = gain_row + k % 2
                    tile = tile * small[at : at + 1, (k // 2) * LANES : (k // 2 + 1) * LANES]
                held[k, pl.ds(s, BLOCK, stride=GROUP), :] = tile

    block_rows = BLOCK * GROUP
    blocks = total // block_rows

    def block_of(t):
        return pl.ds(pl.multiple_of(t * block_rows, block_rows), block_rows)

    ring.step(0, 3)
    pass_on(0, tokens_all)
    exchange(1, out_grad, grads_all)
    exchanged(0, tokens_all)
    fetch_start(tokens, tokens_all, 0, 0)

    @pl.loop(0, blocks)
    def _(t):
        slot = lax.rem(t, 2)

        @pl.when(t + 1 < blocks)
        def _():
            fetch_start(tokens, tokens_all, t + 1, 1 - slot)

        @pl.when(t == blocks - 2)
        def _():
            ring.step(0, 4)
            ring.step(1, 1)

        fetch_wait(tokens, tokens_all, t, slot)
        weave(slot, True)
        for k in range(held.shape[0]):
            normed[block_of(t), k * LANES : (k + 1) * LANES] = held[k].astype(BF16)

    save(normed, normed_out)
    for copy in own_shards:
        copy.wait()
    ring.finish(0)
    save(w_in, w_in_out)

    def cotangent_out_of(t, slot):
        return pltpu.make_async_copy(cotangent.at[slot], cotangent_out.at[block_of(t), :], out_sems.at[slot])

    def weave_grads(first, count):
        fetch_start(out_grad, grads_all, first, first % 2)

        @pl.loop(first, first + count)
        def _(t):
            slot = lax.rem(t, 2)

            @pl.when(t + 1 < first + count)
            def _():
                fetch_start(out_grad, grads_all, t + 1, 1 - slot)

            @pl.when(t >= 2)
            def _():
                cotangent_out_of(t - 2, slot).wait()

            fetch_wait(out_grad, grads_all, t, slot)
            weave(slot, False)
            for k in range(held.shape[0]):
                cotangent[slot, :, k * LANES : (k + 1) * LANES] = held[k].astype(BF16)
            cotangent_out_of(t, slot).start()

    inner[0:pad, :] = jnp.zeros((pad, width), F32)
    part[...] = jnp.zeros_like(part)

    @pl.loop(0, width // chunk)
    def _(c):
        cols = pl.ds(pl.multiple_of(c * chunk, chunk), chunk)
        inner[pad:, cols] = jnp.dot(normed[...], w_in[:, cols], preferred_element_type=F32)

        @pl.when(c == 2)
        def _():
            ring.step(1, 2)

        tap = [small[taps + i : taps + i + 1, cols] for i in range(5)]

        @pl.loop(0, total // rows)
        def _(i):
            start = pl.multiple_of(i * rows, rows)
            value = tap[4] + tap[3] * inner[pl.ds(pad + start, rows), cols]
            for shift in range(1, 4):
                mask = tiled(masks[shift - 1, pl.ds(start, rows), :], chunk)
                before = inner[pl.ds(pad - shift * GROUP + start, rows), cols]
                value = value + tap[3 - shift] * (before * mask)
            here = value * sigmoid(value)
            act[pl.ds(start, rows), cols] = here
            low[pl.ds(start, rows), cols] = here.astype(BF16)

        for j in range(2):
            part[j] += lax.dot_general(
                low[:, cols], few_all[j * LANES : (j + 1) * LANES, cols], (((1,), (1,)), ((), ())),
                preferred_element_type=F32,
            )

    save(inner.at[pl.ds(pad, total), :], inner_out)
    save(act, act_out)
    save(low, low_out)

    near = (near_send, near_recv)
    for j in range(2):
        for s in range(GROUP):
            nat[j, s * length : (s + 1) * length, :] = part[j, pl.ds(s, length, stride=GROUP), :]
    sends = []

    def start(source, target, index, peer):
        copy = remote(source, target, near, index, peer)
        copy.start()
        sends.append(copy)

    def come(target, index, peer):
        remote(target, target, near, index, peer).wait_recv()

    for i in range(2):
        start(nat.at[:, pl.ds((2 * i + 1) * side_rows, side_rows), :], got_near.at[i], i, peers.core)
    pass_on(1, grads_all)
    for i in range(2):
        come(got_near.at[i], i, peers.core)
    to_across[...] = nat[:, 2 * side_rows : 3 * side_rows, :] + got_near[1]
    start(to_across, got_across, 2, peers.across)
    exchanged(1, grads_all)
    weave_grads(0, blocks // 2)
    ring.step(1, 3)
    come(got_across, 2, peers.across)
    mine = nat[:, :side_rows, :] + got_near[0] + got_across[...]
    shared[0, 0] = mine[0].astype(BF16)
    lane = lax.broadcasted_iota(jnp.int32, (side_rows, LANES), 1)
    rest, terms = jnp.where(lane < 2 * nstate, mine[1], 0.0), jnp.zeros((side_rows, LANES), F32)
    for i in range(3):
        term = rest.astype(BF16).astype(F32)
        rest = rest - term
        terms = terms + (pltpu.roll(term, 2 * nstate * i, 1) if i else term)
    shared[0, 1] = terms.astype(BF16)
    start(shared.at[0], shared.at[2], 3, peers.across)
    start(shared.at[0], shared.at[1], 4, peers.core)
    weave_grads(blocks // 2, blocks // 2)
    come(shared.at[2], 3, peers.across)
    start(shared.at[2], shared.at[3], 5, peers.core)
    come(shared.at[1], 4, peers.core)
    come(shared.at[3], 5, peers.core)
    for copy in sends:
        copy.wait_send()
    for k in range(COPIES):
        for b in range(batches):
            for j in range(2):
                part[j, pl.ds(k * batches + b, length, stride=GROUP), :] = shared[
                    k, j, b * length : (b + 1) * length, :
                ].astype(F32)
    step_low[...] = part[0].astype(BF16)
    coef[...] = part[1].astype(BF16)
    save(step_low, step_low_out)
    save(coef, coef_out)

    stride = few_all[rank + 2 * nstate : 2 * rank + 2 * nstate, :]
    side_bias = small[bias_row : bias_row + 1, :]
    carry[...] = jnp.zeros_like(carry)

    state_rows = nstate * GROUP

    def keep_states(t, c):
        there = pl.ds(pl.multiple_of(t * BLOCK * state_rows, BLOCK * state_rows), BLOCK * state_rows)
        return pltpu.make_async_copy(
            states_at.at[c % 2], states_out.at[c, there, :], states_sems.at[c % 2]
        )

    @pl.loop(0, blocks)
    def _(t):
        for tick, which, number in ((0, 1, 4), (0, 2, 1), (4, 2, 2), (7, 2, 3)):

            @pl.when(t == tick)
            def _(which=which, number=number):
                ring.step(which, number)

        base = pl.multiple_of(t * block_rows, block_rows)
        these = block_of(t)
        wide[...] = jnp.dot(coef[these, :], spread_by[...], preferred_element_type=F32)
        pre[...] = jnp.dot(step_low[these, :], stride, preferred_element_type=F32)
        for i in range(BLOCK // 2):
            sub = slice(i * 2 * GROUP, (i + 1) * 2 * GROUP)
            step[pl.ds(base + i * 2 * GROUP, 2 * GROUP), :] = softplus(pre[sub, :] + side_bias)
        for c in range(width // chunk):
            cols = slice(c * chunk, (c + 1) * chunk)

            if c >= 2:
                keep_states(t, c - 2).wait()
            else:

                @pl.when(t > 0)
                def _(c=c):
                    keep_states(t - 1, c + 2).wait()

            def advance(i, states):
                at = pl.ds(pl.multiple_of(base + i * GROUP, GROUP), GROUP)
                here = at_time(i)
                step_t, act_t = step[at, cols], act[at, cols]
                drive = jnp.where(tiled(masks[0, at, :], chunk) > 0.5, step_t, FAR)
                inflow = step_t * act_t
                out = small[skip_row : skip_row + 1, cols] * act_t
                now = []
                for n in range(nstate):
                    write = tiled(wide[here, n * LANES : (n + 1) * LANES], chunk)
                    read = tiled(wide[here, (nstate + n) * LANES : (nstate + n + 1) * LANES], chunk)
                    row = pl.multiple_of(i * state_rows + n * GROUP, GROUP)
                    states_at[c % 2, pl.ds(row, GROUP), :] = states[n]
                    state = jnp.exp2(drive * rate[n, :, cols]) * states[n] + write * inflow
                    out = out + read * state
                    now.append(state)
                readout[at, cols] = out
                return tuple(now)

            states = lax.fori_loop(
                0, BLOCK, advance, tuple(carry[c, n * GROUP : (n + 1) * GROUP, :] for n in range(nstate)), unroll=4
            )
            for n in range(nstate):
                carry[c, n * GROUP : (n + 1) * GROUP, :] = states[n]
            keep_states(t, c).start()

    save(carry, states_out.at[:, pl.ds(total // GROUP * state_rows, state_rows), :])
    save(step, step_out)
    save(readout, readout_out)

    ring.finish(1)
    save(gate_w, gate_w_out)

    def keep_gate(c, slot):
        cols = pl.ds(pl.multiple_of(c * chunk, chunk), chunk)
        return pltpu.make_async_copy(gate.at[slot], gate_out.at[:, cols], gate_sems.at[slot])

    @pl.loop(0, width // chunk)
    def _(c):
        cols = pl.ds(pl.multiple_of(c * chunk, chunk), chunk)
        slot = lax.rem(c, 2)

        @pl.when(c >= 2)
        def _():
            keep_gate(c - 2, slot).wait()

        @pl.when(c == 2)
        def _():
            ring.step(2, 4)

        gate[slot] = jnp.dot(normed[...], gate_w[:, cols], preferred_element_type=F32)
        keep_gate(c, slot).start()

        @pl.loop(0, total // rows)
        def _(i):
            at = pl.ds(pl.multiple_of(i * rows, rows), rows)
            here = gate[slot, at, :]
            value = readout[at, cols] * (here * sigmoid(here))
            gated[at, cols] = value.astype(BF16)
            for k in range(chunk // LANES):
                nat[k, at, :] = value[:, k * LANES : (k + 1) * LANES]

        for k in range(chunk // LANES):
            for s in range(GROUP):
                natural[s * length : (s + 1) * length, pl.ds(pl.multiple_of(c * chunk + k * LANES, LANES), LANES)] = nat[
                    k, pl.ds(s, length, stride=GROUP), :
                ].astype(BF16)

    save(gated, gated_out)
    save(natural, natural_out)
    ring.finish(2)
    ring.sent_all()
    for moving in sent:
        moving.wait_send()
    for slot in range(2):
        keep_states(blocks - 1, width // chunk - 2 + slot).wait()
        keep_gate(width // chunk - 2 + slot, slot).wait()
        cotangent_out_of(blocks - 2 + slot, slot).wait()
    for copy in saved:
        copy.wait()


def forward(size, rank, nstate, entry, few, tokens, out_grad, segments, out_proj):
    batches, length, model = tokens.shape
    total = COPIES * batches * length
    slab, width = entry.shape[0], size * LANES
    blocks = length // BLOCK
    anywhere = pl.BlockSpec(memory_space=pl.ANY)
    half = size // 2
    dma = pltpu.SemaphoreType.DMA
    shape = jax.ShapeDtypeStruct
    full, low = shape((total, width), F32), shape((total, width), BF16)
    thin = shape((total, LANES), BF16)
    rows = shape((total, model), BF16)
    weights = shape((size * slab, width), BF16)
    few_all = shape((few.shape[0], width), BF16)
    masks = shape((3, total, LANES), F32)
    state = shape((nstate, GROUP, width), F32)
    spread_by = shape((LANES, 2 * nstate * LANES), BF16)
    fold_by = shape((2 * nstate * LANES, LANES), BF16)
    outs = dict(
        few=few_all,
        masks=masks,
        rate=state,
        spread_by=spread_by,
        fold_by=fold_by,
        normed=rows,
        cotangent=rows,
        tokens_all=shape((GROUP, length, model), BF16),
        grads_all=shape((GROUP, length, model), BF16),
        segments_all=shape((COPIES,) + segments.shape, segments.dtype),
        inner_in=weights,
        inner=full,
        act=full,
        act_low=low,
        step_low=thin,
        coef=thin,
        step=full,
        states=shape((width // 256, (length + 1) * nstate * GROUP, 256), F32),
        gate=full,
        readout=full,
        gated=low,
        gated_natural=low,
        gate_in=weights,
        out_w=shape((size * out_proj.shape[0] // COPIES, model), BF16),
    )
    quarter = total // COPIES
    scratch = [
        few_all,
        shape((few.shape[0] - 2 * rank - 2 * nstate, width), F32),
        masks,
        state,
        spread_by,
        fold_by,
        rows,
        shape((2, GROUP, BLOCK, model), BF16),
        shape((2, BLOCK * GROUP, model), BF16),
        shape((model // LANES, BLOCK * GROUP, LANES), F32),
        shape((COPIES,) + segments.shape, segments.dtype),
        shape((slab, width), BF16),
        shape((slab, width), BF16),
        weights,
        shape((total + 3 * GROUP, width), F32),
        full,
        low,
        shape((2, total, LANES), F32),
        shape((2, total, LANES), F32),
        shape((2, 2, quarter, LANES), F32),
        shape((2, quarter, LANES), F32),
        shape((2, quarter, LANES), F32),
        shape((COPIES, 2, quarter, LANES), BF16),
        thin,
        thin,
        shape((BLOCK * GROUP, 2 * nstate * LANES), F32),
        shape((BLOCK * GROUP, width), F32),
        full,
        full,
        shape((width // 256, nstate * GROUP, 256), F32),
        shape((2, BLOCK * nstate * GROUP, 256), F32),
        shape((2, total, 256), F32),
        low,
        low,
        weights,
    ]
    sems = [(20,), (2,), (2,), (7,), (2 * size,), (2, 2), (2,), (1,)]
    sems += [(3, 2, half, 2)] * 2 + [(2, half)] * 2 + [(3, 3)] * 2 + [(6,)] * 2
    results = pl.pallas_call(
        functools.partial(forward_kernel, size, rank, nstate),
        in_specs=[anywhere] * 6,
        out_specs=[anywhere] * len(outs),
        out_shape=list(outs.values()),
        scratch_shapes=[pltpu.VMEM(x.shape, x.dtype) for x in scratch] + [dma(n) for n in sems],
        compiler_params=pltpu.CompilerParams(
            collective_id=4, has_side_effects=True, vmem_limit_bytes=62 * 1024 * 1024
        ),
        cost_estimate=cost(8 * total * width * model, 100 * total * width),
        name="forward",
    )(entry, few, tokens, out_grad, segments, out_proj)
    return dict(zip(outs, results))


class Guests:
    def __init__(self, peers, parts, totals, held, sems):
        self.peers = peers
        self.parts, self.totals, self.held, self.sems = parts, totals, held, sems

    def rows(self, which, c):
        half = self.parts[which].shape[1] // 2
        return pl.ds(c * half, half)

    def copy(self, which, way, step, c, source=None):
        target = self.held[which].at[way, step - 1, self.rows(which, c), :]
        index = (which, way, step - 1, c)
        source = target if source is None else source
        return remote(source, target, self.sems, index, self.peers.ring[way])

    def chunks(self, way, step):
        return (way,) if step == 1 else (0, 1)

    def own(self, which, way, step, c):
        away = self.peers.half + 1 - step
        block = self.peers.at(away if way == 0 else -away)
        return self.parts[which].at[block, self.rows(which, c), :]

    def source(self, which, way, step, c):
        own = self.own(which, way, step, c)
        if step == 1 or c not in self.chunks(way, step - 1):
            return own
        self.copy(which, way, step - 1, c).wait_recv()
        there = self.held[which].at[way, step - 2, self.rows(which, c), :]
        there[...] = (own[...].astype(F32) + there[...].astype(F32)).astype(BF16)
        return there

    def step(self, which, step):
        for c in range(2):
            for way in range(2):
                if c in self.chunks(way, step):
                    self.copy(which, way, step, c, self.source(which, way, step, c)).start()

    def finish(self, which):
        last = self.peers.half
        for c in range(2):
            total = self.own(which, 0, last + 1, c)[...].astype(F32)
            for way in range(2):
                self.copy(which, way, last, c).wait_recv()
                there = self.held[which].at[way, last - 1, self.rows(which, c), :]
                total = total + there[...].astype(F32)
            self.totals[which][self.rows(which, c), :] = total.astype(BF16)

    def sent_all(self):
        for which in range(2):
            for step in range(1, self.peers.half + 1):
                for way in range(2):
                    for c in self.chunks(way, step):
                        self.copy(which, way, step, c).wait_send()


def scan_back_kernel(
    nstate, chunk, step_ref, act_ref, grad_ref, coef_ref, spread_ref, fold_ref, keep_ref, rate_ref,
    row_ref, start_ref, *refs,
):
    wide, states_all, decays, parts, sizes = refs[-5:]
    width = step_ref.shape[1]
    step_now = pl.program_id(0)
    pre_grad_ref, direct_ref, coef_grad_ref, carry_ref, sums_ref = refs[-10:-5]

    @pl.when(step_now == 0)
    def _():
        carry_ref[...] = jnp.zeros_like(carry_ref)
        sums_ref[...] = jnp.zeros_like(sums_ref)

    wide[...] = jnp.dot(coef_ref[...], spread_ref[...], preferred_element_type=F32)

    def fold(value):
        total = value[:, :LANES]
        for k in range(1, chunk // LANES):
            total = total + value[:, k * LANES : (k + 1) * LANES]
        return total

    for c in range(width // chunk):
        cols = slice(c * chunk, (c + 1) * chunk)

        def advance(t, states):
            at = at_time(t)
            step = step_ref[at, cols]
            drive = jnp.where(tiled(keep_ref[at, :], chunk) > 0.5, step, FAR)
            inflow = step * act_ref[at, cols]
            now = []
            for n in range(nstate):
                write = tiled(wide[at, n * LANES : (n + 1) * LANES], chunk)
                decay = jnp.exp2(drive * rate_ref[n, :, cols])
                decays[t, n] = decay
                states_all[t, n] = states[n]
                now.append(decay * states[n] + write * inflow)
            return tuple(now)

        start = tuple(start_ref[0, n, :, cols] for n in range(nstate))
        states = lax.fori_loop(0, BLOCK, advance, start, unroll=2)
        for n in range(nstate):
            states_all[BLOCK, n] = states[n]

        def retreat(i, carry):
            t = BLOCK - 1 - i
            at = at_time(t)
            step, act, grad = step_ref[at, cols], act_ref[at, cols], grad_ref[at, cols]
            inflow = step * act
            size = jnp.zeros_like(step)
            direct = jnp.zeros_like(step)
            now = []
            for n in range(nstate):
                tile_w = slice(n * LANES, (n + 1) * LANES)
                tile_r = slice((nstate + n) * LANES, (nstate + n + 1) * LANES)
                state_grad = tiled(wide[at, tile_r], chunk) * grad + carry[n]
                passed = decays[t, n] * state_grad
                through = passed * states_all[t, n]
                size = size + rate_ref[n, :, cols] * through
                direct = direct + state_grad * tiled(wide[at, tile_w], chunk)
                sums_ref[n, :, cols] += step * through
                write_part = fold(state_grad * inflow)
                read_part = fold(grad * states_all[t + 1, n])
                if c == 0:
                    parts[at, tile_w] = write_part
                    parts[at, tile_r] = read_part
                else:
                    parts[at, tile_w] += write_part
                    parts[at, tile_r] += read_part
                now.append(passed)
            sizes[at, cols] = LN2 * size + act * direct
            direct_ref[at, cols] = step * direct + row_ref[1:2, cols] * grad
            sums_ref[nstate, :, cols] += grad * act
            return tuple(now)

        start = tuple(carry_ref[n, :, cols] for n in range(nstate))
        carry = lax.fori_loop(0, BLOCK, retreat, start, unroll=2)
        for n in range(nstate):
            carry_ref[n, :, cols] = carry[n]

    step = step_ref[...]
    series = step * (1.0 - step * (0.5 - step * (1.0 / 6.0)))
    pre_grad = sizes[...] * jnp.where(step < 0.01, series, 1.0 - jnp.exp(-step))
    pre_grad_ref[...] = pre_grad.astype(BF16)
    total = pre_grad[:GROUP]
    for t in range(1, BLOCK):
        total = total + pre_grad[t * GROUP : (t + 1) * GROUP]
    sums_ref[nstate + 1] += total
    high = parts[...].astype(BF16)
    low = (parts[...] - high.astype(F32)).astype(BF16)
    coef_grad_ref[...] = jnp.dot(high, fold_ref[...], preferred_element_type=F32) + jnp.dot(
        low, fold_ref[...], preferred_element_type=F32
    )


def scan_backward(
    step, act, grad, coef, spread_by, fold_by, keep, rate, rows, starts
):
    total, width = step.shape
    nstate = rate.shape[0]
    size = BLOCK * GROUP
    chunk = 256
    count = total // size
    tile = pl.BlockSpec((size, width), lambda t: (count - 1 - t, 0))
    thin = pl.BlockSpec((size, LANES), lambda t: (count - 1 - t, 0))
    state = pl.BlockSpec((nstate, GROUP, width), lambda t: (0, 0, 0))
    tally = pl.BlockSpec((nstate + 2, GROUP, width), lambda t: (0, 0, 0))
    work = count * size * width * nstate
    return pl.pallas_call(
        functools.partial(scan_back_kernel, nstate, chunk),
        grid=(count,),
        in_specs=[
            tile,
            tile,
            tile,
            thin,
            pl.BlockSpec(spread_by.shape, lambda t: (0, 0)),
            pl.BlockSpec(fold_by.shape, lambda t: (0, 0)),
            thin,
            state,
            pl.BlockSpec((8, width), lambda t: (0, 0)),
            pl.BlockSpec((1, nstate, GROUP, width), lambda t: (count - 1 - t, 0, 0, 0)),
        ],
        out_specs=[tile, tile, thin, state, tally],
        out_shape=[
            jax.ShapeDtypeStruct((total, width), BF16),
            jax.ShapeDtypeStruct((total, width), F32),
            jax.ShapeDtypeStruct((total, LANES), F32),
            jax.ShapeDtypeStruct((nstate, GROUP, width), F32),
            jax.ShapeDtypeStruct((nstate + 2, GROUP, width), F32),
        ],
        scratch_shapes=[
            pltpu.VMEM((size, 2 * nstate * LANES), F32),
            pltpu.VMEM((BLOCK + 1, nstate, GROUP, chunk), F32),
            pltpu.VMEM((BLOCK, nstate, GROUP, chunk), F32),
            pltpu.VMEM((size, 2 * nstate * LANES), F32),
            pltpu.VMEM((size, width), F32),
        ],
        compiler_params=params(),
        cost_estimate=cost(40 * work, 24 * count * size * width),
        name="scan_backward",
    )(step, act, grad, coef, spread_by, fold_by, keep, rate, rows, starts)


def backward_kernel(
    size, nstate, rank,
    gated_in, cotangent_in, w_out, readout_in, gate_in, normed_in, step_in, act_in, coef_in, states_in, masks_in, rate_in,
    spread_in, fold_in, few_in, gated_natural_in,
    natural_out, pre_low_out, direct_out, coef_grad_out, sums_out, out_pieces, out_own, out_near, out_far, gate_total,
    gated, cotangent, out_w, normed, out_wgrad, gate_wgrad, out_held, gate_held, gate_grad, natural, grad, nat,
    step_at, act_at, states_at, wide, parts, sizes, sums, carry, coef, spread_by, fold_by, rate, keep, few,
    coef_grad, out_total,
    load_sems, tile_sems, block_sems, states_sems, save_sems, block_saves, ring_send, ring_recv, part_send, part_recv,
    piece_send, piece_recv, own_sem,
):
    peers = Peers(size)
    total, width = gated.shape
    model = normed.shape[1]
    length = total // GROUP
    chunk, rows = 256, 64
    block_rows = BLOCK * GROUP
    blocks = total // block_rows
    loads, saved = {}, []

    def load(name, source, target):
        loads[name] = pltpu.make_async_copy(source, target, load_sems.at[len(loads)])
        loads[name].start()

    def save(source, target):
        saved.append(pltpu.make_async_copy(source, target, save_sems.at[len(saved)]))
        saved[-1].start()

    first_small = 2 * rank + 2 * nstate
    load("gated", gated_in, gated)
    load("cotangent", cotangent_in, cotangent)
    load("out_w", w_out, out_w)
    load("normed", normed_in, normed)
    load("coef", coef_in, coef)
    load("spread", spread_in, spread_by)
    load("fold", fold_in, fold_by)
    load("rate", rate_in, rate)
    load("keep", masks_in.at[0], keep)
    load("few", few_in.at[pl.ds(first_small, few.shape[0]), :], few)

    def tile_copies(c, slot):
        cols = pl.ds(pl.multiple_of(c * chunk, chunk), chunk)
        return [
            pltpu.make_async_copy(
                ref.at[:, cols], states_at.at[slot, pl.ds(i * total, total), :], tile_sems.at[i, slot]
            )
            for i, ref in enumerate((gate_in, readout_in))
        ]

    for copy in tile_copies(0, 0):
        copy.start()
    peers.meet()
    ring = Guests(
        peers, (out_wgrad, gate_wgrad), (out_total, gate_total), (out_held, gate_held), (ring_send, ring_recv),
    )
    out_parts = cotangent
    out_sum = Parts(
        peers, start_send, (part_send, part_recv), out_parts, out_near, out_far, total // COPIES
    )
    pieces = Pieces(
        peers, start_send, (piece_send, piece_recv), own_sem, 0, lambda: out_total, lambda k: out_pieces.at[k],
    )
    loads["gated"].wait()
    loads["cotangent"].wait()
    tn = (((0,), (0,)), ((), ()))
    nt = (((1,), (1,)), ((), ()))

    @pl.loop(0, model // chunk)
    def _(c):
        cols = pl.ds(pl.multiple_of(c * chunk, chunk), chunk)
        value = lax.dot_general(gated[...], cotangent[:, cols], tn, preferred_element_type=F32)
        out_wgrad[:, :, cols] = value.astype(BF16).reshape(size, -1, chunk)

    ring.step(0, 1)
    loads["out_w"].wait()

    @pl.loop(0, width // chunk)
    def _(c):
        cols = pl.ds(pl.multiple_of(c * chunk, chunk), chunk)
        slot = lax.rem(c, 2)

        @pl.when(c + 1 < width // chunk)
        def _():
            for copy in tile_copies(c + 1, 1 - slot):
                copy.start()

        @pl.when(c == 2)
        def _():
            ring.step(0, 2)

        grad[:, cols] = lax.dot_general(cotangent[...], out_w[cols, :], nt, preferred_element_type=F32)
        for copy in tile_copies(c, slot):
            copy.wait()

        @pl.loop(0, total // rows)
        def _(i):
            start = pl.multiple_of(i * rows, rows)
            at = pl.ds(start, rows)
            gate = states_at[slot, at, :]
            readout = states_at[slot, pl.ds(total + start, rows), :]
            value = grad[at, cols]
            sig = sigmoid(gate)
            grad[at, cols] = value * (gate * sig)
            value = value * readout * (sig * (1.0 + gate * (1.0 - sig)))
            gate_grad[at, cols] = value.astype(BF16)
            for k in range(chunk // LANES):
                nat[k, at, :] = value[:, k * LANES : (k + 1) * LANES]

        for k in range(chunk // LANES):
            lanes = pl.ds(pl.multiple_of(c * chunk + k * LANES, LANES), LANES)
            for s in range(GROUP):
                natural[s * length : (s + 1) * length, lanes] = nat[
                    k, pl.ds(s, length, stride=GROUP), :
                ].astype(BF16)

    save(natural, natural_out)

    def block_copies(t, slot):
        these = pl.ds(pl.multiple_of(t * block_rows, block_rows), block_rows)
        return [
            pltpu.make_async_copy(step_in.at[these, :], step_at.at[slot], block_sems.at[0, slot]),
            pltpu.make_async_copy(act_in.at[these, :], act_at.at[slot], block_sems.at[1, slot]),
        ]

    state_rows = nstate * GROUP

    def states_copy(t, c):
        there = pl.ds(pl.multiple_of(t * BLOCK * state_rows, BLOCK * state_rows), (BLOCK + 1) * state_rows)
        slot = states_slot(t, c)
        return pltpu.make_async_copy(states_in.at[c, there, :], states_at.at[slot], states_sems.at[slot])

    slots, ahead = 3, 2

    def states_slot(t, c):
        return lax.rem((blocks - 1 - t) * (width // chunk) + c, slots)

    for c in range(ahead):
        states_copy(blocks - 1, c).start()

    for copy in block_copies(blocks - 1, (blocks - 1) % 2):
        copy.start()
    loads["normed"].wait()

    @pl.loop(0, width // chunk)
    def _(c):
        cols = pl.ds(pl.multiple_of(c * chunk, chunk), chunk)
        value = lax.dot_general(normed[...], gate_grad[:, cols], tn, preferred_element_type=F32)
        gate_wgrad[:, :, cols] = value.astype(BF16).reshape(size, -1, chunk)

    ring.step(1, 1)
    load("natural", gated_natural_in, gate_grad)
    for name in ("coef", "spread", "fold", "rate", "keep", "few"):
        loads[name].wait()
    pre_low = gated
    skip_at = 6 + nstate
    skip_row = few[...].astype(F32)[skip_at : skip_at + 1]
    carry[...] = jnp.zeros_like(carry)
    sums[...] = jnp.zeros_like(sums)

    def near_copy():
        return pltpu.make_async_copy(
            out_near.at[1], normed.at[pl.ds(0, total // COPIES), :], own_sem.at[1]
        )

    loads["natural"].wait()

    def fold(value):
        out = value[:, :LANES]
        for k in range(1, chunk // LANES):
            out = out + value[:, k * LANES : (k + 1) * LANES]
        return out

    def block_keeps(t):
        these = pl.ds(pl.multiple_of(t * block_rows, block_rows), block_rows)
        return [
            pltpu.make_async_copy(pre_low.at[these, :], pre_low_out.at[these, :], block_saves.at[0, t]),
            pltpu.make_async_copy(grad.at[these, :], direct_out.at[these, :], block_saves.at[1, t]),
        ]

    @pl.loop(0, blocks)
    def _(turn):
        t = blocks - 1 - turn
        slot = lax.rem(t, 2)
        for tick, which, number in ((0, 0, 3), (1, 1, 2), (3, 0, 4), (4, 1, 3), (6, 1, 4)):

            @pl.when(turn == tick)
            def _(which=which, number=number):
                ring.step(which, number)

        @pl.when(turn == 1)
        def _():
            out_sum.start()

        @pl.when(turn == 2)
        def _():
            near_copy().wait()
            out_sum.go_far(normed.at[pl.ds(0, total // COPIES), :])

        @pl.when(turn == 5)
        def _():
            ring.finish(0)
            pieces.give()

        @pl.when(turn == 0)
        def _():
            @pl.loop(0, model // chunk)
            def _(i):
                cols = pl.ds(pl.multiple_of(i * chunk, chunk), chunk)
                value = jnp.dot(gate_grad[...], out_w[:, cols], preferred_element_type=F32)
                out_parts[:, cols] = value.astype(BF16)

        @pl.when(t > 0)
        def _():
            for copy in block_copies(t - 1, 1 - slot):
                copy.start()

        base = pl.multiple_of(t * block_rows, block_rows)
        these = pl.ds(base, block_rows)
        wide[...] = jnp.dot(coef[these, :], spread_by[...], preferred_element_type=F32)
        for copy in block_copies(t, slot):
            copy.wait()

        for c in range(width // chunk):
            cols = slice(c * chunk, (c + 1) * chunk)

            if c + ahead < width // chunk:
                states_copy(t, c + ahead).start()
            else:

                @pl.when(t > 0)
                def _(c=c):
                    states_copy(t - 1, c + ahead - width // chunk).start()

            states_copy(t, c).wait()

            def state_at(i, n):
                row = pl.multiple_of(i * state_rows + n * GROUP, GROUP)
                return states_at[states_slot(t, c), pl.ds(row, GROUP), :]

            def retreat(i, carried):
                i = BLOCK - 1 - i
                here = at_time(i)
                at = pl.ds(pl.multiple_of(base + i * GROUP, GROUP), GROUP)
                step, act, flow = step_at[slot, here, cols], act_at[slot, here, cols], grad[at, cols]
                inflow = step * act
                drive = jnp.where(tiled(keep[at, :], chunk) > 0.5, step, FAR)
                size_grad, direct = jnp.zeros_like(step), jnp.zeros_like(step)
                now = []
                for n in range(nstate):
                    tile_w = slice(n * LANES, (n + 1) * LANES)
                    tile_r = slice((nstate + n) * LANES, (nstate + n + 1) * LANES)
                    state_grad = tiled(wide[here, tile_r], chunk) * flow + carried[n]
                    power = drive * rate[n, :, cols]
                    passed = jnp.exp2(power) * state_grad
                    through = power * (passed * state_at(i, n))
                    size_grad = size_grad + through
                    direct = direct + state_grad * tiled(wide[here, tile_w], chunk)
                    sums[n, :, cols] += through
                    write_part = fold(state_grad * inflow)
                    read_part = fold(flow * state_at(i + 1, n))
                    if c == 0:
                        parts[here, tile_w] = write_part
                        parts[here, tile_r] = read_part
                    else:
                        parts[here, tile_w] += write_part
                        parts[here, tile_r] += read_part
                    now.append(passed)
                sizes[here, cols] = LN2 * size_grad / jnp.maximum(step, 1e-30) + act * direct
                grad[at, cols] = step * direct + skip_row[:, cols] * flow
                sums[nstate, :, cols] += flow * act
                return tuple(now)

            start = tuple(carry[n, :, cols] for n in range(nstate))
            carried = lax.fori_loop(0, BLOCK, retreat, start, unroll=4)
            for n in range(nstate):
                carry[n, :, cols] = carried[n]

        step = step_at[slot]
        series = step * (1.0 - step * (0.5 - step * (1.0 / 6.0)))
        pre_grad = sizes[...] * jnp.where(step < 0.01, series, 1.0 - jnp.exp(-step))
        pre_low[these, :] = pre_grad.astype(BF16)
        tally = pre_grad[:GROUP]
        for i in range(1, BLOCK):
            tally = tally + pre_grad[i * GROUP : (i + 1) * GROUP]
        sums[nstate + 1] += tally
        coef_grad[these, :] = jnp.dot(
            parts[...].astype(BF16), fold_by[...], preferred_element_type=F32
        )

        @pl.when(turn == 1)
        def _():
            out_sum.come_near()
            near_copy().start()

        for copy in block_keeps(t):
            copy.start()

    save(coef_grad, coef_grad_out)
    save(sums, sums_out)
    save(out_sum.block(0), out_own)
    pieces.pass_on()
    ring.finish(1)
    pieces.come()
    out_sum.come()
    ring.sent_all()
    out_sum.sent_all()
    pieces.sent_all()
    for t in range(blocks):
        for copy in block_keeps(t):
            copy.wait()
    for copy in saved:
        copy.wait()


def backward(size, nstate, rank, arrays):
    (gated, cotangent, w_out, readout, gate, normed, step, act, coef, states, masks, rate, spread_by, fold_by, few) = arrays[:15]
    total, width = gated.shape
    model = normed.shape[1]
    inside, anywhere = pl.BlockSpec(memory_space=pltpu.VMEM), pl.BlockSpec(memory_space=pl.ANY)
    shape, dma = jax.ShapeDtypeStruct, pltpu.SemaphoreType.DMA
    low, rows, full = shape((total, width), BF16), shape((total, model), BF16), shape((total, width), F32)
    out_unit, gate_unit = (width // size, model), (model // size, width)
    half = size // 2
    block = shape((2, BLOCK * GROUP, width), F32)
    state = shape((nstate, GROUP, width), F32)
    tally = shape((nstate + 2, GROUP, width), F32)
    wide = shape((BLOCK * GROUP, 2 * nstate * LANES), F32)
    thin = shape((total, LANES), F32)
    scratch = [
        low,
        rows,
        shape(w_out.shape, BF16),
        rows,
        shape((size,) + out_unit, BF16),
        shape((size,) + gate_unit, BF16),
        shape((2, half) + out_unit, BF16),
        shape((2, half) + gate_unit, BF16),
        low,
        low,
        full,
        shape((2, total, LANES), F32),
        block,
        block,
        shape((3, (BLOCK + 1) * nstate * GROUP, 256), F32),
        wide,
        wide,
        shape((BLOCK * GROUP, width), F32),
        tally,
        state,
        shape(coef.shape, BF16),
        shape(spread_by.shape, BF16),
        shape(fold_by.shape, BF16),
        state,
        thin,
        shape((few.shape[0] - 2 * rank - 2 * nstate, width), BF16),
        thin,
        shape(out_unit, BF16),
    ]
    blocks = total // (BLOCK * GROUP)
    sems = [(11,), (2, 2), (2, 2), (3,), (4,), (2, blocks), (2, 2, half, 2), (2, 2, half, 2)]
    sems += [(3,), (3,), (1, 3), (1, 3), (2,)]
    part = shape((total // COPIES, model), BF16)
    return pl.pallas_call(
        functools.partial(backward_kernel, size, nstate, rank),
        in_specs=[anywhere] * len(arrays),
        out_specs=[anywhere] * 9 + [inside],
        out_shape=[
            low, low, full, thin, tally, shape((COPIES,) + out_unit, BF16), part, shape((2,) + part.shape, BF16), part,
            shape(gate_unit, BF16),
        ],
        scratch_shapes=[pltpu.VMEM(x.shape, x.dtype) for x in scratch] + [dma(n) for n in sems],
        compiler_params=pltpu.CompilerParams(
            collective_id=3, has_side_effects=True, vmem_limit_bytes=62 * 1024 * 1024
        ),
        cost_estimate=cost(6 * total * width * model, 200 * total * width),
        name="backward",
    )(*arrays)


def finish_kernel(
    size, rank, nstate,
    pre_low_in, coef_in, direct_in, inner_in, act_low_in, step_low_in, masks_in, few_in, normed_in, w_inner, w_gate,
    gate_grad_in, sums_in, gate_total,
    inner_pieces, gate_pieces, norm_own, norm_near, norm_far, small_pieces,
    pre_low, part, nat, got_near, to_across, got_across, shared, low_grad, act_low, step_low, masks, few, normed, gate_grad,
    inner_grad, inner, direct, grad, wgrad, held, small, small_low, small_held, norm_parts, near_at, w_tiles, total_at, gate_own, sums,
    load_sems, tile_sems, w_sems, near_send, near_recv, part_send, part_recv, ring_send, ring_recv, few_send, few_recv,
    piece_send, piece_recv, own_sems,
):
    peers = Peers(size)
    half = peers.half
    total, width = pre_low.shape
    model = normed.shape[1]
    length = total // GROUP
    batches = GROUP // COPIES
    quarter = total // COPIES
    chunk, rows, pad = 256, 64, 3 * GROUP
    tiles = width // chunk
    slab = held.shape[2]
    send, loads = Sends(), {}

    def load(name, source, target):
        loads[name] = pltpu.make_async_copy(source, target, load_sems.at[len(loads)])
        loads[name].start()

    def tile_copies(c, slot):
        cols = slice(c * chunk, (c + 1) * chunk)
        return [
            pltpu.make_async_copy(inner_in.at[:, cols], inner.at[slot, pl.ds(pad, total), :], tile_sems.at[0, slot]),
            pltpu.make_async_copy(direct_in.at[:, cols], direct.at[slot], tile_sems.at[1, slot]),
        ]

    load("pre", pre_low_in, pre_low)
    load("few", few_in, few)
    load("coef", coef_in, part.at[1])
    load("step", step_low_in, step_low)
    load("gate", gate_grad_in, gate_grad)
    load("total", gate_total, gate_own)
    load("act", act_low_in, act_low)
    load("masks", masks_in, masks.at[:, pl.ds(0, total), :])
    load("normed", normed_in, normed)
    load("sums", sums_in, sums)
    for copy in tile_copies(0, 0):
        copy.start()
    w_count = model // chunk

    def w_copy(w, n, slot):
        these = pl.ds(pl.multiple_of(n * chunk, chunk), chunk)
        return pltpu.make_async_copy(w.at[these, :], w_tiles.at[slot], w_sems.at[slot])

    def norm_tiles(w, left, first, count, add):
        @pl.loop(first, first + count)
        def _(n):
            slot = lax.rem(n, 2)

            @pl.when(n + 1 < w_count)
            def _():
                w_copy(w, n + 1, 1 - slot).start()

            w_copy(w, n, slot).wait()
            cols = pl.ds(pl.multiple_of(n * chunk, chunk), chunk)
            value = lax.dot_general(
                left[...], w_tiles[slot], (((1,), (1,)), ((), ())), preferred_element_type=F32
            )
            if add:
                value = value + norm_parts[:, cols].astype(F32)
            norm_parts[:, cols] = value.astype(BF16)

    w_copy(w_gate, 0, 0).start()
    peers.meet()

    near = (near_send, near_recv)

    def come(target, index, peer):
        remote(target, target, near, index, peer).wait_recv()

    first_stride = rank + 2 * nstate
    loads["pre"].wait()
    loads["few"].wait()
    part[0] = lax.dot_general(
        pre_low[...], few[first_stride : first_stride + rank, :], (((1,), (1,)), ((), ())),
        preferred_element_type=F32,
    )
    loads["coef"].wait()
    for j in range(2):
        for s in range(GROUP):
            nat[j, s * length : (s + 1) * length, :] = part[j, pl.ds(s, length, stride=GROUP), :]
    for i in range(2):
        send(nat.at[:, pl.ds((2 * i + 1) * quarter, quarter), :], got_near.at[i], near, i, peers.core)
    near_sends = Sends()
    near_sends.sent, send.sent = send.sent, []
    loads["step"].wait()
    small[first_stride : first_stride + rank, :] = lax.dot_general(
        step_low[...], pre_low[...], (((0,), (0,)), ((), ())), preferred_element_type=F32
    )
    for i in range(2):
        come(got_near.at[i], i, peers.core)
    to_across[...] = nat[:, 2 * quarter : 3 * quarter, :] + got_near[1]
    send(to_across, got_across, near, 2, peers.across)
    loads["gate"].wait()
    norm_tiles(w_gate, gate_grad, 0, w_count // 2, False)
    come(got_across, 2, peers.across)
    mine = nat[:, :quarter, :] + got_near[0] + got_across[...]
    for j in range(2):
        shared[0, j] = mine[j].astype(BF16)
    send(shared.at[0], shared.at[2], near, 3, peers.across)
    send(shared.at[0], shared.at[1], near, 4, peers.core)
    norm_tiles(w_gate, gate_grad, w_count // 2, w_count - w_count // 2, False)
    w_copy(w_inner, 0, 0).start()
    come(shared.at[2], 3, peers.across)
    send(shared.at[2], shared.at[3], near, 5, peers.core)
    come(shared.at[1], 4, peers.core)
    come(shared.at[3], 5, peers.core)
    near_sends.wait()
    for k in range(COPIES):
        for b in range(batches):
            for j in range(2):
                part[j, pl.ds(k * batches + b, length, stride=GROUP), :] = shared[
                    k, j, b * length : (b + 1) * length, :
                ].astype(F32)
    for j in range(2):
        low_grad[j] = part[j].astype(BF16)

    piece_sems = (piece_send, piece_recv)

    def pieces_of(index, own, view):
        return Pieces(peers, send, piece_sems, own_sems, index, own, view)

    gate_all = pieces_of(0, lambda: gate_own, lambda k: gate_pieces.at[k])
    loads["total"].wait()
    gate_all.give()

    loads["act"].wait()
    for j, n in ((0, rank), (1, 2 * nstate)):
        weights = lax.dot_general(
            low_grad[j], act_low[...], (((0,), (0,)), ((), ())), preferred_element_type=F32
        )
        small[j * rank : j * rank + n, :] = weights[:n]

    natural = pre_low
    loads["masks"].wait()
    loads["normed"].wait()
    masks[:, total:, :] = jnp.zeros((3, pad, LANES), F32)
    grad[total:, :] = jnp.zeros((pad, chunk), F32)
    for slot in range(2):
        inner[slot, :pad, :] = jnp.zeros((pad, chunk), F32)
    first_tap = first_stride + rank
    ring_sems, few_sems = (ring_send, ring_recv), (few_send, few_recv)

    def block_rows(member, part_of=None):
        start = pl.multiple_of(member * slab, slab)
        if part_of is None:
            return pl.ds(start, slab)
        return pl.ds(start + part_of * (slab // 2), slab // 2)

    def owner(way, step):
        away = half + 1 - step
        return peers.at(away if way == 0 else -away)

    def landing(way, step, c):
        there = held.at[way, step - 1, :, slice(c * chunk, (c + 1) * chunk)]
        return there.at[pl.ds(way * (slab // 2), slab // 2), :] if step == 1 else there

    def arrive(way, step, c):
        there = landing(way, step, c)
        remote(there, there, ring_sems, (way, step - 1, c), peers.ring[way]).wait_recv()

    def ring_step(step, c):
        cols = slice(c * chunk, (c + 1) * chunk)
        for way in range(2):
            member = owner(way, step)
            if step == 1:
                source = wgrad.at[block_rows(member, way), cols]
            else:
                arrive(way, step - 1, c)
                source = held.at[way, step - 2, :, cols]
                if step == 2:
                    here, other = (slice(w * (slab // 2), (w + 1) * (slab // 2)) for w in (way, 1 - way))
                    source[other, :] = wgrad[block_rows(member, 1 - way), cols]
                    source[here, :] = (
                        source[here, :].astype(F32) + wgrad[block_rows(member, way), cols].astype(F32)
                    ).astype(BF16)
                else:
                    source[...] = (
                        source[...].astype(F32) + wgrad[block_rows(member), cols].astype(F32)
                    ).astype(BF16)
            send(source, landing(way, step, c), ring_sems, (way, step - 1, c), peers.ring[way])

    def fold_rows(value):
        out = value[:GROUP]
        for i in range(1, rows // GROUP):
            out = out + value[i * GROUP : (i + 1) * GROUP]
        return out

    for c in range(tiles):
        cols, slot = slice(c * chunk, (c + 1) * chunk), c % 2
        if c + 1 < tiles:
            for copy in tile_copies(c + 1, 1 - slot):
                copy.start()
        for copy in tile_copies(c, slot):
            copy.wait()
        here, there = inner.at[slot], direct.at[slot]
        there[...] += jnp.dot(low_grad[0], few[:rank, cols], preferred_element_type=F32) + jnp.dot(
            low_grad[1], few[rank : rank + LANES, cols], preferred_element_type=F32
        )
        tap = [few[first_tap : first_tap + 16, cols].astype(F32)[i : i + 1] for i in range(5)]

        def back(i, tallies):
            start = pl.multiple_of(i * rows, rows)
            at = pl.ds(start, rows)
            now = here[pl.ds(pad + start, rows), :]
            earlier = [
                here[pl.ds(pad - shift * GROUP + start, rows), :] * tiled(masks[shift - 1, at, :], chunk)
                for shift in range(1, 4)
            ]
            value = tap[4] + tap[3] * now
            for shift in range(1, 4):
                value = value + tap[3 - shift] * earlier[shift - 1]
            sig = sigmoid(value)
            flow = there[at, :] * (sig * (1.0 + value * (1.0 - sig)))
            grad[at, :] = flow
            terms = [flow * e for e in earlier[::-1]] + [flow * now, flow]
            return tuple(tally + fold_rows(term) for tally, term in zip(tallies, terms))

        zero = jnp.zeros((GROUP, chunk), F32)
        tallies = lax.fori_loop(0, total // rows, back, (zero,) * 5)
        for i, tally in enumerate(tallies):
            small[first_tap + i : first_tap + i + 1, cols] = jnp.sum(tally, axis=0, keepdims=True)

        @pl.loop(0, total // rows)
        def _(i):
            start = pl.multiple_of(i * rows, rows)
            at = pl.ds(start, rows)
            value = tap[3] * grad[at, :]
            for shift in range(1, 4):
                after_it = pl.ds(start + shift * GROUP, rows)
                value = value + tap[3 - shift] * (
                    grad[after_it, :] * tiled(masks[shift - 1, after_it, :], chunk)
                )
            inner_grad[at, cols] = value.astype(BF16)
            for k in range(chunk // LANES):
                nat[k, at, :] = value[:, k * LANES : (k + 1) * LANES]

        for k in range(chunk // LANES):
            lanes = slice(c * chunk + k * LANES, c * chunk + (k + 1) * LANES)
            for s in range(GROUP):
                natural[s * length : (s + 1) * length, lanes] = nat[
                    k, pl.ds(s, length, stride=GROUP), :
                ].astype(BF16)
        wgrad[:, cols] = lax.dot_general(
            normed[...], inner_grad[:, cols], (((0,), (0,)), ((), ())), preferred_element_type=F32
        ).astype(BF16)
        ring_step(1, c)
        if c >= 2:
            ring_step(2, c - 2)

    loads["sums"].wait()
    at = first_tap + 5
    small[at : at + 1, :] = jnp.sum(sums[nstate + 1], axis=0, keepdims=True)
    for n in range(nstate):
        small[at + 1 + n : at + 2 + n, :] = LN2 * jnp.sum(sums[n], axis=0, keepdims=True)
    at = at + 1 + nstate
    small[at : at + 1, :] = jnp.sum(sums[nstate], axis=0, keepdims=True)
    small[at + 1 :, :] = jnp.zeros((small.shape[0] - at - 1, width), F32)
    small_low[...] = small[...].astype(BF16)
    few_half = small.shape[0] // 2

    def few_columns(member):
        return pl.ds(pl.multiple_of(member * LANES, LANES), LANES)

    def few_landing(way, step):
        there = small_held.at[way, step - 1]
        return there.at[pl.ds(way * few_half, few_half), :] if step == 1 else there

    def few_arrive(way, step):
        there = few_landing(way, step)
        remote(there, there, few_sems, (way, step - 1), peers.ring[way]).wait_recv()

    def few_step(step):
        for way in range(2):
            columns = few_columns(owner(way, step))
            here, other = (slice(w * few_half, (w + 1) * few_half) for w in (way, 1 - way))
            if step == 1:
                source = small_low.at[pl.ds(way * few_half, few_half), columns]
            else:
                few_arrive(way, step - 1)
                source = small_held.at[way, step - 2]
                if step == 2:
                    source[other, :] = small_low[other, columns]
                    source[here, :] = (
                        source[here, :].astype(F32) + small_low[here, columns].astype(F32)
                    ).astype(BF16)
                else:
                    source[...] = (source[...].astype(F32) + small_low[:, columns].astype(F32)).astype(BF16)
            send(source, few_landing(way, step), few_sems, (way, step - 1), peers.ring[way])

    norm_sum = Parts(peers, send, (part_send, part_recv), norm_parts, norm_near, norm_far, quarter)
    few_step(1)
    norm_tiles(w_inner, natural, 0, w_count, True)
    norm_sum.start()
    ring_step(2, 2)
    ring_step(2, 3)
    ring_step(3, 0)
    norm_sum.come_near()
    near_copy = pltpu.make_async_copy(norm_near.at[1], near_at, w_sems.at[2])
    near_copy.start()
    ring_step(3, 1)
    near_copy.wait()
    norm_sum.go_far(near_at)
    few_step(2)
    ring_step(3, 2)
    ring_step(3, 3)
    few_step(3)
    own_rows = block_rows(peers.member)
    owns = [
        pltpu.make_async_copy(w_inner.at[own_rows, :], w_tiles.at[0], w_sems.at[0]),
        pltpu.make_async_copy(w_gate.at[own_rows, :], w_tiles.at[1], w_sems.at[1]),
        pltpu.make_async_copy(norm_sum.block(0), norm_own, w_sems.at[3]),
    ]
    for copy in owns:
        copy.start()
    for c in range(tiles):
        ring_step(4, c)
    few_step(4)
    gate_all.pass_on()

    def cols_of(c):
        return slice(c * chunk, (c + 1) * chunk)

    inner_all = [
        pieces_of(
            1 + c, lambda c=c: total_at.at[:, cols_of(c)], lambda k, c=c: inner_pieces.at[k, :, cols_of(c)]
        )
        for c in range(tiles)
    ]
    own_block = block_rows(peers.member)
    for c in range(tiles):
        for way in range(2):
            arrive(way, half, c)
        value = wgrad[own_block, cols_of(c)].astype(F32)
        for way in range(2):
            value = value + held[way, half - 1, :, cols_of(c)].astype(F32)
        total_at[:, cols_of(c)] = value.astype(BF16)
        inner_all[c].give()
    for way in range(2):
        few_arrive(way, half)
    value = small_low[:, few_columns(peers.member)].astype(F32)
    for way in range(2):
        value = value + small_held[way, half - 1].astype(F32)
    small_total = small_pieces.at[0]
    small_total[...] = value.astype(BF16)
    for copy in owns:
        copy.wait()
    value = total_at[...].astype(F32) * w_tiles[0].astype(F32)
    value = value + gate_own[...].astype(F32) * w_tiles[1].astype(F32)
    high = value.astype(BF16)
    low = (value - high.astype(F32)).astype(BF16)
    ones = jnp.ones((GROUP, width), BF16)
    nt = (((1,), (1,)), ((), ()))
    value = lax.dot_general(ones, high, nt, preferred_element_type=F32) + lax.dot_general(
        ones, low, nt, preferred_element_type=F32
    )
    gain_at = first_tap + 7 + nstate
    last = small_total[gain_at - gain_at % 16 :, :].astype(F32)
    line = lax.broadcasted_iota(jnp.int32, last.shape, 0) + (gain_at - gain_at % 16)
    for i in range(slab // LANES):
        last = jnp.where(line == gain_at + i, value[0:1, i * LANES : (i + 1) * LANES], last)
    small_total[gain_at - gain_at % 16 :, :] = last.astype(BF16)
    small_all = Pieces(
        peers, send, piece_sems, None, 1 + tiles, lambda: small_total, lambda k: small_pieces.at[k], False
    )
    small_all.give()
    for pieces in (*inner_all, small_all):
        pieces.pass_on()
    norm_sum.come()
    for pieces in (gate_all, *inner_all, small_all):
        pieces.come()
    send.wait()


def finish(size, rank, nstate, arrays, small_rows):
    (pre_low, coef, direct, inner, act_low, step_low, masks, few, normed) = arrays[:9]
    total, width = pre_low.shape
    model = normed.shape[1]
    sums, gate_total = arrays[-2:]
    slab = gate_total.shape[0]
    quarter, half = total // COPIES, size // 2
    inside, anywhere = pl.BlockSpec(memory_space=pltpu.VMEM), pl.BlockSpec(memory_space=pl.ANY)
    shape, dma = jax.ShapeDtypeStruct, pltpu.SemaphoreType.DMA
    low = shape((total, width), BF16)
    wide = shape((total, model), BF16)
    part = shape((quarter, model), BF16)
    padded = total + 3 * GROUP
    scratch = [
        low,
        shape((2, total, LANES), F32),
        shape((2, total, LANES), F32),
        shape((2, 2, quarter, LANES), F32),
        shape((2, quarter, LANES), F32),
        shape((2, quarter, LANES), F32),
        shape((COPIES, 2, quarter, LANES), BF16),
        shape((2, total, LANES), BF16),
        low,
        shape(step_low.shape, BF16),
        shape((3, padded, LANES), F32),
        shape(few.shape, BF16),
        wide,
        low,
        low,
        shape((2, padded, 256), F32),
        shape((2, total, 256), F32),
        shape((padded, 256), F32),
        shape((size * slab, width), BF16),
        shape((2, half, slab, width), BF16),
        shape((small_rows, width), F32),
        shape((small_rows, width), BF16),
        shape((2, half, small_rows, LANES), BF16),
        wide,
        part,
        shape((2, 256, width), BF16),
        shape((slab, width), BF16),
        shape((slab, width), BF16),
        shape(sums.shape, F32),
    ]
    tiles = width // 256
    sems = [(10,), (2, 2), (4,)] + [(6,)] * 2 + [(3,)] * 2 + [(2, half, tiles)] * 2 + [(2, half)] * 2
    sems += [(2 + tiles, 3)] * 2 + [(1 + tiles,)]
    return pl.pallas_call(
        functools.partial(finish_kernel, size, rank, nstate),
        in_specs=[anywhere] * len(arrays),
        out_specs=[anywhere] * 5 + [inside],
        out_shape=[
            shape((COPIES, slab, width), BF16),
            shape((COPIES, slab, width), BF16),
            part,
            shape((2,) + part.shape, BF16),
            part,
            shape((COPIES, small_rows, LANES), BF16),
        ],
        scratch_shapes=[pltpu.VMEM(x.shape, x.dtype) for x in scratch] + [dma(n) for n in sems],
        compiler_params=pltpu.CompilerParams(
            collective_id=2, has_side_effects=True, vmem_limit_bytes=62 * 1024 * 1024
        ),
        cost_estimate=cost(10 * total * width * model, 100 * total * width),
        name="finish",
    )(*arrays)


def place_kernel(
    sizes, copy_ref, inner_ref, gate_ref, out_ref, small_ref, out_own, out_near, out_far, norm_own, norm_near, norm_far,
    tokens_ref, grads_ref, few_ref,
    entry_ref, out_proj_ref, select_ref, stride_ref, taps_ref, decay_ref, rows_ref, block_out_ref, input_grad_ref,
):
    copy = copy_ref[0]
    width = inner_ref.shape[2]
    for k in range(COPIES):
        for side, ref in enumerate((inner_ref, gate_ref)):
            for f in range(width // LANES):
                start = (side * (width // LANES) + f) * COPIES * LANES + (copy ^ k) * LANES
                entry_ref[:, pl.ds(pl.multiple_of(start, LANES), LANES)] = ref[
                    k, :, f * LANES : (f + 1) * LANES
                ].astype(F32)
        out_proj_ref[copy ^ k] = out_ref[k].astype(F32)

    @pl.when(pl.program_id(0) == 0)
    def _():
        for k in range(COPIES):
            piece = small_ref[k].astype(F32)
            at = pl.ds(pl.multiple_of((copy ^ k) * LANES, LANES), LANES)
            stride_ref[at, :] = piece[sizes[0] : sizes[0] + sizes[1]].T
            start = 0
            for size, ref in zip(sizes, (select_ref, None, taps_ref, None, None, decay_ref)):
                if ref is not None:
                    ref[:, at] = piece[start : start + size]
                start += size
            first = start - start % 8
            low_row = sizes[0] + sizes[1]
            rows_ref[:, at] = jnp.concatenate(
                [piece[low_row : low_row + 8], piece[first : first + 8]], axis=0
            )

    tokens = tokens_ref[...].astype(F32)
    summed = out_own[...].astype(F32) + out_near[0].astype(F32) + out_far[...].astype(F32)
    block_out_ref[...] = (tokens + summed).astype(BF16)
    gains = few_ref[...].astype(F32)
    start = sum(sizes) - (sizes[0] + sizes[1])
    gain = jnp.concatenate(
        [
            gains[start + i : start + i + 1, f * LANES : (f + 1) * LANES]
            for f in range(width // LANES)
            for i in range(tokens.shape[1] // width)
        ],
        axis=1,
    )
    scale = lax.rsqrt(jnp.mean(tokens * tokens, axis=-1, keepdims=True) + EPS)
    summed = norm_own[...].astype(F32) + norm_near[0].astype(F32) + norm_far[...].astype(F32)
    scaled = summed * gain
    lean = jnp.mean(scaled * tokens, axis=-1, keepdims=True)
    input_grad_ref[...] = (
        grads_ref[...].astype(F32) + scale * scaled - tokens * (scale * scale * scale) * lean
    ).astype(BF16)


def place(copy, sizes, inner, gate, out, small, out_terms, norm_terms, tokens, grads, few):
    steps = 4
    _, slab, width = inner.shape
    part, model = out.shape[1:]
    rows = tokens.shape[0]
    share = COPIES * LANES

    def cut_rows(total, columns):
        return pl.BlockSpec((total // steps, columns), lambda i, copy: (i, 0))

    def pieces(total, columns):
        return pl.BlockSpec((COPIES, total // steps, columns), lambda i, copy: (0, i, 0))

    def fixed(*shape):
        return pl.BlockSpec(shape, lambda i, copy: (0,) * len(shape))

    first = sizes[0] + sizes[1]
    last = few.shape[0] - first
    shape = jax.ShapeDtypeStruct
    narrow = [(sizes[0], share), (share, sizes[1]), (sizes[2], share), (sizes[5], share)]
    token_rows = cut_rows(rows, model)
    near_rows = pl.BlockSpec((1, rows // steps, model), lambda i, copy: (0, i, 0))
    return pl.pallas_call(
        functools.partial(place_kernel, sizes),
        grid_spec=pltpu.PrefetchScalarGridSpec(
            num_scalar_prefetch=1,
            grid=(steps,),
            in_specs=[pieces(slab, width)] * 2
            + [pieces(part, model), fixed(*small.shape)]
            + [token_rows, near_rows, token_rows] * 2
            + [token_rows] * 2
            + [pl.BlockSpec((last, width), lambda i, copy: (first // last, 0))],
            out_specs=[cut_rows(slab, 2 * COPIES * width), pieces(part, model)]
            + [fixed(*n) for n in narrow]
            + [fixed(16, share)]
            + [token_rows] * 2,
        ),
        out_shape=[
            shape((slab, 2 * COPIES * width), F32),
            shape(out.shape, F32),
        ]
        + [shape(n, F32) for n in narrow]
        + [shape((16, share), F32)]
        + [shape(tokens.shape, BF16)] * 2,
        compiler_params=params(),
        cost_estimate=cost(40 * rows * model, 20 * slab * width),
        name="place",
    )(copy, inner, gate, out, small, *out_terms, *norm_terms, tokens, grads, few)


def on_device(
    tokens, segment_ids, out_grad, norm_gain, in_proj, conv_weight, conv_bias, x_proj,
    step_proj, step_bias, decay_log, skip_gain, out_proj, *, fsdp,
):
    ring = Ring(fsdp)
    copy = lax.axis_index("rep")
    batches, length, model = tokens.shape
    total = COPIES * batches * length
    slab = in_proj.shape[0]
    share = out_proj.shape[0]
    part = share // COPIES
    width = fsdp * part
    rank, nstate = step_proj.shape[1], decay_log.shape[1]
    taps_n = conv_weight.shape[1]
    gains_n = slab // part

    def mine(value):
        return lax.dynamic_slice_in_dim(value, copy * part, part, 0)

    copy_index = copy.astype(jnp.int32).reshape(1)
    aligned = part % LANES == 0
    if not aligned:
        entry = lax.dynamic_index_in_dim(
            in_proj.reshape(slab, 2, fsdp, COPIES, part), copy, 3, keepdims=False
        )
        inner_shard, gate_shard = (entry[:, i].reshape(slab, width) for i in range(2))
    few = jnp.concatenate(
        [
            mine(x_proj).T,
            mine(step_proj).T,
            mine(conv_weight).T,
            mine(conv_bias)[None],
            mine(step_bias)[None],
            mine(decay_log).T,
            mine(skip_gain)[None],
            norm_gain.reshape(gains_n, part),
        ],
        axis=0,
    )
    few = jnp.pad(few, ((0, -few.shape[0] % 16), (0, 0)))
    small_ring = ring.half == 4
    own = [tokens, out_grad, segment_ids[:, 0, :]]
    fused = small_ring and aligned
    if fused:
        out = forward(fsdp, rank, nstate, in_proj, few, *own, out_proj)
        few_all = out["few"].astype(F32)
    else:
        gathers = [Gather(ring, inner_shard), Gather(ring, few)]
        for gather in gathers:
            gather.rest()
        inner_in, few_all = (gather.whole for gather in gathers)
        few_all = jnp.moveaxis(few_all, 0, 1).reshape(-1, width).astype(F32)
        copies = [jnp.stack(rep_gather(value)) for value in own]
        inner_in = inner_in.reshape(model, width)
        values, cotangent, segments = (c.reshape((GROUP,) + c.shape[2:]) for c in copies)

    sizes = [rank + 2 * nstate, rank, taps_n, 1, 1, nstate, 1, gains_n]
    pieces, start = [], 0
    for size in sizes:
        pieces.append(few_all[start : start + size])
        start += size
    select, stride, taps, shift_bias, size_bias, decay, skip, gain = pieces
    select, stride = select.astype(BF16), stride.astype(BF16)
    gain = jnp.moveaxis(gain.reshape(gains_n, fsdp, part), 0, 1).reshape(model)

    def masks_of(segments):
        masks = []
        for shift in range(1, taps_n):
            earlier = jnp.pad(segments, ((0, 0), (shift, 0)), constant_values=-1)[:, :length]
            masks.append((earlier == segments).astype(F32).T.reshape(total, 1))
        return jnp.broadcast_to(jnp.stack(masks), (taps_n - 1, total, LANES))

    tap_rows = jnp.concatenate([taps, shift_bias, jnp.zeros((7 - taps_n, width), F32)])
    side_rows = jnp.concatenate([size_bias, skip, jnp.zeros((6, width), F32)])
    decay_rate = -jnp.exp(decay)

    if fused:
        (
            masks, rate, spread_by, fold_by, normed, cotangent, inner_in, inner, act, act_low, step_low, coef, step,
            states, gate, readout, gated, gated_natural, gate_in, out_w,
        ) = (
            out[k]
            for k in (
                "masks", "rate", "spread_by", "fold_by", "normed", "cotangent", "inner_in", "inner", "act", "act_low",
                "step_low", "coef", "step", "states", "gate", "readout", "gated", "gated_natural", "gate_in", "out_w",
            )
        )
    else:
        rate = jnp.broadcast_to((decay_rate * LOG2E)[:, None, :], (nstate, GROUP, width))
        masks, spread_by, fold_by = masks_of(segments), spreader(nstate), folder(nstate)
        normed, cotangent = interleave(values, gain), interleave(cotangent)
        gathers = [Gather(ring, gate_shard), Gather(ring, mine(out_proj))]
        for gather in gathers:
            gather.rest()
        gate_in = gathers[0].whole.reshape(model, width)
        out_w = gathers[1].whole.reshape(width, model)
        inner = dot(normed, inner_in, 1, 0)
        act, act_low = conv_forward(inner, masks, tap_rows)
        half_sums = sum_near(by_copy(to_sequence(dot(act_low, select, 1, 1))))
        projected = to_time(sum_far(half_sums).reshape(total, -1))
        step_low = projected[:, :rank].astype(BF16)
        coef = spread(projected[:, rank:], nstate)
        pre = dot(step_low, stride, 1, 0)
        readout, step, starts = scan_forward(pre, act, coef, spread_by, masks[0], rate, side_rows)
        gate = dot(normed, gate_in, 1, 0)
        gated, gated_natural = gate_forward(readout, gate)
    if fused:
        gate_grad_natural, pre_low, direct, coef_part, sums, out_pieces, *out_terms, gate_total = backward(
            fsdp, nstate, rank,
            (
                gated, cotangent, out_w, readout, gate, normed, step, act, coef, states, masks, rate, spread_by, fold_by,
                out["few"], gated_natural,
            ),
        )
    else:
        out_wgrad = dot(gated, cotangent, 0, 0).astype(BF16).reshape(fsdp, part, model)
        read_grad, gate_grad, gate_grad_natural = gate_backward(dot(cotangent, out_w, 1, 1), readout, gate)
        gate_wgrad = dot(normed, gate_grad, 0, 0).astype(BF16).reshape(fsdp, slab, width)
        pre_low, direct, coef_part, _, sums = scan_backward(
            step, act, read_grad, coef, spread_by, fold_by, masks[0], rate, side_rows, starts
        )
        scatters = [Scatter(ring, out_wgrad), Scatter(ring, gate_wgrad)]
        for scatter in scatters:
            scatter.rest()
        totals = [scatter.total.astype(BF16) for scatter in scatters]
    small_rows = few.shape[0]
    if fused:
        inner_pieces, gate_pieces, *norm_terms, small_pieces = finish(
            fsdp, rank, nstate,
            (
                pre_low, coef_part, direct, inner, act_low, step_low, masks, out["few"], normed, inner_in, gate_in,
                gate_grad_natural, sums, gate_total,
            ),
            small_rows,
        )
        flat = (batches * length, model)
        entry_all, out_all, select_g, stride_g, taps_g, decay_g, rows_g, block_out, input_grad = place(
            copy_index, sizes[:-1], inner_pieces, gate_pieces, out_pieces, small_pieces, out_terms, norm_terms,
            tokens.reshape(flat), out_grad.reshape(flat), out["few"],
        )
        gain_at = sum(sizes[:-1])
        gain_sum = jnp.sum(small_pieces[:, gain_at : gain_at + gains_n].astype(F32), axis=0).reshape(slab)
        return (
            block_out.reshape(tokens.shape),
            input_grad.reshape(tokens.shape),
            gain_sum / norm_gain.astype(F32),
            entry_all,
            taps_g.T,
            rows_g[taps_n],
            select_g.T,
            stride_g,
            rows_g[taps_n + 1],
            decay_g.T,
            rows_g[8 + (gain_at - 1) % 8],
            out_all.reshape(share, model),
        )
    else:
        low_part = dot(pre_low, stride, 1, 1)
        proj_part = jnp.concatenate([low_part, coef_part[:, : 2 * nstate]], axis=1)
        half_sums = sum_near(by_copy(to_sequence(proj_part)))
        proj_time = to_time(sum_far(half_sums).reshape(total, -1).astype(BF16))
        act_grad = direct + dot(proj_time, select, 1, 0)
        inner_grad, inner_grad_natural, conv_sums = conv_backward(inner, act_grad, masks, tap_rows)
        inner_wgrad = dot(normed, inner_grad, 0, 0).astype(BF16).reshape(fsdp, slab, width)
        small = jnp.concatenate(
            [
                dot(proj_time, act_low, 0, 0),
                dot(step_low, pre_low, 0, 0),
                conv_sums[: taps_n + 1],
                jnp.sum(sums[nstate + 1 :], axis=1),
                decay_rate * jnp.sum(sums[:nstate], axis=1),
                jnp.sum(sums[nstate : nstate + 1], axis=1),
            ],
            axis=0,
        )
        small = jnp.pad(small, ((0, small_rows - small.shape[0]), (0, 0))).astype(BF16)
        small = jnp.moveaxis(small.reshape(-1, fsdp, part), 1, 0)
        grads = dot(inner_grad_natural, inner_in, 1, 1) + dot(gate_grad_natural, gate_in, 1, 1)
        sums_of = []
        for parts in (dot(gated_natural, out_w, 1, 0), grads):
            sums_of.append(rep_scatter_far(*rep_scatter_near(by_copy(parts.astype(BF16)))))
        out_sum, normed_sum = sums_of
        scatters = [Scatter(ring, inner_wgrad), Scatter(ring, small)]
        for scatter in scatters:
            scatter.rest()
        totals = [scatter.total.astype(BF16) for scatter in scatters] + totals
        inner_pieces, small_pieces, out_pieces, gate_pieces = (rep_gather(t) for t in totals)

    block_out = (tokens.astype(F32) + out_sum.reshape(tokens.shape)).astype(BF16)
    normed_grad = normed_sum.reshape(tokens.shape)
    own_values = tokens.astype(F32)
    own_scale = lax.rsqrt(jnp.mean(own_values * own_values, axis=-1, keepdims=True) + EPS)
    scaled = normed_grad * gain
    lean = jnp.mean(scaled * own_values, axis=-1, keepdims=True)
    input_grad = (
        out_grad.astype(F32) + own_scale * scaled - own_values * (own_scale**3) * lean
    ).astype(BF16)

    order = jnp.arange(COPIES) ^ copy
    out_all = jnp.stack(out_pieces)[order].reshape(share, model).astype(F32)
    halves = jnp.stack([jnp.stack(inner_pieces), jnp.stack(gate_pieces)])[:, order]
    halves = halves.reshape(2, COPIES, slab, fsdp, part).astype(F32)
    entry_all = jnp.transpose(halves, (2, 0, 3, 1, 4)).reshape(slab, -1)
    gain_sum = jnp.sum(entry_all * in_proj.astype(F32), axis=1)
    gain_grad = gain_sum / norm_gain.astype(F32)
    small_all = jnp.stack(small_pieces)[order].astype(F32)
    small_all = jnp.moveaxis(small_all, 0, 1).reshape(-1, share)
    out, start = [], 0
    for size in sizes[:-1]:
        out.append(small_all[start : start + size])
        start += size
    select_g, stride_g, taps_g, shift_g, size_g, decay_g, skip_g = out
    return (
        block_out,
        input_grad,
        gain_grad,
        entry_all,
        taps_g.T,
        shift_g[0],
        select_g.T,
        stride_g.T,
        size_g[0],
        decay_g.T,
        skip_g[0],
        out_all,
    )


def solution(mesh):
    tokens = P(None, ("fsdp", "rep"), None)
    rows, row = P("fsdp", None), P("fsdp")
    return jax.shard_map(
        functools.partial(on_device, fsdp=mesh.shape["fsdp"]),
        mesh=mesh,
        in_specs=(tokens, tokens, tokens, row, rows, rows, row, rows, rows, row, rows, row, rows),
        out_specs=(tokens, tokens, row, rows, rows, row, rows, rows, row, rows, row, rows),
        check_vma=False,
    )
```

```python
import functools

import jax
import jax.numpy as jnp
from jax import lax
from jax.experimental import pallas as pl
from jax.experimental.pallas import tpu as pltpu
from jax.sharding import PartitionSpec as P

EPS = 1e-05
BLOCK = 16
LANES = 128
GROUP = 8
COPIES = 4
LOG2E = 1.4426950408889634
LN2 = 0.6931471805599453
FAR = 1e30
F32 = jnp.float32
BF16 = jnp.bfloat16
VMEM_LIMIT = 56 * 1024 * 1024


def dot(left, right, left_dim, right_dim):
    return lax.dot_general(
        left, right, (((left_dim,), (right_dim,)), ((), ())), preferred_element_type=F32
    )


def params():
    return pltpu.CompilerParams(vmem_limit_bytes=VMEM_LIMIT)


def cost(flops, moved):
    return pl.CostEstimate(flops=int(flops), bytes_accessed=int(moved), transcendentals=0)


def blank(shape, dtype):
    return pl.pallas_call(
        lambda ref: None,
        out_shape=jax.ShapeDtypeStruct(shape, dtype),
        out_specs=pl.BlockSpec(memory_space=pl.ANY),
        name="blank",
    )()


def ring_order(size):
    half = size // 2
    return [2 * p if p < half else 2 * (size - 1 - p) + 1 for p in range(size)]


class Ring:
    def __init__(self, size):
        order = ring_order(size)
        place = [0] * size
        for spot, member in enumerate(order):
            place[member] = spot
        self.size, self.half = size, size // 2
        self.order = jnp.array(order, jnp.int32)
        self.spot = jnp.array(place, jnp.int32)[lax.axis_index("fsdp")]
        self.above = [(order[p], order[(p + 1) % size]) for p in range(size)]
        self.below = [(order[p], order[(p - 1) % size]) for p in range(size)]

    def member(self, offset):
        return self.order[(self.spot + offset + self.size) % self.size]

    def up(self, value):
        return lax.ppermute(value, "fsdp", self.above)

    def down(self, value):
        return lax.ppermute(value, "fsdp", self.below)


class Gather:
    def __init__(self, ring, shard):
        self.ring, self.cut = ring, shard.shape[0] // 2
        self.whole = blank((ring.size,) + shard.shape, shard.dtype)
        self.held = (shard, shard)
        self.put(shard, 0)

    def put(self, piece, offset, start=0):
        at = (self.ring.member(offset), jnp.int32(start), jnp.int32(0))
        self.whole = lax.dynamic_update_slice(self.whole, piece[None], at)

    def step(self, number):
        low, high = self.held
        if number == self.ring.half:
            low, high = low[: self.cut], high[self.cut :]
        return self.ring.up(low), self.ring.down(high)

    def take(self, number, got):
        self.held = got
        last = number == self.ring.half
        self.put(got[0], -number)
        self.put(got[1], number, self.cut if last else 0)

    def rest(self):
        def body(number, state):
            whole, low, high = state
            low, high = self.ring.up(low), self.ring.down(high)
            self.whole = whole
            self.put(low, -number)
            self.put(high, number)
            return self.whole, low, high

        self.whole, low, high = lax.fori_loop(1, self.ring.half, body, (self.whole,) + self.held)
        self.held = (low, high)
        self.take(self.ring.half, self.step(self.ring.half))


class Scatter:
    def __init__(self, ring, parts):
        self.ring, self.parts, self.cut = ring, parts, parts.shape[1] // 2
        far = self.own(ring.half)
        self.sent = (far[: self.cut], far[self.cut :])
        self.total = None

    def own(self, offset):
        return lax.dynamic_index_in_dim(self.parts, self.ring.member(offset), 0, keepdims=False)

    def step(self, number):
        return self.ring.up(self.sent[0]), self.ring.down(self.sent[1])

    def take(self, number, got):
        left = self.ring.half - number
        low, high = got
        near_low, near_high = self.own(left), self.own(-left)
        if number == 1:
            low = jnp.concatenate([low, jnp.zeros_like(near_low[self.cut :])])
            high = jnp.concatenate([jnp.zeros_like(near_high[: self.cut]), high])
        if left == 0:
            self.total = near_low.astype(F32) + low.astype(F32) + high.astype(F32)
        else:
            self.sent = (self.add(near_low, low), self.add(near_high, high))

    def add(self, near, got):
        return (near.astype(F32) + got.astype(F32)).astype(near.dtype)

    def rest(self):
        self.take(1, self.step(1))

        def body(number, sent):
            left = self.ring.half - number
            low, high = self.ring.up(sent[0]), self.ring.down(sent[1])
            return self.add(self.own(left), low), self.add(self.own(-left), high)

        self.sent = lax.fori_loop(2, self.ring.half, body, self.sent)
        self.take(self.ring.half, self.step(self.ring.half))


def swap(value, bit):
    return lax.ppermute(value, "rep", [(r, r ^ bit) for r in range(COPIES)])


def rep_gather(value):
    across = swap(value, 2)
    return [value, swap(value, 1), across, swap(across, 1)]


def rep_scatter_near(parts):
    pair = swap(jnp.stack([parts[1], parts[3]]), 1)
    near = parts[0].astype(F32) + pair[0].astype(F32)
    far = parts[2].astype(F32) + pair[1].astype(F32)
    return near, far.astype(parts.dtype)


def rep_scatter_far(near, far):
    return near + swap(far, 2).astype(F32)


def sum_near(parts):
    pair = swap(jnp.stack([parts[1], parts[3]]), 1)
    mine = jnp.stack([parts[0], parts[2]]) + pair
    return mine + swap(jnp.stack([mine[1], mine[0]]), 2)


def sum_far(mine):
    next_to = swap(mine, 1)
    return jnp.stack([mine[0], next_to[0], mine[1], next_to[1]])


def to_time(value):
    return jnp.swapaxes(value.reshape(GROUP, -1, value.shape[-1]), 0, 1).reshape(value.shape)


def to_sequence(value):
    return jnp.swapaxes(value.reshape(-1, GROUP, value.shape[-1]), 0, 1).reshape(value.shape)


def by_copy(value):
    return value.reshape(COPIES, -1, value.shape[-1])


def sigmoid(value):
    return 1.0 / (1.0 + jnp.exp(-value))


def later(value, shift):
    rows = shift * GROUP
    return jnp.concatenate([jnp.zeros_like(value[:rows]), value[:-rows]], axis=0)


def sooner(value, shift):
    rows = shift * GROUP
    return jnp.concatenate([value[rows:], jnp.zeros_like(value[:rows])], axis=0)


def conv_of(inner, masks, taps):
    total = taps[4:5] + taps[3:4] * inner
    for shift in range(1, 4):
        total = total + taps[3 - shift : 4 - shift] * (later(inner, shift) * masks[shift - 1])
    return total


def by_sequence(held, out_ref, value):
    length = value.shape[0] // GROUP
    held[...] = value
    for s in range(GROUP):
        out_ref[s * length : (s + 1) * length, :] = held[
            pl.ds(s, length, stride=GROUP), :
        ].astype(out_ref.dtype)


def conv_kernel(inner_ref, masks_ref, taps_ref, act_ref, low_ref):
    value = conv_of(inner_ref[...], masks_ref, taps_ref[...])
    act = value * sigmoid(value)
    act_ref[...] = act
    low_ref[...] = act.astype(BF16)


def conv_forward(inner, masks, taps):
    rows, width = inner.shape
    tile = pl.BlockSpec((rows, LANES), lambda c: (0, c))
    return pl.pallas_call(
        conv_kernel,
        grid=(width // LANES,),
        in_specs=[
            tile,
            pl.BlockSpec((3, rows, LANES), lambda c: (0, 0, 0)),
            pl.BlockSpec((8, LANES), lambda c: (0, c)),
        ],
        out_specs=[tile, tile],
        out_shape=[
            jax.ShapeDtypeStruct((rows, width), F32),
            jax.ShapeDtypeStruct((rows, width), BF16),
        ],
        compiler_params=params(),
        cost_estimate=cost(30 * rows * width, 10 * rows * width),
        name="conv_forward",
    )(inner, masks, taps)


def conv_back_kernel(inner_ref, grad_ref, masks_ref, taps_ref, out_ref, natural_ref, sums_ref, held):
    inner, taps = inner_ref[...], taps_ref[...]
    value = conv_of(inner, masks_ref, taps)
    gate = sigmoid(value)
    grad = grad_ref[...] * (gate * (1.0 + value * (1.0 - gate)))
    total = taps[3:4] * grad
    sums = [None] * 4 + [jnp.sum(grad, axis=0, keepdims=True)]
    sums[3] = jnp.sum(grad * inner, axis=0, keepdims=True)
    for shift in range(1, 4):
        masked = grad * masks_ref[shift - 1]
        total = total + taps[3 - shift : 4 - shift] * sooner(masked, shift)
        sums[3 - shift] = jnp.sum(masked * later(inner, shift), axis=0, keepdims=True)
    out_ref[...] = total.astype(BF16)
    by_sequence(held, natural_ref, total)
    sums_ref[...] = jnp.concatenate(sums + [jnp.zeros((3, inner.shape[1]), F32)], axis=0)


def conv_backward(inner, grad, masks, taps):
    rows, width = inner.shape
    tile = pl.BlockSpec((rows, LANES), lambda c: (0, c))
    few = pl.BlockSpec((8, LANES), lambda c: (0, c))
    return pl.pallas_call(
        conv_back_kernel,
        grid=(width // LANES,),
        in_specs=[tile, tile, pl.BlockSpec((3, rows, LANES), lambda c: (0, 0, 0)), few],
        out_specs=[tile, tile, few],
        out_shape=[
            jax.ShapeDtypeStruct((rows, width), BF16),
            jax.ShapeDtypeStruct((rows, width), BF16),
            jax.ShapeDtypeStruct((8, width), F32),
        ],
        scratch_shapes=[pltpu.VMEM((rows, LANES), F32)],
        compiler_params=params(),
        cost_estimate=cost(60 * rows * width, 10 * rows * width),
        name="conv_backward",
    )(inner, grad, masks, taps)


def gate_kernel(readout_ref, gate_ref, out_ref, natural_ref, held):
    gate = gate_ref[...]
    gated = readout_ref[...] * (gate * sigmoid(gate))
    out_ref[...] = gated.astype(BF16)
    by_sequence(held, natural_ref, gated)


def gate_forward(readout, gate):
    rows, width = gate.shape
    tile = pl.BlockSpec((rows, LANES), lambda c: (0, c))
    return pl.pallas_call(
        gate_kernel,
        grid=(width // LANES,),
        in_specs=[tile] * 2,
        out_specs=[tile] * 2,
        out_shape=[jax.ShapeDtypeStruct((rows, width), BF16)] * 2,
        scratch_shapes=[pltpu.VMEM((rows, LANES), F32)],
        compiler_params=params(),
        cost_estimate=cost(20 * rows * width, 12 * rows * width),
        name="gate_forward",
    )(readout, gate)


def gate_back_kernel(grad_ref, readout_ref, gate_ref, read_ref, out_ref, natural_ref, held):
    gate, grad = gate_ref[...], grad_ref[...]
    sig = sigmoid(gate)
    read_ref[...] = grad * (gate * sig)
    gate_grad = grad * readout_ref[...] * (sig * (1.0 + gate * (1.0 - sig)))
    out_ref[...] = gate_grad.astype(BF16)
    by_sequence(held, natural_ref, gate_grad)


def gate_backward(grad, readout, gate):
    rows, width = gate.shape
    tile = pl.BlockSpec((rows, LANES), lambda c: (0, c))
    return pl.pallas_call(
        gate_back_kernel,
        grid=(width // LANES,),
        in_specs=[tile] * 3,
        out_specs=[tile] * 3,
        out_shape=[jax.ShapeDtypeStruct((rows, width), F32)]
        + [jax.ShapeDtypeStruct((rows, width), BF16)] * 2,
        scratch_shapes=[pltpu.VMEM((rows, LANES), F32)],
        compiler_params=params(),
        cost_estimate=cost(20 * rows * width, 20 * rows * width),
        name="gate_backward",
    )(grad, readout, gate)


def rows_kernel(scaled, *refs):
    values_ref, out_ref, held = refs[0], refs[-2], refs[-1]
    for s in range(GROUP):
        value = values_ref[s].astype(F32)
        if scaled:
            square = jnp.mean(value * value, axis=-1, keepdims=True)
            value = value * lax.rsqrt(square + EPS) * refs[1][...]
        for k in range(held.shape[0]):
            held[k, pl.ds(s, value.shape[0], stride=GROUP), :] = value[
                :, k * LANES : (k + 1) * LANES
            ]
    for k in range(held.shape[0]):
        out_ref[:, k * LANES : (k + 1) * LANES] = held[k].astype(BF16)


def interleave(values, gain=None):
    _, length, model = values.shape
    extra = [] if gain is None else [gain.reshape(1, model)]
    return pl.pallas_call(
        functools.partial(rows_kernel, gain is not None),
        grid=(length // BLOCK,),
        in_specs=[pl.BlockSpec((GROUP, BLOCK, model), lambda t: (0, t, 0))]
        + [pl.BlockSpec((1, model), lambda t: (0, 0))] * len(extra),
        out_specs=pl.BlockSpec((BLOCK * GROUP, model), lambda t: (t, 0)),
        out_shape=jax.ShapeDtypeStruct((length * GROUP, model), BF16),
        scratch_shapes=[pltpu.VMEM((model // LANES, BLOCK * GROUP, LANES), F32)],
        compiler_params=params(),
        cost_estimate=cost(8 * GROUP * length * model, 4 * GROUP * length * model),
        name="interleave",
    )(values, *extra)


class Peers:
    def __init__(self, size):
        self.size, self.half = size, size // 2
        self.member, self.copy = lax.axis_index("fsdp"), lax.axis_index("rep")
        row, column = lax.div(self.member, 2), lax.rem(self.member, 2)
        self.spot = row * (1 - column) + (size - 1 - row) * column
        side = lax.rem(self.copy, 2)
        self.core = (self.member, self.copy - side + (1 - side))
        self.across = (self.member, lax.rem(self.copy + 2, COPIES))
        self.ring = ((self.at(1), self.copy), (self.at(-1), self.copy))

    def at(self, offset):
        spot = lax.rem(self.spot + (offset + self.size), self.size)
        second = lax.div(spot, self.half)
        return 2 * spot * (1 - second) + (2 * (self.size - 1 - spot) + 1) * second

    def meet(self):
        barrier = pltpu.get_barrier_semaphore()
        peers = (*self.ring, self.core, self.across)
        for peer in peers:
            pl.semaphore_signal(barrier, inc=1, device_id=peer, device_id_type=pl.DeviceIdType.MESH)
        pl.semaphore_wait(barrier, len(peers))


def remote(source, target, sems, index, peer):
    return pltpu.make_async_remote_copy(
        src_ref=source,
        dst_ref=target,
        send_sem=sems[0].at[index],
        recv_sem=sems[1].at[index],
        device_id=peer,
        device_id_type=pl.DeviceIdType.MESH,
    )


def spread(coefs, nstate):
    terms = []
    for _ in range(3):
        term = coefs.astype(BF16)
        terms.append(term)
        coefs = coefs - term.astype(F32)
    joined = jnp.concatenate(terms, axis=1)
    return jnp.pad(joined, ((0, 0), (0, LANES - joined.shape[1])))


def spreader(nstate):
    row = lax.broadcasted_iota(jnp.int32, (LANES, 2 * nstate * LANES), 0)
    tile = lax.broadcasted_iota(jnp.int32, (LANES, 2 * nstate * LANES), 1) // LANES
    return ((row % (2 * nstate) == tile) & (row < 6 * nstate)).astype(BF16)


def folder(nstate):
    tile = lax.broadcasted_iota(jnp.int32, (2 * nstate * LANES, LANES), 0) // LANES
    column = lax.broadcasted_iota(jnp.int32, (2 * nstate * LANES, LANES), 1)
    return (tile == column).astype(BF16)


def tiled(value, width):
    return jnp.concatenate([value] * (width // LANES), axis=1)


def at_time(t):
    return pl.ds(pl.multiple_of(t * GROUP, GROUP), GROUP)


def scan_kernel(
    nstate, chunk, pre_ref, act_ref, coef_ref, spread_ref, keep_ref, rate_ref, row_ref,
    out_ref, step_ref, start_ref, carry_ref, wide,
):
    width = pre_ref.shape[1]

    @pl.when(pl.program_id(0) == 0)
    def _():
        carry_ref[...] = jnp.zeros_like(carry_ref)

    start_ref[0] = carry_ref[...]
    wide[...] = jnp.dot(coef_ref[...], spread_ref[...], preferred_element_type=F32)
    pre = pre_ref[...] + row_ref[0:1]
    step_ref[...] = jnp.maximum(pre, 0.0) + jnp.log1p(jnp.exp(-jnp.abs(pre)))
    for c in range(width // chunk):
        cols = slice(c * chunk, (c + 1) * chunk)

        def advance(t, states):
            at = at_time(t)
            step, act = step_ref[at, cols], act_ref[at, cols]
            drive = jnp.where(tiled(keep_ref[at, :], chunk) > 0.5, step, FAR)
            inflow = step * act
            total = row_ref[1:2, cols] * act
            now = []
            for n in range(nstate):
                write = tiled(wide[at, n * LANES : (n + 1) * LANES], chunk)
                read = tiled(wide[at, (nstate + n) * LANES : (nstate + n + 1) * LANES], chunk)
                state = jnp.exp2(drive * rate_ref[n, :, cols]) * states[n] + write * inflow
                total = total + read * state
                now.append(state)
            out_ref[at, cols] = total
            return tuple(now)

        start = tuple(carry_ref[n, :, cols] for n in range(nstate))
        states = lax.fori_loop(0, BLOCK, advance, start, unroll=4)
        for n in range(nstate):
            carry_ref[n, :, cols] = states[n]


def scan_forward(pre, act, coef, spread_by, keep, rate, rows):
    total, width = pre.shape
    nstate = rate.shape[0]
    size = BLOCK * GROUP
    tile = pl.BlockSpec((size, width), lambda t: (t, 0))
    thin = pl.BlockSpec((size, LANES), lambda t: (t, 0))
    state = pl.BlockSpec((nstate, GROUP, width), lambda t: (0, 0, 0))
    count = total // size
    work = total * width * nstate
    return pl.pallas_call(
        functools.partial(scan_kernel, nstate, 256),
        grid=(count,),
        in_specs=[
            tile,
            tile,
            thin,
            pl.BlockSpec(spread_by.shape, lambda t: (0, 0)),
            thin,
            state,
            pl.BlockSpec((8, width), lambda t: (0, 0)),
        ],
        out_specs=[
            tile,
            tile,
            pl.BlockSpec((1, nstate, GROUP, width), lambda t: (t, 0, 0, 0)),
        ],
        out_shape=[
            jax.ShapeDtypeStruct((total, width), F32),
            jax.ShapeDtypeStruct((total, width), F32),
            jax.ShapeDtypeStruct((total // size, nstate, GROUP, width), F32),
        ],
        scratch_shapes=[
            pltpu.VMEM((nstate, GROUP, width), F32),
            pltpu.VMEM((size, 2 * nstate * LANES), F32),
        ],
        compiler_params=params(),
        cost_estimate=cost(16 * work, 16 * count * size * width),
        name="scan_forward",
    )(pre, act, coef, spread_by, keep, rate, rows)


def start_send(*copy):
    remote(*copy).start()


class Sends:
    def __init__(self):
        self.sent = []

    def __call__(self, *copy):
        moving = remote(*copy)
        moving.start()
        self.sent.append(moving)

    def wait(self):
        for moving in self.sent:
            moving.wait_send()
        self.sent = []


class Pieces:
    def __init__(self, peers, send, sems, own_sems, index, own, view, kept=True):
        self.peers, self.send, self.sems, self.own_sems = peers, send, sems, own_sems
        self.index, self.own, self.view, self.kept = index, own, view, kept

    def keep(self):
        return pltpu.make_async_copy(self.own(), self.view(0), self.own_sems.at[self.index])

    def give(self):
        if self.kept:
            self.keep().start()
        self.send(self.own(), self.view(2), self.sems, (self.index, 0), self.peers.across)
        self.send(self.own(), self.view(1), self.sems, (self.index, 1), self.peers.core)

    def pass_on(self):
        there = self.view(2)
        remote(there, there, self.sems, (self.index, 0), self.peers.across).wait_recv()
        self.send(there, self.view(3), self.sems, (self.index, 2), self.peers.core)

    def come(self):
        for k, which in ((1, 1), (3, 2)):
            there = self.view(k)
            remote(there, there, self.sems, (self.index, which), self.peers.core).wait_recv()
        if self.kept:
            self.keep().wait()

    def sent_all(self):
        for which, target in ((0, 2), (1, 1), (2, 3)):
            there = self.view(target)
            remote(there, there, self.sems, (self.index, which), self.peers.core).wait_send()


class Parts:
    def __init__(self, peers, send, sems, parts, near, far, rows, base=0):
        self.peers, self.send, self.sems, self.base = peers, send, sems, base
        self.parts, self.near, self.far, self.rows = parts, near, far, rows

    def block(self, k):
        return self.parts.at[pl.ds(k * self.rows, self.rows), :]

    def start(self):
        for i in range(2):
            self.send(self.block(2 * i + 1), self.near.at[i], self.sems, self.base + i, self.peers.core)

    def come_near(self):
        for i in range(2):
            there = self.near.at[i]
            remote(there, there, self.sems, self.base + i, self.peers.core).wait_recv()

    def go_far(self, here):
        there = self.block(2)
        there[...] = (there[...].astype(F32) + here[...].astype(F32)).astype(BF16)
        self.send(there, self.far, self.sems, self.base + 2, self.peers.across)

    def come(self):
        remote(self.far, self.far, self.sems, self.base + 2, self.peers.across).wait_recv()

    def sent_all(self):
        for i in range(2):
            there = self.near.at[i]
            remote(there, there, self.sems, self.base + i, self.peers.core).wait_send()
        remote(self.far, self.far, self.sems, self.base + 2, self.peers.across).wait_send()


class Shares:
    def __init__(self, peers, shards, wholes, sems):
        self.peers, self.shards, self.wholes, self.sems = peers, shards, wholes, sems
        self.sent = []

    def place(self, which, member, c):
        rows = self.shards[which].shape[0]
        start = pl.multiple_of(member * rows + c * (rows // 2), rows // 2)
        return self.wholes[which].at[pl.ds(start, rows // 2), :]

    def owner(self, way, step):
        return self.peers.at(-step if way == 0 else step)

    def chunks(self, way, step):
        return (way,) if step == self.peers.half else (0, 1)

    def come(self, which, way, step, c):
        there = self.place(which, self.owner(way, step), c)
        remote(there, there, self.sems, (which, way, step - 1, c), self.peers.ring[way]).wait_recv()

    def step(self, which, step):
        for c in range(2):
            for way in range(2):
                if c not in self.chunks(way, step):
                    continue
                target = self.place(which, self.owner(way, step - 1), c)
                source = target
                if step == 1:
                    rows = self.shards[which].shape[0] // 2
                    source = self.shards[which].at[pl.ds(c * rows, rows), :]
                else:
                    self.come(which, way, step - 1, c)
                index = (which, way, step - 1, c)
                remote(source, target, self.sems, index, self.peers.ring[way]).start()

    def finish(self, which):
        half = self.peers.half
        for way in range(2):
            self.come(which, way, half - 1, 1 - way)
            self.come(which, way, half, way)

    def sent_all(self):
        for which in range(len(self.shards)):
            for step in range(1, self.peers.half + 1):
                for way in range(2):
                    for c in self.chunks(way, step):
                        place = self.place(which, self.owner(way, step - 1), c)
                        index = (which, way, step - 1, c)
                        remote(place, place, self.sems, index, self.peers.ring[way]).wait_send()


def softplus(value):
    return jnp.maximum(value, 0.0) + jnp.log1p(jnp.exp(-jnp.abs(value)))


def forward_kernel(
    size, rank, nstate,
    entry, few, tokens, out_grad, segments, out_proj,
    few_out, masks_out, rate_out, spread_out, fold_out, normed_out, cotangent_out, tokens_all, grads_all, segments_all,
    w_in_out, inner_out, act_out, low_out, step_low_out, coef_out, step_out, states_out, gate_out, readout_out,
    gated_out, natural_out, gate_w_out, out_w_out,
    few_all, small, masks, rate, spread_by, fold_by, normed, stage, cotangent, held, seg, inner_shard, gate_shard, w_in,
    inner, act, low, part, nat, got_near, to_across, got_across, shared, step_low, coef, wide, pre, step, readout,
    carry, states_at, gate, gated, natural, gate_w,
    local, states_sems, gate_sems, own_sems, entry_sems, stage_sems, out_sems, seg_sems,
    ring_send, ring_recv, few_send, few_recv, rep_send, rep_recv, near_send, near_recv,
):
    peers = Peers(size)
    total, width = normed.shape[0], w_in.shape[1]
    pad = 3 * GROUP
    chunk = 256
    rows = 64
    length = total // GROUP
    batches = GROUP // COPIES
    half = peers.half
    side_rows = total // COPIES
    saved = []

    def save(source, target):
        copy = pltpu.make_async_copy(source, target, local.at[len(saved)])
        copy.start()
        saved.append(copy)

    picks = []
    for side_of, target in enumerate((inner_shard, gate_shard)):
        for f in range(size):
            source = ((side_of * size + f) * COPIES + peers.copy) * LANES
            picks.append(
                pltpu.make_async_copy(
                    entry.at[:, pl.ds(pl.multiple_of(source, LANES), LANES)],
                    target.at[:, pl.ds(f * LANES, LANES)],
                    entry_sems.at[len(picks)],
                )
            )
    for pick in picks:
        pick.start()
    peers.meet()
    sent = []

    def send(*copy):
        moving = remote(*copy)
        moving.start()
        sent.append(moving)

    rep_sems = (rep_send, rep_recv)

    def of_copy(ref, k):
        return ref.at[k] if ref is segments_all else ref.at[pl.ds(k * batches, batches)]

    def exchange(i, own, everyone):
        send(own, of_copy(everyone, 2), rep_sems, (i, 0), peers.across)
        send(own, of_copy(everyone, 1), rep_sems, (i, 1), peers.core)

    def pass_on(i, everyone):
        far = of_copy(everyone, 2)
        remote(far, far, rep_sems, (i, 0), peers.across).wait_recv()
        send(far, of_copy(everyone, 3), rep_sems, (i, 2), peers.core)

    def exchanged(i, everyone):
        for k, which in ((1, 1), (3, 2)):
            there = of_copy(everyone, k)
            remote(there, there, rep_sems, (i, which), peers.core).wait_recv()

    out_rows = out_proj.shape[0] // COPIES
    out_shard = out_proj.at[pl.ds(pl.multiple_of(peers.copy * out_rows, out_rows), out_rows), :]
    ring = Shares(
        peers, (inner_shard, gate_shard, out_shard), (w_in, gate_w, out_w_out), (ring_send, ring_recv),
    )
    gate_rows = gate_shard.shape[0]
    shard_rows = pl.ds(pl.multiple_of(peers.member * gate_rows, gate_rows), gate_rows)
    own_rows = pl.ds(pl.multiple_of(peers.member * out_rows, out_rows), out_rows)
    own_columns = pl.ds(pl.multiple_of(peers.member * LANES, LANES), LANES)

    few_sems = (few_send, few_recv)
    few_rows = few.shape[0] // 2

    def few_place(way, number, split):
        columns = pl.ds(pl.multiple_of(ring.owner(way, number) * LANES, LANES), LANES)
        place = pl.ds(way * few_rows, few_rows) if split else pl.ds(0, 2 * few_rows)
        return few_all.at[place, columns]

    def few_come(way, number):
        there = few_place(way, number, number == half)
        remote(there, there, few_sems, (way, number - 1), peers.ring[way]).wait_recv()

    def few_step(number):
        for way in range(2):
            if number > 1:
                few_come(way, number - 1)
            target = few_place(way, number - 1, number == half)
            source = few if number == 1 else target
            send(source, target, few_sems, (way, number - 1), peers.ring[way])

    few_step(1)
    exchange(2, segments, segments_all)
    exchange(0, tokens, tokens_all)
    own = [
        pltpu.make_async_copy(few, few_all.at[:, own_columns], own_sems.at[0]),
        pltpu.make_async_copy(out_shard, cotangent.at[1], own_sems.at[1]),
        pltpu.make_async_copy(segments, seg.at[0], own_sems.at[3]),
    ]
    for copy in own:
        copy.start()
    for pick in picks[:size]:
        pick.wait()
    ring.step(0, 1)
    own[1].wait()
    own_out = pltpu.make_async_copy(cotangent.at[1], out_w_out.at[own_rows, :], own_sems.at[4])
    own_out.start()
    for pick in picks[size:]:
        pick.wait()
    own_shards = [
        pltpu.make_async_copy(inner_shard, w_in.at[shard_rows, :], own_sems.at[6]),
        pltpu.make_async_copy(gate_shard, gate_w.at[shard_rows, :], own_sems.at[2]),
    ]
    for copy in own_shards:
        copy.start()

    wide_shape, thin_shape = spread_by.shape, fold_by.shape
    tile = lax.broadcasted_iota(jnp.int32, wide_shape, 1) // LANES
    row = lax.broadcasted_iota(jnp.int32, wide_shape, 0)
    spread_by[...] = jnp.where(
        (lax.rem(row, 2 * nstate) == tile) & (row < 6 * nstate), 1.0, 0.0
    ).astype(BF16)
    tile = lax.broadcasted_iota(jnp.int32, thin_shape, 0) // LANES
    column = lax.broadcasted_iota(jnp.int32, thin_shape, 1)
    fold_by[...] = jnp.where(tile == column, 1.0, 0.0).astype(BF16)
    save(spread_by, spread_out)
    save(fold_by, fold_out)

    few_step(2)
    pass_on(2, segments_all)
    few_step(3)
    ring.step(0, 2)
    few_step(4)
    exchanged(2, segments_all)
    others = pl.ds(1, COPIES - 1)
    numbers = pltpu.make_async_copy(segments_all.at[others], seg.at[others], seg_sems.at[0])
    numbers.start()
    for way in range(2):
        few_come(way, half - 1) if half < 2 else None
        few_come(way, half)
    own[0].wait()
    own[2].wait()
    numbers.wait()
    own_out.wait()

    numbers = jnp.concatenate([seg[k] for k in range(COPIES)], axis=0).astype(F32)
    lane = lax.broadcasted_iota(jnp.int32, (total, LANES), 1)
    time = lax.broadcasted_iota(jnp.int32, (total, LANES), 0) // GROUP
    picked = jnp.where(lane == time, jnp.concatenate([numbers] * length, axis=0), 0.0).astype(BF16)
    numbers = jnp.dot(picked, jnp.ones((LANES, LANES), BF16), preferred_element_type=F32)
    for shift in range(1, 4):
        earlier = jnp.concatenate(
            [jnp.full((shift * GROUP, LANES), -1.0, F32), numbers[: -shift * GROUP]], axis=0
        )
        masks[shift - 1] = jnp.where(earlier == numbers, 1.0, 0.0)
    save(masks, masks_out)
    save(few_all, few_out)
    first_small = 2 * rank + 2 * nstate
    small[...] = few_all[first_small : first_small + small.shape[0], :].astype(F32)
    taps, bias_row, skip_row, gain_row = 0, 5, 6 + nstate, 7 + nstate
    for n in range(nstate):
        rate[n] = jnp.broadcast_to(-LOG2E * jnp.exp(small[6 + n : 7 + n, :]), (GROUP, width))
    save(rate, rate_out)

    def fetch(own, everyone, t, slot):
        these = pl.ds(pl.multiple_of(t * BLOCK, BLOCK), BLOCK)
        others = pl.ds(batches, GROUP - batches)
        return [
            pltpu.make_async_copy(own.at[:, these, :], stage.at[slot, pl.ds(0, batches)], stage_sems.at[0, slot]),
            pltpu.make_async_copy(everyone.at[others, these, :], stage.at[slot, others], stage_sems.at[1, slot]),
        ]

    def fetch_start(*what):
        for copy in fetch(*what):
            copy.start()

    def fetch_wait(*what):
        for copy in fetch(*what):
            copy.wait()

    def weave(slot, scaled):
        for s in range(GROUP):
            value = stage[slot, s].astype(F32)
            if scaled:
                square = jnp.mean(value * value, axis=-1, keepdims=True)
                value = value * lax.rsqrt(square + EPS)
            for k in range(held.shape[0]):
                tile = value[:, k * LANES : (k + 1) * LANES]
                if scaled:
                    at = gain_row + k % 2
                    tile = tile * small[at : at + 1, (k // 2) * LANES : (k // 2 + 1) * LANES]
                held[k, pl.ds(s, BLOCK, stride=GROUP), :] = tile

    block_rows = BLOCK * GROUP
    blocks = total // block_rows

    def block_of(t):
        return pl.ds(pl.multiple_of(t * block_rows, block_rows), block_rows)

    ring.step(0, 3)
    pass_on(0, tokens_all)
    exchange(1, out_grad, grads_all)
    exchanged(0, tokens_all)
    fetch_start(tokens, tokens_all, 0, 0)

    @pl.loop(0, blocks)
    def _(t):
        slot = lax.rem(t, 2)

        @pl.when(t + 1 < blocks)
        def _():
            fetch_start(tokens, tokens_all, t + 1, 1 - slot)

        @pl.when(t == blocks - 2)
        def _():
            ring.step(0, 4)
            ring.step(1, 1)

        fetch_wait(tokens, tokens_all, t, slot)
        weave(slot, True)
        for k in range(held.shape[0]):
            normed[block_of(t), k * LANES : (k + 1) * LANES] = held[k].astype(BF16)

    save(normed, normed_out)
    for copy in own_shards:
        copy.wait()
    ring.finish(0)
    save(w_in, w_in_out)

    def cotangent_out_of(t, slot):
        return pltpu.make_async_copy(cotangent.at[slot], cotangent_out.at[block_of(t), :], out_sems.at[slot])

    def weave_grads(first, count):
        fetch_start(out_grad, grads_all, first, first % 2)

        @pl.loop(first, first + count)
        def _(t):
            slot = lax.rem(t, 2)

            @pl.when(t + 1 < first + count)
            def _():
                fetch_start(out_grad, grads_all, t + 1, 1 - slot)

            @pl.when(t >= 2)
            def _():
                cotangent_out_of(t - 2, slot).wait()

            fetch_wait(out_grad, grads_all, t, slot)
            weave(slot, False)
            for k in range(held.shape[0]):
                cotangent[slot, :, k * LANES : (k + 1) * LANES] = held[k].astype(BF16)
            cotangent_out_of(t, slot).start()

    inner[0:pad, :] = jnp.zeros((pad, width), F32)
    part[...] = jnp.zeros_like(part)

    @pl.loop(0, width // chunk)
    def _(c):
        cols = pl.ds(pl.multiple_of(c * chunk, chunk), chunk)
        inner[pad:, cols] = jnp.dot(normed[...], w_in[:, cols], preferred_element_type=F32)

        @pl.when(c == 2)
        def _():
            ring.step(1, 2)

        tap = [small[taps + i : taps + i + 1, cols] for i in range(5)]

        @pl.loop(0, total // rows)
        def _(i):
            start = pl.multiple_of(i * rows, rows)
            value = tap[4] + tap[3] * inner[pl.ds(pad + start, rows), cols]
            for shift in range(1, 4):
                mask = tiled(masks[shift - 1, pl.ds(start, rows), :], chunk)
                before = inner[pl.ds(pad - shift * GROUP + start, rows), cols]
                value = value + tap[3 - shift] * (before * mask)
            here = value * sigmoid(value)
            act[pl.ds(start, rows), cols] = here
            low[pl.ds(start, rows), cols] = here.astype(BF16)

        for j in range(2):
            part[j] += lax.dot_general(
                low[:, cols], few_all[j * LANES : (j + 1) * LANES, cols], (((1,), (1,)), ((), ())),
                preferred_element_type=F32,
            )

    save(inner.at[pl.ds(pad, total), :], inner_out)
    save(act, act_out)
    save(low, low_out)

    near = (near_send, near_recv)
    for j in range(2):
        for s in range(GROUP):
            nat[j, s * length : (s + 1) * length, :] = part[j, pl.ds(s, length, stride=GROUP), :]
    sends = []

    def start(source, target, index, peer):
        copy = remote(source, target, near, index, peer)
        copy.start()
        sends.append(copy)

    def come(target, index, peer):
        remote(target, target, near, index, peer).wait_recv()

    for i in range(2):
        start(nat.at[:, pl.ds((2 * i + 1) * side_rows, side_rows), :], got_near.at[i], i, peers.core)
    pass_on(1, grads_all)
    for i in range(2):
        come(got_near.at[i], i, peers.core)
    to_across[...] = nat[:, 2 * side_rows : 3 * side_rows, :] + got_near[1]
    start(to_across, got_across, 2, peers.across)
    exchanged(1, grads_all)
    weave_grads(0, blocks // 2)
    ring.step(1, 3)
    come(got_across, 2, peers.across)
    mine = nat[:, :side_rows, :] + got_near[0] + got_across[...]
    shared[0, 0] = mine[0].astype(BF16)
    lane = lax.broadcasted_iota(jnp.int32, (side_rows, LANES), 1)
    rest, terms = jnp.where(lane < 2 * nstate, mine[1], 0.0), jnp.zeros((side_rows, LANES), F32)
    for i in range(3):
        term = rest.astype(BF16).astype(F32)
        rest = rest - term
        terms = terms + (pltpu.roll(term, 2 * nstate * i, 1) if i else term)
    shared[0, 1] = terms.astype(BF16)
    start(shared.at[0], shared.at[2], 3, peers.across)
    start(shared.at[0], shared.at[1], 4, peers.core)
    weave_grads(blocks // 2, blocks // 2)
    come(shared.at[2], 3, peers.across)
    start(shared.at[2], shared.at[3], 5, peers.core)
    come(shared.at[1], 4, peers.core)
    come(shared.at[3], 5, peers.core)
    for copy in sends:
        copy.wait_send()
    for k in range(COPIES):
        for b in range(batches):
            for j in range(2):
                part[j, pl.ds(k * batches + b, length, stride=GROUP), :] = shared[
                    k, j, b * length : (b + 1) * length, :
                ].astype(F32)
    step_low[...] = part[0].astype(BF16)
    coef[...] = part[1].astype(BF16)
    save(step_low, step_low_out)
    save(coef, coef_out)

    stride = few_all[rank + 2 * nstate : 2 * rank + 2 * nstate, :]
    side_bias = small[bias_row : bias_row + 1, :]
    carry[...] = jnp.zeros_like(carry)

    state_rows = nstate * GROUP

    def keep_states(t, c):
        there = pl.ds(pl.multiple_of(t * BLOCK * state_rows, BLOCK * state_rows), BLOCK * state_rows)
        return pltpu.make_async_copy(
            states_at.at[c % 2], states_out.at[c, there, :], states_sems.at[c % 2]
        )

    @pl.loop(0, blocks)
    def _(t):
        for tick, which, number in ((0, 1, 4), (0, 2, 1), (4, 2, 2), (7, 2, 3)):

            @pl.when(t == tick)
            def _(which=which, number=number):
                ring.step(which, number)

        base = pl.multiple_of(t * block_rows, block_rows)
        these = block_of(t)
        wide[...] = jnp.dot(coef[these, :], spread_by[...], preferred_element_type=F32)
        pre[...] = jnp.dot(step_low[these, :], stride, preferred_element_type=F32)
        for i in range(BLOCK // 2):
            sub = slice(i * 2 * GROUP, (i + 1) * 2 * GROUP)
            step[pl.ds(base + i * 2 * GROUP, 2 * GROUP), :] = softplus(pre[sub, :] + side_bias)
        for c in range(width // chunk):
            cols = slice(c * chunk, (c + 1) * chunk)

            if c >= 2:
                keep_states(t, c - 2).wait()
            else:

                @pl.when(t > 0)
                def _(c=c):
                    keep_states(t - 1, c + 2).wait()

            def advance(i, states):
                at = pl.ds(pl.multiple_of(base + i * GROUP, GROUP), GROUP)
                here = at_time(i)
                step_t, act_t = step[at, cols], act[at, cols]
                drive = jnp.where(tiled(masks[0, at, :], chunk) > 0.5, step_t, FAR)
                inflow = step_t * act_t
                out = small[skip_row : skip_row + 1, cols] * act_t
                now = []
                for n in range(nstate):
                    write = tiled(wide[here, n * LANES : (n + 1) * LANES], chunk)
                    read = tiled(wide[here, (nstate + n) * LANES : (nstate + n + 1) * LANES], chunk)
                    row = pl.multiple_of(i * state_rows + n * GROUP, GROUP)
                    states_at[c % 2, pl.ds(row, GROUP), :] = states[n]
                    state = jnp.exp2(drive * rate[n, :, cols]) * states[n] + write * inflow
                    out = out + read * state
                    now.append(state)
                readout[at, cols] = out
                return tuple(now)

            states = lax.fori_loop(
                0, BLOCK, advance, tuple(carry[c, n * GROUP : (n + 1) * GROUP, :] for n in range(nstate)), unroll=4
            )
            for n in range(nstate):
                carry[c, n * GROUP : (n + 1) * GROUP, :] = states[n]
            keep_states(t, c).start()

    save(carry, states_out.at[:, pl.ds(total // GROUP * state_rows, state_rows), :])
    save(step, step_out)
    save(readout, readout_out)

    ring.finish(1)
    save(gate_w, gate_w_out)

    def keep_gate(c, slot):
        cols = pl.ds(pl.multiple_of(c * chunk, chunk), chunk)
        return pltpu.make_async_copy(gate.at[slot], gate_out.at[:, cols], gate_sems.at[slot])

    @pl.loop(0, width // chunk)
    def _(c):
        cols = pl.ds(pl.multiple_of(c * chunk, chunk), chunk)
        slot = lax.rem(c, 2)

        @pl.when(c >= 2)
        def _():
            keep_gate(c - 2, slot).wait()

        @pl.when(c == 2)
        def _():
            ring.step(2, 4)

        gate[slot] = jnp.dot(normed[...], gate_w[:, cols], preferred_element_type=F32)
        keep_gate(c, slot).start()

        @pl.loop(0, total // rows)
        def _(i):
            at = pl.ds(pl.multiple_of(i * rows, rows), rows)
            here = gate[slot, at, :]
            value = readout[at, cols] * (here * sigmoid(here))
            gated[at, cols] = value.astype(BF16)
            for k in range(chunk // LANES):
                nat[k, at, :] = value[:, k * LANES : (k + 1) * LANES]

        for k in range(chunk // LANES):
            for s in range(GROUP):
                natural[s * length : (s + 1) * length, pl.ds(pl.multiple_of(c * chunk + k * LANES, LANES), LANES)] = nat[
                    k, pl.ds(s, length, stride=GROUP), :
                ].astype(BF16)

    save(gated, gated_out)
    save(natural, natural_out)
    ring.finish(2)
    ring.sent_all()
    for moving in sent:
        moving.wait_send()
    for slot in range(2):
        keep_states(blocks - 1, width // chunk - 2 + slot).wait()
        keep_gate(width // chunk - 2 + slot, slot).wait()
        cotangent_out_of(blocks - 2 + slot, slot).wait()
    for copy in saved:
        copy.wait()


def forward(size, rank, nstate, entry, few, tokens, out_grad, segments, out_proj):
    batches, length, model = tokens.shape
    total = COPIES * batches * length
    slab, width = entry.shape[0], size * LANES
    blocks = length // BLOCK
    anywhere = pl.BlockSpec(memory_space=pl.ANY)
    half = size // 2
    dma = pltpu.SemaphoreType.DMA
    shape = jax.ShapeDtypeStruct
    full, low = shape((total, width), F32), shape((total, width), BF16)
    thin = shape((total, LANES), BF16)
    rows = shape((total, model), BF16)
    weights = shape((size * slab, width), BF16)
    few_all = shape((few.shape[0], width), BF16)
    masks = shape((3, total, LANES), F32)
    state = shape((nstate, GROUP, width), F32)
    spread_by = shape((LANES, 2 * nstate * LANES), BF16)
    fold_by = shape((2 * nstate * LANES, LANES), BF16)
    outs = dict(
        few=few_all,
        masks=masks,
        rate=state,
        spread_by=spread_by,
        fold_by=fold_by,
        normed=rows,
        cotangent=rows,
        tokens_all=shape((GROUP, length, model), BF16),
        grads_all=shape((GROUP, length, model), BF16),
        segments_all=shape((COPIES,) + segments.shape, segments.dtype),
        inner_in=weights,
        inner=full,
        act=full,
        act_low=low,
        step_low=thin,
        coef=thin,
        step=full,
        states=shape((width // 256, (length + 1) * nstate * GROUP, 256), F32),
        gate=full,
        readout=full,
        gated=low,
        gated_natural=low,
        gate_in=weights,
        out_w=shape((size * out_proj.shape[0] // COPIES, model), BF16),
    )
    quarter = total // COPIES
    scratch = [
        few_all,
        shape((few.shape[0] - 2 * rank - 2 * nstate, width), F32),
        masks,
        state,
        spread_by,
        fold_by,
        rows,
        shape((2, GROUP, BLOCK, model), BF16),
        shape((2, BLOCK * GROUP, model), BF16),
        shape((model // LANES, BLOCK * GROUP, LANES), F32),
        shape((COPIES,) + segments.shape, segments.dtype),
        shape((slab, width), BF16),
        shape((slab, width), BF16),
        weights,
        shape((total + 3 * GROUP, width), F32),
        full,
        low,
        shape((2, total, LANES), F32),
        shape((2, total, LANES), F32),
        shape((2, 2, quarter, LANES), F32),
        shape((2, quarter, LANES), F32),
        shape((2, quarter, LANES), F32),
        shape((COPIES, 2, quarter, LANES), BF16),
        thin,
        thin,
        shape((BLOCK * GROUP, 2 * nstate * LANES), F32),
        shape((BLOCK * GROUP, width), F32),
        full,
        full,
        shape((width // 256, nstate * GROUP, 256), F32),
        shape((2, BLOCK * nstate * GROUP, 256), F32),
        shape((2, total, 256), F32),
        low,
        low,
        weights,
    ]
    sems = [(20,), (2,), (2,), (7,), (2 * size,), (2, 2), (2,), (1,)]
    sems += [(3, 2, half, 2)] * 2 + [(2, half)] * 2 + [(3, 3)] * 2 + [(6,)] * 2
    results = pl.pallas_call(
        functools.partial(forward_kernel, size, rank, nstate),
        in_specs=[anywhere] * 6,
        out_specs=[anywhere] * len(outs),
        out_shape=list(outs.values()),
        scratch_shapes=[pltpu.VMEM(x.shape, x.dtype) for x in scratch] + [dma(n) for n in sems],
        compiler_params=pltpu.CompilerParams(
            collective_id=4, has_side_effects=True, vmem_limit_bytes=62 * 1024 * 1024
        ),
        cost_estimate=cost(8 * total * width * model, 100 * total * width),
        name="forward",
    )(entry, few, tokens, out_grad, segments, out_proj)
    return dict(zip(outs, results))


class Guests:
    def __init__(self, peers, parts, totals, held, sems):
        self.peers = peers
        self.parts, self.totals, self.held, self.sems = parts, totals, held, sems

    def rows(self, which, c):
        half = self.parts[which].shape[1] // 2
        return pl.ds(c * half, half)

    def copy(self, which, way, step, c, source=None):
        target = self.held[which].at[way, step - 1, self.rows(which, c), :]
        index = (which, way, step - 1, c)
        source = target if source is None else source
        return remote(source, target, self.sems, index, self.peers.ring[way])

    def chunks(self, way, step):
        return (way,) if step == 1 else (0, 1)

    def own(self, which, way, step, c):
        away = self.peers.half + 1 - step
        block = self.peers.at(away if way == 0 else -away)
        return self.parts[which].at[block, self.rows(which, c), :]

    def source(self, which, way, step, c):
        own = self.own(which, way, step, c)
        if step == 1 or c not in self.chunks(way, step - 1):
            return own
        self.copy(which, way, step - 1, c).wait_recv()
        there = self.held[which].at[way, step - 2, self.rows(which, c), :]
        there[...] = own[...] + there[...]
        return there

    def step(self, which, step):
        for c in range(2):
            for way in range(2):
                if c in self.chunks(way, step):
                    self.copy(which, way, step, c, self.source(which, way, step, c)).start()

    def finish(self, which):
        last = self.peers.half
        for c in range(2):
            total = self.own(which, 0, last + 1, c)[...].astype(F32)
            for way in range(2):
                self.copy(which, way, last, c).wait_recv()
                there = self.held[which].at[way, last - 1, self.rows(which, c), :]
                total = total + there[...].astype(F32)
            self.totals[which][self.rows(which, c), :] = total.astype(BF16)

    def sent_all(self):
        for which in range(2):
            for step in range(1, self.peers.half + 1):
                for way in range(2):
                    for c in self.chunks(way, step):
                        self.copy(which, way, step, c).wait_send()


def scan_back_kernel(
    nstate, chunk, step_ref, act_ref, grad_ref, coef_ref, spread_ref, fold_ref, keep_ref, rate_ref,
    row_ref, start_ref, *refs,
):
    wide, states_all, decays, parts, sizes = refs[-5:]
    width = step_ref.shape[1]
    step_now = pl.program_id(0)
    pre_grad_ref, direct_ref, coef_grad_ref, carry_ref, sums_ref = refs[-10:-5]

    @pl.when(step_now == 0)
    def _():
        carry_ref[...] = jnp.zeros_like(carry_ref)
        sums_ref[...] = jnp.zeros_like(sums_ref)

    wide[...] = jnp.dot(coef_ref[...], spread_ref[...], preferred_element_type=F32)

    def fold(value):
        total = value[:, :LANES]
        for k in range(1, chunk // LANES):
            total = total + value[:, k * LANES : (k + 1) * LANES]
        return total

    for c in range(width // chunk):
        cols = slice(c * chunk, (c + 1) * chunk)

        def advance(t, states):
            at = at_time(t)
            step = step_ref[at, cols]
            drive = jnp.where(tiled(keep_ref[at, :], chunk) > 0.5, step, FAR)
            inflow = step * act_ref[at, cols]
            now = []
            for n in range(nstate):
                write = tiled(wide[at, n * LANES : (n + 1) * LANES], chunk)
                decay = jnp.exp2(drive * rate_ref[n, :, cols])
                decays[t, n] = decay
                states_all[t, n] = states[n]
                now.append(decay * states[n] + write * inflow)
            return tuple(now)

        start = tuple(start_ref[0, n, :, cols] for n in range(nstate))
        states = lax.fori_loop(0, BLOCK, advance, start, unroll=2)
        for n in range(nstate):
            states_all[BLOCK, n] = states[n]

        def retreat(i, carry):
            t = BLOCK - 1 - i
            at = at_time(t)
            step, act, grad = step_ref[at, cols], act_ref[at, cols], grad_ref[at, cols]
            inflow = step * act
            size = jnp.zeros_like(step)
            direct = jnp.zeros_like(step)
            now = []
            for n in range(nstate):
                tile_w = slice(n * LANES, (n + 1) * LANES)
                tile_r = slice((nstate + n) * LANES, (nstate + n + 1) * LANES)
                state_grad = tiled(wide[at, tile_r], chunk) * grad + carry[n]
                passed = decays[t, n] * state_grad
                through = passed * states_all[t, n]
                size = size + rate_ref[n, :, cols] * through
                direct = direct + state_grad * tiled(wide[at, tile_w], chunk)
                sums_ref[n, :, cols] += step * through
                write_part = fold(state_grad * inflow)
                read_part = fold(grad * states_all[t + 1, n])
                if c == 0:
                    parts[at, tile_w] = write_part
                    parts[at, tile_r] = read_part
                else:
                    parts[at, tile_w] += write_part
                    parts[at, tile_r] += read_part
                now.append(passed)
            sizes[at, cols] = LN2 * size + act * direct
            direct_ref[at, cols] = step * direct + row_ref[1:2, cols] * grad
            sums_ref[nstate, :, cols] += grad * act
            return tuple(now)

        start = tuple(carry_ref[n, :, cols] for n in range(nstate))
        carry = lax.fori_loop(0, BLOCK, retreat, start, unroll=2)
        for n in range(nstate):
            carry_ref[n, :, cols] = carry[n]

    step = step_ref[...]
    series = step * (1.0 - step * (0.5 - step * (1.0 / 6.0)))
    pre_grad = sizes[...] * jnp.where(step < 0.01, series, 1.0 - jnp.exp(-step))
    pre_grad_ref[...] = pre_grad.astype(BF16)
    total = pre_grad[:GROUP]
    for t in range(1, BLOCK):
        total = total + pre_grad[t * GROUP : (t + 1) * GROUP]
    sums_ref[nstate + 1] += total
    high = parts[...].astype(BF16)
    low = (parts[...] - high.astype(F32)).astype(BF16)
    coef_grad_ref[...] = jnp.dot(high, fold_ref[...], preferred_element_type=F32) + jnp.dot(
        low, fold_ref[...], preferred_element_type=F32
    )


def scan_backward(
    step, act, grad, coef, spread_by, fold_by, keep, rate, rows, starts
):
    total, width = step.shape
    nstate = rate.shape[0]
    size = BLOCK * GROUP
    chunk = 256
    count = total // size
    tile = pl.BlockSpec((size, width), lambda t: (count - 1 - t, 0))
    thin = pl.BlockSpec((size, LANES), lambda t: (count - 1 - t, 0))
    state = pl.BlockSpec((nstate, GROUP, width), lambda t: (0, 0, 0))
    tally = pl.BlockSpec((nstate + 2, GROUP, width), lambda t: (0, 0, 0))
    work = count * size * width * nstate
    return pl.pallas_call(
        functools.partial(scan_back_kernel, nstate, chunk),
        grid=(count,),
        in_specs=[
            tile,
            tile,
            tile,
            thin,
            pl.BlockSpec(spread_by.shape, lambda t: (0, 0)),
            pl.BlockSpec(fold_by.shape, lambda t: (0, 0)),
            thin,
            state,
            pl.BlockSpec((8, width), lambda t: (0, 0)),
            pl.BlockSpec((1, nstate, GROUP, width), lambda t: (count - 1 - t, 0, 0, 0)),
        ],
        out_specs=[tile, tile, thin, state, tally],
        out_shape=[
            jax.ShapeDtypeStruct((total, width), BF16),
            jax.ShapeDtypeStruct((total, width), F32),
            jax.ShapeDtypeStruct((total, LANES), F32),
            jax.ShapeDtypeStruct((nstate, GROUP, width), F32),
            jax.ShapeDtypeStruct((nstate + 2, GROUP, width), F32),
        ],
        scratch_shapes=[
            pltpu.VMEM((size, 2 * nstate * LANES), F32),
            pltpu.VMEM((BLOCK + 1, nstate, GROUP, chunk), F32),
            pltpu.VMEM((BLOCK, nstate, GROUP, chunk), F32),
            pltpu.VMEM((size, 2 * nstate * LANES), F32),
            pltpu.VMEM((size, width), F32),
        ],
        compiler_params=params(),
        cost_estimate=cost(40 * work, 24 * count * size * width),
        name="scan_backward",
    )(step, act, grad, coef, spread_by, fold_by, keep, rate, rows, starts)


def backward_kernel(
    size, nstate, rank,
    gated_in, cotangent_in, w_out, readout_in, gate_in, normed_in, step_in, act_in, coef_in, states_in, masks_in, rate_in,
    spread_in, fold_in, few_in, gated_natural_in,
    natural_out, pre_low_out, direct_out, coef_grad_out, sums_out, out_pieces, out_own, out_near, out_far, gate_total,
    gated, cotangent, out_w, normed, out_wgrad, gate_wgrad, out_held, gate_held, gate_grad, natural, grad, nat,
    step_at, act_at, states_at, wide, parts, sizes, sums, carry, coef, spread_by, fold_by, rate, keep, few,
    coef_grad, out_total,
    load_sems, tile_sems, block_sems, states_sems, save_sems, block_saves, ring_send, ring_recv, part_send, part_recv,
    piece_send, piece_recv, own_sem,
):
    peers = Peers(size)
    total, width = gated.shape
    model = normed.shape[1]
    length = total // GROUP
    chunk, rows = 256, 64
    block_rows = BLOCK * GROUP
    blocks = total // block_rows
    loads, saved = {}, []

    def load(name, source, target):
        loads[name] = pltpu.make_async_copy(source, target, load_sems.at[len(loads)])
        loads[name].start()

    def save(source, target):
        saved.append(pltpu.make_async_copy(source, target, save_sems.at[len(saved)]))
        saved[-1].start()

    first_small = 2 * rank + 2 * nstate
    load("gated", gated_in, gated)
    load("cotangent", cotangent_in, cotangent)
    load("out_w", w_out, out_w)
    load("normed", normed_in, normed)
    load("coef", coef_in, coef)
    load("spread", spread_in, spread_by)
    load("fold", fold_in, fold_by)
    load("rate", rate_in, rate)
    load("keep", masks_in.at[0], keep)
    load("few", few_in.at[pl.ds(first_small, few.shape[0]), :], few)

    def tile_copies(c, slot):
        cols = pl.ds(pl.multiple_of(c * chunk, chunk), chunk)
        return [
            pltpu.make_async_copy(
                ref.at[:, cols], states_at.at[slot, pl.ds(i * total, total), :], tile_sems.at[i, slot]
            )
            for i, ref in enumerate((gate_in, readout_in))
        ]

    for copy in tile_copies(0, 0):
        copy.start()
    peers.meet()
    ring = Guests(
        peers, (out_wgrad, gate_wgrad), (out_total, gate_total), (out_held, gate_held), (ring_send, ring_recv),
    )
    out_parts = cotangent
    out_sum = Parts(
        peers, start_send, (part_send, part_recv), out_parts, out_near, out_far, total // COPIES
    )
    pieces = Pieces(
        peers, start_send, (piece_send, piece_recv), own_sem, 0, lambda: out_total, lambda k: out_pieces.at[k],
    )
    loads["gated"].wait()
    loads["cotangent"].wait()
    tn = (((0,), (0,)), ((), ()))
    nt = (((1,), (1,)), ((), ()))

    @pl.loop(0, model // chunk)
    def _(c):
        cols = pl.ds(pl.multiple_of(c * chunk, chunk), chunk)
        value = lax.dot_general(gated[...], cotangent[:, cols], tn, preferred_element_type=F32)
        out_wgrad[:, :, cols] = value.astype(BF16).reshape(size, -1, chunk)

    ring.step(0, 1)
    loads["out_w"].wait()

    @pl.loop(0, width // chunk)
    def _(c):
        cols = pl.ds(pl.multiple_of(c * chunk, chunk), chunk)
        slot = lax.rem(c, 2)

        @pl.when(c + 1 < width // chunk)
        def _():
            for copy in tile_copies(c + 1, 1 - slot):
                copy.start()

        @pl.when(c == 2)
        def _():
            ring.step(0, 2)

        grad[:, cols] = lax.dot_general(cotangent[...], out_w[cols, :], nt, preferred_element_type=F32)
        for copy in tile_copies(c, slot):
            copy.wait()

        @pl.loop(0, total // rows)
        def _(i):
            start = pl.multiple_of(i * rows, rows)
            at = pl.ds(start, rows)
            gate = states_at[slot, at, :]
            readout = states_at[slot, pl.ds(total + start, rows), :]
            value = grad[at, cols]
            sig = sigmoid(gate)
            grad[at, cols] = value * (gate * sig)
            value = value * readout * (sig * (1.0 + gate * (1.0 - sig)))
            gate_grad[at, cols] = value.astype(BF16)
            for k in range(chunk // LANES):
                nat[k, at, :] = value[:, k * LANES : (k + 1) * LANES]

        for k in range(chunk // LANES):
            lanes = pl.ds(pl.multiple_of(c * chunk + k * LANES, LANES), LANES)
            for s in range(GROUP):
                natural[s * length : (s + 1) * length, lanes] = nat[
                    k, pl.ds(s, length, stride=GROUP), :
                ].astype(BF16)

    save(natural, natural_out)

    def block_copies(t, slot):
        these = pl.ds(pl.multiple_of(t * block_rows, block_rows), block_rows)
        return [
            pltpu.make_async_copy(step_in.at[these, :], step_at.at[slot], block_sems.at[0, slot]),
            pltpu.make_async_copy(act_in.at[these, :], act_at.at[slot], block_sems.at[1, slot]),
        ]

    state_rows = nstate * GROUP

    def states_copy(t, c):
        there = pl.ds(pl.multiple_of(t * BLOCK * state_rows, BLOCK * state_rows), (BLOCK + 1) * state_rows)
        slot = states_slot(t, c)
        return pltpu.make_async_copy(states_in.at[c, there, :], states_at.at[slot], states_sems.at[slot])

    slots, ahead = 3, 2

    def states_slot(t, c):
        return lax.rem((blocks - 1 - t) * (width // chunk) + c, slots)

    for c in range(ahead):
        states_copy(blocks - 1, c).start()

    for copy in block_copies(blocks - 1, (blocks - 1) % 2):
        copy.start()
    loads["normed"].wait()

    @pl.loop(0, width // chunk)
    def _(c):
        cols = pl.ds(pl.multiple_of(c * chunk, chunk), chunk)
        value = lax.dot_general(normed[...], gate_grad[:, cols], tn, preferred_element_type=F32)
        gate_wgrad[:, :, cols] = value.astype(BF16).reshape(size, -1, chunk)

    ring.step(1, 1)
    load("natural", gated_natural_in, gate_grad)
    for name in ("coef", "spread", "fold", "rate", "keep", "few"):
        loads[name].wait()
    pre_low = gated
    skip_at = 6 + nstate
    skip_row = few[...].astype(F32)[skip_at : skip_at + 1]
    carry[...] = jnp.zeros_like(carry)
    sums[...] = jnp.zeros_like(sums)

    def near_copy():
        return pltpu.make_async_copy(
            out_near.at[1], normed.at[pl.ds(0, total // COPIES), :], own_sem.at[1]
        )

    loads["natural"].wait()

    def fold(value):
        out = value[:, :LANES]
        for k in range(1, chunk // LANES):
            out = out + value[:, k * LANES : (k + 1) * LANES]
        return out

    def block_keeps(t):
        these = pl.ds(pl.multiple_of(t * block_rows, block_rows), block_rows)
        return [
            pltpu.make_async_copy(pre_low.at[these, :], pre_low_out.at[these, :], block_saves.at[0, t]),
            pltpu.make_async_copy(grad.at[these, :], direct_out.at[these, :], block_saves.at[1, t]),
        ]

    @pl.loop(0, blocks)
    def _(turn):
        t = blocks - 1 - turn
        slot = lax.rem(t, 2)
        for tick, which, number in ((0, 0, 3), (1, 1, 2), (3, 0, 4), (4, 1, 3), (6, 1, 4)):

            @pl.when(turn == tick)
            def _(which=which, number=number):
                ring.step(which, number)

        @pl.when(turn == 1)
        def _():
            out_sum.start()

        @pl.when(turn == 2)
        def _():
            near_copy().wait()
            out_sum.go_far(normed.at[pl.ds(0, total // COPIES), :])

        @pl.when(turn == 5)
        def _():
            ring.finish(0)
            pieces.give()

        @pl.when(turn == 0)
        def _():
            @pl.loop(0, model // chunk)
            def _(i):
                cols = pl.ds(pl.multiple_of(i * chunk, chunk), chunk)
                value = jnp.dot(gate_grad[...], out_w[:, cols], preferred_element_type=F32)
                out_parts[:, cols] = value.astype(BF16)

        @pl.when(t > 0)
        def _():
            for copy in block_copies(t - 1, 1 - slot):
                copy.start()

        base = pl.multiple_of(t * block_rows, block_rows)
        these = pl.ds(base, block_rows)
        wide[...] = jnp.dot(coef[these, :], spread_by[...], preferred_element_type=F32)
        for copy in block_copies(t, slot):
            copy.wait()

        for c in range(width // chunk):
            cols = slice(c * chunk, (c + 1) * chunk)

            if c + ahead < width // chunk:
                states_copy(t, c + ahead).start()
            else:

                @pl.when(t > 0)
                def _(c=c):
                    states_copy(t - 1, c + ahead - width // chunk).start()

            states_copy(t, c).wait()

            def state_at(i, n):
                row = pl.multiple_of(i * state_rows + n * GROUP, GROUP)
                return states_at[states_slot(t, c), pl.ds(row, GROUP), :]

            def retreat(i, carried):
                i = BLOCK - 1 - i
                here = at_time(i)
                at = pl.ds(pl.multiple_of(base + i * GROUP, GROUP), GROUP)
                step, act, flow = step_at[slot, here, cols], act_at[slot, here, cols], grad[at, cols]
                inflow = step * act
                drive = jnp.where(tiled(keep[at, :], chunk) > 0.5, step, FAR)
                size_grad, direct = jnp.zeros_like(step), jnp.zeros_like(step)
                now = []
                for n in range(nstate):
                    tile_w = slice(n * LANES, (n + 1) * LANES)
                    tile_r = slice((nstate + n) * LANES, (nstate + n + 1) * LANES)
                    state_grad = tiled(wide[here, tile_r], chunk) * flow + carried[n]
                    power = drive * rate[n, :, cols]
                    passed = jnp.exp2(power) * state_grad
                    through = power * (passed * state_at(i, n))
                    size_grad = size_grad + through
                    direct = direct + state_grad * tiled(wide[here, tile_w], chunk)
                    sums[n, :, cols] += through
                    write_part = fold(state_grad * inflow)
                    read_part = fold(flow * state_at(i + 1, n))
                    if c == 0:
                        parts[here, tile_w] = write_part
                        parts[here, tile_r] = read_part
                    else:
                        parts[here, tile_w] += write_part
                        parts[here, tile_r] += read_part
                    now.append(passed)
                sizes[here, cols] = LN2 * size_grad / jnp.maximum(step, 1e-30) + act * direct
                grad[at, cols] = step * direct + skip_row[:, cols] * flow
                sums[nstate, :, cols] += flow * act
                return tuple(now)

            start = tuple(carry[n, :, cols] for n in range(nstate))
            carried = lax.fori_loop(0, BLOCK, retreat, start, unroll=4)
            for n in range(nstate):
                carry[n, :, cols] = carried[n]

        step = step_at[slot]
        series = step * (1.0 - step * (0.5 - step * (1.0 / 6.0)))
        pre_grad = sizes[...] * jnp.where(step < 0.01, series, 1.0 - jnp.exp(-step))
        pre_low[these, :] = pre_grad.astype(BF16)
        tally = pre_grad[:GROUP]
        for i in range(1, BLOCK):
            tally = tally + pre_grad[i * GROUP : (i + 1) * GROUP]
        sums[nstate + 1] += tally
        coef_grad[these, :] = jnp.dot(
            parts[...].astype(BF16), fold_by[...], preferred_element_type=F32
        )

        @pl.when(turn == 1)
        def _():
            out_sum.come_near()
            near_copy().start()

        for copy in block_keeps(t):
            copy.start()

    save(coef_grad, coef_grad_out)
    save(sums, sums_out)
    save(out_sum.block(0), out_own)
    pieces.pass_on()
    ring.finish(1)
    pieces.come()
    out_sum.come()
    ring.sent_all()
    out_sum.sent_all()
    pieces.sent_all()
    for t in range(blocks):
        for copy in block_keeps(t):
            copy.wait()
    for copy in saved:
        copy.wait()


def backward(size, nstate, rank, arrays):
    (gated, cotangent, w_out, readout, gate, normed, step, act, coef, states, masks, rate, spread_by, fold_by, few) = arrays[:15]
    total, width = gated.shape
    model = normed.shape[1]
    inside, anywhere = pl.BlockSpec(memory_space=pltpu.VMEM), pl.BlockSpec(memory_space=pl.ANY)
    shape, dma = jax.ShapeDtypeStruct, pltpu.SemaphoreType.DMA
    low, rows, full = shape((total, width), BF16), shape((total, model), BF16), shape((total, width), F32)
    out_unit, gate_unit = (width // size, model), (model // size, width)
    half = size // 2
    block = shape((2, BLOCK * GROUP, width), F32)
    state = shape((nstate, GROUP, width), F32)
    tally = shape((nstate + 2, GROUP, width), F32)
    wide = shape((BLOCK * GROUP, 2 * nstate * LANES), F32)
    thin = shape((total, LANES), F32)
    scratch = [
        low,
        rows,
        shape(w_out.shape, BF16),
        rows,
        shape((size,) + out_unit, BF16),
        shape((size,) + gate_unit, BF16),
        shape((2, half) + out_unit, BF16),
        shape((2, half) + gate_unit, BF16),
        low,
        low,
        full,
        shape((2, total, LANES), F32),
        block,
        block,
        shape((3, (BLOCK + 1) * nstate * GROUP, 256), F32),
        wide,
        wide,
        shape((BLOCK * GROUP, width), F32),
        tally,
        state,
        shape(coef.shape, BF16),
        shape(spread_by.shape, BF16),
        shape(fold_by.shape, BF16),
        state,
        thin,
        shape((few.shape[0] - 2 * rank - 2 * nstate, width), BF16),
        thin,
        shape(out_unit, BF16),
    ]
    blocks = total // (BLOCK * GROUP)
    sems = [(11,), (2, 2), (2, 2), (3,), (4,), (2, blocks), (2, 2, half, 2), (2, 2, half, 2)]
    sems += [(3,), (3,), (1, 3), (1, 3), (2,)]
    part = shape((total // COPIES, model), BF16)
    return pl.pallas_call(
        functools.partial(backward_kernel, size, nstate, rank),
        in_specs=[anywhere] * len(arrays),
        out_specs=[anywhere] * 9 + [inside],
        out_shape=[
            low, low, full, thin, tally, shape((COPIES,) + out_unit, BF16), part, shape((2,) + part.shape, BF16), part,
            shape(gate_unit, BF16),
        ],
        scratch_shapes=[pltpu.VMEM(x.shape, x.dtype) for x in scratch] + [dma(n) for n in sems],
        compiler_params=pltpu.CompilerParams(
            collective_id=3, has_side_effects=True, vmem_limit_bytes=62 * 1024 * 1024
        ),
        cost_estimate=cost(6 * total * width * model, 200 * total * width),
        name="backward",
    )(*arrays)


def finish_kernel(
    size, rank, nstate,
    pre_low_in, coef_in, direct_in, inner_in, act_low_in, step_low_in, masks_in, few_in, normed_in, w_inner, w_gate,
    gate_grad_in, sums_in, gate_total,
    inner_pieces, gate_pieces, norm_own, norm_near, norm_far, small_pieces,
    pre_low, part, nat, got_near, to_across, got_across, shared, low_grad, act_low, step_low, masks, few, normed, gate_grad,
    inner_grad, inner, direct, grad, wgrad, held, small, small_low, small_held, norm_parts, near_at, w_tiles, total_at, gate_own, sums,
    load_sems, tile_sems, w_sems, near_send, near_recv, part_send, part_recv, ring_send, ring_recv, few_send, few_recv,
    piece_send, piece_recv, own_sems,
):
    peers = Peers(size)
    half = peers.half
    total, width = pre_low.shape
    model = normed.shape[1]
    length = total // GROUP
    batches = GROUP // COPIES
    quarter = total // COPIES
    chunk, rows, pad = 256, 64, 3 * GROUP
    tiles = width // chunk
    slab = held.shape[2]
    send, loads = Sends(), {}

    def load(name, source, target):
        loads[name] = pltpu.make_async_copy(source, target, load_sems.at[len(loads)])
        loads[name].start()

    def tile_copies(c, slot):
        cols = slice(c * chunk, (c + 1) * chunk)
        return [
            pltpu.make_async_copy(inner_in.at[:, cols], inner.at[slot, pl.ds(pad, total), :], tile_sems.at[0, slot]),
            pltpu.make_async_copy(direct_in.at[:, cols], direct.at[slot], tile_sems.at[1, slot]),
        ]

    load("pre", pre_low_in, pre_low)
    load("few", few_in, few)
    load("coef", coef_in, part.at[1])
    load("step", step_low_in, step_low)
    load("gate", gate_grad_in, gate_grad)
    load("total", gate_total, gate_own)
    load("act", act_low_in, act_low)
    load("masks", masks_in, masks.at[:, pl.ds(0, total), :])
    load("normed", normed_in, normed)
    load("sums", sums_in, sums)
    for copy in tile_copies(0, 0):
        copy.start()
    w_count = model // chunk

    def w_copy(w, n, slot):
        these = pl.ds(pl.multiple_of(n * chunk, chunk), chunk)
        return pltpu.make_async_copy(w.at[these, :], w_tiles.at[slot], w_sems.at[slot])

    def norm_tiles(w, left, first, count, add):
        @pl.loop(first, first + count)
        def _(n):
            slot = lax.rem(n, 2)

            @pl.when(n + 1 < w_count)
            def _():
                w_copy(w, n + 1, 1 - slot).start()

            w_copy(w, n, slot).wait()
            cols = pl.ds(pl.multiple_of(n * chunk, chunk), chunk)
            value = lax.dot_general(
                left[...], w_tiles[slot], (((1,), (1,)), ((), ())), preferred_element_type=F32
            )
            if add:
                value = value + norm_parts[:, cols].astype(F32)
            norm_parts[:, cols] = value.astype(BF16)

    w_copy(w_gate, 0, 0).start()
    peers.meet()

    near = (near_send, near_recv)

    def come(target, index, peer):
        remote(target, target, near, index, peer).wait_recv()

    first_stride = rank + 2 * nstate
    loads["pre"].wait()
    loads["few"].wait()
    part[0] = lax.dot_general(
        pre_low[...], few[first_stride : first_stride + rank, :], (((1,), (1,)), ((), ())),
        preferred_element_type=F32,
    )
    loads["coef"].wait()
    for j in range(2):
        for s in range(GROUP):
            nat[j, s * length : (s + 1) * length, :] = part[j, pl.ds(s, length, stride=GROUP), :]
    for i in range(2):
        send(nat.at[:, pl.ds((2 * i + 1) * quarter, quarter), :], got_near.at[i], near, i, peers.core)
    near_sends = Sends()
    near_sends.sent, send.sent = send.sent, []
    loads["step"].wait()
    small[first_stride : first_stride + rank, :] = lax.dot_general(
        step_low[...], pre_low[...], (((0,), (0,)), ((), ())), preferred_element_type=F32
    )
    for i in range(2):
        come(got_near.at[i], i, peers.core)
    to_across[...] = (nat[:, 2 * quarter : 3 * quarter, :] + got_near[1]).astype(BF16)
    send(to_across, got_across, near, 2, peers.across)
    loads["gate"].wait()
    norm_tiles(w_gate, gate_grad, 0, w_count // 2, False)
    come(got_across, 2, peers.across)
    mine = nat[:, :quarter, :] + got_near[0] + got_across[...].astype(F32)
    for j in range(2):
        shared[0, j] = mine[j].astype(BF16)
    send(shared.at[0], shared.at[2], near, 3, peers.across)
    send(shared.at[0], shared.at[1], near, 4, peers.core)
    norm_tiles(w_gate, gate_grad, w_count // 2, w_count - w_count // 2, False)
    w_copy(w_inner, 0, 0).start()
    come(shared.at[2], 3, peers.across)
    send(shared.at[2], shared.at[3], near, 5, peers.core)
    come(shared.at[1], 4, peers.core)
    come(shared.at[3], 5, peers.core)
    near_sends.wait()
    for k in range(COPIES):
        for b in range(batches):
            for j in range(2):
                part[j, pl.ds(k * batches + b, length, stride=GROUP), :] = shared[
                    k, j, b * length : (b + 1) * length, :
                ].astype(F32)
    for j in range(2):
        low_grad[j] = part[j].astype(BF16)

    piece_sems = (piece_send, piece_recv)

    def pieces_of(index, own, view):
        return Pieces(peers, send, piece_sems, own_sems, index, own, view)

    gate_all = pieces_of(0, lambda: gate_own, lambda k: gate_pieces.at[k])
    loads["total"].wait()
    gate_all.give()

    loads["act"].wait()
    for j, n in ((0, rank), (1, 2 * nstate)):
        weights = lax.dot_general(
            low_grad[j], act_low[...], (((0,), (0,)), ((), ())), preferred_element_type=F32
        )
        small[j * rank : j * rank + n, :] = weights[:n]

    natural = pre_low
    loads["masks"].wait()
    loads["normed"].wait()
    masks[:, total:, :] = jnp.zeros((3, pad, LANES), F32)
    grad[total:, :] = jnp.zeros((pad, chunk), F32)
    for slot in range(2):
        inner[slot, :pad, :] = jnp.zeros((pad, chunk), F32)
    first_tap = first_stride + rank
    ring_sems, few_sems = (ring_send, ring_recv), (few_send, few_recv)

    def block_rows(member, part_of=None):
        start = pl.multiple_of(member * slab, slab)
        if part_of is None:
            return pl.ds(start, slab)
        return pl.ds(start + part_of * (slab // 2), slab // 2)

    def owner(way, step):
        away = half + 1 - step
        return peers.at(away if way == 0 else -away)

    def landing(way, step, c):
        there = held.at[way, step - 1, :, slice(c * chunk, (c + 1) * chunk)]
        return there.at[pl.ds(way * (slab // 2), slab // 2), :] if step == 1 else there

    def arrive(way, step, c):
        there = landing(way, step, c)
        remote(there, there, ring_sems, (way, step - 1, c), peers.ring[way]).wait_recv()

    def ring_step(step, c):
        cols = slice(c * chunk, (c + 1) * chunk)
        for way in range(2):
            member = owner(way, step)
            if step == 1:
                source = wgrad.at[block_rows(member, way), cols]
            else:
                arrive(way, step - 1, c)
                source = held.at[way, step - 2, :, cols]
                if step == 2:
                    here, other = (slice(w * (slab // 2), (w + 1) * (slab // 2)) for w in (way, 1 - way))
                    source[other, :] = wgrad[block_rows(member, 1 - way), cols]
                    source[here, :] = source[here, :] + wgrad[block_rows(member, way), cols]
                else:
                    source[...] = source[...] + wgrad[block_rows(member), cols]
            send(source, landing(way, step, c), ring_sems, (way, step - 1, c), peers.ring[way])

    def fold_rows(value):
        out = value[:GROUP]
        for i in range(1, rows // GROUP):
            out = out + value[i * GROUP : (i + 1) * GROUP]
        return out

    for c in range(tiles):
        cols, slot = slice(c * chunk, (c + 1) * chunk), c % 2
        if c + 1 < tiles:
            for copy in tile_copies(c + 1, 1 - slot):
                copy.start()
        for copy in tile_copies(c, slot):
            copy.wait()
        here, there = inner.at[slot], direct.at[slot]
        there[...] += jnp.dot(low_grad[0], few[:rank, cols], preferred_element_type=F32) + jnp.dot(
            low_grad[1], few[rank : rank + LANES, cols], preferred_element_type=F32
        )
        tap = [few[first_tap : first_tap + 16, cols].astype(F32)[i : i + 1] for i in range(5)]

        def back(i, tallies):
            start = pl.multiple_of(i * rows, rows)
            at = pl.ds(start, rows)
            now = here[pl.ds(pad + start, rows), :]
            earlier = [
                here[pl.ds(pad - shift * GROUP + start, rows), :] * tiled(masks[shift - 1, at, :], chunk)
                for shift in range(1, 4)
            ]
            value = tap[4] + tap[3] * now
            for shift in range(1, 4):
                value = value + tap[3 - shift] * earlier[shift - 1]
            sig = sigmoid(value)
            flow = there[at, :] * (sig * (1.0 + value * (1.0 - sig)))
            grad[at, :] = flow
            terms = [flow * e for e in earlier[::-1]] + [flow * now, flow]
            return tuple(tally + fold_rows(term) for tally, term in zip(tallies, terms))

        zero = jnp.zeros((GROUP, chunk), F32)
        tallies = lax.fori_loop(0, total // rows, back, (zero,) * 5)
        for i, tally in enumerate(tallies):
            small[first_tap + i : first_tap + i + 1, cols] = jnp.sum(tally, axis=0, keepdims=True)

        @pl.loop(0, total // rows)
        def _(i):
            start = pl.multiple_of(i * rows, rows)
            at = pl.ds(start, rows)
            value = tap[3] * grad[at, :]
            for shift in range(1, 4):
                after_it = pl.ds(start + shift * GROUP, rows)
                value = value + tap[3 - shift] * (
                    grad[after_it, :] * tiled(masks[shift - 1, after_it, :], chunk)
                )
            inner_grad[at, cols] = value.astype(BF16)
            for k in range(chunk // LANES):
                nat[k, at, :] = value[:, k * LANES : (k + 1) * LANES]

        for k in range(chunk // LANES):
            lanes = slice(c * chunk + k * LANES, c * chunk + (k + 1) * LANES)
            for s in range(GROUP):
                natural[s * length : (s + 1) * length, lanes] = nat[
                    k, pl.ds(s, length, stride=GROUP), :
                ].astype(BF16)
        wgrad[:, cols] = lax.dot_general(
            normed[...], inner_grad[:, cols], (((0,), (0,)), ((), ())), preferred_element_type=F32
        ).astype(BF16)
        ring_step(1, c)
        if c >= 2:
            ring_step(2, c - 2)

    few_half = small.shape[0] // 2

    def few_columns(member):
        return pl.ds(pl.multiple_of(member * LANES, LANES), LANES)

    def few_landing(way, step):
        there = small_held.at[way, step - 1]
        return there.at[pl.ds(way * few_half, few_half), :] if step == 1 else there

    def few_arrive(way, step):
        there = few_landing(way, step)
        remote(there, there, few_sems, (way, step - 1), peers.ring[way]).wait_recv()

    def few_step(step):
        for way in range(2):
            columns = few_columns(owner(way, step))
            here, other = (slice(w * few_half, (w + 1) * few_half) for w in (way, 1 - way))
            if step == 1:
                source = small_low.at[pl.ds(way * few_half, few_half), columns]
            else:
                few_arrive(way, step - 1)
                source = small_held.at[way, step - 2]
                if step == 2:
                    source[other, :] = small_low[other, columns]
                    source[here, :] = (
                        source[here, :].astype(F32) + small_low[here, columns].astype(F32)
                    ).astype(BF16)
                else:
                    source[...] = (source[...].astype(F32) + small_low[:, columns].astype(F32)).astype(BF16)
            send(source, few_landing(way, step), few_sems, (way, step - 1), peers.ring[way])

    half_model = model // 2

    def norm_half(i):
        cols = pl.ds(i * half_model, half_model)
        return Parts(
            peers, send, (part_send, part_recv), norm_parts.at[:, cols], norm_near.at[:, :, cols],
            norm_far.at[:, cols], quarter, 3 * i,
        )

    norm_sums = [norm_half(i) for i in range(2)]
    near_copies = [
        pltpu.make_async_copy(norm_sums[i].near.at[1], near_at.at[i], w_sems.at[2 + i]) for i in range(2)
    ]
    norm_tiles(w_inner, natural, 0, w_count // 2, True)
    norm_sums[0].start()
    norm_tiles(w_inner, natural, w_count // 2, w_count - w_count // 2, True)
    norm_sums[1].start()
    norm_sums[0].come_near()
    near_copies[0].start()
    ring_step(2, 2)
    near_copies[0].wait()
    norm_sums[0].go_far(near_at.at[0])
    norm_sums[1].come_near()
    near_copies[1].start()
    ring_step(2, 3)
    near_copies[1].wait()
    norm_sums[1].go_far(near_at.at[1])

    loads["sums"].wait()
    at = first_tap + 5
    small[at : at + 1, :] = jnp.sum(sums[nstate + 1], axis=0, keepdims=True)
    for n in range(nstate):
        small[at + 1 + n : at + 2 + n, :] = LN2 * jnp.sum(sums[n], axis=0, keepdims=True)
    at = at + 1 + nstate
    small[at : at + 1, :] = jnp.sum(sums[nstate], axis=0, keepdims=True)
    small[at + 1 :, :] = jnp.zeros((small.shape[0] - at - 1, width), F32)
    small_low[...] = small[...].astype(BF16)
    few_step(1)
    for c in range(tiles):
        ring_step(3, c)
    few_step(2)
    few_step(3)
    own_rows = block_rows(peers.member)
    owns = [
        pltpu.make_async_copy(w_inner.at[own_rows, :], w_tiles.at[0], w_sems.at[0]),
        pltpu.make_async_copy(w_gate.at[own_rows, :], w_tiles.at[1], w_sems.at[1]),
        pltpu.make_async_copy(norm_parts.at[pl.ds(0, quarter), :], norm_own, w_sems.at[2]),
    ]
    for copy in owns:
        copy.start()
    for c in range(tiles):
        ring_step(4, c)
    few_step(4)
    gate_all.pass_on()

    def cols_of(c):
        return slice(c * chunk, (c + 1) * chunk)

    inner_all = [
        pieces_of(
            1 + c, lambda c=c: total_at.at[:, cols_of(c)], lambda k, c=c: inner_pieces.at[k, :, cols_of(c)]
        )
        for c in range(tiles)
    ]
    own_block = block_rows(peers.member)
    for c in range(tiles):
        for way in range(2):
            arrive(way, half, c)
        value = wgrad[own_block, cols_of(c)].astype(F32)
        for way in range(2):
            value = value + held[way, half - 1, :, cols_of(c)].astype(F32)
        total_at[:, cols_of(c)] = value.astype(BF16)
        inner_all[c].give()
    for way in range(2):
        few_arrive(way, half)
    value = small_low[:, few_columns(peers.member)].astype(F32)
    for way in range(2):
        value = value + small_held[way, half - 1].astype(F32)
    small_total = small_pieces.at[0]
    small_total[...] = value.astype(BF16)
    for copy in owns:
        copy.wait()
    value = total_at[...].astype(F32) * w_tiles[0].astype(F32)
    value = value + gate_own[...].astype(F32) * w_tiles[1].astype(F32)
    high = value.astype(BF16)
    low = (value - high.astype(F32)).astype(BF16)
    ones = jnp.ones((GROUP, width), BF16)
    nt = (((1,), (1,)), ((), ()))
    value = lax.dot_general(ones, high, nt, preferred_element_type=F32) + lax.dot_general(
        ones, low, nt, preferred_element_type=F32
    )
    gain_at = first_tap + 7 + nstate
    last = small_total[gain_at - gain_at % 16 :, :].astype(F32)
    line = lax.broadcasted_iota(jnp.int32, last.shape, 0) + (gain_at - gain_at % 16)
    for i in range(slab // LANES):
        last = jnp.where(line == gain_at + i, value[0:1, i * LANES : (i + 1) * LANES], last)
    small_total[gain_at - gain_at % 16 :, :] = last.astype(BF16)
    small_all = Pieces(
        peers, send, piece_sems, None, 1 + tiles, lambda: small_total, lambda k: small_pieces.at[k], False
    )
    small_all.give()
    for pieces in (*inner_all, small_all):
        pieces.pass_on()
    for norm_sum in norm_sums:
        norm_sum.come()
    for pieces in (gate_all, *inner_all, small_all):
        pieces.come()
    send.wait()


def finish(size, rank, nstate, arrays, small_rows):
    (pre_low, coef, direct, inner, act_low, step_low, masks, few, normed) = arrays[:9]
    total, width = pre_low.shape
    model = normed.shape[1]
    sums, gate_total = arrays[-2:]
    slab = gate_total.shape[0]
    quarter, half = total // COPIES, size // 2
    inside, anywhere = pl.BlockSpec(memory_space=pltpu.VMEM), pl.BlockSpec(memory_space=pl.ANY)
    shape, dma = jax.ShapeDtypeStruct, pltpu.SemaphoreType.DMA
    low = shape((total, width), BF16)
    wide = shape((total, model), BF16)
    part = shape((quarter, model), BF16)
    padded = total + 3 * GROUP
    scratch = [
        low,
        shape((2, total, LANES), F32),
        shape((2, total, LANES), F32),
        shape((2, 2, quarter, LANES), F32),
        shape((2, quarter, LANES), BF16),
        shape((2, quarter, LANES), BF16),
        shape((COPIES, 2, quarter, LANES), BF16),
        shape((2, total, LANES), BF16),
        low,
        shape(step_low.shape, BF16),
        shape((3, padded, LANES), F32),
        shape(few.shape, BF16),
        wide,
        low,
        low,
        shape((2, padded, 256), F32),
        shape((2, total, 256), F32),
        shape((padded, 256), F32),
        shape((size * slab, width), BF16),
        shape((2, half, slab, width), BF16),
        shape((small_rows, width), F32),
        shape((small_rows, width), BF16),
        shape((2, half, small_rows, LANES), BF16),
        wide,
        shape((2, quarter, model // 2), BF16),
        shape((2, 256, width), BF16),
        shape((slab, width), BF16),
        shape((slab, width), BF16),
        shape(sums.shape, F32),
    ]
    tiles = width // 256
    sems = [(10,), (2, 2), (4,)] + [(6,)] * 2 + [(6,)] * 2 + [(2, half, tiles)] * 2 + [(2, half)] * 2
    sems += [(2 + tiles, 3)] * 2 + [(1 + tiles,)]
    return pl.pallas_call(
        functools.partial(finish_kernel, size, rank, nstate),
        in_specs=[anywhere] * len(arrays),
        out_specs=[anywhere] * 5 + [inside],
        out_shape=[
            shape((COPIES, slab, width), BF16),
            shape((COPIES, slab, width), BF16),
            part,
            shape((2,) + part.shape, BF16),
            part,
            shape((COPIES, small_rows, LANES), BF16),
        ],
        scratch_shapes=[pltpu.VMEM(x.shape, x.dtype) for x in scratch] + [dma(n) for n in sems],
        compiler_params=pltpu.CompilerParams(
            collective_id=2, has_side_effects=True, vmem_limit_bytes=62 * 1024 * 1024
        ),
        cost_estimate=cost(10 * total * width * model, 100 * total * width),
        name="finish",
    )(*arrays)


def place_kernel(
    sizes, copy_ref, inner_ref, gate_ref, out_ref, small_ref, out_own, out_near, out_far, norm_own, norm_near, norm_far,
    tokens_ref, grads_ref, few_ref,
    entry_ref, out_proj_ref, select_ref, stride_ref, taps_ref, decay_ref, rows_ref, block_out_ref, input_grad_ref,
):
    copy = copy_ref[0]
    width = inner_ref.shape[2]
    for k in range(COPIES):
        for side, ref in enumerate((inner_ref, gate_ref)):
            for f in range(width // LANES):
                start = (side * (width // LANES) + f) * COPIES * LANES + (copy ^ k) * LANES
                entry_ref[:, pl.ds(pl.multiple_of(start, LANES), LANES)] = ref[
                    k, :, f * LANES : (f + 1) * LANES
                ].astype(F32)
        out_proj_ref[copy ^ k] = out_ref[k].astype(F32)

    @pl.when(pl.program_id(0) == 0)
    def _():
        for k in range(COPIES):
            piece = small_ref[k].astype(F32)
            at = pl.ds(pl.multiple_of((copy ^ k) * LANES, LANES), LANES)
            stride_ref[at, :] = piece[sizes[0] : sizes[0] + sizes[1]].T
            start = 0
            for size, ref in zip(sizes, (select_ref, None, taps_ref, None, None, decay_ref)):
                if ref is not None:
                    ref[:, at] = piece[start : start + size]
                start += size
            first = start - start % 8
            low_row = sizes[0] + sizes[1]
            rows_ref[:, at] = jnp.concatenate(
                [piece[low_row : low_row + 8], piece[first : first + 8]], axis=0
            )

    tokens = tokens_ref[...].astype(F32)
    summed = out_own[...].astype(F32) + out_near[0].astype(F32) + out_far[...].astype(F32)
    block_out_ref[...] = (tokens + summed).astype(BF16)
    gains = few_ref[...].astype(F32)
    start = sum(sizes) - (sizes[0] + sizes[1])
    gain = jnp.concatenate(
        [
            gains[start + i : start + i + 1, f * LANES : (f + 1) * LANES]
            for f in range(width // LANES)
            for i in range(tokens.shape[1] // width)
        ],
        axis=1,
    )
    scale = lax.rsqrt(jnp.mean(tokens * tokens, axis=-1, keepdims=True) + EPS)
    summed = norm_own[...].astype(F32) + norm_near[0].astype(F32) + norm_far[...].astype(F32)
    scaled = summed * gain
    lean = jnp.mean(scaled * tokens, axis=-1, keepdims=True)
    input_grad_ref[...] = (
        grads_ref[...].astype(F32) + scale * scaled - tokens * (scale * scale * scale) * lean
    ).astype(BF16)


def place(copy, sizes, inner, gate, out, small, out_terms, norm_terms, tokens, grads, few):
    steps = 2
    _, slab, width = inner.shape
    part, model = out.shape[1:]
    rows = tokens.shape[0]
    share = COPIES * LANES

    def cut_rows(total, columns):
        return pl.BlockSpec((total // steps, columns), lambda i, copy: (i, 0))

    def pieces(total, columns):
        return pl.BlockSpec((COPIES, total // steps, columns), lambda i, copy: (0, i, 0))

    def fixed(*shape):
        return pl.BlockSpec(shape, lambda i, copy: (0,) * len(shape))

    first = sizes[0] + sizes[1]
    last = few.shape[0] - first
    shape = jax.ShapeDtypeStruct
    narrow = [(sizes[0], share), (share, sizes[1]), (sizes[2], share), (sizes[5], share)]
    token_rows = cut_rows(rows, model)
    near_rows = pl.BlockSpec((1, rows // steps, model), lambda i, copy: (0, i, 0))
    return pl.pallas_call(
        functools.partial(place_kernel, sizes),
        grid_spec=pltpu.PrefetchScalarGridSpec(
            num_scalar_prefetch=1,
            grid=(steps,),
            in_specs=[pieces(slab, width)] * 2
            + [pieces(part, model), fixed(*small.shape)]
            + [token_rows, near_rows, token_rows] * 2
            + [token_rows] * 2
            + [pl.BlockSpec((last, width), lambda i, copy: (first // last, 0))],
            out_specs=[cut_rows(slab, 2 * COPIES * width), pieces(part, model)]
            + [fixed(*n) for n in narrow]
            + [fixed(16, share)]
            + [token_rows] * 2,
        ),
        out_shape=[
            shape((slab, 2 * COPIES * width), F32),
            shape(out.shape, F32),
        ]
        + [shape(n, F32) for n in narrow]
        + [shape((16, share), F32)]
        + [shape(tokens.shape, BF16)] * 2,
        compiler_params=params(),
        cost_estimate=cost(40 * rows * model, 20 * slab * width),
        name="place",
    )(copy, inner, gate, out, small, *out_terms, *norm_terms, tokens, grads, few)


def on_device(
    tokens, segment_ids, out_grad, norm_gain, in_proj, conv_weight, conv_bias, x_proj,
    step_proj, step_bias, decay_log, skip_gain, out_proj, *, fsdp,
):
    ring = Ring(fsdp)
    copy = lax.axis_index("rep")
    batches, length, model = tokens.shape
    total = COPIES * batches * length
    slab = in_proj.shape[0]
    share = out_proj.shape[0]
    part = share // COPIES
    width = fsdp * part
    rank, nstate = step_proj.shape[1], decay_log.shape[1]
    taps_n = conv_weight.shape[1]
    gains_n = slab // part

    def mine(value):
        return lax.dynamic_slice_in_dim(value, copy * part, part, 0)

    copy_index = copy.astype(jnp.int32).reshape(1)
    aligned = part % LANES == 0
    if not aligned:
        entry = lax.dynamic_index_in_dim(
            in_proj.reshape(slab, 2, fsdp, COPIES, part), copy, 3, keepdims=False
        )
        inner_shard, gate_shard = (entry[:, i].reshape(slab, width) for i in range(2))
    few = jnp.concatenate(
        [
            mine(x_proj).T,
            mine(step_proj).T,
            mine(conv_weight).T,
            mine(conv_bias)[None],
            mine(step_bias)[None],
            mine(decay_log).T,
            mine(skip_gain)[None],
            norm_gain.reshape(gains_n, part),
        ],
        axis=0,
    )
    few = jnp.pad(few, ((0, -few.shape[0] % 16), (0, 0)))
    small_ring = ring.half == 4
    own = [tokens, out_grad, segment_ids[:, 0, :]]
    fused = small_ring and aligned
    if fused:
        out = forward(fsdp, rank, nstate, in_proj, few, *own, out_proj)
        few_all = out["few"].astype(F32)
    else:
        gathers = [Gather(ring, inner_shard), Gather(ring, few)]
        for gather in gathers:
            gather.rest()
        inner_in, few_all = (gather.whole for gather in gathers)
        few_all = jnp.moveaxis(few_all, 0, 1).reshape(-1, width).astype(F32)
        copies = [jnp.stack(rep_gather(value)) for value in own]
        inner_in = inner_in.reshape(model, width)
        values, cotangent, segments = (c.reshape((GROUP,) + c.shape[2:]) for c in copies)

    sizes = [rank + 2 * nstate, rank, taps_n, 1, 1, nstate, 1, gains_n]
    pieces, start = [], 0
    for size in sizes:
        pieces.append(few_all[start : start + size])
        start += size
    select, stride, taps, shift_bias, size_bias, decay, skip, gain = pieces
    select, stride = select.astype(BF16), stride.astype(BF16)
    gain = jnp.moveaxis(gain.reshape(gains_n, fsdp, part), 0, 1).reshape(model)

    def masks_of(segments):
        masks = []
        for shift in range(1, taps_n):
            earlier = jnp.pad(segments, ((0, 0), (shift, 0)), constant_values=-1)[:, :length]
            masks.append((earlier == segments).astype(F32).T.reshape(total, 1))
        return jnp.broadcast_to(jnp.stack(masks), (taps_n - 1, total, LANES))

    tap_rows = jnp.concatenate([taps, shift_bias, jnp.zeros((7 - taps_n, width), F32)])
    side_rows = jnp.concatenate([size_bias, skip, jnp.zeros((6, width), F32)])
    decay_rate = -jnp.exp(decay)

    if fused:
        (
            masks, rate, spread_by, fold_by, normed, cotangent, inner_in, inner, act, act_low, step_low, coef, step,
            states, gate, readout, gated, gated_natural, gate_in, out_w,
        ) = (
            out[k]
            for k in (
                "masks", "rate", "spread_by", "fold_by", "normed", "cotangent", "inner_in", "inner", "act", "act_low",
                "step_low", "coef", "step", "states", "gate", "readout", "gated", "gated_natural", "gate_in", "out_w",
            )
        )
    else:
        rate = jnp.broadcast_to((decay_rate * LOG2E)[:, None, :], (nstate, GROUP, width))
        masks, spread_by, fold_by = masks_of(segments), spreader(nstate), folder(nstate)
        normed, cotangent = interleave(values, gain), interleave(cotangent)
        gathers = [Gather(ring, gate_shard), Gather(ring, mine(out_proj))]
        for gather in gathers:
            gather.rest()
        gate_in = gathers[0].whole.reshape(model, width)
        out_w = gathers[1].whole.reshape(width, model)
        inner = dot(normed, inner_in, 1, 0)
        act, act_low = conv_forward(inner, masks, tap_rows)
        half_sums = sum_near(by_copy(to_sequence(dot(act_low, select, 1, 1))))
        projected = to_time(sum_far(half_sums).reshape(total, -1))
        step_low = projected[:, :rank].astype(BF16)
        coef = spread(projected[:, rank:], nstate)
        pre = dot(step_low, stride, 1, 0)
        readout, step, starts = scan_forward(pre, act, coef, spread_by, masks[0], rate, side_rows)
        gate = dot(normed, gate_in, 1, 0)
        gated, gated_natural = gate_forward(readout, gate)
    if fused:
        gate_grad_natural, pre_low, direct, coef_part, sums, out_pieces, *out_terms, gate_total = backward(
            fsdp, nstate, rank,
            (
                gated, cotangent, out_w, readout, gate, normed, step, act, coef, states, masks, rate, spread_by, fold_by,
                out["few"], gated_natural,
            ),
        )
    else:
        out_wgrad = dot(gated, cotangent, 0, 0).astype(BF16).reshape(fsdp, part, model)
        read_grad, gate_grad, gate_grad_natural = gate_backward(dot(cotangent, out_w, 1, 1), readout, gate)
        gate_wgrad = dot(normed, gate_grad, 0, 0).astype(BF16).reshape(fsdp, slab, width)
        pre_low, direct, coef_part, _, sums = scan_backward(
            step, act, read_grad, coef, spread_by, fold_by, masks[0], rate, side_rows, starts
        )
        scatters = [Scatter(ring, out_wgrad), Scatter(ring, gate_wgrad)]
        for scatter in scatters:
            scatter.rest()
        totals = [scatter.total.astype(BF16) for scatter in scatters]
    small_rows = few.shape[0]
    if fused:
        inner_pieces, gate_pieces, *norm_terms, small_pieces = finish(
            fsdp, rank, nstate,
            (
                pre_low, coef_part, direct, inner, act_low, step_low, masks, out["few"], normed, inner_in, gate_in,
                gate_grad_natural, sums, gate_total,
            ),
            small_rows,
        )
        flat = (batches * length, model)
        entry_all, out_all, select_g, stride_g, taps_g, decay_g, rows_g, block_out, input_grad = place(
            copy_index, sizes[:-1], inner_pieces, gate_pieces, out_pieces, small_pieces, out_terms, norm_terms,
            tokens.reshape(flat), out_grad.reshape(flat), out["few"],
        )
        gain_at = sum(sizes[:-1])
        gain_sum = jnp.sum(small_pieces[:, gain_at : gain_at + gains_n].astype(F32), axis=0).reshape(slab)
        return (
            block_out.reshape(tokens.shape),
            input_grad.reshape(tokens.shape),
            gain_sum / norm_gain.astype(F32),
            entry_all,
            taps_g.T,
            rows_g[taps_n],
            select_g.T,
            stride_g,
            rows_g[taps_n + 1],
            decay_g.T,
            rows_g[8 + (gain_at - 1) % 8],
            out_all.reshape(share, model),
        )
    else:
        low_part = dot(pre_low, stride, 1, 1)
        proj_part = jnp.concatenate([low_part, coef_part[:, : 2 * nstate]], axis=1)
        half_sums = sum_near(by_copy(to_sequence(proj_part)))
        proj_time = to_time(sum_far(half_sums).reshape(total, -1).astype(BF16))
        act_grad = direct + dot(proj_time, select, 1, 0)
        inner_grad, inner_grad_natural, conv_sums = conv_backward(inner, act_grad, masks, tap_rows)
        inner_wgrad = dot(normed, inner_grad, 0, 0).astype(BF16).reshape(fsdp, slab, width)
        small = jnp.concatenate(
            [
                dot(proj_time, act_low, 0, 0),
                dot(step_low, pre_low, 0, 0),
                conv_sums[: taps_n + 1],
                jnp.sum(sums[nstate + 1 :], axis=1),
                decay_rate * jnp.sum(sums[:nstate], axis=1),
                jnp.sum(sums[nstate : nstate + 1], axis=1),
            ],
            axis=0,
        )
        small = jnp.pad(small, ((0, small_rows - small.shape[0]), (0, 0))).astype(BF16)
        small = jnp.moveaxis(small.reshape(-1, fsdp, part), 1, 0)
        grads = dot(inner_grad_natural, inner_in, 1, 1) + dot(gate_grad_natural, gate_in, 1, 1)
        sums_of = []
        for parts in (dot(gated_natural, out_w, 1, 0), grads):
            sums_of.append(rep_scatter_far(*rep_scatter_near(by_copy(parts.astype(BF16)))))
        out_sum, normed_sum = sums_of
        scatters = [Scatter(ring, inner_wgrad), Scatter(ring, small)]
        for scatter in scatters:
            scatter.rest()
        totals = [scatter.total.astype(BF16) for scatter in scatters] + totals
        inner_pieces, small_pieces, out_pieces, gate_pieces = (rep_gather(t) for t in totals)

    block_out = (tokens.astype(F32) + out_sum.reshape(tokens.shape)).astype(BF16)
    normed_grad = normed_sum.reshape(tokens.shape)
    own_values = tokens.astype(F32)
    own_scale = lax.rsqrt(jnp.mean(own_values * own_values, axis=-1, keepdims=True) + EPS)
    scaled = normed_grad * gain
    lean = jnp.mean(scaled * own_values, axis=-1, keepdims=True)
    input_grad = (
        out_grad.astype(F32) + own_scale * scaled - own_values * (own_scale**3) * lean
    ).astype(BF16)

    order = jnp.arange(COPIES) ^ copy
    out_all = jnp.stack(out_pieces)[order].reshape(share, model).astype(F32)
    halves = jnp.stack([jnp.stack(inner_pieces), jnp.stack(gate_pieces)])[:, order]
    halves = halves.reshape(2, COPIES, slab, fsdp, part).astype(F32)
    entry_all = jnp.transpose(halves, (2, 0, 3, 1, 4)).reshape(slab, -1)
    gain_sum = jnp.sum(entry_all * in_proj.astype(F32), axis=1)
    gain_grad = gain_sum / norm_gain.astype(F32)
    small_all = jnp.stack(small_pieces)[order].astype(F32)
    small_all = jnp.moveaxis(small_all, 0, 1).reshape(-1, share)
    out, start = [], 0
    for size in sizes[:-1]:
        out.append(small_all[start : start + size])
        start += size
    select_g, stride_g, taps_g, shift_g, size_g, decay_g, skip_g = out
    return (
        block_out,
        input_grad,
        gain_grad,
        entry_all,
        taps_g.T,
        shift_g[0],
        select_g.T,
        stride_g.T,
        size_g[0],
        decay_g.T,
        skip_g[0],
        out_all,
    )


def solution(mesh):
    tokens = P(None, ("fsdp", "rep"), None)
    rows, row = P("fsdp", None), P("fsdp")
    return jax.shard_map(
        functools.partial(on_device, fsdp=mesh.shape["fsdp"]),
        mesh=mesh,
        in_specs=(tokens, tokens, tokens, row, rows, rows, row, rows, rows, row, rows, row, rows),
        out_specs=(tokens, tokens, row, rows, rows, row, rows, rows, row, rows, row, rows),
        check_vma=False,
    )
```
